32 devices in a mesh: section: 2 (over core), wide: 4 (over z), narrow: 4 (over y, x).
Axes of the slice: x: 2, y: 2, z: 4, core: 2. Of those that a mesh axis runs over, the one named last changes fastest.
Arguments:
- inputs: bfloat16 [2, 4096, 1152], P(None, ('wide', 'narrow')), may hold values from -6 to 6
- cotangent: bfloat16 [2, 4096, 1152], P(None, ('wide', 'narrow')), may hold values from -6 to 6
- lengths: int32 [2, 4], P(None, 'wide'), may hold values from 256 to 1024, as said below
- norm_gains: bfloat16 [2, 4, 1152], P('section', None, 'wide'), may hold values from 0.25 to 1.75
- head_gains: bfloat16 [2, 2, 256], P('section', None, 'wide'), may hold values from 0.25 to 1.75
- w_q: bfloat16 [2, 1152, 1024], P('section', 'wide', 'narrow'), may hold values from -0.1875 to 0.1875
- w_kv: bfloat16 [2, 1152, 512], P('section', 'wide'), may hold values from -0.1875 to 0.1875
- w_o: bfloat16 [2, 1024, 1152], P('section', 'narrow', 'wide'), may hold values from -0.1875 to 0.1875
- w_gate_up: bfloat16 [2, 1152, 2, 6912], P('section', 'wide', None, 'narrow'), may hold values from -0.1875 to 0.1875
- w_down: bfloat16 [2, 6912, 1152], P('section', 'narrow', 'wide'), may hold values from -0.078125 to 0.078125
Outputs:
- section_out: bfloat16 [2, 2, 4096, 1152], P('section', None, ('wide', 'narrow'))
- input_grad: float32 [2, 2, 4096, 1152], P('section', None, ('wide', 'narrow'))
- grad_norm_gains: float32 [2, 4, 1152], P('section', None, 'wide')
- grad_head_gains: float32 [2, 2, 256], P('section', None, 'wide')
- grad_w_q: float32 [2, 1152, 1024], P('section', 'wide', 'narrow')
- grad_w_kv: float32 [2, 1152, 512], P('section', 'wide')
- grad_w_o: float32 [2, 1024, 1152], P('section', 'narrow', 'wide')
- grad_w_gate_up: float32 [2, 1152, 2, 6912], P('section', 'wide', None, 'narrow')
- grad_w_down: float32 [2, 6912, 1152], P('section', 'narrow', 'wide')
The draws below stay inside these ranges and needn't reach their ends.
Inputs may be any that keep to these rules, and one draw needn't show every extreme that they name: `lengths`: in every micro-batch the sequence of one wide index, drawn from the seed, has exactly 1024 tokens, and that of another exactly 256.
All inputs are finite; a program needn't handle non-finite values.
Results may differ from the reference program's by a relative error of at most 0.033.
Values may be sent and summed in bfloat16 or wider, within the bound.
A program may use at most 256 MiB of HBM per device.

```python
import jax
import jax.numpy as jnp
from jax import lax

D = 1152
FF = 6912
HEADS = 4
HEAD_DIM = 256
WINDOW = 512
SEQ = 1024
MICRO = 2
TOKENS = 4096
N_WIDE = 4
N_NARROW = 4


def draw_lengths(key, part):
    key = jax.random.fold_in(key, 7)
    base_key, pick_key, other_key = jax.random.split(key, 3)
    drawn = jax.random.randint(base_key, (MICRO, N_WIDE), SEQ // 4, SEQ + 1)
    chosen = jax.random.randint(pick_key, (MICRO, 1), 0, N_WIDE)
    step_over = jax.random.randint(other_key, (MICRO, 1), 1, N_WIDE)
    shortest = (chosen + step_over) % N_WIDE
    columns = jnp.arange(N_WIDE, dtype=jnp.int32)[None, :]
    result = jnp.where(columns == chosen, SEQ, drawn)
    result = jnp.where(columns == shortest, SEQ // 4, result)
    return result.astype(jnp.int32)


def shard_levels(stream_key, shape, cuts, low, high):
    loudness, own = 1.0, jax.random.fold_in(stream_key, 6)
    for axis_at, parts in cuts:
        draws = jnp.exp(jax.random.uniform(jax.random.fold_in(own, axis_at), (parts,), jnp.float32, low / len(cuts), high / len(cuts)))
        loudness = loudness * jnp.repeat(draws, shape[axis_at] // parts).reshape([-1 if axis == axis_at else 1 for axis in range(len(shape))])
    return loudness


def noise(own_key, shape, deviation, reach, cuts=(), kind=jnp.bfloat16):
    level = shard_levels(own_key, shape, cuts, -0.22, 0.18) if cuts else 1.0
    values = jax.random.normal(own_key, shape, jnp.float32) * deviation * level
    return jnp.minimum(jnp.maximum(values, -reach), reach).astype(kind)


def setup_inputs(seed: int = 0) -> dict:
    key_list = jax.random.split(jax.random.key(seed), 11)
    return {
        "inputs": noise(key_list[0], (MICRO, TOKENS, D), 1.0, 6.0, ((1, 16),)),
        "cotangent": noise(key_list[1], (MICRO, TOKENS, D), 1.0, 6.0, ((1, 16),)),
        "lengths": draw_lengths(jax.random.fold_in(key_list[10], 71), 0),
        "norm_gains": jnp.clip(1.0 + 0.15 * jax.random.normal(key_list[3], (2, 4, D), jnp.float32), 0.25, 1.75).astype(jnp.bfloat16),
        "head_gains": jnp.clip(1.0 + 0.15 * jax.random.normal(key_list[4], (2, 2, HEAD_DIM), jnp.float32), 0.25, 1.75).astype(jnp.bfloat16),
        "w_q": noise(key_list[5], (2, D, HEADS * HEAD_DIM), D ** -0.5, 0.1875, ((0, 2), (1, 4), (2, 4))),
        "w_kv": noise(key_list[6], (2, D, 2 * HEAD_DIM), D ** -0.5, 0.1875, ((0, 2), (1, 4))),
        "w_o": noise(key_list[7], (2, HEADS * HEAD_DIM, D), (HEADS * HEAD_DIM) ** -0.5, 0.1875, ((0, 2), (1, 4), (2, 4))),
        "w_gate_up": noise(key_list[8], (2, D, 2, FF), D ** -0.5, 0.1875, ((0, 2), (1, 4), (3, 4))),
        "w_down": noise(key_list[9], (2, FF, D), FF ** -0.5, 0.078125, ((0, 2), (1, 4), (2, 4))),
    }


@jax.custom_vjp
def low(v):
    return lax.optimization_barrier(v.astype(jnp.bfloat16)).astype(jnp.float32)

@jax.custom_vjp
def low_back(v):
    return v

def low_keep(v):
    return (low(v), None)

def low_pass(kept, grad):
    return (grad,)

def back_keep(v):
    return (v, None)

def back_low(kept, grad):
    return (low(grad),)
low.defvjp(low_keep, low_pass)
low_back.defvjp(back_keep, back_low)
EPSILON = 1e-06
NEGATIVE = -1e+30
ROPE_BASE = 10000.0
EXACT = lax.Precision.HIGHEST

def normed(operand, gain_vec):
    return operand * lax.rsqrt(lax.optimization_barrier(jnp.mean(operand * operand, axis=-1, keepdims=True)) + EPSILON) * gain_vec

def tables(row_count, head_width):
    half_width = head_width // 2
    positions = jnp.arange(row_count, dtype=jnp.float32)
    frequency = ROPE_BASE ** (-jnp.arange(half_width, dtype=jnp.float32) * (2.0 / head_width))
    angles = positions[:, None] * frequency[None, :]
    return (jnp.cos(angles), jnp.sin(angles))

def rotate(operand, cosine, sine_table):
    half_width = operand.shape[-1] // 2
    front_half = operand[..., :half_width]
    back_half = operand[..., half_width:]
    return jnp.concatenate([front_half * cosine - back_half * sine_table, back_half * cosine + front_half * sine_table], axis=-1)

def attend(q_rot, k_rot, v_rot, seq_length):
    per_heads = q_rot.shape[1]
    padding = jnp.zeros((WINDOW, HEAD_DIM), jnp.float32)
    key_rows = jnp.concatenate([padding, k_rot], axis=0)
    value_rows = jnp.concatenate([padding, v_rot], axis=0)
    scaling = HEAD_DIM ** (-0.5)

    @jax.checkpoint
    def one_block(block_index):
        offset = block_index * WINDOW
        q_block = lax.dynamic_slice_in_dim(q_rot, offset, WINDOW, 0)
        k_block = lax.dynamic_slice_in_dim(key_rows, offset, 2 * WINDOW, 0)
        v_block = lax.dynamic_slice_in_dim(value_rows, offset, 2 * WINDOW, 0)
        scores = jnp.einsum('qhd,kd->hqk', q_block, k_block, precision=EXACT) * scaling
        rows_at = offset + jnp.arange(WINDOW, dtype=jnp.int32)[:, None]
        cols_at = offset - WINDOW + jnp.arange(2 * WINDOW, dtype=jnp.int32)[None, :]
        visible = (cols_at <= rows_at) & (rows_at - cols_at < WINDOW) & (cols_at >= 0) & ((cols_at < seq_length) | (cols_at == rows_at))
        scores = low_back(jnp.where(visible[None], scores, NEGATIVE))
        maximum = lax.optimization_barrier(jnp.max(scores, axis=-1, keepdims=True))
        exponent = jnp.exp(scores - maximum)
        probabilities = low(exponent / lax.optimization_barrier(jnp.sum(exponent, axis=-1, keepdims=True)))
        return jnp.einsum('hqk,kd->qhd', probabilities, v_block, precision=EXACT)
    blocks_out = lax.map(one_block, jnp.arange(SEQ // WINDOW, dtype=jnp.int32))
    return blocks_out.reshape(SEQ, per_heads, HEAD_DIM)

def layer(layer_in, seq_length, params):
    norm_gain, head_gain, w_query, w_keyval, w_out, w_gateup, w_downp = params
    per_heads = HEADS // N_NARROW
    group_width = per_heads * HEAD_DIM
    cosine, sine_table = tables(SEQ, HEAD_DIM)
    normed_in = low(normed(layer_in, norm_gain[0]))
    q_raw = low_back(jnp.dot(normed_in, w_query, precision=EXACT))
    kv_raw = jnp.dot(normed_in, w_keyval, precision=EXACT)
    pieces = []
    for group_index in range(N_NARROW):
        kv_use = low_back(kv_raw)
        queries = q_raw[:, group_index * group_width:(group_index + 1) * group_width].reshape(SEQ, per_heads, HEAD_DIM)
        q_rot = low(rotate(normed(queries, head_gain[0]), cosine[:, None, :], sine_table[:, None, :]))
        k_rot = low(rotate(normed(kv_use[:, :HEAD_DIM], head_gain[1]), cosine, sine_table))
        v_rot = low(kv_use[:, HEAD_DIM:])
        attn_group = attend(q_rot, k_rot, v_rot, seq_length)
        pieces.append(low(low_back(attn_group)).reshape(SEQ, group_width))
    attn_all = jnp.concatenate(pieces, axis=1)
    branch_a = low_back(jnp.dot(attn_all, w_out, precision=EXACT))
    hidden_res = layer_in + normed(branch_a, norm_gain[1])
    normed_mid = low(normed(hidden_res, norm_gain[2]))
    gate_up = low_back(jnp.einsum('sd,dcf->scf', normed_mid, w_gateup, precision=EXACT))
    product = low(jax.nn.gelu(gate_up[:, 0], approximate=True) * gate_up[:, 1])
    branch_f = low_back(jnp.dot(product, w_downp, precision=EXACT))
    return hidden_res + normed(branch_f, norm_gain[3])

def reference(inputs, cotangent, lengths, norm_gains, head_gains, w_q, w_kv, w_o, w_gate_up, w_down):
    seq_count = MICRO * N_WIDE
    first_in = inputs.astype(jnp.float32).reshape(seq_count, SEQ, D)
    seq_lengths = lengths.reshape(seq_count).astype(jnp.int32)
    real_rows = (jnp.arange(SEQ, dtype=jnp.int32)[None, :] < seq_lengths[:, None]).astype(jnp.float32)
    cot_rows = cotangent.astype(jnp.float32).reshape(seq_count, SEQ, D) * real_rows[:, :, None]
    stacked = (norm_gains, head_gains, w_q, w_kv, w_o, w_gate_up, w_down)
    params_first = tuple((member[0].astype(jnp.float32) for member in stacked))
    params_second = tuple((member[1].astype(jnp.float32) for member in stacked))
    middle = lax.map(lambda seq_pair: low(layer(seq_pair[0], seq_pair[1], params_first)), (first_in, seq_lengths))

    def backward(params, layer_inputs, cot_inputs):

        def one_seq(running, packed):
            layer_in, seq_length, cot_in = packed
            layer_out, pullback = jax.vjp(lambda input_rows, param_set: layer(input_rows, seq_length, param_set), layer_in, params)
            grad_in, grad_params = pullback(cot_in)
            return (jax.tree.map(jnp.add, running, grad_params), (layer_out, grad_in))
        start_total = jax.tree.map(jnp.zeros_like, params)
        return lax.scan(one_seq, start_total, (layer_inputs, seq_lengths, cot_inputs))
    grads_second, (last_out, grad_middle) = backward(params_second, middle, cot_rows)
    grads_first, (unused_out, grad_first) = backward(params_first, first_in, low(grad_middle))
    shape_out = (2, MICRO, TOKENS, D)
    section_out = jnp.stack([middle, last_out]).reshape(shape_out).astype(jnp.bfloat16)
    input_grad = jnp.stack([grad_first, grad_middle]).reshape(shape_out)
    return (section_out, input_grad, jnp.stack([grads_first[0], grads_second[0]]), jnp.stack([grads_first[1], grads_second[1]]), jnp.stack([grads_first[2], grads_second[2]]), jnp.stack([grads_first[3], grads_second[3]]), jnp.stack([grads_first[4], grads_second[4]]), jnp.stack([grads_first[5], grads_second[5]]), jnp.stack([grads_first[6], grads_second[6]]))
```

```python
import functools

import jax
import jax.numpy as jnp
from jax import lax
from jax.experimental import pallas as pl
from jax.experimental.pallas import tpu as pltpu
from jax.sharding import PartitionSpec as P

WINDOW = 512
EPSILON = 1e-06
NEGATIVE = -1e30
ROPE_BASE = 10000.0
MESH = pl.DeviceIdType.MESH
MIB = 2**20
GAIN_ROWS = 16
F32 = jnp.float32
BF16 = jnp.bfloat16


def dot(a, b, dims):
    return lax.dot_general(a, b, ((dims[0], dims[1]), ((), ())), preferred_element_type=F32)


def nn(a, b):
    return dot(a, b, ((1,), (0,)))


def nt(a, b):
    return dot(a, b, ((1,), (1,)))


def tn(a, b):
    return dot(a, b, ((0,), (0,)))


def normed(operand, gain_vec):
    return (
        operand
        * lax.rsqrt(jnp.mean(operand * operand, axis=-1, keepdims=True) + EPSILON)
        * gain_vec
    )


def geglu(gate, up):
    return jax.nn.gelu(gate, approximate=True) * up


def neighbours():
    me = lax.axis_index("narrow")
    return me, jnp.bitwise_xor(me, 1), jnp.bitwise_xor(me, 2)


def meet(nx, ny):
    barrier = pltpu.get_barrier_semaphore()
    for other in (nx, ny):
        pl.semaphore_signal(barrier, inc=1, device_id={"narrow": other}, device_id_type=MESH)
    pl.semaphore_wait(barrier, 2)


def remote(src, dst, send_sem, recv_sem, other):
    return pltpu.make_async_remote_copy(
        src_ref=src,
        dst_ref=dst,
        send_sem=send_sem,
        recv_sem=recv_sem,
        device_id={"narrow": other},
        device_id_type=MESH,
    )


def gather_kernel(a_ref, o_ref, local_sem, send, recv):
    me, nx, ny = neighbours()
    half = a_ref.shape[0] // 2
    first, second = pl.ds(0, half), pl.ds(half, half)
    meet(nx, ny)
    to_x1 = remote(a_ref.at[first], o_ref.at[me, first], send.at[0], recv.at[0], nx)
    to_y2 = remote(a_ref.at[second], o_ref.at[me, second], send.at[1], recv.at[1], ny)
    to_x2 = remote(a_ref.at[second], o_ref.at[me, second], send.at[2], recv.at[2], nx)
    to_y1 = remote(a_ref.at[first], o_ref.at[me, first], send.at[3], recv.at[3], ny)
    for copy in (to_x1, to_y2, to_x2, to_y1):
        copy.start()
    own = pltpu.make_async_copy(a_ref, o_ref.at[me], local_sem)
    own.start()
    to_x1.wait_recv()
    on_y = remote(o_ref.at[nx, first], o_ref.at[nx, first], send.at[4], recv.at[4], ny)
    on_y.start()
    to_y2.wait_recv()
    on_x = remote(o_ref.at[ny, second], o_ref.at[ny, second], send.at[5], recv.at[5], nx)
    on_x.start()
    for copy in (to_x2, to_y1, on_y, on_x):
        copy.wait_recv()
    for copy in (to_x1, to_y2, to_x2, to_y1, on_y, on_x):
        copy.wait_send()
    own.wait()


def gather_rows(rows, collective_id):
    count, width = rows.shape
    gathered = pl.pallas_call(
        gather_kernel,
        out_shape=jax.ShapeDtypeStruct((4, count, width), rows.dtype),
        in_specs=[pl.BlockSpec(memory_space=pltpu.VMEM)],
        out_specs=pl.BlockSpec(memory_space=pltpu.VMEM),
        scratch_shapes=[
            pltpu.SemaphoreType.DMA,
            pltpu.SemaphoreType.DMA((6,)),
            pltpu.SemaphoreType.DMA((6,)),
        ],
        compiler_params=pltpu.CompilerParams(
            collective_id=collective_id, has_side_effects=True, vmem_limit_bytes=32 * MIB
        ),
    )(rows)
    return gathered.reshape(4 * count, width)


def reduce_kernel(p_ref, o_ref, land, passing, send, recv):
    me, nx, ny = neighbours()
    diag = jnp.bitwise_xor(me, 3)
    half = p_ref.shape[1] // 2
    first, second = pl.ds(0, half), pl.ds(half, half)
    meet(nx, ny)
    copies = [
        remote(p_ref.at[diag, first], land.at[0], send.at[0], recv.at[0], nx),
        remote(p_ref.at[diag, second], land.at[1], send.at[1], recv.at[1], ny),
        remote(p_ref.at[nx, first], land.at[2], send.at[2], recv.at[2], nx),
        remote(p_ref.at[ny, second], land.at[3], send.at[3], recv.at[3], ny),
    ]
    for copy in copies:
        copy.start()
    copies[0].wait_recv()
    passing[0] = (p_ref[ny, first, :].astype(F32) + land[0].astype(F32)).astype(BF16)
    copies.append(remote(passing.at[0], land.at[4], send.at[4], recv.at[4], ny))
    copies[4].start()
    copies[1].wait_recv()
    passing[1] = (p_ref[nx, second, :].astype(F32) + land[1].astype(F32)).astype(BF16)
    copies.append(remote(passing.at[1], land.at[5], send.at[5], recv.at[5], nx))
    copies[5].start()
    for copy in copies[2:]:
        copy.wait_recv()
    o_ref[first, :] = p_ref[me, first, :].astype(F32) + land[2].astype(F32) + land[4].astype(F32)
    o_ref[second, :] = p_ref[me, second, :].astype(F32) + land[3].astype(F32) + land[5].astype(F32)
    for copy in copies:
        copy.wait_send()


def reduce_rows(parts, collective_id):
    count, width = parts.shape[0] // 4, parts.shape[1]
    return pl.pallas_call(
        reduce_kernel,
        out_shape=jax.ShapeDtypeStruct((count, width), F32),
        in_specs=[pl.BlockSpec(memory_space=pltpu.VMEM)],
        out_specs=pl.BlockSpec(memory_space=pltpu.VMEM),
        scratch_shapes=[
            pltpu.VMEM((6, count // 2, width), BF16),
            pltpu.VMEM((2, count // 2, width), BF16),
            pltpu.SemaphoreType.DMA((6,)),
            pltpu.SemaphoreType.DMA((6,)),
        ],
        compiler_params=pltpu.CompilerParams(
            collective_id=collective_id, has_side_effects=True, vmem_limit_bytes=32 * MIB
        ),
    )(parts.reshape(4, count, width))


def tables(positions, head_width):
    half_width = head_width // 2
    frequency = ROPE_BASE ** (-jnp.arange(half_width, dtype=F32) * (2.0 / head_width))
    angles = positions.astype(F32)[:, None] * frequency[None, :]
    return (jnp.cos(angles), jnp.sin(angles))


def rotate(operand, cosine, sine_table):
    half_width = operand.shape[-1] // 2
    front_half = operand[..., :half_width]
    back_half = operand[..., half_width:]
    return jnp.concatenate(
        [
            front_half * cosine - back_half * sine_table,
            back_half * cosine + front_half * sine_table,
        ],
        axis=-1,
    )


def shape_heads(q_raw, k_raw, head_gain, cosine, sine_table):
    head_width = head_gain.shape[-1]
    queries = q_raw.reshape(q_raw.shape[0], -1, head_width)
    q_rot = rotate(normed(queries, head_gain[0]), cosine[:, None, :], sine_table[:, None, :])
    k_rot = rotate(normed(k_raw, head_gain[1]), cosine, sine_table)
    return (q_rot, k_rot)


def window_of(rows, start):
    padded = jnp.concatenate([jnp.zeros((WINDOW, rows.shape[1]), rows.dtype), rows], axis=0)
    return lax.dynamic_slice_in_dim(padded, start, rows.shape[0] // 4 + WINDOW, 0)


def scores_of(q_bf, k_win, start, length, scaling):
    scores = jnp.einsum("qhd,kd->hqk", q_bf, k_win, preferred_element_type=F32) * scaling
    rows_at = start + jnp.arange(q_bf.shape[0], dtype=jnp.int32)[:, None]
    cols_at = start - WINDOW + jnp.arange(k_win.shape[0], dtype=jnp.int32)[None, :]
    visible = (
        (cols_at <= rows_at)
        & (rows_at - cols_at < WINDOW)
        & (cols_at >= 0)
        & ((cols_at < length) | (cols_at == rows_at))
    )
    return jnp.where(visible[None], scores, NEGATIVE)


def attention_forward(x, length, weights, start, trig):
    gains, head_gains, w_q, w_ot, w_kv = weights[:5]
    head_width = head_gains.shape[-1]
    scaling = head_width ** (-0.5)
    rows = x.shape[0]
    xn = normed(x, gains[0]).astype(BF16)
    q_raw = nn(xn, w_q)
    kv_raw = nn(xn, w_kv)
    q_rot, k_rot = shape_heads(q_raw, kv_raw[:, :head_width], head_gains, *trig)
    q_bf = q_rot.astype(BF16)
    kv_own = jnp.concatenate([k_rot, kv_raw[:, head_width:]], axis=1).astype(BF16)
    kv_win = window_of(gather_rows(kv_own, 0), start)
    k_win, v_win = kv_win[:, :head_width], kv_win[:, head_width:]
    scores = scores_of(q_bf, k_win, start, length, scaling)
    maximum = jnp.max(scores, axis=-1, keepdims=True)
    exponent = jnp.exp(scores - maximum)
    row_total = jnp.sum(exponent, axis=-1, keepdims=True)
    probs = (exponent / row_total).astype(BF16)
    o_bf = jnp.einsum("hqk,kd->qhd", probs, v_win, preferred_element_type=F32)
    o_bf = o_bf.reshape(rows, -1).astype(BF16)
    a = nt(o_bf, w_ot)
    h = x + normed(a, gains[1])
    kept = (x, xn, q_raw, kv_raw[:, :head_width], q_bf, k_win, v_win, maximum + jnp.log(row_total), o_bf, a)
    return h, kept


def attention_backward(dh, length, weights, kept, start, trig):
    gains, head_gains, w_q, w_ot, w_kv = weights[:5]
    x, xn, q_raw, k_raw, q_bf, k_win, v_win, log_totals, o_bf, a = kept
    head_width = head_gains.shape[-1]
    scaling = head_width ** (-0.5)
    rows = x.shape[0]
    _, pull = jax.vjp(normed, a, gains[1])
    da, dg1 = pull(dh)
    da = da.astype(BF16)
    do = nn(da, w_ot).astype(BF16)
    d_w_ot = tn(da, o_bf)
    do = do.reshape(q_bf.shape)
    scores = scores_of(q_bf, k_win, start, length, scaling)
    probs = jnp.exp(scores - log_totals)
    dp = jnp.einsum("qhd,kd->hqk", do, v_win, preferred_element_type=F32)
    ds = (probs * (dp - jnp.sum(probs * dp, axis=-1, keepdims=True))).astype(BF16)
    dqr = jnp.einsum("hqk,kd->qhd", ds, k_win, preferred_element_type=F32) * scaling
    dkr = jnp.einsum("hqk,qhd->kd", ds, q_bf, preferred_element_type=F32) * scaling
    dv = jnp.einsum("hqk,qhd->kd", probs.astype(BF16), do, preferred_element_type=F32)
    dkv_win = jnp.concatenate([dkr, dv], axis=1).astype(BF16)
    dkv_all = jnp.zeros((4 * rows + WINDOW, 2 * head_width), BF16)
    dkv_all = lax.dynamic_update_slice_in_dim(dkv_all, dkv_win, start, 0)
    dkv = reduce_rows(dkv_all[WINDOW:], 1)
    _, pull = jax.vjp(lambda q, k, g: shape_heads(q, k, g, *trig), q_raw, k_raw, head_gains)
    dq, dk, d_head = pull((dqr, dkv[:, :head_width]))
    dq = dq.astype(BF16)
    dkv = jnp.concatenate([dk, dkv[:, head_width:]], axis=1).astype(BF16)
    dxn = nt(dq, w_q) + nt(dkv, w_kv)
    d_w_q = tn(xn, dq)
    d_w_kv = tn(xn, dkv)
    _, pull = jax.vjp(normed, x, gains[0])
    dx, dg0 = pull(dxn)
    return dh + dx, (dg0, dg1, d_head, d_w_q, d_w_ot, d_w_kv)


def feed_forward(h, weights):
    gains, w_gate, w_up, w_dt = weights[0], *weights[5:]
    hn = normed(h, gains[2]).astype(BF16)
    rows = gather_rows(hn, 2)
    gate = nn(rows, w_gate)
    up = nn(rows, w_up)
    act = geglu(gate, up).astype(BF16)
    f = reduce_rows(nt(act, w_dt).astype(BF16), 3)
    out = h + normed(f, gains[3])
    return out, (h, rows, gate.astype(BF16), up.astype(BF16), f)


def feed_backward(dy, weights, kept):
    gains, w_gate, w_up, w_dt = weights[0], *weights[5:]
    h, rows, gate, up, f = kept
    _, pull = jax.vjp(normed, f, gains[3])
    df, dg3 = pull(dy)
    df_rows = gather_rows(df.astype(BF16), 2)
    act, pull = jax.vjp(geglu, gate.astype(F32), up.astype(F32))
    d_w_dt = tn(df_rows, act.astype(BF16)).astype(BF16)
    dgate, dup = pull(nn(df_rows, w_dt))
    dgate, dup = dgate.astype(BF16), dup.astype(BF16)
    dhn = reduce_rows((nt(dgate, w_gate) + nt(dup, w_up)).astype(BF16), 3)
    d_w_gate = tn(rows, dgate).astype(BF16)
    d_w_up = tn(rows, dup).astype(BF16)
    _, pull = jax.vjp(normed, h, gains[2])
    dh, dg2 = pull(dhn)
    return dy + dh, (dg2, dg3, d_w_gate, d_w_up, d_w_dt)


def on_device(
    inputs, cotangent, lengths, norm_gains, head_gains, w_q, w_kv, w_o, w_gate_up, w_down
):
    core = lax.axis_index("section")
    narrow = lax.axis_index("narrow")
    n_narrow = lax.axis_size("narrow")
    is_zero = core == 0
    rows, model = inputs.shape[1], inputs.shape[2]
    block = w_q.shape[1]
    head_width = w_q.shape[2]
    n_wide = lax.axis_size("wide")
    hidden = w_down.shape[1]
    kv_part = w_kv.shape[2] // n_narrow

    def swap(value):
        return lax.ppermute(value, "section", [(0, 1), (1, 0)])

    def by_core(first, second):
        return jnp.where(is_zero, first, second)

    kv_own = lax.dynamic_slice_in_dim(w_kv[0], narrow * kv_part, kv_part, 1)
    pack_width = 2 * head_width + kv_part
    pack = jnp.concatenate([w_q[0], w_o[0].T, kv_own], axis=1)
    gain_rows = jnp.zeros((GAIN_ROWS, pack_width), BF16)
    gain_rows = lax.dynamic_update_slice(gain_rows, norm_gains[0], (0, 0))
    gain_rows = lax.dynamic_update_slice(gain_rows, head_gains[0], (4, 0))
    pack = jnp.concatenate([pack, gain_rows], axis=0)
    pack = lax.all_gather(pack, "wide", axis=0)
    pack = lax.all_gather(pack, "narrow", axis=0)
    pack_peer = swap(pack)

    def unpack(whole):
        body = whole[:, :, :block]
        tail = whole[0, :, block:]

        def columns(first, last):
            return body[..., first:last].transpose(1, 2, 0, 3).reshape(model, -1)

        norm_part = tail[:, :4, :block].transpose(1, 0, 2).reshape(4, model).astype(F32)
        head_part = tail[:, 4:6, : head_width // n_wide].transpose(1, 0, 2).reshape(2, head_width)
        return (
            norm_part,
            head_part.astype(F32),
            columns(0, head_width),
            columns(head_width, 2 * head_width),
            columns(2 * head_width, pack_width),
        )

    attention_own, attention_peer = unpack(pack), unpack(pack_peer)

    w_gate, w_up = w_gate_up[0, :, 0], w_gate_up[0, :, 1]
    came = swap(by_core(w_up, w_gate))
    stays = by_core(w_gate, w_up)
    role = [by_core(stays, came), by_core(came, stays)]
    role = [lax.all_gather(member, "wide", axis=0, tiled=True) for member in role]
    role_peer = [swap(member) for member in role]
    down_own = lax.all_gather(w_down[0].T, "wide", axis=0, tiled=True)
    down_peer = swap(down_own)
    layers = []
    for section in range(2):
        mine = is_zero if section == 0 else jnp.logical_not(is_zero)
        attention = jax.tree.map(
            lambda own, peer: jnp.where(mine, own, peer), attention_own, attention_peer
        )
        layers.append(
            (
                *attention,
                by_core(role[section], role_peer[section]),
                by_core(role_peer[section], role[section]),
                jnp.where(mine, down_own, down_peer),
            )
        )

    start = narrow * rows
    positions = start + jnp.arange(rows, dtype=jnp.int32)
    trig = tables(positions, head_width)
    length = lax.dynamic_index_in_dim(lengths[:, 0], core, 0, keepdims=False)

    x = lax.dynamic_index_in_dim(inputs, core, 0, keepdims=False).astype(F32)
    outs, kept = [], []
    for section in range(2):
        h, kept_a = attention_forward(x, length, layers[section], start, trig)
        x, kept_f = feed_forward(h, layers[section])
        outs.append(x.astype(BF16))
        kept.append((kept_a, kept_f))
        x = outs[-1].astype(F32)

    real = (positions < length).astype(F32)[:, None]
    dy = lax.dynamic_index_in_dim(cotangent, core, 0, keepdims=False).astype(F32) * real
    dxs, grads = [None, None], [None, None]
    for section in (1, 0):
        dh, grads_f = feed_backward(dy, layers[section], kept[section][1])
        dx, grads_a = attention_backward(
            dh, length, layers[section], kept[section][0], start, trig
        )
        dxs[section] = dx
        grads[section] = (grads_a, grads_f)
        dy = dx.astype(BF16).astype(F32)

    role_sums = [None, None]
    for section in (1, 0):
        d_gate, d_up = grads[section][1][2:4]
        total = by_core(d_gate, d_up) + swap(by_core(d_up, d_gate))
        role_sums[section] = lax.psum_scatter(total, "wide", scatter_dimension=0, tiled=True)
    came = swap(by_core(role_sums[1], role_sums[0]))
    stays = by_core(role_sums[0], role_sums[1])
    grad_gate_up = jnp.stack([by_core(stays, came), by_core(came, stays)], axis=1).astype(F32)

    d_downs = [grads[section][1][4] for section in range(2)]
    down_sum = by_core(*d_downs) + swap(by_core(*d_downs[::-1]))
    down_sum = lax.psum_scatter(down_sum, "wide", scatter_dimension=0, tiled=True)
    grad_down = down_sum.T.astype(F32)

    packs = []
    for section in range(2):
        dg0, dg1, d_head, d_w_q, d_w_ot, d_w_kv = grads[section][0]
        dg2, dg3 = grads[section][1][:2]

        def blocks(member):
            return member.astype(BF16).reshape(n_wide, block, n_narrow, -1).transpose(2, 0, 1, 3)

        body = jnp.concatenate([blocks(d_w_q), blocks(d_w_ot), blocks(d_w_kv)], axis=3)
        norm_part = jnp.stack([dg0, dg1, dg2, dg3]).astype(BF16)
        norm_part = norm_part.reshape(4, n_wide, block).transpose(1, 0, 2)
        head_part = d_head.astype(BF16).reshape(2, n_wide, head_width // n_wide).transpose(1, 0, 2)
        tail = jnp.zeros((n_wide, GAIN_ROWS, pack_width), BF16)
        tail = lax.dynamic_update_slice(tail, norm_part, (0, 0, 0))
        tail = lax.dynamic_update_slice(tail, head_part, (0, 4, 0))
        tail = jnp.broadcast_to(tail[None], (n_narrow, *tail.shape))
        packs.append(jnp.concatenate([body, tail], axis=2))
    pack_sum = by_core(*packs) + swap(by_core(*packs[::-1]))
    pack_sum = lax.psum_scatter(pack_sum, "narrow", scatter_dimension=0, tiled=False)
    pack_sum = lax.psum_scatter(pack_sum, "wide", scatter_dimension=0, tiled=False)
    grad_q = pack_sum[:block, :head_width].astype(F32)
    grad_o = pack_sum[:block, head_width : 2 * head_width].T.astype(F32)
    grad_kv = lax.all_gather(
        pack_sum[:block, 2 * head_width :], "narrow", axis=1, tiled=True
    ).astype(F32)
    grad_norm = pack_sum[block : block + 4, :block].astype(F32)
    grad_head = pack_sum[block + 4 : block + 6, : head_width // n_wide].astype(F32)

    def by_section(first, second):
        stays, came = by_core(first, second), swap(by_core(second, first))
        return jnp.stack([by_core(stays, came), by_core(came, stays)])

    return (
        by_section(*outs)[None],
        by_section(*dxs)[None],
        grad_norm[None],
        grad_head[None],
        grad_q[None],
        grad_kv[None],
        grad_o[None],
        grad_gate_up[None],
        grad_down[None],
    )


def solution(mesh):
    return jax.shard_map(
        on_device,
        mesh=mesh,
        in_specs=(
            P(None, ("wide", "narrow"), None),
            P(None, ("wide", "narrow"), None),
            P(None, "wide"),
            P("section", None, "wide"),
            P("section", None, "wide"),
            P("section", "wide", "narrow"),
            P("section", "wide", None),
            P("section", "narrow", "wide"),
            P("section", "wide", None, "narrow"),
            P("section", "narrow", "wide"),
        ),
        out_specs=(
            P("section", None, ("wide", "narrow"), None),
            P("section", None, ("wide", "narrow"), None),
            P("section", None, "wide"),
            P("section", None, "wide"),
            P("section", "wide", "narrow"),
            P("section", "wide", None),
            P("section", "narrow", "wide"),
            P("section", "wide", None, "narrow"),
            P("section", "narrow", "wide"),
        ),
        check_vma=False,
    )
```

```python
import functools

import jax
import jax.numpy as jnp
from jax import lax
from jax.experimental import pallas as pl
from jax.experimental.pallas import tpu as pltpu
from jax.sharding import PartitionSpec as P

WINDOW = 512
EPSILON = 1e-06
NEGATIVE = -1e30
ROPE_BASE = 10000.0
MESH = pl.DeviceIdType.MESH
MIB = 2**20
GAIN_ROWS = 16
F32 = jnp.float32
BF16 = jnp.bfloat16


def dot(a, b, dims):
    return lax.dot_general(a, b, ((dims[0], dims[1]), ((), ())), preferred_element_type=F32)


def nn(a, b):
    return dot(a, b, ((1,), (0,)))


def nt(a, b):
    return dot(a, b, ((1,), (1,)))


def tn(a, b):
    return dot(a, b, ((0,), (0,)))


def normed(operand, gain_vec):
    return (
        operand
        * lax.rsqrt(jnp.mean(operand * operand, axis=-1, keepdims=True) + EPSILON)
        * gain_vec
    )


def geglu(gate, up):
    return jax.nn.gelu(gate, approximate=True) * up


def neighbours():
    me = lax.axis_index("narrow")
    return me, jnp.bitwise_xor(me, 1), jnp.bitwise_xor(me, 2)


def meet(nx, ny):
    barrier = pltpu.get_barrier_semaphore()
    for other in (nx, ny):
        pl.semaphore_signal(barrier, inc=1, device_id={"narrow": other}, device_id_type=MESH)
    pl.semaphore_wait(barrier, 2)


def remote(src, dst, send_sem, recv_sem, other):
    return pltpu.make_async_remote_copy(
        src_ref=src,
        dst_ref=dst,
        send_sem=send_sem,
        recv_sem=recv_sem,
        device_id={"narrow": other},
        device_id_type=MESH,
    )


def gather_kernel(a_ref, o_ref, local_sem, send, recv):
    me, nx, ny = neighbours()
    half = a_ref.shape[0] // 2
    first, second = pl.ds(0, half), pl.ds(half, half)
    meet(nx, ny)
    to_x1 = remote(a_ref.at[first], o_ref.at[me, first], send.at[0], recv.at[0], nx)
    to_y2 = remote(a_ref.at[second], o_ref.at[me, second], send.at[1], recv.at[1], ny)
    to_x2 = remote(a_ref.at[second], o_ref.at[me, second], send.at[2], recv.at[2], nx)
    to_y1 = remote(a_ref.at[first], o_ref.at[me, first], send.at[3], recv.at[3], ny)
    for copy in (to_x1, to_y2, to_x2, to_y1):
        copy.start()
    own = pltpu.make_async_copy(a_ref, o_ref.at[me], local_sem)
    own.start()
    to_x1.wait_recv()
    on_y = remote(o_ref.at[nx, first], o_ref.at[nx, first], send.at[4], recv.at[4], ny)
    on_y.start()
    to_y2.wait_recv()
    on_x = remote(o_ref.at[ny, second], o_ref.at[ny, second], send.at[5], recv.at[5], nx)
    on_x.start()
    for copy in (to_x2, to_y1, on_y, on_x):
        copy.wait_recv()
    for copy in (to_x1, to_y2, to_x2, to_y1, on_y, on_x):
        copy.wait_send()
    own.wait()


def gather_rows(rows, collective_id):
    count, width = rows.shape
    gathered = pl.pallas_call(
        gather_kernel,
        out_shape=jax.ShapeDtypeStruct((4, count, width), rows.dtype),
        in_specs=[pl.BlockSpec(memory_space=pltpu.VMEM)],
        out_specs=pl.BlockSpec(memory_space=pltpu.VMEM),
        scratch_shapes=[
            pltpu.SemaphoreType.DMA,
            pltpu.SemaphoreType.DMA((6,)),
            pltpu.SemaphoreType.DMA((6,)),
        ],
        compiler_params=pltpu.CompilerParams(
            collective_id=collective_id, has_side_effects=True, vmem_limit_bytes=32 * MIB
        ),
    )(rows)
    return gathered.reshape(4 * count, width)


def reduce_kernel(p_ref, o_ref, land, passing, send, recv):
    me, nx, ny = neighbours()
    diag = jnp.bitwise_xor(me, 3)
    half = p_ref.shape[1] // 2
    first, second = pl.ds(0, half), pl.ds(half, half)
    meet(nx, ny)
    copies = [
        remote(p_ref.at[diag, first], land.at[0], send.at[0], recv.at[0], nx),
        remote(p_ref.at[diag, second], land.at[1], send.at[1], recv.at[1], ny),
        remote(p_ref.at[nx, first], land.at[2], send.at[2], recv.at[2], nx),
        remote(p_ref.at[ny, second], land.at[3], send.at[3], recv.at[3], ny),
    ]
    for copy in copies:
        copy.start()
    copies[0].wait_recv()
    passing[0] = (p_ref[ny, first, :].astype(F32) + land[0].astype(F32)).astype(BF16)
    copies.append(remote(passing.at[0], land.at[4], send.at[4], recv.at[4], ny))
    copies[4].start()
    copies[1].wait_recv()
    passing[1] = (p_ref[nx, second, :].astype(F32) + land[1].astype(F32)).astype(BF16)
    copies.append(remote(passing.at[1], land.at[5], send.at[5], recv.at[5], nx))
    copies[5].start()
    for copy in copies[2:]:
        copy.wait_recv()
    one = p_ref[me, first, :].astype(F32) + land[2].astype(F32) + land[4].astype(F32)
    two = p_ref[me, second, :].astype(F32) + land[3].astype(F32) + land[5].astype(F32)
    o_ref[first, :] = one.astype(o_ref.dtype)
    o_ref[second, :] = two.astype(o_ref.dtype)
    for copy in copies:
        copy.wait_send()


def reduce_rows(parts, collective_id, dtype=F32):
    count, width = parts.shape[0] // 4, parts.shape[1]
    return pl.pallas_call(
        reduce_kernel,
        out_shape=jax.ShapeDtypeStruct((count, width), dtype),
        in_specs=[pl.BlockSpec(memory_space=pltpu.VMEM)],
        out_specs=pl.BlockSpec(memory_space=pltpu.VMEM),
        scratch_shapes=[
            pltpu.VMEM((6, count // 2, width), BF16),
            pltpu.VMEM((2, count // 2, width), BF16),
            pltpu.SemaphoreType.DMA((6,)),
            pltpu.SemaphoreType.DMA((6,)),
        ],
        compiler_params=pltpu.CompilerParams(
            collective_id=collective_id, has_side_effects=True, vmem_limit_bytes=32 * MIB
        ),
    )(parts.reshape(4, count, width))


def tables(positions, head_width):
    half_width = head_width // 2
    frequency = ROPE_BASE ** (-jnp.arange(half_width, dtype=F32) * (2.0 / head_width))
    angles = positions.astype(F32)[:, None] * frequency[None, :]
    return (jnp.cos(angles), jnp.sin(angles))


def rotate(operand, cosine, sine_table):
    half_width = operand.shape[-1] // 2
    front_half = operand[..., :half_width]
    back_half = operand[..., half_width:]
    return jnp.concatenate(
        [
            front_half * cosine - back_half * sine_table,
            back_half * cosine + front_half * sine_table,
        ],
        axis=-1,
    )


def shape_heads(q_raw, k_raw, head_gain, cosine, sine_table):
    head_width = head_gain.shape[-1]
    queries = q_raw.reshape(q_raw.shape[0], -1, head_width)
    q_rot = rotate(normed(queries, head_gain[0]), cosine[:, None, :], sine_table[:, None, :])
    k_rot = rotate(normed(k_raw, head_gain[1]), cosine, sine_table)
    return (q_rot, k_rot)


def window_of(rows, start):
    padded = jnp.concatenate([jnp.zeros((WINDOW, rows.shape[1]), rows.dtype), rows], axis=0)
    return lax.dynamic_slice_in_dim(padded, start, rows.shape[0] // 4 + WINDOW, 0)


def scores_of(q_bf, k_win, start, length, scaling):
    scores = jnp.einsum("qhd,kd->hqk", q_bf, k_win, preferred_element_type=F32) * scaling
    rows_at = start + jnp.arange(q_bf.shape[0], dtype=jnp.int32)[:, None]
    cols_at = start - WINDOW + jnp.arange(k_win.shape[0], dtype=jnp.int32)[None, :]
    visible = (
        (cols_at <= rows_at)
        & (rows_at - cols_at < WINDOW)
        & (cols_at >= 0)
        & ((cols_at < length) | (cols_at == rows_at))
    )
    return jnp.where(visible[None], scores, NEGATIVE)


def attention_forward(x, length, weights, start, trig):
    gains, head_gains, w_q, w_ot, w_kv = weights[:5]
    head_width = head_gains.shape[-1]
    scaling = head_width ** (-0.5)
    rows = x.shape[0]
    xn = normed(x, gains[0]).astype(BF16)
    q_raw = nn(xn, w_q)
    kv_raw = nn(xn, w_kv)
    q_rot, k_rot = shape_heads(q_raw, kv_raw[:, :head_width], head_gains, *trig)
    q_bf = q_rot.astype(BF16)
    kv_own = jnp.concatenate([k_rot, kv_raw[:, head_width:]], axis=1).astype(BF16)
    kv_win = window_of(gather_rows(kv_own, 0), start)
    k_win, v_win = kv_win[:, :head_width], kv_win[:, head_width:]
    scores = scores_of(q_bf, k_win, start, length, scaling)
    maximum = jnp.max(scores, axis=-1, keepdims=True)
    exponent = jnp.exp(scores - maximum)
    row_total = jnp.sum(exponent, axis=-1, keepdims=True)
    probs = (exponent / row_total).astype(BF16)
    o_bf = jnp.einsum("hqk,kd->qhd", probs, v_win, preferred_element_type=F32)
    o_bf = o_bf.reshape(rows, -1).astype(BF16)
    a = nt(o_bf, w_ot)
    h = x + normed(a, gains[1])
    kept = (x, xn, q_raw, kv_raw[:, :head_width], q_bf, k_win, v_win, maximum + jnp.log(row_total), o_bf, a)
    return h, kept


def attention_backward(dh, length, weights, kept, start, trig):
    gains, head_gains, w_q, w_ot, w_kv = weights[:5]
    x, xn, q_raw, k_raw, q_bf, k_win, v_win, log_totals, o_bf, a = kept
    head_width = head_gains.shape[-1]
    scaling = head_width ** (-0.5)
    rows = x.shape[0]
    _, pull = jax.vjp(normed, a, gains[1])
    da, dg1 = pull(dh)
    da = da.astype(BF16)
    do = nn(da, w_ot).astype(BF16)
    d_w_ot = tn(da, o_bf)
    do = do.reshape(q_bf.shape)
    scores = scores_of(q_bf, k_win, start, length, scaling)
    probs = jnp.exp(scores - log_totals)
    dp = jnp.einsum("qhd,kd->hqk", do, v_win, preferred_element_type=F32)
    ds = (probs * (dp - jnp.sum(probs * dp, axis=-1, keepdims=True))).astype(BF16)
    dqr = jnp.einsum("hqk,kd->qhd", ds, k_win, preferred_element_type=F32) * scaling
    dkr = jnp.einsum("hqk,qhd->kd", ds, q_bf, preferred_element_type=F32) * scaling
    dv = jnp.einsum("hqk,qhd->kd", probs.astype(BF16), do, preferred_element_type=F32)
    dkv_win = jnp.concatenate([dkr, dv], axis=1).astype(BF16)
    dkv_all = jnp.zeros((4 * rows + WINDOW, 2 * head_width), BF16)
    dkv_all = lax.dynamic_update_slice_in_dim(dkv_all, dkv_win, start, 0)
    dkv = reduce_rows(dkv_all[WINDOW:], 1)
    _, pull = jax.vjp(lambda q, k, g: shape_heads(q, k, g, *trig), q_raw, k_raw, head_gains)
    dq, dk, d_head = pull((dqr, dkv[:, :head_width]))
    dq = dq.astype(BF16)
    dkv = jnp.concatenate([dk, dkv[:, head_width:]], axis=1).astype(BF16)
    dxn = nt(dq, w_q) + nt(dkv, w_kv)
    d_w_q = tn(xn, dq)
    d_w_kv = tn(xn, dkv)
    _, pull = jax.vjp(normed, x, gains[0])
    dx, dg0 = pull(dxn)
    return dh + dx, (dg0, dg1, d_head, d_w_q, d_w_ot, d_w_kv)


GELU_SCALE = 0.7978845608028654
GELU_CUBE = 0.044715


def vmem_spec():
    return pl.BlockSpec(memory_space=pltpu.VMEM)


def any_spec():
    return pl.BlockSpec(memory_space=pl.ANY)


def rows_of(block, count):
    return pl.ds(pl.multiple_of(block * count, count), count)


def columns_of(tile, width, offset=0):
    return pl.ds(pl.multiple_of(tile * width + offset, 128), width)


def inverse_rms(value):
    return lax.rsqrt(jnp.mean(value * value, axis=-1, keepdims=True) + EPSILON)


def normed_gradient(value, gain, grad):
    inverse = inverse_rms(value)
    unit = value * inverse
    scaled = grad * gain
    by_value = inverse * (scaled - unit * jnp.mean(scaled * unit, axis=-1, keepdims=True))
    return by_value, jnp.sum(grad * unit, axis=0, keepdims=True)


class Spread:
    def __init__(self, rows_ref, count, send, recv):
        self.me, self.nx, self.ny = neighbours()
        self.far = jnp.bitwise_xor(self.me, 3)
        half = count // 2

        def part(block, which):
            return rows_ref.at[pl.ds(pl.multiple_of(block * count + which * half, half), half)]

        def copy(block, which, at, other):
            ref = part(block, which)
            return remote(ref, ref, send.at[at], recv.at[at], other)

        self.to_x1 = copy(self.me, 0, 0, self.nx)
        self.to_y2 = copy(self.me, 1, 1, self.ny)
        self.to_x2 = copy(self.me, 1, 2, self.nx)
        self.to_y1 = copy(self.me, 0, 3, self.ny)
        self.on_y = copy(self.nx, 0, 4, self.ny)
        self.on_x = copy(self.ny, 1, 5, self.nx)

    def start(self):
        for copy in (self.to_x1, self.to_y2, self.to_x2, self.to_y1):
            copy.start()

    def pass_on(self):
        self.to_x1.wait_recv()
        self.on_y.start()
        self.to_y2.wait_recv()
        self.on_x.start()

    def x_here(self):
        self.to_x2.wait_recv()

    def y_here(self):
        self.to_y1.wait_recv()

    def far_here(self):
        self.on_y.wait_recv()
        self.on_x.wait_recv()

    def finish(self):
        for copy in (self.to_x1, self.to_y2, self.to_x2, self.to_y1, self.on_y, self.on_x):
            copy.wait_send()


class Fold:
    def __init__(self, parts_ref, count, land, passing, send, recv):
        self.me, self.nx, self.ny = neighbours()
        self.far = jnp.bitwise_xor(self.me, 3)
        self.parts, self.count, self.land, self.passing = parts_ref, count, land, passing
        half = count // 2

        def copy(src, at, other):
            return remote(src, land.at[at], send.at[at], recv.at[at], other)

        self.far_x = copy(self.part(self.far, 0), 0, self.nx)
        self.far_y = copy(self.part(self.far, 1), 1, self.ny)
        self.near_x = copy(self.part(self.nx, 0), 2, self.nx)
        self.near_y = copy(self.part(self.ny, 1), 3, self.ny)
        self.on_y = copy(passing.at[0], 4, self.ny)
        self.on_x = copy(passing.at[1], 5, self.nx)

    def part(self, block, which):
        half = self.count // 2
        return self.parts.at[pl.ds(pl.multiple_of(block * self.count + which * half, half), half)]

    def send_far(self):
        self.far_x.start()
        self.far_y.start()

    def send_near(self):
        self.near_x.start()
        self.near_y.start()

    def pass_on(self):
        self.far_x.wait_recv()
        self.passing[0] = (self.part(self.ny, 0)[...].astype(F32) + self.land[0].astype(F32)).astype(BF16)
        self.on_y.start()
        self.far_y.wait_recv()
        self.passing[1] = (self.part(self.nx, 1)[...].astype(F32) + self.land[1].astype(F32)).astype(BF16)
        self.on_x.start()

    def total(self, own):
        half = self.count // 2
        for copy in (self.near_x, self.near_y, self.on_y, self.on_x):
            copy.wait_recv()
        first = own[:half] + (self.land[2].astype(F32) + self.land[4].astype(F32))
        second = own[half:] + (self.land[3].astype(F32) + self.land[5].astype(F32))
        return jnp.concatenate([first, second], axis=0)

    def finish(self):
        for copy in (self.far_x, self.far_y, self.near_x, self.near_y, self.on_y, self.on_x):
            copy.wait_send()


def greet(*others):
    barrier = pltpu.get_barrier_semaphore()
    for other in others:
        pl.semaphore_signal(barrier, inc=1, device_id=other, device_id_type=MESH)
    return lambda: pl.semaphore_wait(barrier, len(others))


def spread_spec():
    return [pltpu.SemaphoreType.DMA((6,)), pltpu.SemaphoreType.DMA((6,))]


def fold_spec(count, width):
    return [
        pltpu.VMEM((6, count // 2, width), BF16),
        pltpu.VMEM((2, count // 2, width), BF16),
        pltpu.SemaphoreType.DMA((6,)),
        pltpu.SemaphoreType.DMA((6,)),
    ]


def params(collective_id, mib):
    return pltpu.CompilerParams(
        collective_id=collective_id, has_side_effects=True, vmem_limit_bytes=mib * MIB
    )


TILE = 256


def up_kernel(
    h_ref, gain_ref, w_ref, rows_out, gu_out, act_out, rows, w, gu, act, load, store, send, recv
):
    count = h_ref.shape[0]
    hidden = act.shape[1]
    weights = pltpu.make_async_copy(w_ref, w, load)
    weights.start()
    me, nx, ny = neighbours()
    met = greet({"narrow": nx}, {"narrow": ny})
    value = h_ref[...]
    rows[rows_of(me, count), :] = (value * inverse_rms(value) * gain_ref[...]).astype(BF16)
    spread = Spread(rows, count, send, recv)
    met()
    spread.start()
    weights.wait()

    def one(block, at):
        here = rows_of(block, count)

        def tile(j, _):
            left = rows[here, :]
            gate = nn(left, w[:, columns_of(j, TILE)])
            up = nn(left, w[:, columns_of(j, TILE, hidden)])
            inner = jnp.tanh(GELU_SCALE * (gate + GELU_CUBE * (gate * gate * gate)))
            gu[here, columns_of(j, TILE)] = gate.astype(BF16)
            gu[here, columns_of(j, TILE, hidden)] = up.astype(BF16)
            act[here, columns_of(j, TILE)] = (0.5 * gate * (1.0 + inner) * up).astype(BF16)
            return 0

        lax.fori_loop(0, hidden // TILE, tile, 0)
        copies = [
            pltpu.make_async_copy(ref.at[here], out.at[here], store.at[k, at])
            for k, (ref, out) in enumerate(((gu, gu_out), (act, act_out), (rows, rows_out)))
        ]
        for copy in copies:
            copy.start()
        return copies

    copies = one(me, 0)
    spread.pass_on()
    spread.x_here()
    copies += one(nx, 1)
    spread.y_here()
    copies += one(ny, 2)
    spread.far_here()
    copies += one(spread.far, 3)
    spread.finish()
    for copy in copies:
        copy.wait()


def feed_up(h, gain, w_gu, collective_id):
    count, model = h.shape
    hidden = w_gu.shape[1] // 2
    total = 4 * count
    shapes = [(total, model), (total, 2 * hidden), (total, hidden)]
    return pl.pallas_call(
        up_kernel,
        out_shape=[jax.ShapeDtypeStruct(shape, BF16) for shape in shapes],
        in_specs=[vmem_spec(), vmem_spec(), any_spec()],
        out_specs=[any_spec()] * 3,
        scratch_shapes=[
            pltpu.VMEM((total, model), BF16),
            pltpu.VMEM(w_gu.shape, BF16),
            pltpu.VMEM((total, 2 * hidden), BF16),
            pltpu.VMEM((total, hidden), BF16),
            pltpu.SemaphoreType.DMA,
            pltpu.SemaphoreType.DMA((3, 4)),
            *spread_spec(),
        ],
        compiler_params=params(collective_id, 48),
    )(h, gain, w_gu)


def down_kernel(
    h_ref, gain_ref, act_ref, w_ref, x_out, f_out, act, w, parts, load, land, passing, send, recv
):
    count, model = h_ref.shape
    me, nx, ny = neighbours()
    met = greet({"narrow": nx}, {"narrow": ny})
    far = jnp.bitwise_xor(me, 3)
    weights = pltpu.make_async_copy(w_ref, w, load.at[0])
    weights.start()
    arrivals = []
    for at, block in enumerate((far, nx, ny, me)):
        here = rows_of(block, count)
        arrivals.append(pltpu.make_async_copy(act_ref.at[here], act.at[here], load.at[1 + at]))
        arrivals[-1].start()
    fold = Fold(parts, count, land, passing, send, recv)
    weights.wait()
    met()

    def one(block, at):
        arrivals[at].wait()
        return nt(act[rows_of(block, count), :], w[...])

    parts[rows_of(far, count), :] = one(far, 0).astype(BF16)
    fold.send_far()
    parts[rows_of(nx, count), :] = one(nx, 1).astype(BF16)
    parts[rows_of(ny, count), :] = one(ny, 2).astype(BF16)
    fold.send_near()
    f_out[...] = one(me, 3)
    fold.pass_on()
    total = fold.total(f_out[...])
    f_out[...] = total
    x_out[...] = (h_ref[...] + total * inverse_rms(total) * gain_ref[...]).astype(BF16)
    fold.finish()


def feed_down(h, gain, act, w_dt, collective_id):
    count, model = h.shape
    return pl.pallas_call(
        down_kernel,
        out_shape=[
            jax.ShapeDtypeStruct((count, model), BF16),
            jax.ShapeDtypeStruct((count, model), F32),
        ],
        in_specs=[vmem_spec(), vmem_spec(), any_spec(), any_spec()],
        out_specs=[vmem_spec(), vmem_spec()],
        scratch_shapes=[
            pltpu.VMEM(act.shape, BF16),
            pltpu.VMEM(w_dt.shape, BF16),
            pltpu.VMEM((4 * count, model), BF16),
            pltpu.SemaphoreType.DMA((5,)),
            *fold_spec(count, model),
        ],
        compiler_params=params(collective_id, 40),
    )(h, gain, act, w_dt)


def swap_sum(make, tiles, ours, theirs, came, send, recv, out, out_sems):
    other = {"section": 1 - lax.axis_index("section")}
    sends = []
    for at, (first, width) in enumerate(tiles):
        columns = pl.ds(first, width)
        theirs[:, columns] = make(False, first, width).astype(BF16)
        copy = pltpu.make_async_remote_copy(
            src_ref=theirs.at[:, columns],
            dst_ref=came.at[:, columns],
            send_sem=send.at[at],
            recv_sem=recv.at[at],
            device_id=other,
            device_id_type=MESH,
        )
        copy.start()
        sends.append(copy)
    stores = []
    for at, (first, width) in enumerate(tiles):
        columns = pl.ds(first, width)
        own = make(True, first, width)
        sends[at].wait_recv()
        ours[:, columns] = (own + came[:, columns].astype(F32)).astype(BF16)
        copy = pltpu.make_async_copy(ours.at[:, columns], out.at[:, columns], out_sems.at[at])
        copy.start()
        stores.append(copy)
    return sends, stores


def column_tiles(width):
    return [(first, min(TILE, width - first)) for first in range(0, width, TILE)]


def back_up_kernel(
    dy_ref, f_ref, gain_ref, gu_ref, act_ref, w_ref, dgu_out, dw_out, dgain_out,
    df, gu, act, w, ours, theirs, came, load, store, send, recv, swap_send, swap_recv, out_sems,
):
    count, model = dy_ref.shape
    hidden = act.shape[1]
    me, nx, ny = neighbours()
    core = lax.axis_index("section")
    met = greet({"narrow": nx}, {"narrow": ny}, {"section": 1 - core})
    far = jnp.bitwise_xor(me, 3)
    weights = pltpu.make_async_copy(w_ref, w, load.at[0, 0])
    weights.start()
    arrivals = []
    for at, block in enumerate((me, nx, ny, far)):
        here = rows_of(block, count)
        pair = [
            pltpu.make_async_copy(gu_ref.at[here], gu.at[here], load.at[1, at]),
            pltpu.make_async_copy(act_ref.at[here], act.at[here], load.at[2, at]),
        ]
        for copy in pair:
            copy.start()
        arrivals.append(pair)
    by_value, by_gain = normed_gradient(f_ref[...], gain_ref[...], dy_ref[...])
    df[rows_of(me, count), :] = by_value.astype(BF16)
    spread = Spread(df, count, send, recv)
    met()
    spread.start()
    dgain_out[...] = by_gain
    weights.wait()

    def one(block, at):
        here = rows_of(block, count)
        for copy in arrivals[at]:
            copy.wait()

        def tile(j, _):
            dact = nn(df[here, :], w[:, columns_of(j, TILE)])
            gate = gu[here, columns_of(j, TILE)].astype(F32)
            up = gu[here, columns_of(j, TILE, hidden)].astype(F32)
            square = gate * gate
            inner = jnp.tanh(GELU_SCALE * gate * (1.0 + GELU_CUBE * square))
            half = 0.5 * (1.0 + inner)
            slope = half + 0.5 * GELU_SCALE * gate * (1.0 - inner * inner) * (
                1.0 + 3.0 * GELU_CUBE * square
            )
            gu[here, columns_of(j, TILE)] = (dact * up * slope).astype(BF16)
            gu[here, columns_of(j, TILE, hidden)] = (dact * gate * half).astype(BF16)
            return 0

        lax.fori_loop(0, hidden // TILE, tile, 0)
        copy = pltpu.make_async_copy(gu.at[here], dgu_out.at[here], store.at[at])
        copy.start()
        return copy

    copies = [one(me, 0)]
    spread.pass_on()
    spread.x_here()
    copies.append(one(nx, 1))
    spread.y_here()
    copies.append(one(ny, 2))
    spread.far_here()
    copies.append(one(far, 3))

    def make(mine, first, width):
        side = core if mine else 1 - core
        start = pl.multiple_of(side * (hidden // 2) + first, 128)
        return tn(df[...], act[:, pl.ds(start, width)])

    sends, stores = swap_sum(
        make, column_tiles(hidden // 2), ours, theirs, came, swap_send, swap_recv, dw_out, out_sems
    )
    spread.finish()
    for copy in sends:
        copy.wait_send()
    for copy in copies + stores:
        copy.wait()


def feed_back_up(dy, f, gain, gu, act, w_dt, collective_id):
    count, model = dy.shape
    total, hidden = act.shape
    tiles = len(column_tiles(hidden // 2))
    return pl.pallas_call(
        back_up_kernel,
        out_shape=[
            jax.ShapeDtypeStruct(gu.shape, BF16),
            jax.ShapeDtypeStruct((model, hidden // 2), BF16),
            jax.ShapeDtypeStruct((1, model), F32),
        ],
        in_specs=[vmem_spec()] * 3 + [any_spec()] * 3,
        out_specs=[any_spec(), any_spec(), vmem_spec()],
        scratch_shapes=[
            pltpu.VMEM((total, model), BF16),
            pltpu.VMEM(gu.shape, BF16),
            pltpu.VMEM(act.shape, BF16),
            pltpu.VMEM(w_dt.shape, BF16),
            pltpu.VMEM((model, hidden // 2), BF16),
            pltpu.VMEM((model, hidden // 2), BF16),
            pltpu.VMEM((model, hidden // 2), BF16),
            pltpu.SemaphoreType.DMA((3, 4)),
            pltpu.SemaphoreType.DMA((4,)),
            *spread_spec(),
            pltpu.SemaphoreType.DMA((tiles,)),
            pltpu.SemaphoreType.DMA((tiles,)),
            pltpu.SemaphoreType.DMA((tiles,)),
        ],
        compiler_params=params(collective_id, 48),
    )(dy, f, gain, gu, act, w_dt)


def back_down_kernel(
    dy_ref, h_ref, gain_ref, dgu_ref, rows_ref, w_ref, dh_out, dw_out, dgain_out,
    dgu, rows, w, parts, ours, theirs, came, load, land, passing, send, recv, swap_send, swap_recv, out_sems,
):
    count, model = dy_ref.shape
    hidden = dgu.shape[1] // 2
    me, nx, ny = neighbours()
    core = lax.axis_index("section")
    met = greet({"narrow": nx}, {"narrow": ny}, {"section": 1 - core})
    far = jnp.bitwise_xor(me, 3)
    weights = pltpu.make_async_copy(w_ref, w, load.at[0])
    weights.start()
    arrivals = []
    for at, block in enumerate((far, nx, ny, me)):
        here = rows_of(block, count)
        arrivals.append(pltpu.make_async_copy(dgu_ref.at[here], dgu.at[here], load.at[1 + at]))
        arrivals[-1].start()
    kept = pltpu.make_async_copy(rows_ref, rows, load.at[5])
    kept.start()
    fold = Fold(parts, count, land, passing, send, recv)
    weights.wait()
    met()
    step = model // 3

    def one(block, at, out, here):
        arrivals[at].wait()

        def tile(j, _):
            part = nt(dgu[rows_of(block, count), :], w[pl.ds(pl.multiple_of(j * step, step), step), :])
            out[here, columns_of(j, step)] = part.astype(out.dtype)
            return 0

        lax.fori_loop(0, 3, tile, 0)

    one(far, 0, parts, rows_of(far, count))
    fold.send_far()
    one(nx, 1, parts, rows_of(nx, count))
    one(ny, 2, parts, rows_of(ny, count))
    fold.send_near()
    one(me, 3, dh_out, pl.ds(0, count))
    fold.pass_on()
    kept.wait()

    def make(mine, first, width):
        side = core if mine else 1 - core
        start = pl.multiple_of(side * hidden + first, 128)
        return tn(rows[...], dgu[:, pl.ds(start, width)])

    sends, stores = swap_sum(
        make, column_tiles(hidden), ours, theirs, came, swap_send, swap_recv, dw_out, out_sems
    )
    total = fold.total(dh_out[...])
    by_value, by_gain = normed_gradient(h_ref[...], gain_ref[...], total)
    dh_out[...] = dy_ref[...] + by_value
    dgain_out[...] = by_gain
    fold.finish()
    for copy in sends:
        copy.wait_send()
    for copy in stores:
        copy.wait()


def feed_back_down(dy, h, gain, dgu, rows, w_gu, collective_id):
    count, model = dy.shape
    total, hidden = dgu.shape[0], dgu.shape[1] // 2
    tiles = len(column_tiles(hidden))
    return pl.pallas_call(
        back_down_kernel,
        out_shape=[
            jax.ShapeDtypeStruct((count, model), F32),
            jax.ShapeDtypeStruct((model, hidden), BF16),
            jax.ShapeDtypeStruct((1, model), F32),
        ],
        in_specs=[vmem_spec()] * 3 + [any_spec()] * 3,
        out_specs=[vmem_spec(), any_spec(), vmem_spec()],
        scratch_shapes=[
            pltpu.VMEM(dgu.shape, BF16),
            pltpu.VMEM(rows.shape, BF16),
            pltpu.VMEM(w_gu.shape, BF16),
            pltpu.VMEM((total, model), BF16),
            pltpu.VMEM((model, hidden), BF16),
            pltpu.VMEM((model, hidden), BF16),
            pltpu.VMEM((model, hidden), BF16),
            pltpu.SemaphoreType.DMA((6,)),
            *fold_spec(count, model),
            pltpu.SemaphoreType.DMA((tiles,)),
            pltpu.SemaphoreType.DMA((tiles,)),
            pltpu.SemaphoreType.DMA((tiles,)),
        ],
        compiler_params=params(collective_id, 56),
    )(dy, h, gain, dgu, rows, w_gu)


def pack_kernel(p_ref, o_ref, local, send, recv, peer_send, peer_recv):
    count = p_ref.shape[0]
    core = lax.axis_index("section")
    me, nx, ny = neighbours()
    met = greet({"narrow": nx}, {"narrow": ny}, {"section": 1 - core})
    side = o_ref.at[core]
    own = pltpu.make_async_copy(p_ref, side.at[rows_of(me, count)], local)
    own.start()
    spread = Spread(side, count, send, recv)
    own.wait()
    met()
    spread.start()
    copies = []

    def across(block, at):
        ref = side.at[rows_of(block, count)]
        copy = pltpu.make_async_remote_copy(
            src_ref=ref,
            dst_ref=ref,
            send_sem=peer_send.at[at],
            recv_sem=peer_recv.at[at],
            device_id={"section": 1 - core},
            device_id_type=MESH,
        )
        copy.start()
        copies.append(copy)

    across(me, 0)
    spread.pass_on()
    spread.x_here()
    across(nx, 1)
    spread.y_here()
    across(ny, 2)
    spread.far_here()
    across(spread.far, 3)
    for copy in copies:
        copy.wait_recv()
    spread.finish()
    for copy in copies:
        copy.wait_send()


def gather_pack(pack, collective_id):
    count, width = pack.shape
    return pl.pallas_call(
        pack_kernel,
        out_shape=jax.ShapeDtypeStruct((2, 4 * count, width), pack.dtype),
        in_specs=[vmem_spec()],
        out_specs=vmem_spec(),
        scratch_shapes=[
            pltpu.SemaphoreType.DMA,
            *spread_spec(),
            pltpu.SemaphoreType.DMA((4,)),
            pltpu.SemaphoreType.DMA((4,)),
        ],
        compiler_params=params(collective_id, 24),
    )(pack)


def after(value, *others):
    return pl.pallas_call(
        lambda *refs: None,
        out_shape=jax.ShapeDtypeStruct(value.shape, value.dtype),
        in_specs=[any_spec()] * (1 + len(others)),
        out_specs=any_spec(),
        input_output_aliases={0: 0},
    )(value, *others)


def feed_forward(h, weights):
    gains, w_gu, w_dt = weights[0], *weights[5:]
    rows, gu, act = feed_up(h, gains[2:3], w_gu, 2)
    out, f = feed_down(h, gains[3:4], act, w_dt, 3)
    return out, (h, rows, gu, act, f)


def scatter(member):
    return lax.psum_scatter(member, "wide", scatter_dimension=0, tiled=True)


def feed_backward(dy, weights, kept):
    gains, w_gu, w_dt = weights[0], *weights[5:]
    h, rows, gu, act, f = kept
    dgu, d_w_dt, dg3 = feed_back_up(dy, f, gains[3:4], gu, act, w_dt, 4)
    dh, d_w_gu, dg2 = feed_back_down(dy, h, gains[2:3], dgu, rows, w_gu, 5)
    return dh, (dg2[0], dg3[0], scatter(d_w_gu), scatter(d_w_dt))


def on_device(
    inputs, cotangent, lengths, norm_gains, head_gains, w_q, w_kv, w_o, w_gate_up, w_down
):
    core = lax.axis_index("section")
    narrow = lax.axis_index("narrow")
    n_narrow = lax.axis_size("narrow")
    is_zero = core == 0
    rows, model = inputs.shape[1], inputs.shape[2]
    block = w_q.shape[1]
    head_width = w_q.shape[2]
    n_wide = lax.axis_size("wide")
    hidden = w_down.shape[1]
    kv_part = w_kv.shape[2] // n_narrow

    def swap(value):
        return lax.ppermute(value, "section", [(0, 1), (1, 0)])

    def by_core(first, second):
        return jnp.where(is_zero, first, second)

    half = block // 2

    def by_halves(member):
        keep = lax.dynamic_slice_in_dim(member, core * half, half, 0)
        give = lax.dynamic_slice_in_dim(member, (1 - core) * half, half, 0)
        came = swap(give)
        return by_core(keep, came), by_core(came, keep)

    pad = -hidden % TILE
    kv_own = lax.dynamic_slice_in_dim(w_kv[0], narrow * kv_part, kv_part, 1)
    pack_width = 2 * head_width + kv_part
    gain_rows = jnp.zeros((GAIN_ROWS, pack_width), BF16)
    gain_rows = lax.dynamic_update_slice(gain_rows, norm_gains[0], (0, 0))
    gain_rows = lax.dynamic_update_slice(gain_rows, head_gains[0], (4, 0))
    gains_came = swap(gain_rows)
    gain_rows = (by_core(gain_rows, gains_came), by_core(gains_came, gain_rows))
    pack = by_halves(jnp.concatenate([w_q[0], w_o[0].T, kv_own], axis=1))
    pack = jnp.concatenate([pack[0], gain_rows[0], pack[1], gain_rows[1]], axis=0)
    pack = lax.all_gather(pack, "wide", axis=0).reshape(n_wide, 2, half + GAIN_ROWS, pack_width)

    gate_up = jnp.pad(w_gate_up[0], ((0, 0), (0, 0), (0, pad))).reshape(block, -1)
    gate_up = [lax.all_gather(m, ("wide", "section"), axis=0, tiled=True) for m in by_halves(gate_up)]
    down = jnp.pad(w_down[0].T, ((0, 0), (0, pad)))
    down = [lax.all_gather(m, ("wide", "section"), axis=0, tiled=True) for m in by_halves(down)]

    def unpack(section):
        whole = gather_pack(pack[:, section].reshape(-1, pack_width), 6)
        whole = whole.reshape(2, n_narrow, n_wide, half + GAIN_ROWS, pack_width)
        body, tail = whole[:, :, :, :half], whole[0, 0, :, half:]

        def columns(first, last):
            return body[..., first:last].transpose(2, 0, 3, 1, 4).reshape(model, -1)

        norm_part = tail[:, :4, :block].transpose(1, 0, 2).reshape(4, model).astype(F32)
        head_part = tail[:, 4:6, : head_width // n_wide].transpose(1, 0, 2).reshape(2, head_width)
        return (
            norm_part,
            head_part.astype(F32),
            columns(0, head_width),
            columns(head_width, 2 * head_width),
            columns(2 * head_width, pack_width),
        )

    layers = [(*unpack(section), gate_up[section], down[section]) for section in range(2)]

    start = narrow * rows
    positions = start + jnp.arange(rows, dtype=jnp.int32)
    trig = tables(positions, head_width)
    length = lax.dynamic_index_in_dim(lengths[:, 0], core, 0, keepdims=False)

    x = lax.dynamic_index_in_dim(inputs, core, 0, keepdims=False).astype(F32)
    outs, kept = [], []
    for section in range(2):
        h, kept_a = attention_forward(x, length, layers[section], start, trig)
        x, kept_f = feed_forward(h, layers[section])
        outs.append(x.astype(BF16))
        kept.append((kept_a, kept_f))
        x = outs[-1].astype(F32)

    real = (positions < length).astype(F32)[:, None]
    dy = lax.dynamic_index_in_dim(cotangent, core, 0, keepdims=False).astype(F32) * real
    dxs, grads = [None, None], [None, None]
    for section in (1, 0):
        if section == 0:
            dy = after(dy, grads[1][1][3])
        dh, grads_f = feed_backward(dy, layers[section], kept[section][1])
        if section == 0:
            dh = after(dh, grads[1][1][2])
        dx, grads_a = attention_backward(
            dh, length, layers[section], kept[section][0], start, trig
        )
        dxs[section] = dx
        grads[section] = (grads_a, grads_f)
        dy = dx.astype(BF16).astype(F32)

    sums = [[grads[section][1][k] for k in (2, 3)] for section in range(2)]

    def own_section(k):
        first, second = sums[0][k], sums[1][k]
        came = swap(by_core(second, first))
        stays = by_core(first, second)
        return by_core(stays, came).astype(F32), by_core(came, stays).astype(F32)

    grad_gate_up = jnp.stack(own_section(0), axis=1)[:, :, :hidden]
    grad_down = jnp.concatenate(own_section(1), axis=1)[:, :hidden].T

    packs = []
    for section in range(2):
        dg0, dg1, d_head, d_w_q, d_w_ot, d_w_kv = grads[section][0]
        dg2, dg3 = grads[section][1][:2]

        def blocks(member):
            return member.astype(BF16).reshape(n_wide, block, n_narrow, -1).transpose(2, 0, 1, 3)

        body = jnp.concatenate([blocks(d_w_q), blocks(d_w_ot), blocks(d_w_kv)], axis=3)
        norm_part = jnp.stack([dg0, dg1, dg2, dg3]).astype(BF16)
        norm_part = norm_part.reshape(4, n_wide, block).transpose(1, 0, 2)
        head_part = d_head.astype(BF16).reshape(2, n_wide, head_width // n_wide).transpose(1, 0, 2)
        tail = jnp.zeros((n_wide, GAIN_ROWS, pack_width), BF16)
        tail = lax.dynamic_update_slice(tail, norm_part, (0, 0, 0))
        tail = lax.dynamic_update_slice(tail, head_part, (0, 4, 0))
        tail = jnp.broadcast_to(tail[None], (n_narrow, *tail.shape))
        packs.append(jnp.concatenate([body, tail], axis=2))
    pack_sum = by_core(*packs) + swap(by_core(*packs[::-1]))
    pack_sum = after(pack_sum, grads[0][1][3])
    pack_sum = reduce_rows(pack_sum.reshape(-1, pack_width), 7, BF16)
    pack_sum = scatter(pack_sum)
    grad_q = pack_sum[:block, :head_width].astype(F32)
    grad_o = pack_sum[:block, head_width : 2 * head_width].T.astype(F32)
    grad_kv = lax.all_gather(
        pack_sum[:block, 2 * head_width :], "narrow", axis=1, tiled=True
    ).astype(F32)
    grad_norm = pack_sum[block : block + 4, :block].astype(F32)
    grad_head = pack_sum[block + 4 : block + 6, : head_width // n_wide].astype(F32)

    def by_section(first, second):
        stays, came = by_core(first, second), swap(by_core(second, first))
        return jnp.stack([by_core(stays, came), by_core(came, stays)])

    return (
        by_section(*outs)[None],
        by_section(*dxs)[None],
        grad_norm[None],
        grad_head[None],
        grad_q[None],
        grad_kv[None],
        grad_o[None],
        grad_gate_up[None],
        grad_down[None],
    )


def solution(mesh):
    return jax.shard_map(
        on_device,
        mesh=mesh,
        in_specs=(
            P(None, ("wide", "narrow"), None),
            P(None, ("wide", "narrow"), None),
            P(None, "wide"),
            P("section", None, "wide"),
            P("section", None, "wide"),
            P("section", "wide", "narrow"),
            P("section", "wide", None),
            P("section", "narrow", "wide"),
            P("section", "wide", None, "narrow"),
            P("section", "narrow", "wide"),
        ),
        out_specs=(
            P("section", None, ("wide", "narrow"), None),
            P("section", None, ("wide", "narrow"), None),
            P("section", None, "wide"),
            P("section", None, "wide"),
            P("section", "wide", "narrow"),
            P("section", "wide", None),
            P("section", "narrow", "wide"),
            P("section", "wide", None, "narrow"),
            P("section", "narrow", "wide"),
        ),
        check_vma=False,
    )
```

```python
import functools

import jax
import jax.numpy as jnp
from jax import lax
from jax.experimental import pallas as pl
from jax.experimental.pallas import tpu as pltpu
from jax.sharding import PartitionSpec as P

WINDOW = 512
EPSILON = 1e-06
NEGATIVE = -1e30
ROPE_BASE = 10000.0
MESH = pl.DeviceIdType.MESH
MIB = 2**20
GAIN_COLUMNS = 128
F32 = jnp.float32
BF16 = jnp.bfloat16


def dot(a, b, dims):
    return lax.dot_general(a, b, ((dims[0], dims[1]), ((), ())), preferred_element_type=F32)


def nn(a, b):
    return dot(a, b, ((1,), (0,)))


def nt(a, b):
    return dot(a, b, ((1,), (1,)))


def tn(a, b):
    return dot(a, b, ((0,), (0,)))


def normed(operand, gain_vec):
    return (
        operand
        * lax.rsqrt(jnp.mean(operand * operand, axis=-1, keepdims=True) + EPSILON)
        * gain_vec
    )


def geglu(gate, up):
    return jax.nn.gelu(gate, approximate=True) * up


def neighbours():
    me = lax.axis_index("narrow")
    return me, jnp.bitwise_xor(me, 1), jnp.bitwise_xor(me, 2)


def meet(nx, ny):
    barrier = pltpu.get_barrier_semaphore()
    for other in (nx, ny):
        pl.semaphore_signal(barrier, inc=1, device_id={"narrow": other}, device_id_type=MESH)
    pl.semaphore_wait(barrier, 2)


def remote(src, dst, send_sem, recv_sem, other):
    return pltpu.make_async_remote_copy(
        src_ref=src,
        dst_ref=dst,
        send_sem=send_sem,
        recv_sem=recv_sem,
        device_id={"narrow": other},
        device_id_type=MESH,
    )


def tables(positions, head_width):
    half_width = head_width // 2
    frequency = ROPE_BASE ** (-jnp.arange(half_width, dtype=F32) * (2.0 / head_width))
    angles = positions.astype(F32)[:, None] * frequency[None, :]
    return jnp.concatenate([jnp.cos(angles), jnp.sin(angles)], axis=1)


def rotate(operand, cosine, sine_table):
    half_width = operand.shape[-1] // 2
    front_half = operand[..., :half_width]
    back_half = operand[..., half_width:]
    return jnp.concatenate(
        [
            front_half * cosine - back_half * sine_table,
            back_half * cosine + front_half * sine_table,
        ],
        axis=-1,
    )


GELU_SCALE = 0.7978845608028654
GELU_CUBE = 0.044715


def vmem_spec():
    return pl.BlockSpec(memory_space=pltpu.VMEM)


def any_spec():
    return pl.BlockSpec(memory_space=pl.ANY)


def rows_of(block, count):
    return pl.ds(pl.multiple_of(block * count, count), count)


def columns_of(tile, width, offset=0):
    return pl.ds(pl.multiple_of(tile * width + offset, 128), width)


def inverse_rms(value):
    return lax.rsqrt(jnp.mean(value * value, axis=-1, keepdims=True) + EPSILON)


def normed_gradient(value, gain, grad):
    inverse = inverse_rms(value)
    unit = value * inverse
    scaled = grad * gain
    by_value = inverse * (scaled - unit * jnp.mean(scaled * unit, axis=-1, keepdims=True))
    return by_value, jnp.sum(grad * unit, axis=0, keepdims=True)


def halves_of(ref, count, base=0):
    half = count // 2

    def part(block, which):
        return ref.at[pl.ds(pl.multiple_of(base + block * count + which * half, half), half)]

    return part


class Spread:
    def __init__(self, part, send, recv):
        self.me, self.nx, self.ny = neighbours()
        self.far = jnp.bitwise_xor(self.me, 3)

        def copy(block, which, at, other):
            ref = part(block, which)
            return remote(ref, ref, send.at[at], recv.at[at], other)

        self.to_x1 = copy(self.me, 0, 0, self.nx)
        self.to_y2 = copy(self.me, 1, 1, self.ny)
        self.to_x2 = copy(self.me, 1, 2, self.nx)
        self.to_y1 = copy(self.me, 0, 3, self.ny)
        self.on_y = copy(self.nx, 0, 4, self.ny)
        self.on_x = copy(self.ny, 1, 5, self.nx)

    def start(self):
        for copy in (self.to_x1, self.to_y2, self.to_x2, self.to_y1):
            copy.start()

    def pass_on(self):
        self.to_x1.wait_recv()
        self.on_y.start()
        self.to_y2.wait_recv()
        self.on_x.start()

    def x_here(self):
        self.to_x2.wait_recv()

    def y_here(self):
        self.to_y1.wait_recv()

    def far_here(self):
        self.on_y.wait_recv()
        self.on_x.wait_recv()

    def all_here(self):
        self.x_here()
        self.y_here()
        self.far_here()

    def finish(self):
        for copy in (self.to_x1, self.to_y2, self.to_x2, self.to_y1, self.on_y, self.on_x):
            copy.wait_send()


class Fold:
    def __init__(self, part, land, passing, send, recv):
        self.me, self.nx, self.ny = neighbours()
        self.far = jnp.bitwise_xor(self.me, 3)
        self.part, self.land, self.passing = part, land, passing

        def copy(src, at, other):
            return remote(src, land.at[at], send.at[at], recv.at[at], other)

        self.far_x = copy(part(self.far, 0), 0, self.nx)
        self.far_y = copy(part(self.far, 1), 1, self.ny)
        self.near_x = copy(part(self.nx, 0), 2, self.nx)
        self.near_y = copy(part(self.ny, 1), 3, self.ny)
        self.on_y = copy(passing.at[0], 4, self.ny)
        self.on_x = copy(passing.at[1], 5, self.nx)

    def send_far(self):
        self.far_x.start()
        self.far_y.start()

    def send_near(self):
        self.near_x.start()
        self.near_y.start()

    def pass_on(self):
        self.far_x.wait_recv()
        self.passing[0] = (self.part(self.ny, 0)[...].astype(F32) + self.land[0].astype(F32)).astype(BF16)
        self.on_y.start()
        self.far_y.wait_recv()
        self.passing[1] = (self.part(self.nx, 1)[...].astype(F32) + self.land[1].astype(F32)).astype(BF16)
        self.on_x.start()

    def total(self, own):
        half = own.shape[0] // 2
        for copy in (self.near_x, self.near_y, self.on_y, self.on_x):
            copy.wait_recv()
        first = own[:half] + (self.land[2].astype(F32) + self.land[4].astype(F32))
        second = own[half:] + (self.land[3].astype(F32) + self.land[5].astype(F32))
        return jnp.concatenate([first, second], axis=0)

    def finish(self):
        for copy in (self.far_x, self.far_y, self.near_x, self.near_y, self.on_y, self.on_x):
            copy.wait_send()


class Deal:
    def __init__(self, src, place, send, recv):
        me, nx, ny = neighbours()
        far = jnp.bitwise_xor(me, 3)
        self.copies = [
            remote(src(other), place(me), send.at[at], recv.at[at], other)
            for at, other in enumerate((far, nx, ny))
        ]

    def start(self):
        for copy in self.copies:
            copy.start()

    def here(self):
        for copy in self.copies:
            copy.wait_recv()

    def finish(self):
        for copy in self.copies:
            copy.wait_send()


def greet(*others):
    barrier = pltpu.get_barrier_semaphore()
    for other in others:
        pl.semaphore_signal(barrier, inc=1, device_id=other, device_id_type=MESH)
    return lambda: pl.semaphore_wait(barrier, len(others))


def spread_spec():
    return [pltpu.SemaphoreType.DMA((6,)), pltpu.SemaphoreType.DMA((6,))]


def fold_spec(count, width):
    return [
        pltpu.VMEM((6, count // 2, width), BF16),
        pltpu.VMEM((2, count // 2, width), BF16),
        pltpu.SemaphoreType.DMA((6,)),
        pltpu.SemaphoreType.DMA((6,)),
    ]


def params(collective_id, mib):
    return pltpu.CompilerParams(
        collective_id=collective_id, has_side_effects=True, vmem_limit_bytes=mib * MIB
    )


TILE = 256


def up_kernel(h_ref, gain_ref, w_ref, *refs):
    sharing = len(refs) > 11
    if sharing:
        xn_ref, o_ref, rows_out, gu_out, act_out, xn_out, o_out, *refs = refs
        rows, w, gu, act, load, store, send, recv, *share_refs = refs
        share = Share(xn_ref, o_ref, *share_refs)
    else:
        rows_out, gu_out, act_out, rows, w, gu, act, load, store, send, recv = refs
    count = h_ref.shape[0]
    hidden = act.shape[1]
    weights = pltpu.make_async_copy(w_ref.at[:, pl.ds(0, 2 * hidden)], w, load)
    weights.start()
    me, nx, ny = neighbours()
    met = greet({"narrow": nx}, {"narrow": ny}, {"narrow": jnp.bitwise_xor(me, 3)})
    value = h_ref[...]
    rows[rows_of(me, count), :] = (value * inverse_rms(value) * gain_ref[...]).astype(BF16)
    spread = Spread(halves_of(rows, count), send, recv)
    met()
    spread.start()
    weights.wait()

    def one(block, at):
        here = rows_of(block, count)

        def tile(j, _):
            left = rows[here, :]
            gate = nn(left, w[:, columns_of(j, TILE)])
            up = nn(left, w[:, columns_of(j, TILE, hidden)])
            inner = jnp.tanh(GELU_SCALE * (gate + GELU_CUBE * (gate * gate * gate)))
            gu[here, columns_of(j, TILE)] = gate.astype(BF16)
            gu[here, columns_of(j, TILE, hidden)] = up.astype(BF16)
            act[here, columns_of(j, TILE)] = (0.5 * gate * (1.0 + inner) * up).astype(BF16)
            return 0

        lax.fori_loop(0, hidden // TILE, tile, 0)
        copies = [
            pltpu.make_async_copy(ref.at[here], out.at[here], store.at[k, at])
            for k, (ref, out) in enumerate(((gu, gu_out), (act, act_out), (rows, rows_out)))
        ]
        for copy in copies:
            copy.start()
        return copies

    copies = one(me, 0)
    spread.pass_on()
    if sharing:
        share.start_rows()
        share.start_deal()
    spread.x_here()
    copies += one(nx, 1)
    spread.y_here()
    copies += one(ny, 2)
    spread.far_here()
    if sharing:
        share.spread.pass_on()
    copies += one(spread.far, 3)
    spread.finish()
    if sharing:
        share.all_here()
        share.finish()
        xn, o, loads = share_refs[:3]
        copies += [pltpu.make_async_copy(xn, xn_out, loads.at[2]), pltpu.make_async_copy(o, o_out, loads.at[3])]
        for copy in copies[-2:]:
            copy.start()
    for copy in copies:
        copy.wait()


def feed_up(h, gain, w_gu, hidden, shared, collective_id):
    count, model = h.shape
    total = 4 * count
    shapes = [(total, model), (total, 2 * hidden), (total, hidden)]
    shapes = [jax.ShapeDtypeStruct(shape, BF16) for shape in shapes]
    if shared:
        shapes += share_shapes(*shared)
    return pl.pallas_call(
        up_kernel,
        out_shape=shapes,
        in_specs=[vmem_spec(), vmem_spec(), any_spec()] + [vmem_spec()] * len(shared),
        out_specs=[any_spec()] * len(shapes),
        scratch_shapes=[
            pltpu.VMEM((total, model), BF16),
            pltpu.VMEM((model, 2 * hidden), BF16),
            pltpu.VMEM((total, 2 * hidden), BF16),
            pltpu.VMEM((total, hidden), BF16),
            pltpu.SemaphoreType.DMA,
            pltpu.SemaphoreType.DMA((3, 4)),
            *spread_spec(),
            *(share_spec(count, model, shared[1].shape[1] // 4) if shared else []),
        ],
        compiler_params=params(collective_id, 48),
    )(h, gain, w_gu, *shared)


def down_kernel(
    h_ref, gain_ref, act_ref, w_ref, x_out, f_out, act, w, parts, load, land, passing, send, recv
):
    count, model = h_ref.shape
    me, nx, ny = neighbours()
    met = greet({"narrow": nx}, {"narrow": ny})
    far = jnp.bitwise_xor(me, 3)
    first = w_ref.shape[1] - w.shape[1]
    weights = pltpu.make_async_copy(w_ref.at[:, pl.ds(first, w.shape[1])], w, load.at[0])
    weights.start()
    arrivals = []
    for at, block in enumerate((far, nx, ny, me)):
        here = rows_of(block, count)
        arrivals.append(pltpu.make_async_copy(act_ref.at[here], act.at[here], load.at[1 + at]))
        arrivals[-1].start()
    fold = Fold(halves_of(parts, count), land, passing, send, recv)
    weights.wait()
    met()

    def one(block, at):
        arrivals[at].wait()
        return nt(act[rows_of(block, count), :], w[...])

    parts[rows_of(far, count), :] = one(far, 0).astype(BF16)
    fold.send_far()
    parts[rows_of(nx, count), :] = one(nx, 1).astype(BF16)
    parts[rows_of(ny, count), :] = one(ny, 2).astype(BF16)
    fold.send_near()
    f_out[...] = one(me, 3)
    fold.pass_on()
    total = fold.total(f_out[...])
    f_out[...] = total
    x_out[...] = (h_ref[...] + total * inverse_rms(total) * gain_ref[...]).astype(BF16)
    fold.finish()


def feed_down(h, gain, act, w_dt, collective_id):
    count, model = h.shape
    return pl.pallas_call(
        down_kernel,
        out_shape=[
            jax.ShapeDtypeStruct((count, model), BF16),
            jax.ShapeDtypeStruct((count, model), F32),
        ],
        in_specs=[vmem_spec(), vmem_spec(), any_spec(), any_spec()],
        out_specs=[vmem_spec(), vmem_spec()],
        scratch_shapes=[
            pltpu.VMEM(act.shape, BF16),
            pltpu.VMEM((model, act.shape[1]), BF16),
            pltpu.VMEM((4 * count, model), BF16),
            pltpu.SemaphoreType.DMA((5,)),
            *fold_spec(count, model),
        ],
        compiler_params=params(collective_id, 40),
    )(h, gain, act, w_dt)


def swap_sum(make, tiles, ours, theirs, came, send, recv, out, out_sems, between=None):
    other = {"section": 1 - lax.axis_index("section")}
    sends = []
    for at, (first, width) in enumerate(tiles):
        columns = pl.ds(first, width)
        theirs[:, columns] = make(False, first, width).astype(BF16)
        copy = pltpu.make_async_remote_copy(
            src_ref=theirs.at[:, columns],
            dst_ref=came.at[:, columns],
            send_sem=send.at[at],
            recv_sem=recv.at[at],
            device_id=other,
            device_id_type=MESH,
        )
        copy.start()
        sends.append(copy)
    if between is not None:
        between()
    stores = []
    for at, (first, width) in enumerate(tiles):
        columns = pl.ds(first, width)
        own = make(True, first, width)
        sends[at].wait_recv()
        ours[:, columns] = (own + came[:, columns].astype(F32)).astype(BF16)
        copy = pltpu.make_async_copy(ours.at[:, columns], out.at[:, columns], out_sems.at[at])
        copy.start()
        stores.append(copy)
    return sends, stores


def column_tiles(width):
    return [(first, min(TILE, width - first)) for first in range(0, width, TILE)]


def back_up_kernel(dy_ref, f_ref, gain_ref, gu_ref, act_ref, w_ref, *refs):
    if len(refs) == 18:
        extra_ref, *refs = refs
    else:
        extra_ref = None
    (
        dgu_out, dw_out, dgain_out, df, gu, act, w, ours, theirs, came,
        load, store, send, recv, swap_send, swap_recv, out_sems,
    ) = refs
    if extra_ref is not None:
        first = ours.shape[1]
        extra = pltpu.make_async_copy(
            extra_ref, dw_out.at[:, pl.ds(first, extra_ref.shape[1])], load.at[0, 1]
        )
        extra.start()
    count, model = dy_ref.shape
    hidden = act.shape[1]
    me, nx, ny = neighbours()
    core = lax.axis_index("section")
    met = greet({"narrow": nx}, {"narrow": ny}, {"section": 1 - core})
    far = jnp.bitwise_xor(me, 3)
    start = w_ref.shape[1] - hidden
    weights = pltpu.make_async_copy(w_ref.at[:, pl.ds(start, hidden)], w, load.at[0, 0])
    weights.start()
    arrivals = []
    for at, block in enumerate((me, nx, ny, far)):
        here = rows_of(block, count)
        pair = [
            pltpu.make_async_copy(gu_ref.at[here], gu.at[here], load.at[1, at]),
            pltpu.make_async_copy(act_ref.at[here], act.at[here], load.at[2, at]),
        ]
        for copy in pair:
            copy.start()
        arrivals.append(pair)
    dy = dy_ref[...].astype(BF16).astype(F32)
    by_value, by_gain = normed_gradient(f_ref[...], gain_ref[...], dy)
    df[rows_of(me, count), :] = by_value.astype(BF16)
    spread = Spread(halves_of(df, count), send, recv)
    met()
    spread.start()
    dgain_out[...] = by_gain
    weights.wait()

    def one(block, at):
        here = rows_of(block, count)
        for copy in arrivals[at]:
            copy.wait()

        def tile(j, _):
            dact = nn(df[here, :], w[:, columns_of(j, TILE)])
            gate = gu[here, columns_of(j, TILE)].astype(F32)
            up = gu[here, columns_of(j, TILE, hidden)].astype(F32)
            square = gate * gate
            inner = jnp.tanh(GELU_SCALE * gate * (1.0 + GELU_CUBE * square))
            half = 0.5 * (1.0 + inner)
            slope = half + 0.5 * GELU_SCALE * gate * (1.0 - inner * inner) * (
                1.0 + 3.0 * GELU_CUBE * square
            )
            gu[here, columns_of(j, TILE)] = (dact * up * slope).astype(BF16)
            gu[here, columns_of(j, TILE, hidden)] = (dact * gate * half).astype(BF16)
            return 0

        lax.fori_loop(0, hidden // TILE, tile, 0)
        copy = pltpu.make_async_copy(gu.at[here], dgu_out.at[here], store.at[at])
        copy.start()
        return copy

    copies = [one(me, 0)]
    spread.pass_on()
    spread.x_here()
    copies.append(one(nx, 1))
    spread.y_here()
    copies.append(one(ny, 2))
    spread.far_here()
    copies.append(one(far, 3))

    def make(mine, first, width):
        side = core if mine else 1 - core
        start = pl.multiple_of(side * (hidden // 2) + first, 128)
        return tn(df[...], act[:, pl.ds(start, width)])

    sends, stores = swap_sum(
        make, column_tiles(hidden // 2), ours, theirs, came, swap_send, swap_recv, dw_out, out_sems
    )
    spread.finish()
    for copy in sends:
        copy.wait_send()
    for copy in copies + stores:
        copy.wait()
    if extra_ref is not None:
        extra.wait()


def feed_back_up(dy, f, gain, gu, act, w_dt, extra, collective_id):
    count, model = dy.shape
    total, hidden = act.shape
    tiles = len(column_tiles(hidden // 2))
    extras = () if extra is None else (extra,)
    return pl.pallas_call(
        back_up_kernel,
        out_shape=[
            jax.ShapeDtypeStruct(gu.shape, BF16),
            jax.ShapeDtypeStruct((model, hidden // 2 + sum(e.shape[1] for e in extras)), BF16),
            jax.ShapeDtypeStruct((1, model), F32),
        ],
        in_specs=[vmem_spec()] * 3 + [any_spec()] * (3 + len(extras)),
        out_specs=[any_spec(), any_spec(), vmem_spec()],
        scratch_shapes=[
            pltpu.VMEM((total, model), BF16),
            pltpu.VMEM(gu.shape, BF16),
            pltpu.VMEM(act.shape, BF16),
            pltpu.VMEM((model, hidden), BF16),
            pltpu.VMEM((model, hidden // 2), BF16),
            pltpu.VMEM((model, hidden // 2), BF16),
            pltpu.VMEM((model, hidden // 2), BF16),
            pltpu.SemaphoreType.DMA((3, 4)),
            pltpu.SemaphoreType.DMA((4,)),
            *spread_spec(),
            pltpu.SemaphoreType.DMA((tiles,)),
            pltpu.SemaphoreType.DMA((tiles,)),
            pltpu.SemaphoreType.DMA((tiles,)),
        ],
        compiler_params=params(collective_id, 48),
    )(dy, f, gain, gu, act, w_dt, *extras)


def back_down_kernel(
    dy_ref, h_ref, gain_ref, dgu_ref, rows_ref, w_ref, dh_out, dw_out, dgain_out,
    dgu, rows, w, parts, ours, theirs, came, load, land, passing, send, recv, swap_send, swap_recv, out_sems,
):
    count, model = dy_ref.shape
    hidden = dgu.shape[1] // 2
    me, nx, ny = neighbours()
    core = lax.axis_index("section")
    far = jnp.bitwise_xor(me, 3)
    met = greet({"narrow": nx}, {"narrow": ny}, {"section": 1 - core})
    weights = pltpu.make_async_copy(w_ref.at[:, pl.ds(0, 2 * hidden)], w, load.at[0])
    weights.start()
    arrivals = []
    for at, block in enumerate((far, nx, ny, me)):
        here = rows_of(block, count)
        arrivals.append(pltpu.make_async_copy(dgu_ref.at[here], dgu.at[here], load.at[1 + at]))
        arrivals[-1].start()
    kept = pltpu.make_async_copy(rows_ref, rows, load.at[5])
    kept.start()
    fold = Fold(halves_of(parts, count), land, passing, send, recv)
    weights.wait()
    met()
    step = model // 3

    def one(block, at, out, here):
        arrivals[at].wait()

        def tile(j, _):
            part = nt(dgu[rows_of(block, count), :], w[pl.ds(pl.multiple_of(j * step, step), step), :])
            out[here, columns_of(j, step)] = part.astype(out.dtype)
            return 0

        lax.fori_loop(0, 3, tile, 0)

    one(far, 0, parts, rows_of(far, count))
    fold.send_far()
    one(nx, 1, parts, rows_of(nx, count))
    one(ny, 2, parts, rows_of(ny, count))
    fold.send_near()
    one(me, 3, dh_out, pl.ds(0, count))
    fold.pass_on()
    kept.wait()

    def make(mine, first, width):
        side = core if mine else 1 - core
        start = pl.multiple_of(side * hidden + first, 128)
        return tn(rows[...], dgu[:, pl.ds(start, width)])

    sends, stores = swap_sum(
        make, column_tiles(hidden), ours, theirs, came, swap_send, swap_recv, dw_out, out_sems
    )
    total = fold.total(dh_out[...])
    by_value, by_gain = normed_gradient(h_ref[...], gain_ref[...], total)
    dh_out[...] = dy_ref[...].astype(BF16).astype(F32) + by_value
    dgain_out[...] = by_gain
    fold.finish()
    for copy in sends:
        copy.wait_send()
    for copy in stores:
        copy.wait()


def feed_back_down(dy, h, gain, dgu, rows, w_gu, collective_id):
    count, model = dy.shape
    total, hidden = dgu.shape[0], dgu.shape[1] // 2
    tiles = len(column_tiles(hidden))
    return pl.pallas_call(
        back_down_kernel,
        out_shape=[
            jax.ShapeDtypeStruct((count, model), F32),
            jax.ShapeDtypeStruct((model, hidden), BF16),
            jax.ShapeDtypeStruct((1, model), F32),
        ],
        in_specs=[vmem_spec()] * 3 + [any_spec()] * 3,
        out_specs=[vmem_spec(), any_spec(), vmem_spec()],
        scratch_shapes=[
            pltpu.VMEM(dgu.shape, BF16),
            pltpu.VMEM(rows.shape, BF16),
            pltpu.VMEM((model, 2 * hidden), BF16),
            pltpu.VMEM((total, model), BF16),
            pltpu.VMEM((model, hidden), BF16),
            pltpu.VMEM((model, hidden), BF16),
            pltpu.VMEM((model, hidden), BF16),
            pltpu.SemaphoreType.DMA((6,)),
            *fold_spec(count, model),
            pltpu.SemaphoreType.DMA((tiles,)),
            pltpu.SemaphoreType.DMA((tiles,)),
            pltpu.SemaphoreType.DMA((tiles,)),
        ],
        compiler_params=params(collective_id, 56),
    )(dy, h, gain, dgu, rows, w_gu)


def pack_kernel(p_ref, o_ref, local, send, recv, peer_send, peer_recv):
    model = p_ref.shape[0]
    half = model // 2
    core = lax.axis_index("section")
    first = core * half
    me, nx, ny = neighbours()
    met = greet({"narrow": nx}, {"narrow": ny}, {"section": 1 - core})
    width = o_ref.shape[2]
    own = pltpu.make_async_copy(p_ref.at[:, pl.ds(0, width)], o_ref.at[me], local)
    own.start()

    def part(block, which):
        start = pl.multiple_of(first + which * (half // 2), half // 2)
        return o_ref.at[block, pl.ds(start, half // 2)]

    spread = Spread(part, send, recv)
    own.wait()
    met()
    spread.start()
    copies = []

    def across(block, at):
        ref = o_ref.at[block, pl.ds(pl.multiple_of(first, half), half)]
        copy = pltpu.make_async_remote_copy(
            src_ref=ref,
            dst_ref=ref,
            send_sem=peer_send.at[at],
            recv_sem=peer_recv.at[at],
            device_id={"section": 1 - core},
            device_id_type=MESH,
        )
        copy.start()
        copies.append(copy)

    spread.pass_on()
    spread.x_here()
    across(nx, 0)
    spread.y_here()
    across(ny, 1)
    spread.far_here()
    across(spread.far, 2)
    for copy in copies:
        copy.wait_recv()
    spread.finish()
    for copy in copies:
        copy.wait_send()


def gather_pack(pack, width, collective_id):
    return pl.pallas_call(
        pack_kernel,
        out_shape=jax.ShapeDtypeStruct((4, pack.shape[0], width), pack.dtype),
        in_specs=[any_spec()],
        out_specs=vmem_spec(),
        scratch_shapes=[
            pltpu.SemaphoreType.DMA,
            *spread_spec(),
            pltpu.SemaphoreType.DMA((3,)),
            pltpu.SemaphoreType.DMA((3,)),
        ],
        compiler_params=params(collective_id, 24),
    )(pack)


class Share:
    def __init__(self, xn_ref, o_ref, xn, o, loads, spread_send, spread_recv, deal_send, deal_recv):
        count, head = xn_ref.shape[0], o.shape[1]
        me = lax.axis_index("narrow")
        self.loads = [
            pltpu.make_async_copy(xn_ref, xn.at[rows_of(me, count)], loads.at[0]),
            pltpu.make_async_copy(o_ref.at[:, columns_of(me, head)], o.at[rows_of(me, count)], loads.at[1]),
        ]
        self.spread = Spread(halves_of(xn, count), spread_send, spread_recv)
        self.deal = Deal(
            lambda other: o_ref.at[:, columns_of(other, head)],
            lambda mine: o.at[rows_of(mine, count)],
            deal_send,
            deal_recv,
        )

    def start_rows(self):
        self.loads[0].start()
        self.loads[0].wait()
        self.spread.start()

    def start_deal(self):
        self.loads[1].start()
        self.deal.start()

    def all_here(self):
        self.spread.all_here()
        self.deal.here()

    def finish(self):
        self.spread.finish()
        self.deal.finish()
        self.loads[1].wait()


def share_spec(count, model, head):
    return [
        pltpu.VMEM((4 * count, model), BF16),
        pltpu.VMEM((4 * count, head), BF16),
        pltpu.SemaphoreType.DMA((4,)),
        *spread_spec(),
        pltpu.SemaphoreType.DMA((3,)),
        pltpu.SemaphoreType.DMA((3,)),
    ]


def share_shapes(xn, o):
    total = 4 * xn.shape[0]
    return [
        jax.ShapeDtypeStruct((total, xn.shape[1]), BF16),
        jax.ShapeDtypeStruct((total, o.shape[1] // 4), BF16),
    ]


def gain_kernel(g_ref, o_ref, land, total, send, recv):
    core, wide = lax.axis_index("section"), lax.axis_index("wide")
    wides = land.shape[0] - 3
    me, nx, ny = neighbours()
    far = jnp.bitwise_xor(me, 3)
    stages = [
        [{"narrow": nx}, {"narrow": ny}, {"narrow": far}],
        [{"section": 1 - core}],
        [{"wide": lax.rem(wide + step, wides)} for step in range(1, wides)],
    ]
    met = greet(*stages[0], *stages[1], *stages[2])
    total[0] = g_ref[...]
    met()
    at = 0
    copies = []
    for stage, others in enumerate(stages):
        mine = []
        for other in others:
            mine.append(
                pltpu.make_async_remote_copy(
                    src_ref=total.at[stage],
                    dst_ref=land.at[at],
                    send_sem=send.at[at],
                    recv_sem=recv.at[at],
                    device_id=other,
                    device_id_type=MESH,
                )
            )
            mine[-1].start()
            at += 1
        value = total[stage]
        for place, copy in enumerate(mine, at - len(mine)):
            copy.wait_recv()
            value = value + land[place]
        total[stage + 1] = value
        copies += mine
    o_ref[...] = total[3]
    for copy in copies:
        copy.wait_send()


def sum_gains(block, wides, collective_id):
    return pl.pallas_call(
        gain_kernel,
        out_shape=jax.ShapeDtypeStruct(block.shape, F32),
        in_specs=[vmem_spec()],
        out_specs=vmem_spec(),
        scratch_shapes=[
            pltpu.VMEM((wides + 3, *block.shape), F32),
            pltpu.VMEM((4, *block.shape), F32),
            pltpu.SemaphoreType.DMA((wides + 3,)),
            pltpu.SemaphoreType.DMA((wides + 3,)),
        ],
        compiler_params=params(collective_id, 16),
    )(block)


def turn_back(grad, cosine, sine_table):
    half = grad.shape[1] // 2
    front, back = grad[:, :half], grad[:, half:]
    return jnp.concatenate(
        [front * cosine + back * sine_table, back * cosine - front * sine_table], axis=1
    )


def pack_loads(pack_ref, head, wq, wot, wkv, sems):
    kv_part = wkv.shape[1] // 4
    loads = []
    for at, (w, first, width) in enumerate(
        ((wq, 0, head), (wot, head, head), (wkv, 2 * head, kv_part))
    ):
        loads.append(
            [
                pltpu.make_async_copy(
                    pack_ref.at[n, :, pl.ds(first, width)], w.at[:, pl.ds(n * width, width)], sems.at[at, n]
                )
                for n in range(4)
            ]
        )
    return loads


def start_all(copies):
    for copy in copies:
        copy.start()


def wait_all(copies):
    for copy in copies:
        copy.wait()


def window_mask(me, count, window, length):
    rows_at = me * count + lax.broadcasted_iota(jnp.int32, (count, 1), 0)
    cols_at = me * count - WINDOW + lax.broadcasted_iota(jnp.int32, (1, window), 1)
    return (
        (cols_at <= rows_at)
        & (rows_at - cols_at < WINDOW)
        & (cols_at >= 0)
        & ((cols_at < length) | (cols_at == rows_at))
    )


def attend_kernel(length_ref, x_ref, gains_ref, head_ref, trig_ref, pack_ref, *refs):
    (
        h_out, xn_out, q_out, k_out, win_out, lse_out, o_out, a_out, *refs
    ) = refs
    sharing = len(refs) > 9
    if sharing:
        xn_all_out, o_all_out, *refs = refs
    kv, wq, wot, wkv, load, send, recv, *share_refs = refs
    count, model = x_ref.shape
    head = k_out.shape[1]
    heads = q_out.shape[1] // head
    me, nx, ny = neighbours()
    met = greet({"narrow": nx}, {"narrow": ny}, {"narrow": jnp.bitwise_xor(me, 3)})
    q_loads, out_loads, kv_loads = pack_loads(pack_ref, head, wq, wot, wkv, load)
    start_all(kv_loads + q_loads + out_loads)
    scaling = head ** (-0.5)
    cosine, sine_table = trig_ref[:, : head // 2], trig_ref[:, head // 2 :]
    x = x_ref[...].astype(F32)
    xn_out[...] = (x * inverse_rms(x) * gains_ref[0:1, :]).astype(BF16)
    kv[pl.ds(0, WINDOW), :] = jnp.zeros((WINDOW, 2 * head), BF16)
    wait_all(kv_loads)
    raw = nn(xn_out[...], wkv[...])
    k_raw = raw[:, :head]
    k_out[...] = k_raw
    k_rot = rotate(k_raw * inverse_rms(k_raw) * head_ref[1:2, :], cosine, sine_table)
    here = pl.ds(pl.multiple_of(WINDOW + me * count, count), count)
    kv[here, :head] = k_rot.astype(BF16)
    kv[here, head:] = raw[:, head:].astype(BF16)
    spread = Spread(halves_of(kv, count, WINDOW), send, recv)
    met()
    spread.start()
    if sharing:
        share = Share(xn_out, o_out, *share_refs)
    wait_all(q_loads)
    q_out[...] = nn(xn_out[...], wq[...])
    spread.pass_on()
    if sharing:
        share.start_rows()
    spread.all_here()
    window = win_out.shape[0]
    win_out[...] = kv[pl.ds(pl.multiple_of(me * count, count), window), :]
    visible = window_mask(me, count, window, length_ref[0])
    k_win, v_win = win_out[:, :head], win_out[:, head:]
    q_gain = head_ref[0:1, :]

    def one_head(i, _):
        columns = columns_of(i, head)
        q_raw = q_out[:, columns]
        qr = rotate(q_raw * inverse_rms(q_raw) * q_gain, cosine, sine_table).astype(BF16)
        scores = jnp.where(visible, nt(qr, k_win) * scaling, NEGATIVE)
        most = jnp.max(scores, axis=-1, keepdims=True)
        exponent = jnp.exp(scores - most)
        total = jnp.sum(exponent, axis=-1, keepdims=True)
        lse_out[i] = most + jnp.log(total)
        o_out[:, columns] = nn((exponent / total).astype(BF16), v_win).astype(BF16)
        return 0

    lax.fori_loop(0, heads, one_head, 0)
    if sharing:
        share.start_deal()
        share.spread.pass_on()
    wait_all(out_loads)
    a = nt(o_out[...], wot[...])
    a_out[...] = a
    h_out[...] = x_ref[...].astype(F32) + a * inverse_rms(a) * gains_ref[1:2, :]
    spread.finish()
    if sharing:
        share.all_here()
        share.finish()
        xn, o, loads = share_refs[:3]
        stores = [
            pltpu.make_async_copy(xn, xn_all_out, loads.at[2]),
            pltpu.make_async_copy(o, o_all_out, loads.at[3]),
        ]
        start_all(stores)
        wait_all(stores)


def attend(length, x, gains, head_gains, trig, pack, head, sharing, collective_id):
    count, model = x.shape
    kv_width = 2 * head
    width = 4 * head
    window = count + WINDOW
    xn_shape = jax.ShapeDtypeStruct((count, model), BF16)
    o_shape = jax.ShapeDtypeStruct((count, width), BF16)
    shapes = [
        jax.ShapeDtypeStruct((count, model), F32),
        xn_shape,
        jax.ShapeDtypeStruct((count, width), F32),
        jax.ShapeDtypeStruct((count, head), F32),
        jax.ShapeDtypeStruct((window, kv_width), BF16),
        jax.ShapeDtypeStruct((4, count, 1), F32),
        o_shape,
        jax.ShapeDtypeStruct((count, model), F32),
    ]
    outs = [vmem_spec()] * 8
    if sharing:
        shapes += share_shapes(xn_shape, o_shape)
        outs += [any_spec()] * 2
    return pl.pallas_call(
        attend_kernel,
        out_shape=shapes,
        in_specs=[pl.BlockSpec(memory_space=pltpu.SMEM)] + [vmem_spec()] * 4 + [any_spec()],
        out_specs=outs,
        scratch_shapes=[
            pltpu.VMEM((4 * count + WINDOW, kv_width), BF16),
            pltpu.VMEM((model, width), BF16),
            pltpu.VMEM((model, width), BF16),
            pltpu.VMEM((model, kv_width), BF16),
            pltpu.SemaphoreType.DMA((3, 4)),
            *spread_spec(),
            *(share_spec(count, model, head) if sharing else []),
        ],
        compiler_params=params(collective_id, 40),
    )(length, x, gains, head_gains, trig, pack)


def attend_back_kernel(
    length_ref, dh_ref, a_ref, x_ref, gains_ref, head_ref, trig_ref, q_ref, k_ref, win_ref, lse_ref,
    pack_ref, xn_ref, o_ref,
    dx_out, dw_out, dgain_out, dhead_out,
    da, do, dq, dk, dv, parts, dq_all, dkv, dkv_all, wq, wot, wkv, xn, o, ours, theirs, came,
    pack_load, load, send, recv, land, passing, fold_send, fold_recv, q_send, q_recv, kv_send, kv_recv, swap_send, swap_recv, out_sem,
):
    count = dh_ref.shape[0]
    head = k_ref.shape[1]
    heads = q_ref.shape[1] // head
    kv_part = dkv_all.shape[1]
    me, nx, ny = neighbours()
    core = lax.axis_index("section")
    far = jnp.bitwise_xor(me, 3)
    met = greet({"narrow": nx}, {"narrow": ny}, {"narrow": far}, {"section": 1 - core})
    q_loads, out_loads, kv_loads = pack_loads(pack_ref, head, wq, wot, wkv, pack_load)
    loads = [
        pltpu.make_async_copy(src, dst, load.at[at])
        for at, (src, dst) in enumerate(((xn_ref, xn), (o_ref, o)))
    ]
    start_all(out_loads + q_loads + kv_loads + loads)
    here = rows_of(me, count)
    scaling = head ** (-0.5)
    cosine, sine_table = trig_ref[:, : head // 2], trig_ref[:, head // 2 :]

    dh = dh_ref[...]
    by_value, dg1 = normed_gradient(a_ref[...], gains_ref[1:2, :], dh)
    da[here, :] = by_value.astype(BF16)
    dgain_out[1:2, :] = dg1
    spread = Spread(halves_of(da, count), send, recv)
    met()
    spread.start()
    wait_all(out_loads)
    do[...] = nn(da[here, :], wot[...]).astype(BF16)

    visible = window_mask(me, count, win_ref.shape[0], length_ref[0])
    k_win, v_win = win_ref[:, :head], win_ref[:, head:]
    dk[...] = jnp.zeros_like(dk)
    dv[...] = jnp.zeros_like(dv)
    dhead_out[...] = jnp.zeros_like(dhead_out)
    q_gain, k_gain = head_ref[0:1, :], head_ref[1:2, :]

    def one_head(i, _):
        columns = columns_of(i, head)
        raw = q_ref[:, columns]
        inverse = inverse_rms(raw)
        unit = raw * inverse
        qr = rotate(unit * q_gain, cosine, sine_table).astype(BF16)
        scores = jnp.where(visible, nt(qr, k_win) * scaling, NEGATIVE)
        probs = jnp.exp(scores - lse_ref[i])
        do_head = do[:, columns]
        dp = nt(do_head, v_win)
        ds = (probs * (dp - jnp.sum(probs * dp, axis=-1, keepdims=True))).astype(BF16)
        dk[...] += tn(ds, qr)
        dv[...] += tn(probs.astype(BF16), do_head)
        grad = turn_back(nn(ds, k_win) * scaling, cosine, sine_table)
        scaled = grad * q_gain
        dq_raw = inverse * (scaled - unit * jnp.mean(scaled * unit, axis=-1, keepdims=True))
        dq[:, columns] = dq_raw.astype(BF16)
        dhead_out[0:1, :] += jnp.sum(grad * unit, axis=0, keepdims=True)
        return 0

    lax.fori_loop(0, heads, one_head, 0)
    parts[...] = jnp.zeros_like(parts)
    window = pl.ds(pl.multiple_of(me * count, count), win_ref.shape[0])
    parts[window, :head] = (dk[...] * scaling).astype(BF16)
    parts[window, head:] = dv[...].astype(BF16)
    fold = Fold(halves_of(parts, count, WINDOW), land, passing, fold_send, fold_recv)
    fold.send_far()
    fold.send_near()
    deal_q = Deal(
        lambda other: dq.at[:, columns_of(other, head)],
        lambda mine: dq_all.at[rows_of(mine, count)],
        q_send,
        q_recv,
    )
    deal_q.start()
    dq_all[here, :] = dq[:, columns_of(me, head)]
    spread.pass_on()
    wait_all(q_loads)
    dx_out[...] = nt(dq[...], wq[...])
    fold.pass_on()
    spread.all_here()
    wait_all(loads)
    first = core == 0
    swaps = []

    def exchange(at, columns, a, b):
        ours[:, columns] = jnp.where(first, a, b).astype(BF16)
        theirs[:, columns] = jnp.where(first, b, a).astype(BF16)
        copy = pltpu.make_async_remote_copy(
            src_ref=theirs.at[:, columns],
            dst_ref=came.at[:, columns],
            send_sem=swap_send.at[at],
            recv_sem=swap_recv.at[at],
            device_id={"section": 1 - core},
            device_id_type=MESH,
        )
        copy.start()
        swaps.append(copy)

    by_out = tn(da[...], o[...])
    deal_q.here()
    exchange(0, pl.ds(0, head), tn(xn[...], dq_all[...]), by_out)
    own = jnp.concatenate([dk[WINDOW:, :] * scaling, dv[WINDOW:, :]], axis=1)
    total = fold.total(own)
    grad = turn_back(total[:, :head], cosine, sine_table)
    dk_raw, dk_gain = normed_gradient(k_ref[...], k_gain, grad)
    dhead_out[1:2, :] = dk_gain
    dkv[:, :head] = dk_raw.astype(BF16)
    dkv[:, head:] = total[:, head:].astype(BF16)
    deal_kv = Deal(
        lambda other: dkv.at[:, columns_of(other, kv_part)],
        lambda mine: dkv_all.at[rows_of(mine, count)],
        kv_send,
        kv_recv,
    )
    deal_kv.start()
    dkv_all[here, :] = dkv[:, columns_of(me, kv_part)]
    wait_all(kv_loads)
    dxn = dx_out[...] + nt(dkv[...], wkv[...])
    by_value, dg0 = normed_gradient(x_ref[...].astype(F32), gains_ref[0:1, :], dxn)
    dx_out[...] = dh_ref[...] + by_value
    dgain_out[0:1, :] = dg0

    deal_kv.here()
    by_kv = tn(xn[...], dkv_all[...])
    exchange(1, pl.ds(head, kv_part), by_kv, jnp.zeros_like(by_kv))
    for copy in swaps:
        copy.wait_recv()
    ours[...] = (ours[...].astype(F32) + came[...].astype(F32)).astype(BF16)
    out = pltpu.make_async_copy(ours, dw_out, out_sem)
    out.start()
    spread.finish()
    fold.finish()
    deal_q.finish()
    deal_kv.finish()
    for copy in swaps:
        copy.wait_send()
    out.wait()


def attend_back(length, dh, a, x, gains, head_gains, trig, q_raw, k_raw, window, lse, pack, xn, o, collective_id):
    count, model = dh.shape
    head = k_raw.shape[1]
    width = q_raw.shape[1]
    kv_part = pack.shape[2] - 2 * head
    deal = pltpu.SemaphoreType.DMA((3,))
    dw = pltpu.VMEM((model, head + kv_part), BF16)
    return pl.pallas_call(
        attend_back_kernel,
        out_shape=[
            jax.ShapeDtypeStruct((count, model), F32),
            jax.ShapeDtypeStruct((model, head + kv_part), BF16),
            jax.ShapeDtypeStruct((2, model), F32),
            jax.ShapeDtypeStruct((2, head), F32),
        ],
        in_specs=[pl.BlockSpec(memory_space=pltpu.SMEM)] + [vmem_spec()] * 10 + [any_spec()] * 3,
        out_specs=[vmem_spec(), any_spec(), vmem_spec(), vmem_spec()],
        scratch_shapes=[
            pltpu.VMEM((4 * count, model), BF16),
            pltpu.VMEM((count, width), BF16),
            pltpu.VMEM((count, width), BF16),
            pltpu.VMEM((window.shape[0], head), F32),
            pltpu.VMEM((window.shape[0], head), F32),
            pltpu.VMEM((4 * count + WINDOW, 2 * head), BF16),
            pltpu.VMEM((4 * count, head), BF16),
            pltpu.VMEM((count, 2 * head), BF16),
            pltpu.VMEM((4 * count, kv_part), BF16),
            pltpu.VMEM((model, width), BF16),
            pltpu.VMEM((model, width), BF16),
            pltpu.VMEM((model, 2 * head), BF16),
            pltpu.VMEM(xn.shape, BF16),
            pltpu.VMEM(o.shape, BF16),
            dw,
            dw,
            dw,
            pltpu.SemaphoreType.DMA((3, 4)),
            pltpu.SemaphoreType.DMA((2,)),
            *spread_spec(),
            *fold_spec(count, 2 * head),
            deal,
            deal,
            deal,
            deal,
            pltpu.SemaphoreType.DMA((2,)),
            pltpu.SemaphoreType.DMA((2,)),
            pltpu.SemaphoreType.DMA,
        ],
        compiler_params=params(collective_id, 48),
    )(length, dh, a, x, gains, head_gains, trig, q_raw, k_raw, window, lse, pack, xn, o)


def after(value, *others):
    return pl.pallas_call(
        lambda *refs: None,
        out_shape=jax.ShapeDtypeStruct(value.shape, value.dtype),
        in_specs=[any_spec()] * (1 + len(others)),
        out_specs=any_spec(),
        input_output_aliases={0: 0},
    )(value, *others)


def feed_forward(h, gains, weights, shared, layer):
    w_up, w_down, hidden = weights
    rows, gu, act, *shared = feed_up(h, gains[2:3], w_up, hidden, shared, 10 + layer)
    out, f = feed_down(h, gains[3:4], act, w_down, 12 + layer)
    return out, (h, rows, gu, act, f), shared


def scatter(member):
    return lax.psum_scatter(member, "wide", scatter_dimension=0, tiled=True)


def feed_backward(dy, gains, weights, kept, extra, layer):
    w_up, w_down, _ = weights
    h, rows, gu, act, f = kept
    dgu, d_down, dg3 = feed_back_up(dy, f, gains[3:4], gu, act, w_down, extra, 14 + layer)
    dh, d_up, dg2 = feed_back_down(dy, h, gains[2:3], dgu, rows, w_up, 16 + layer)
    return dh, (dg2, dg3), scatter(d_up), scatter(d_down)


def on_device(
    inputs, cotangent, lengths, norm_gains, head_gains, w_q, w_kv, w_o, w_gate_up, w_down
):
    core = lax.axis_index("section")
    narrow = lax.axis_index("narrow")
    n_narrow = lax.axis_size("narrow")
    is_zero = core == 0
    rows, model = inputs.shape[1], inputs.shape[2]
    block = w_q.shape[1]
    head_width = w_q.shape[2]
    n_wide = lax.axis_size("wide")
    hidden = w_down.shape[1]
    kv_part = w_kv.shape[2] // n_narrow

    def swap(value):
        return lax.ppermute(value, "section", [(0, 1), (1, 0)])

    def by_core(first, second):
        return jnp.where(is_zero, first, second)

    half = block // 2

    def by_halves(member):
        keep = lax.dynamic_slice_in_dim(member, core * half, half, 0)
        give = lax.dynamic_slice_in_dim(member, (1 - core) * half, half, 0)
        came = swap(give)
        return by_core(keep, came), by_core(came, keep)

    pad = -hidden % TILE
    kv_own = lax.dynamic_slice_in_dim(w_kv[0], narrow * kv_part, kv_part, 1)
    pack_width = 2 * head_width + kv_part
    gain_columns = jnp.zeros((block, GAIN_COLUMNS), BF16)
    gain_columns = lax.dynamic_update_slice(gain_columns, norm_gains[0].T, (0, 0))
    gain_columns = lax.dynamic_update_slice(gain_columns, head_gains[0].T, (0, 4))
    pack = by_halves(jnp.concatenate([w_q[0], w_o[0].T, kv_own, gain_columns], axis=1))

    gate_up = jnp.pad(w_gate_up[0], ((0, 0), (0, 0), (0, pad))).reshape(block, -1)
    down = jnp.pad(w_down[0].T, ((0, 0), (0, pad)))
    feed = by_halves(jnp.concatenate([gate_up, down], axis=1))
    padded = hidden + pad

    def gather(member):
        return lax.all_gather(member, ("wide", "section"), axis=0, tiled=True)

    pack = gather(jnp.concatenate(pack, axis=1))
    both = gather(feed[0])
    feeds = [
        (both, both, padded),
        (gather(feed[1][:, : 2 * padded]), gather(feed[1][:, 2 * padded :]), padded),
    ]
    full_width = pack_width + GAIN_COLUMNS
    packs = [pack[:, :full_width], pack[:, full_width:]]

    def gains_of(section):
        columns = packs[section][:, pack_width:].astype(F32)
        heads = columns.reshape(n_wide, block, -1)[:, : head_width // n_wide, 4:6]
        return columns[:, :4].T, heads.transpose(2, 0, 1).reshape(2, head_width)

    start = narrow * rows
    positions = start + jnp.arange(rows, dtype=jnp.int32)
    trig = tables(positions, head_width)
    length = lax.dynamic_index_in_dim(lengths[:, 0], core, 0, keepdims=False)

    x = lax.dynamic_index_in_dim(inputs, core, 0, keepdims=False)
    length_one = length.reshape(1)
    outs, kept, gains = [], [], []
    for section in range(2):
        layer_gains, head_gain = gains_of(section)
        gains.append((layer_gains, head_gain))
        own_pack = packs[section] if section == 0 else after(packs[1], kept[0][0][0])
        whole = gather_pack(own_pack, pack_width, 6)
        h, xn, q_raw, k_raw, window, lse, o, a, *shared = attend(
            length_one, x, layer_gains, head_gain, trig, whole, head_width, section == 0, 8 + section
        )
        kept_a = (h, a, x, q_raw, k_raw, window, lse, whole)
        x, kept_f, more = feed_forward(
            h, layer_gains, feeds[section], () if section == 0 else (xn, o), section
        )
        outs.append(x)
        kept.append((kept_a, kept_f, shared or more))

    real = (positions < length).astype(F32)[:, None]
    dy = lax.dynamic_index_in_dim(cotangent, core, 0, keepdims=False).astype(F32) * real
    dxs, gain_grads = [None, None], [None, None]
    up_sums, down_sums, attention_sums = [None, None], [None, None], [None, None]
    extra = None
    for section in (1, 0):
        kept_a, kept_f, (xn, o) = kept[section]
        layer_gains, head_gain = gains[section]
        if section == 0:
            dy = after(dy, down_sums[1])
        dh, dg23, up_sums[section], down_sums[section] = feed_backward(
            dy, layer_gains, feeds[section], kept_f, extra, section
        )
        if section == 0:
            dh = after(dh, up_sums[1])
        _, a, x, q_raw, k_raw, window, lse, whole = kept_a
        dx, extra, dg01, dhead = attend_back(
            length_one, dh, a, x, layer_gains, head_gain, trig, q_raw, k_raw, window, lse, whole, xn, o, 1
        )
        dxs[section] = dx
        head_row = jnp.pad(dhead.reshape(1, -1), ((0, 0), (0, model - dhead.size)))
        gain_grads[section] = jnp.concatenate([dg01, *dg23, head_row, jnp.zeros((3, model), F32)])
        dy = dx
    extra = after(extra, up_sums[0])
    split = down_sums[1].shape[1]
    attention_sums = (scatter(extra), down_sums[0][:, split:])
    down_sums[0] = down_sums[0][:, :split]

    def own_section(first, second):
        came = swap(by_core(second, first))
        stays = by_core(first, second)
        return by_core(stays, came).astype(F32), by_core(came, stays).astype(F32)

    grad_gate_up = jnp.stack(own_section(*up_sums), axis=1)[:, :, :hidden]
    grad_down = jnp.concatenate(own_section(*down_sums), axis=1)[:, :hidden].T
    by_qkv, by_out = own_section(*attention_sums)
    grad_q = by_qkv[:, :head_width]
    grad_o = by_out[:, :head_width].T
    grad_kv = lax.all_gather(
        by_qkv[:, head_width:].astype(BF16), "narrow", axis=1, tiled=True
    ).astype(F32)
    gain_sums = sum_gains(jnp.concatenate(gain_grads), n_wide, 7)
    gain_sums = lax.dynamic_slice_in_dim(gain_sums, core * 8, 8, 0)
    wide = lax.axis_index("wide")
    grad_norm = lax.dynamic_slice_in_dim(gain_sums[:4], wide * block, block, 1)
    grad_head = gain_sums[4, : 2 * head_width].reshape(2, head_width)
    head_block = head_width // n_wide
    grad_head = lax.dynamic_slice_in_dim(grad_head, wide * head_block, head_block, 1)

    def by_section(first, second):
        stays, came = by_core(first, second), swap(by_core(second, first))
        return jnp.stack([by_core(stays, came), by_core(came, stays)])

    return (
        by_section(*outs)[None],
        by_section(*dxs)[None],
        grad_norm[None],
        grad_head[None],
        grad_q[None],
        grad_kv[None],
        grad_o[None],
        grad_gate_up[None],
        grad_down[None],
    )


def solution(mesh):
    return jax.shard_map(
        on_device,
        mesh=mesh,
        in_specs=(
            P(None, ("wide", "narrow"), None),
            P(None, ("wide", "narrow"), None),
            P(None, "wide"),
            P("section", None, "wide"),
            P("section", None, "wide"),
            P("section", "wide", "narrow"),
            P("section", "wide", None),
            P("section", "narrow", "wide"),
            P("section", "wide", None, "narrow"),
            P("section", "narrow", "wide"),
        ),
        out_specs=(
            P("section", None, ("wide", "narrow"), None),
            P("section", None, ("wide", "narrow"), None),
            P("section", None, "wide"),
            P("section", None, "wide"),
            P("section", "wide", "narrow"),
            P("section", "wide", None),
            P("section", "narrow", "wide"),
            P("section", "wide", None, "narrow"),
            P("section", "narrow", "wide"),
        ),
        check_vma=False,
    )
```

```python
import functools

import jax
import jax.numpy as jnp
from jax import lax
from jax.experimental import pallas as pl
from jax.experimental.pallas import tpu as pltpu
from jax.sharding import PartitionSpec as P

WINDOW = 512
EPSILON = 1e-06
NEGATIVE = -1e30
ROPE_BASE = 10000.0
MESH = pl.DeviceIdType.MESH
MIB = 2**20
GAIN_COLUMNS = 128
F32 = jnp.float32
BF16 = jnp.bfloat16


def dot(a, b, dims):
    return lax.dot_general(a, b, ((dims[0], dims[1]), ((), ())), preferred_element_type=F32)


def nn(a, b):
    return dot(a, b, ((1,), (0,)))


def nt(a, b):
    return dot(a, b, ((1,), (1,)))


def tn(a, b):
    return dot(a, b, ((0,), (0,)))


def normed(operand, gain_vec):
    return (
        operand
        * lax.rsqrt(jnp.mean(operand * operand, axis=-1, keepdims=True) + EPSILON)
        * gain_vec
    )


def geglu(gate, up):
    return jax.nn.gelu(gate, approximate=True) * up


def neighbours():
    me = lax.axis_index("narrow")
    return me, jnp.bitwise_xor(me, 1), jnp.bitwise_xor(me, 2)


def meet(nx, ny):
    barrier = pltpu.get_barrier_semaphore()
    for other in (nx, ny):
        pl.semaphore_signal(barrier, inc=1, device_id={"narrow": other}, device_id_type=MESH)
    pl.semaphore_wait(barrier, 2)


def remote(src, dst, send_sem, recv_sem, other):
    return pltpu.make_async_remote_copy(
        src_ref=src,
        dst_ref=dst,
        send_sem=send_sem,
        recv_sem=recv_sem,
        device_id={"narrow": other},
        device_id_type=MESH,
    )


def tables(positions, head_width):
    half_width = head_width // 2
    frequency = ROPE_BASE ** (-jnp.arange(half_width, dtype=F32) * (2.0 / head_width))
    angles = positions.astype(F32)[:, None] * frequency[None, :]
    return jnp.concatenate([jnp.cos(angles), jnp.sin(angles)], axis=1)


def rotate(operand, cosine, sine_table):
    half_width = operand.shape[-1] // 2
    front_half = operand[..., :half_width]
    back_half = operand[..., half_width:]
    return jnp.concatenate(
        [
            front_half * cosine - back_half * sine_table,
            back_half * cosine + front_half * sine_table,
        ],
        axis=-1,
    )


GELU_SCALE = 0.7978845608028654
GELU_CUBE = 0.044715


def vmem_spec():
    return pl.BlockSpec(memory_space=pltpu.VMEM)


def any_spec():
    return pl.BlockSpec(memory_space=pl.ANY)


def rows_of(block, count):
    return pl.ds(pl.multiple_of(block * count, count), count)


def columns_of(tile, width, offset=0):
    if isinstance(tile, int):
        return pl.ds(tile * width + offset, width)
    return pl.ds(pl.multiple_of(tile * width + offset, 128), width)


def inverse_rms(value):
    return lax.rsqrt(jnp.mean(value * value, axis=-1, keepdims=True) + EPSILON)


def normed_gradient(value, gain, grad):
    inverse = inverse_rms(value)
    unit = value * inverse
    scaled = grad * gain
    by_value = inverse * (scaled - unit * jnp.mean(scaled * unit, axis=-1, keepdims=True))
    return by_value, jnp.sum(grad * unit, axis=0, keepdims=True)


def halves_of(ref, count, base=0):
    half = count // 2

    def part(block, which):
        return ref.at[pl.ds(pl.multiple_of(base + block * count + which * half, half), half)]

    return part


class Spread:
    def __init__(self, part, send, recv):
        self.me, self.nx, self.ny = neighbours()
        self.far = jnp.bitwise_xor(self.me, 3)

        def copy(block, which, at, other):
            ref = part(block, which)
            return remote(ref, ref, send.at[at], recv.at[at], other)

        self.to_x1 = copy(self.me, 0, 0, self.nx)
        self.to_y2 = copy(self.me, 1, 1, self.ny)
        self.to_x2 = copy(self.me, 1, 2, self.nx)
        self.to_y1 = copy(self.me, 0, 3, self.ny)
        self.on_y = copy(self.nx, 0, 4, self.ny)
        self.on_x = copy(self.ny, 1, 5, self.nx)

    def start(self):
        for copy in (self.to_x1, self.to_y2, self.to_x2, self.to_y1):
            copy.start()

    def pass_on(self):
        self.to_x1.wait_recv()
        self.on_y.start()
        self.to_y2.wait_recv()
        self.on_x.start()

    def x_here(self):
        self.to_x2.wait_recv()

    def y_here(self):
        self.to_y1.wait_recv()

    def far_here(self):
        self.on_y.wait_recv()
        self.on_x.wait_recv()

    def all_here(self):
        self.x_here()
        self.y_here()
        self.far_here()

    def finish(self):
        for copy in (self.to_x1, self.to_y2, self.to_x2, self.to_y1, self.on_y, self.on_x):
            copy.wait_send()


class Fold:
    def __init__(self, part, land, passing, send, recv):
        self.me, self.nx, self.ny = neighbours()
        self.far = jnp.bitwise_xor(self.me, 3)
        self.part, self.land, self.passing = part, land, passing

        def copy(src, at, other):
            return remote(src, land.at[at], send.at[at], recv.at[at], other)

        self.far_x = copy(part(self.far, 0), 0, self.nx)
        self.far_y = copy(part(self.far, 1), 1, self.ny)
        self.near_x = copy(part(self.nx, 0), 2, self.nx)
        self.near_y = copy(part(self.ny, 1), 3, self.ny)
        self.on_y = copy(passing.at[0], 4, self.ny)
        self.on_x = copy(passing.at[1], 5, self.nx)

    def send_far(self):
        self.far_x.start()
        self.far_y.start()

    def send_near(self):
        self.near_x.start()
        self.near_y.start()

    def pass_on(self):
        self.far_x.wait_recv()
        self.passing[0] = (self.part(self.ny, 0)[...].astype(F32) + self.land[0].astype(F32)).astype(BF16)
        self.on_y.start()
        self.far_y.wait_recv()
        self.passing[1] = (self.part(self.nx, 1)[...].astype(F32) + self.land[1].astype(F32)).astype(BF16)
        self.on_x.start()

    def total(self, own):
        half = own.shape[0] // 2
        for copy in (self.near_x, self.near_y, self.on_y, self.on_x):
            copy.wait_recv()
        first = own[:half] + (self.land[2].astype(F32) + self.land[4].astype(F32))
        second = own[half:] + (self.land[3].astype(F32) + self.land[5].astype(F32))
        return jnp.concatenate([first, second], axis=0)

    def finish(self):
        for copy in (self.far_x, self.far_y, self.near_x, self.near_y, self.on_y, self.on_x):
            copy.wait_send()


class Deal:
    def __init__(self, src, place, send, recv):
        me, nx, ny = neighbours()
        far = jnp.bitwise_xor(me, 3)
        self.copies = [
            remote(src(other), place(me), send.at[at], recv.at[at], other)
            for at, other in enumerate((far, nx, ny))
        ]

    def start(self):
        for copy in self.copies:
            copy.start()

    def here(self):
        for copy in self.copies:
            copy.wait_recv()

    def finish(self):
        for copy in self.copies:
            copy.wait_send()


def greet(*others):
    barrier = pltpu.get_barrier_semaphore()
    for other in others:
        pl.semaphore_signal(barrier, inc=1, device_id=other, device_id_type=MESH)
    return lambda: pl.semaphore_wait(barrier, len(others))


def spread_spec():
    return [pltpu.SemaphoreType.DMA((6,)), pltpu.SemaphoreType.DMA((6,))]


def fold_spec(count, width):
    return [
        pltpu.VMEM((6, count // 2, width), BF16),
        pltpu.VMEM((2, count // 2, width), BF16),
        pltpu.SemaphoreType.DMA((6,)),
        pltpu.SemaphoreType.DMA((6,)),
    ]


def params(collective_id, mib):
    return pltpu.CompilerParams(
        collective_id=collective_id, has_side_effects=True, vmem_limit_bytes=mib * MIB
    )


TILE = 256


def up_kernel(h_ref, gain_ref, w_ref, *refs):
    sharing = len(refs) > 11
    if sharing:
        xn_ref, o_ref, rows_out, gu_out, act_out, xn_out, o_out, *refs = refs
        rows, w, gu, act, load, store, send, recv, *share_refs = refs
        share = Share(xn_ref, o_ref, *share_refs)
    else:
        rows_out, gu_out, act_out, rows, w, gu, act, load, store, send, recv = refs
    count = h_ref.shape[0]
    hidden = act.shape[1]
    weights = pltpu.make_async_copy(w_ref.at[:, pl.ds(0, 2 * hidden)], w, load)
    weights.start()
    me, nx, ny = neighbours()
    met = greet({"narrow": nx}, {"narrow": ny}, {"narrow": jnp.bitwise_xor(me, 3)})
    value = h_ref[...]
    rows[rows_of(me, count), :] = (value * inverse_rms(value) * gain_ref[...]).astype(BF16)
    spread = Spread(halves_of(rows, count), send, recv)
    met()
    spread.start()
    weights.wait()

    def one(block, at):
        here = rows_of(block, count)

        def tile(j):
            left = rows[here, :]
            gate = nn(left, w[:, columns_of(j, TILE)])
            up = nn(left, w[:, columns_of(j, TILE, hidden)])
            inner = jnp.tanh(GELU_SCALE * (gate + GELU_CUBE * (gate * gate * gate)))
            gu[here, columns_of(j, TILE)] = gate.astype(BF16)
            gu[here, columns_of(j, TILE, hidden)] = up.astype(BF16)
            act[here, columns_of(j, TILE)] = (0.5 * gate * (1.0 + inner) * up).astype(BF16)

        for j in range(hidden // TILE):
            tile(j)
        copies = [
            pltpu.make_async_copy(ref.at[here], out.at[here], store.at[k, at])
            for k, (ref, out) in enumerate(((gu, gu_out), (act, act_out), (rows, rows_out)))
        ]
        for copy in copies:
            copy.start()
        return copies

    copies = one(me, 0)
    spread.pass_on()
    if sharing:
        share.start_rows()
        share.start_deal()
    spread.x_here()
    copies += one(nx, 1)
    spread.y_here()
    copies += one(ny, 2)
    spread.far_here()
    if sharing:
        share.spread.pass_on()
    copies += one(spread.far, 3)
    spread.finish()
    if sharing:
        share.all_here()
        share.finish()
        xn, o, loads = share_refs[:3]
        copies += [pltpu.make_async_copy(xn, xn_out, loads.at[2]), pltpu.make_async_copy(o, o_out, loads.at[3])]
        for copy in copies[-2:]:
            copy.start()
    for copy in copies:
        copy.wait()


def feed_up(h, gain, w_gu, hidden, shared, collective_id):
    count, model = h.shape
    total = 4 * count
    shapes = [(total, model), (total, 2 * hidden), (total, hidden)]
    shapes = [jax.ShapeDtypeStruct(shape, BF16) for shape in shapes]
    if shared:
        shapes += share_shapes(*shared)
    return pl.pallas_call(
        up_kernel,
        out_shape=shapes,
        in_specs=[vmem_spec(), vmem_spec(), any_spec()] + [vmem_spec()] * len(shared),
        out_specs=[any_spec()] * len(shapes),
        scratch_shapes=[
            pltpu.VMEM((total, model), BF16),
            pltpu.VMEM((model, 2 * hidden), BF16),
            pltpu.VMEM((total, 2 * hidden), BF16),
            pltpu.VMEM((total, hidden), BF16),
            pltpu.SemaphoreType.DMA,
            pltpu.SemaphoreType.DMA((3, 4)),
            *spread_spec(),
            *(share_spec(count, model, shared[1].shape[1] // 4) if shared else []),
        ],
        compiler_params=params(collective_id, 60),
    )(h, gain, w_gu, *shared)


def down_kernel(
    h_ref, gain_ref, act_ref, w_ref, x_out, f_out, act, w, parts, load, land, passing, send, recv
):
    count, model = h_ref.shape
    me, nx, ny = neighbours()
    met = greet({"narrow": nx}, {"narrow": ny})
    far = jnp.bitwise_xor(me, 3)
    first = w_ref.shape[1] - w.shape[1]
    weights = pltpu.make_async_copy(w_ref.at[:, pl.ds(first, w.shape[1])], w, load.at[0])
    weights.start()
    arrivals = []
    for at, block in enumerate((far, nx, ny, me)):
        here = rows_of(block, count)
        arrivals.append(pltpu.make_async_copy(act_ref.at[here], act.at[here], load.at[1 + at]))
        arrivals[-1].start()
    fold = Fold(halves_of(parts, count), land, passing, send, recv)
    weights.wait()
    met()

    def one(block, at):
        arrivals[at].wait()
        return nt(act[rows_of(block, count), :], w[...])

    parts[rows_of(far, count), :] = one(far, 0).astype(BF16)
    fold.send_far()
    parts[rows_of(nx, count), :] = one(nx, 1).astype(BF16)
    parts[rows_of(ny, count), :] = one(ny, 2).astype(BF16)
    fold.send_near()
    f_out[...] = one(me, 3)
    fold.pass_on()
    total = fold.total(f_out[...])
    f_out[...] = total
    x_out[...] = (h_ref[...] + total * inverse_rms(total) * gain_ref[...]).astype(BF16)
    fold.finish()


def feed_down(h, gain, act, w_dt, collective_id):
    count, model = h.shape
    return pl.pallas_call(
        down_kernel,
        out_shape=[
            jax.ShapeDtypeStruct((count, model), BF16),
            jax.ShapeDtypeStruct((count, model), F32),
        ],
        in_specs=[vmem_spec(), vmem_spec(), any_spec(), any_spec()],
        out_specs=[vmem_spec(), vmem_spec()],
        scratch_shapes=[
            pltpu.VMEM(act.shape, BF16),
            pltpu.VMEM((model, act.shape[1]), BF16),
            pltpu.VMEM((4 * count, model), BF16),
            pltpu.SemaphoreType.DMA((5,)),
            *fold_spec(count, model),
        ],
        compiler_params=params(collective_id, 60),
    )(h, gain, act, w_dt)


def swap_sum(make, tiles, ours, theirs, came, send, recv, out, out_sems, between=None):
    other = {"section": 1 - lax.axis_index("section")}
    sends = []
    for at, (first, width) in enumerate(tiles):
        columns = pl.ds(first, width)
        theirs[:, columns] = make(False, first, width).astype(BF16)
        copy = pltpu.make_async_remote_copy(
            src_ref=theirs.at[:, columns],
            dst_ref=came.at[:, columns],
            send_sem=send.at[at],
            recv_sem=recv.at[at],
            device_id=other,
            device_id_type=MESH,
        )
        copy.start()
        sends.append(copy)
    if between is not None:
        between()
    stores = []
    for at, (first, width) in enumerate(tiles):
        columns = pl.ds(first, width)
        own = make(True, first, width)
        sends[at].wait_recv()
        ours[:, columns] = (own + came[:, columns].astype(F32)).astype(BF16)
        copy = pltpu.make_async_copy(ours.at[:, columns], out.at[:, columns], out_sems.at[at])
        copy.start()
        stores.append(copy)
    return sends, stores


def column_tiles(width):
    return [(first, min(2 * TILE, width - first)) for first in range(0, width, 2 * TILE)]


def gate_up_gradient(df, here, w, gu, hidden):
    for j in range(hidden // TILE):
        dact = nn(df[here, :], w[:, columns_of(j, TILE)])
        gate = gu[here, columns_of(j, TILE)].astype(F32)
        up = gu[here, columns_of(j, TILE, hidden)].astype(F32)
        square = gate * gate
        inner = jnp.tanh(GELU_SCALE * gate * (1.0 + GELU_CUBE * square))
        half = 0.5 * (1.0 + inner)
        slope = half + 0.5 * GELU_SCALE * gate * (1.0 - inner * inner) * (
            1.0 + 3.0 * GELU_CUBE * square
        )
        gu[here, columns_of(j, TILE)] = (dact * up * slope).astype(BF16)
        gu[here, columns_of(j, TILE, hidden)] = (dact * gate * half).astype(BF16)


def back_up_kernel(dy_ref, f_ref, gain_ref, gu_ref, act_ref, w_ref, *refs):
    if len(refs) == 19:
        extra_ref, _, *refs = refs
    else:
        extra_ref = None
    (
        dgu_out, dw_out, dgain_out, df, gu, act, w, ours, theirs, came,
        load, store, send, recv, swap_send, swap_recv, out_sems,
    ) = refs
    if extra_ref is not None:
        first = ours.shape[1]
        extra = pltpu.make_async_copy(
            extra_ref, dw_out.at[:, pl.ds(first, extra_ref.shape[1])], load.at[0, 1]
        )
        extra.start()
    count, model = dy_ref.shape
    hidden = act.shape[1]
    me, nx, ny = neighbours()
    core = lax.axis_index("section")
    met = greet({"narrow": nx}, {"narrow": ny}, {"section": 1 - core})
    far = jnp.bitwise_xor(me, 3)
    start = w_ref.shape[1] - hidden
    weights = pltpu.make_async_copy(w_ref.at[:, pl.ds(start, hidden)], w, load.at[0, 0])
    weights.start()
    arrivals = []
    for at, block in enumerate((me, nx, ny, far)):
        here = rows_of(block, count)
        pair = [
            pltpu.make_async_copy(gu_ref.at[here], gu.at[here], load.at[1, at]),
            pltpu.make_async_copy(act_ref.at[here], act.at[here], load.at[2, at]),
        ]
        for copy in pair:
            copy.start()
        arrivals.append(pair)
    dy = dy_ref[...].astype(BF16).astype(F32)
    by_value, by_gain = normed_gradient(f_ref[...], gain_ref[...], dy)
    df[rows_of(me, count), :] = by_value.astype(BF16)
    spread = Spread(halves_of(df, count), send, recv)
    met()
    spread.start()
    dgain_out[...] = by_gain
    weights.wait()

    def one(block, at):
        here = rows_of(block, count)
        for copy in arrivals[at]:
            copy.wait()

        gate_up_gradient(df, here, w, gu, hidden)
        copy = pltpu.make_async_copy(gu.at[here], dgu_out.at[here], store.at[at])
        copy.start()
        return copy

    copies = [one(me, 0)]
    spread.pass_on()
    spread.x_here()
    copies.append(one(nx, 1))
    spread.y_here()
    copies.append(one(ny, 2))
    spread.far_here()
    copies.append(one(far, 3))

    def make(mine, first, width):
        side = core if mine else 1 - core
        start = pl.multiple_of(side * (hidden // 2) + first, 128)
        return tn(df[...], act[:, pl.ds(start, width)])

    sends, stores = swap_sum(
        make, column_tiles(hidden // 2), ours, theirs, came, swap_send, swap_recv, dw_out, out_sems
    )
    spread.finish()
    for copy in sends:
        copy.wait_send()
    for copy in copies + stores:
        copy.wait()
    if extra_ref is not None:
        extra.wait()


def turn_kernel(
    h_ref, gain_ref, dy_ref, act_ref, w_ref, gu_ref, x_out, dgu_out, dw_out, dgain_out,
    act, w, parts, df, gu, ours, theirs, came, load, store, land, passing, fold_send, fold_recv, send, recv,
    swap_send, swap_recv, out_sems,
):
    count, model = h_ref.shape
    hidden = act.shape[1]
    me, nx, ny = neighbours()
    core = lax.axis_index("section")
    far = jnp.bitwise_xor(me, 3)
    met = greet({"narrow": nx}, {"narrow": ny}, {"section": 1 - core})
    first = w_ref.shape[1] - hidden
    weights = pltpu.make_async_copy(w_ref.at[:, pl.ds(first, hidden)], w, load.at[0, 0])
    weights.start()
    blocks = (far, nx, ny, me)
    for at, block in enumerate(blocks):
        here = rows_of(block, count)
        pltpu.make_async_copy(act_ref.at[here], act.at[here], load.at[1, at]).start()
    for at, block in enumerate(blocks):
        here = rows_of(block, count)
        pltpu.make_async_copy(gu_ref.at[here], gu.at[here], load.at[2, at]).start()

    def here_now(row, at):
        here = rows_of(blocks[at], count)
        src, dst = ((act_ref, act), (gu_ref, gu))[row - 1]
        pltpu.make_async_copy(src.at[here], dst.at[here], load.at[row, at]).wait()
        return here

    fold = Fold(halves_of(parts, count), land, passing, fold_send, fold_recv)
    weights.wait()
    met()

    def part(at):
        here = here_now(1, at)
        return here, nt(act[here, :], w[...])

    here, value = part(0)
    parts[here, :] = value.astype(BF16)
    fold.send_far()
    for at in (1, 2):
        here, value = part(at)
        parts[here, :] = value.astype(BF16)
    fold.send_near()
    _, value = part(3)
    fold.pass_on()
    f = fold.total(value)
    gain = gain_ref[...]
    by_value, by_gain = normed_gradient(f, gain, dy_ref[...])
    df[rows_of(me, count), :] = by_value.astype(BF16)
    spread = Spread(halves_of(df, count), send, recv)
    spread.start()
    dgain_out[...] = by_gain
    x_out[...] = (h_ref[...] + f * inverse_rms(f) * gain).astype(BF16)

    def one(at):
        here = here_now(2, at)
        gate_up_gradient(df, here, w, gu, hidden)
        copy = pltpu.make_async_copy(gu.at[here], dgu_out.at[here], store.at[at])
        copy.start()
        return copy

    copies = [one(3)]
    spread.pass_on()
    spread.x_here()
    copies.append(one(1))
    spread.y_here()
    copies.append(one(2))
    spread.far_here()
    copies.append(one(0))

    def make(mine, first, width):
        side = core if mine else 1 - core
        start = pl.multiple_of(side * (hidden // 2) + first, 128)
        return tn(df[...], act[:, pl.ds(start, width)])

    sends, stores = swap_sum(
        make, column_tiles(hidden // 2), ours, theirs, came, swap_send, swap_recv, dw_out, out_sems
    )
    spread.finish()
    fold.finish()
    for copy in sends:
        copy.wait_send()
    for copy in copies + stores:
        copy.wait()


def feed_turn(h, gain, dy, act, w_dt, gu, collective_id):
    count, model = h.shape
    total, hidden = act.shape
    tiles = pltpu.SemaphoreType.DMA((len(column_tiles(hidden // 2)),))
    dw = pltpu.VMEM((model, hidden // 2), BF16)
    return pl.pallas_call(
        turn_kernel,
        out_shape=[
            jax.ShapeDtypeStruct((count, model), BF16),
            jax.ShapeDtypeStruct(gu.shape, BF16),
            jax.ShapeDtypeStruct((model, hidden // 2), BF16),
            jax.ShapeDtypeStruct((1, model), F32),
        ],
        in_specs=[vmem_spec()] * 3 + [any_spec()] * 3,
        out_specs=[vmem_spec(), any_spec(), any_spec(), vmem_spec()],
        scratch_shapes=[
            pltpu.VMEM(act.shape, BF16),
            pltpu.VMEM((model, hidden), BF16),
            pltpu.VMEM((total, model), BF16),
            pltpu.VMEM((total, model), BF16),
            pltpu.VMEM(gu.shape, BF16),
            dw,
            dw,
            dw,
            pltpu.SemaphoreType.DMA((3, 4)),
            pltpu.SemaphoreType.DMA((4,)),
            *fold_spec(count, model),
            *spread_spec(),
            tiles,
            tiles,
            tiles,
        ],
        compiler_params=params(collective_id, 60),
    )(h, gain, dy, act, w_dt, gu)


def feed_back_up(dy, f, gain, gu, act, w_dt, extra, collective_id):
    count, model = dy.shape
    total, hidden = act.shape
    tiles = len(column_tiles(hidden // 2))
    extras = () if extra is None else extra
    return pl.pallas_call(
        back_up_kernel,
        out_shape=[
            jax.ShapeDtypeStruct(gu.shape, BF16),
            jax.ShapeDtypeStruct((model, hidden // 2 + sum(e.shape[1] for e in extras[:1])), BF16),
            jax.ShapeDtypeStruct((1, model), F32),
        ],
        in_specs=[vmem_spec()] * 3 + [any_spec()] * (3 + len(extras)),
        out_specs=[any_spec(), any_spec(), vmem_spec()],
        scratch_shapes=[
            pltpu.VMEM((total, model), BF16),
            pltpu.VMEM(gu.shape, BF16),
            pltpu.VMEM(act.shape, BF16),
            pltpu.VMEM((model, hidden), BF16),
            pltpu.VMEM((model, hidden // 2), BF16),
            pltpu.VMEM((model, hidden // 2), BF16),
            pltpu.VMEM((model, hidden // 2), BF16),
            pltpu.SemaphoreType.DMA((3, 4)),
            pltpu.SemaphoreType.DMA((4,)),
            *spread_spec(),
            pltpu.SemaphoreType.DMA((tiles,)),
            pltpu.SemaphoreType.DMA((tiles,)),
            pltpu.SemaphoreType.DMA((tiles,)),
        ],
        compiler_params=params(collective_id, 60),
    )(dy, f, gain, gu, act, w_dt, *extras)


def back_down_kernel(
    dy_ref, h_ref, gain_ref, dgu_ref, rows_ref, w_ref, dh_out, dw_out, dgain_out,
    dgu, rows, w, parts, ours, theirs, came, load, land, passing, send, recv, swap_send, swap_recv, out_sems,
):
    count, model = dy_ref.shape
    hidden = dgu.shape[1] // 2
    me, nx, ny = neighbours()
    core = lax.axis_index("section")
    far = jnp.bitwise_xor(me, 3)
    met = greet({"narrow": nx}, {"narrow": ny}, {"section": 1 - core})
    weights = pltpu.make_async_copy(w_ref.at[:, pl.ds(0, 2 * hidden)], w, load.at[0])
    weights.start()
    arrivals = []
    for at, block in enumerate((far, nx, ny, me)):
        here = rows_of(block, count)
        arrivals.append(pltpu.make_async_copy(dgu_ref.at[here], dgu.at[here], load.at[1 + at]))
        arrivals[-1].start()
    kept = pltpu.make_async_copy(rows_ref, rows, load.at[5])
    kept.start()
    fold = Fold(halves_of(parts, count), land, passing, send, recv)
    weights.wait()
    met()

    def one(block, at, out, here):
        arrivals[at].wait()
        out[here, :] = nt(dgu[rows_of(block, count), :], w[...]).astype(out.dtype)

    one(far, 0, parts, rows_of(far, count))
    fold.send_far()
    one(nx, 1, parts, rows_of(nx, count))
    one(ny, 2, parts, rows_of(ny, count))
    fold.send_near()
    one(me, 3, dh_out, pl.ds(0, count))
    fold.pass_on()
    kept.wait()

    def make(mine, first, width):
        side = core if mine else 1 - core
        start = pl.multiple_of(side * hidden + first, 128)
        return tn(rows[...], dgu[:, pl.ds(start, width)])

    sends, stores = swap_sum(
        make, column_tiles(hidden), ours, theirs, came, swap_send, swap_recv, dw_out, out_sems
    )
    total = fold.total(dh_out[...])
    by_value, by_gain = normed_gradient(h_ref[...], gain_ref[...], total)
    dh_out[...] = dy_ref[...].astype(BF16).astype(F32) + by_value
    dgain_out[...] = by_gain
    fold.finish()
    for copy in sends:
        copy.wait_send()
    for copy in stores:
        copy.wait()


def feed_back_down(dy, h, gain, dgu, rows, w_gu, collective_id):
    count, model = dy.shape
    total, hidden = dgu.shape[0], dgu.shape[1] // 2
    tiles = len(column_tiles(hidden))
    return pl.pallas_call(
        back_down_kernel,
        out_shape=[
            jax.ShapeDtypeStruct((count, model), F32),
            jax.ShapeDtypeStruct((model, hidden), BF16),
            jax.ShapeDtypeStruct((1, model), F32),
        ],
        in_specs=[vmem_spec()] * 3 + [any_spec()] * 3,
        out_specs=[vmem_spec(), any_spec(), vmem_spec()],
        scratch_shapes=[
            pltpu.VMEM(dgu.shape, BF16),
            pltpu.VMEM(rows.shape, BF16),
            pltpu.VMEM((model, 2 * hidden), BF16),
            pltpu.VMEM((total, model), BF16),
            pltpu.VMEM((model, hidden), BF16),
            pltpu.VMEM((model, hidden), BF16),
            pltpu.VMEM((model, hidden), BF16),
            pltpu.SemaphoreType.DMA((6,)),
            *fold_spec(count, model),
            pltpu.SemaphoreType.DMA((tiles,)),
            pltpu.SemaphoreType.DMA((tiles,)),
            pltpu.SemaphoreType.DMA((tiles,)),
        ],
        compiler_params=params(collective_id, 60),
    )(dy, h, gain, dgu, rows, w_gu)


def pack_kernel(p_ref, o_ref, g_ref, local, send, recv, peer_send, peer_recv):
    half = p_ref.shape[0] // 2
    width = o_ref.shape[3]
    core = lax.axis_index("section")
    me, nx, ny = neighbours()
    met = greet({"narrow": nx}, {"narrow": ny}, {"section": 1 - core})
    owns = [
        pltpu.make_async_copy(p_ref.at[:, pl.ds(0, width)], o_ref.at[core, me], local.at[0]),
        pltpu.make_async_copy(p_ref.at[:, pl.ds(width, g_ref.shape[2])], g_ref.at[core], local.at[1]),
    ]
    for copy in owns:
        copy.start()
    spread = Spread(lambda block, which: o_ref.at[core, block, pl.ds(which * half, half)], send, recv)
    for copy in owns:
        copy.wait()
    met()
    spread.start()
    copies = []

    def across(ref):
        copy = pltpu.make_async_remote_copy(
            src_ref=ref,
            dst_ref=ref,
            send_sem=peer_send.at[len(copies)],
            recv_sem=peer_recv.at[len(copies)],
            device_id={"section": 1 - core},
            device_id_type=MESH,
        )
        copy.start()
        copies.append(copy)

    across(g_ref.at[core])
    across(o_ref.at[core, me])
    spread.pass_on()
    spread.x_here()
    across(o_ref.at[core, nx])
    spread.y_here()
    across(o_ref.at[core, ny])
    spread.far_here()
    across(o_ref.at[core, spread.far])
    for copy in copies:
        copy.wait_recv()
    spread.finish()
    for copy in copies:
        copy.wait_send()


def gather_pack(pack, width, collective_id):
    model = pack.shape[0]
    return pl.pallas_call(
        pack_kernel,
        out_shape=[
            jax.ShapeDtypeStruct((2, 4, model, width), pack.dtype),
            jax.ShapeDtypeStruct((2, model, pack.shape[1] - width), pack.dtype),
        ],
        in_specs=[any_spec()],
        out_specs=[vmem_spec()] * 2,
        scratch_shapes=[
            pltpu.SemaphoreType.DMA((2,)),
            *spread_spec(),
            pltpu.SemaphoreType.DMA((5,)),
            pltpu.SemaphoreType.DMA((5,)),
        ],
        compiler_params=params(collective_id, 32),
    )(pack)


def finish_kernel(zero_ref, one_ref, dep_ref, q_out, kv_out, o_out, give, came, kv, send, recv, kv_send, kv_recv):
    core = lax.axis_index("section")
    me, nx, ny = neighbours()
    others = (nx, ny, jnp.bitwise_xor(me, 3))
    met = greet({"section": 1 - core}, *[{"narrow": other} for other in others])
    head = q_out.shape[1]
    first = core == 0
    zero, one = zero_ref[...], one_ref[...]
    give[...] = jnp.where(first, one, zero)
    keep = jnp.where(first, zero, one)
    met()
    across = pltpu.make_async_remote_copy(
        src_ref=give,
        dst_ref=came,
        send_sem=send,
        recv_sem=recv,
        device_id={"section": 1 - core},
        device_id_type=MESH,
    )
    across.start()
    across.wait_recv()
    by_qkv = jnp.where(first, keep, came[...])
    by_out = jnp.where(first, came[...], keep)
    kv[me] = by_qkv[:, head:]
    copies = []
    for at, other in enumerate(others):
        copies.append(remote(kv.at[me], kv.at[me], kv_send.at[at], kv_recv.at[at], other))
        copies[-1].start()
    q_out[...] = by_qkv[:, :head].astype(F32)
    o_out[...] = by_out[:, :head].astype(F32)
    for copy in copies:
        copy.wait_recv()
    width = kv.shape[2]
    for n in range(4):
        kv_out[:, n * width : (n + 1) * width] = kv[n].astype(F32)
    across.wait_send()
    for copy in copies:
        copy.wait_send()


def finish_attention(zero, one, dep, head, collective_id):
    block, width = zero.shape
    return pl.pallas_call(
        finish_kernel,
        out_shape=[
            jax.ShapeDtypeStruct((block, head), F32),
            jax.ShapeDtypeStruct((block, 4 * (width - head)), F32),
            jax.ShapeDtypeStruct((block, head), F32),
        ],
        in_specs=[vmem_spec()] * 2 + [any_spec()],
        out_specs=[vmem_spec()] * 3,
        scratch_shapes=[
            pltpu.VMEM((block, width), BF16),
            pltpu.VMEM((block, width), BF16),
            pltpu.VMEM((4, block, width - head), BF16),
            pltpu.SemaphoreType.DMA,
            pltpu.SemaphoreType.DMA,
            pltpu.SemaphoreType.DMA((3,)),
            pltpu.SemaphoreType.DMA((3,)),
        ],
        compiler_params=params(collective_id, 16),
    )(zero, one, dep)


class Share:
    def __init__(self, xn_ref, o_ref, xn, o, loads, spread_send, spread_recv, deal_send, deal_recv):
        count, head = xn_ref.shape[0], o.shape[1]
        me = lax.axis_index("narrow")
        self.loads = [
            pltpu.make_async_copy(xn_ref, xn.at[rows_of(me, count)], loads.at[0]),
            pltpu.make_async_copy(o_ref.at[:, columns_of(me, head)], o.at[rows_of(me, count)], loads.at[1]),
        ]
        self.spread = Spread(halves_of(xn, count), spread_send, spread_recv)
        self.deal = Deal(
            lambda other: o_ref.at[:, columns_of(other, head)],
            lambda mine: o.at[rows_of(mine, count)],
            deal_send,
            deal_recv,
        )

    def start_rows(self):
        self.loads[0].start()
        self.loads[0].wait()
        self.spread.start()

    def start_deal(self):
        self.loads[1].start()
        self.deal.start()

    def all_here(self):
        self.spread.all_here()
        self.deal.here()

    def finish(self):
        self.spread.finish()
        self.deal.finish()
        self.loads[1].wait()


def share_spec(count, model, head):
    return [
        pltpu.VMEM((4 * count, model), BF16),
        pltpu.VMEM((4 * count, head), BF16),
        pltpu.SemaphoreType.DMA((4,)),
        *spread_spec(),
        pltpu.SemaphoreType.DMA((3,)),
        pltpu.SemaphoreType.DMA((3,)),
    ]


def share_shapes(xn, o):
    total = 4 * xn.shape[0]
    return [
        jax.ShapeDtypeStruct((total, xn.shape[1]), BF16),
        jax.ShapeDtypeStruct((total, o.shape[1] // 4), BF16),
    ]


def gain_kernel(g_ref, o_ref, land, total, send, recv):
    core, wide = lax.axis_index("section"), lax.axis_index("wide")
    wides = land.shape[0] - 3
    me, nx, ny = neighbours()
    far = jnp.bitwise_xor(me, 3)
    stages = [
        [{"narrow": nx}, {"narrow": ny}, {"narrow": far}],
        [{"section": 1 - core}],
        [{"wide": lax.rem(wide + step, wides)} for step in range(1, wides)],
    ]
    met = greet(*stages[0], *stages[1], *stages[2])
    total[0] = g_ref[...]
    met()
    at = 0
    copies = []
    for stage, others in enumerate(stages):
        mine = []
        for other in others:
            mine.append(
                pltpu.make_async_remote_copy(
                    src_ref=total.at[stage],
                    dst_ref=land.at[at],
                    send_sem=send.at[at],
                    recv_sem=recv.at[at],
                    device_id=other,
                    device_id_type=MESH,
                )
            )
            mine[-1].start()
            at += 1
        value = total[stage]
        for place, copy in enumerate(mine, at - len(mine)):
            copy.wait_recv()
            value = value + land[place]
        total[stage + 1] = value
        copies += mine
    o_ref[...] = total[3]
    for copy in copies:
        copy.wait_send()


def sum_gains(block, wides, collective_id):
    return pl.pallas_call(
        gain_kernel,
        out_shape=jax.ShapeDtypeStruct(block.shape, F32),
        in_specs=[vmem_spec()],
        out_specs=vmem_spec(),
        scratch_shapes=[
            pltpu.VMEM((wides + 3, *block.shape), F32),
            pltpu.VMEM((4, *block.shape), F32),
            pltpu.SemaphoreType.DMA((wides + 3,)),
            pltpu.SemaphoreType.DMA((wides + 3,)),
        ],
        compiler_params=params(collective_id, 16),
    )(block)


def turn_back(grad, cosine, sine_table):
    half = grad.shape[1] // 2
    front, back = grad[:, :half], grad[:, half:]
    return jnp.concatenate(
        [front * cosine + back * sine_table, back * cosine - front * sine_table], axis=1
    )


def pack_loads(pack_ref, layer, head, wq, wot, wkv, sems):
    kv_part = wkv.shape[1] // 4
    loads = []
    for at, (w, first, width) in enumerate(
        ((wq, 0, head), (wot, head, head), (wkv, 2 * head, kv_part))
    ):
        loads.append(
            [
                pltpu.make_async_copy(
                    pack_ref.at[layer, n, :, pl.ds(first, width)], w.at[:, pl.ds(n * width, width)], sems.at[at, n]
                )
                for n in range(4)
            ]
        )
    return loads


def start_all(copies):
    for copy in copies:
        copy.start()


def wait_all(copies):
    for copy in copies:
        copy.wait()


def window_mask(me, count, window, length):
    rows_at = me * count + lax.broadcasted_iota(jnp.int32, (count, 1), 0)
    cols_at = me * count - WINDOW + lax.broadcasted_iota(jnp.int32, (1, window), 1)
    return (
        (cols_at <= rows_at)
        & (rows_at - cols_at < WINDOW)
        & (cols_at >= 0)
        & ((cols_at < length) | (cols_at == rows_at))
    )


def attend_kernel(layer, length_ref, x_ref, gains_ref, head_ref, trig_ref, pack_ref, *refs):
    (
        h_out, xn_out, q_out, k_out, win_out, lse_out, o_out, a_out, *refs
    ) = refs
    sharing = len(refs) > 9
    if sharing:
        xn_all_out, o_all_out, *refs = refs
    kv, wq, wot, wkv, load, send, recv, *share_refs = refs
    count, model = x_ref.shape
    head = k_out.shape[1]
    heads = q_out.shape[1] // head
    me, nx, ny = neighbours()
    met = greet({"narrow": nx}, {"narrow": ny}, {"narrow": jnp.bitwise_xor(me, 3)})
    q_loads, out_loads, kv_loads = pack_loads(pack_ref, layer, head, wq, wot, wkv, load)
    start_all(kv_loads + q_loads + out_loads)
    scaling = head ** (-0.5)
    cosine, sine_table = trig_ref[:, : head // 2], trig_ref[:, head // 2 :]
    x = x_ref[...].astype(F32)
    xn_out[...] = (x * inverse_rms(x) * gains_ref[0:1, :]).astype(BF16)
    kv[pl.ds(0, WINDOW), :] = jnp.zeros((WINDOW, 2 * head), BF16)
    wait_all(kv_loads)
    raw = nn(xn_out[...], wkv[...])
    k_raw = raw[:, :head]
    k_out[...] = k_raw
    k_rot = rotate(k_raw * inverse_rms(k_raw) * head_ref[1:2, :], cosine, sine_table)
    here = pl.ds(pl.multiple_of(WINDOW + me * count, count), count)
    kv[here, :head] = k_rot.astype(BF16)
    kv[here, head:] = raw[:, head:].astype(BF16)
    spread = Spread(halves_of(kv, count, WINDOW), send, recv)
    met()
    spread.start()
    if sharing:
        share = Share(xn_out, o_out, *share_refs)
    wait_all(q_loads)
    q_out[...] = nn(xn_out[...], wq[...])
    spread.pass_on()
    if sharing:
        share.start_rows()
    spread.all_here()
    window = win_out.shape[0]
    win_out[...] = kv[pl.ds(pl.multiple_of(me * count, count), window), :]
    visible = window_mask(me, count, window, length_ref[0])
    k_win, v_win = win_out[:, :head], win_out[:, head:]
    q_gain = head_ref[0:1, :]

    def one_head(i):
        columns = columns_of(i, head)
        q_raw = q_out[:, columns]
        qr = rotate(q_raw * inverse_rms(q_raw) * q_gain, cosine, sine_table).astype(BF16)
        scores = jnp.where(visible, nt(qr, k_win) * scaling, NEGATIVE)
        most = jnp.max(scores, axis=-1, keepdims=True)
        exponent = jnp.exp(scores - most)
        total = jnp.sum(exponent, axis=-1, keepdims=True)
        lse_out[i] = most + jnp.log(total)
        o_out[:, columns] = nn((exponent / total).astype(BF16), v_win).astype(BF16)

    for i in range(heads):
        one_head(i)
    if sharing:
        share.start_deal()
        share.spread.pass_on()
    wait_all(out_loads)
    a = nt(o_out[...], wot[...])
    a_out[...] = a
    h_out[...] = x_ref[...].astype(F32) + a * inverse_rms(a) * gains_ref[1:2, :]
    spread.finish()
    if sharing:
        share.all_here()
        share.finish()
        xn, o, loads = share_refs[:3]
        stores = [
            pltpu.make_async_copy(xn, xn_all_out, loads.at[2]),
            pltpu.make_async_copy(o, o_all_out, loads.at[3]),
        ]
        start_all(stores)
        wait_all(stores)


def attend(length, x, gains, head_gains, trig, pack, head, layer, collective_id):
    count, model = x.shape
    kv_width = 2 * head
    width = 4 * head
    window = count + WINDOW
    sharing = True
    xn_shape = jax.ShapeDtypeStruct((count, model), BF16)
    o_shape = jax.ShapeDtypeStruct((count, width), BF16)
    shapes = [
        jax.ShapeDtypeStruct((count, model), F32),
        xn_shape,
        jax.ShapeDtypeStruct((count, width), F32),
        jax.ShapeDtypeStruct((count, head), F32),
        jax.ShapeDtypeStruct((window, kv_width), BF16),
        jax.ShapeDtypeStruct((4, count, 1), F32),
        o_shape,
        jax.ShapeDtypeStruct((count, model), F32),
    ]
    outs = [vmem_spec()] * 8
    if sharing:
        shapes += share_shapes(xn_shape, o_shape)
        outs += [any_spec()] * 2
    return pl.pallas_call(
        functools.partial(attend_kernel, layer),
        out_shape=shapes,
        in_specs=[pl.BlockSpec(memory_space=pltpu.SMEM)] + [vmem_spec()] * 4 + [any_spec()],
        out_specs=outs,
        scratch_shapes=[
            pltpu.VMEM((4 * count + WINDOW, kv_width), BF16),
            pltpu.VMEM((model, width), BF16),
            pltpu.VMEM((model, width), BF16),
            pltpu.VMEM((model, kv_width), BF16),
            pltpu.SemaphoreType.DMA((3, 4)),
            *spread_spec(),
            *(share_spec(count, model, head) if sharing else []),
        ],
        compiler_params=params(collective_id, 40),
    )(length, x, gains, head_gains, trig, pack)


def attend_back_kernel(
    layer, length_ref, dh_ref, a_ref, x_ref, gains_ref, head_ref, trig_ref, q_ref, k_ref, win_ref, lse_ref,
    pack_ref, xn_ref, o_ref, *refs
):
    (
    dx_out, dw_out, dgain_out, dhead_out,
    da, do, dq, dk, dv, parts, dq_all, dkv, dkv_all, wq, wot, wkv, xn, o, ours, theirs, came,
    pack_load, load, send, recv, land, passing, fold_send, fold_recv, q_send, q_recv, kv_send, kv_recv, swap_send, swap_recv, out_sem,
    ) = refs[-36:]
    count = dh_ref.shape[0]
    head = k_ref.shape[1]
    heads = q_ref.shape[1] // head
    kv_part = dkv_all.shape[1]
    me, nx, ny = neighbours()
    core = lax.axis_index("section")
    far = jnp.bitwise_xor(me, 3)
    met = greet({"narrow": nx}, {"narrow": ny}, {"narrow": far}, {"section": 1 - core})
    q_loads, out_loads, kv_loads = pack_loads(pack_ref, layer, head, wq, wot, wkv, pack_load)
    loads = [
        pltpu.make_async_copy(src, dst, load.at[at])
        for at, (src, dst) in enumerate(((xn_ref, xn), (o_ref, o)))
    ]
    start_all(out_loads + q_loads + kv_loads + loads)
    here = rows_of(me, count)
    scaling = head ** (-0.5)
    cosine, sine_table = trig_ref[:, : head // 2], trig_ref[:, head // 2 :]

    dh = dh_ref[...]
    by_value, dg1 = normed_gradient(a_ref[...], gains_ref[1:2, :], dh)
    da[here, :] = by_value.astype(BF16)
    dgain_out[1:2, :] = dg1
    spread = Spread(halves_of(da, count), send, recv)
    met()
    spread.start()
    wait_all(out_loads)
    do[...] = nn(da[here, :], wot[...]).astype(BF16)

    visible = window_mask(me, count, win_ref.shape[0], length_ref[0])
    k_win, v_win = win_ref[:, :head], win_ref[:, head:]
    dk[...] = jnp.zeros_like(dk)
    dv[...] = jnp.zeros_like(dv)
    dhead_out[...] = jnp.zeros_like(dhead_out)
    q_gain, k_gain = head_ref[0:1, :], head_ref[1:2, :]

    def one_head(i):
        columns = columns_of(i, head)
        raw = q_ref[:, columns]
        inverse = inverse_rms(raw)
        unit = raw * inverse
        qr = rotate(unit * q_gain, cosine, sine_table).astype(BF16)
        scores = jnp.where(visible, nt(qr, k_win) * scaling, NEGATIVE)
        probs = jnp.exp(scores - lse_ref[i])
        do_head = do[:, columns]
        dp = nt(do_head, v_win)
        ds = (probs * (dp - jnp.sum(probs * dp, axis=-1, keepdims=True))).astype(BF16)
        dk[...] += tn(ds, qr)
        dv[...] += tn(probs.astype(BF16), do_head)
        grad = turn_back(nn(ds, k_win) * scaling, cosine, sine_table)
        scaled = grad * q_gain
        dq_raw = inverse * (scaled - unit * jnp.mean(scaled * unit, axis=-1, keepdims=True))
        dq[:, columns] = dq_raw.astype(BF16)
        dhead_out[0:1, :] += jnp.sum(grad * unit, axis=0, keepdims=True)

    for i in range(heads):
        one_head(i)
    parts[...] = jnp.zeros_like(parts)
    window = pl.ds(pl.multiple_of(me * count, count), win_ref.shape[0])
    parts[window, :head] = (dk[...] * scaling).astype(BF16)
    parts[window, head:] = dv[...].astype(BF16)
    fold = Fold(halves_of(parts, count, WINDOW), land, passing, fold_send, fold_recv)
    fold.send_far()
    fold.send_near()
    deal_q = Deal(
        lambda other: dq.at[:, columns_of(other, head)],
        lambda mine: dq_all.at[rows_of(mine, count)],
        q_send,
        q_recv,
    )
    deal_q.start()
    dq_all[here, :] = dq[:, columns_of(me, head)]
    spread.pass_on()
    wait_all(q_loads)
    dx_out[...] = nt(dq[...], wq[...])
    fold.pass_on()
    spread.all_here()
    wait_all(loads)
    first = core == 0
    swaps = []

    def exchange(at, columns, a, b):
        ours[:, columns] = jnp.where(first, a, b).astype(BF16)
        theirs[:, columns] = jnp.where(first, b, a).astype(BF16)
        copy = pltpu.make_async_remote_copy(
            src_ref=theirs.at[:, columns],
            dst_ref=came.at[:, columns],
            send_sem=swap_send.at[at],
            recv_sem=swap_recv.at[at],
            device_id={"section": 1 - core},
            device_id_type=MESH,
        )
        copy.start()
        swaps.append(copy)

    by_out = tn(da[...], o[...])
    deal_q.here()
    exchange(0, pl.ds(0, head), tn(xn[...], dq_all[...]), by_out)
    own = jnp.concatenate([dk[WINDOW:, :] * scaling, dv[WINDOW:, :]], axis=1)
    total = fold.total(own)
    grad = turn_back(total[:, :head], cosine, sine_table)
    dk_raw, dk_gain = normed_gradient(k_ref[...], k_gain, grad)
    dhead_out[1:2, :] = dk_gain
    dkv[:, :head] = dk_raw.astype(BF16)
    dkv[:, head:] = total[:, head:].astype(BF16)
    deal_kv = Deal(
        lambda other: dkv.at[:, columns_of(other, kv_part)],
        lambda mine: dkv_all.at[rows_of(mine, count)],
        kv_send,
        kv_recv,
    )
    deal_kv.start()
    dkv_all[here, :] = dkv[:, columns_of(me, kv_part)]
    wait_all(kv_loads)
    dxn = dx_out[...] + nt(dkv[...], wkv[...])
    by_value, dg0 = normed_gradient(x_ref[...].astype(F32), gains_ref[0:1, :], dxn)
    dx_out[...] = dh_ref[...] + by_value
    dgain_out[0:1, :] = dg0

    deal_kv.here()
    by_kv = tn(xn[...], dkv_all[...])
    exchange(1, pl.ds(head, kv_part), by_kv, jnp.zeros_like(by_kv))
    for copy in swaps:
        copy.wait_recv()
    ours[...] = (ours[...].astype(F32) + came[...].astype(F32)).astype(BF16)
    out = pltpu.make_async_copy(ours, dw_out, out_sem)
    out.start()
    spread.finish()
    fold.finish()
    deal_q.finish()
    deal_kv.finish()
    for copy in swaps:
        copy.wait_send()
    out.wait()


def attend_back(length, dh, a, x, gains, head_gains, trig, q_raw, k_raw, window, lse, pack, xn, o, deps, layer, collective_id):
    count, model = dh.shape
    head = k_raw.shape[1]
    width = q_raw.shape[1]
    kv_part = pack.shape[3] - 2 * head
    deal = pltpu.SemaphoreType.DMA((3,))
    dw = pltpu.VMEM((model, head + kv_part), BF16)
    return pl.pallas_call(
        functools.partial(attend_back_kernel, layer),
        out_shape=[
            jax.ShapeDtypeStruct((count, model), F32),
            jax.ShapeDtypeStruct((model, head + kv_part), BF16),
            jax.ShapeDtypeStruct((2, model), F32),
            jax.ShapeDtypeStruct((2, head), F32),
        ],
        in_specs=[pl.BlockSpec(memory_space=pltpu.SMEM)] + [vmem_spec()] * 10 + [any_spec()] * (3 + len(deps)),
        out_specs=[vmem_spec(), any_spec(), vmem_spec(), vmem_spec()],
        scratch_shapes=[
            pltpu.VMEM((4 * count, model), BF16),
            pltpu.VMEM((count, width), BF16),
            pltpu.VMEM((count, width), BF16),
            pltpu.VMEM((window.shape[0], head), F32),
            pltpu.VMEM((window.shape[0], head), F32),
            pltpu.VMEM((4 * count + WINDOW, 2 * head), BF16),
            pltpu.VMEM((4 * count, head), BF16),
            pltpu.VMEM((count, 2 * head), BF16),
            pltpu.VMEM((4 * count, kv_part), BF16),
            pltpu.VMEM((model, width), BF16),
            pltpu.VMEM((model, width), BF16),
            pltpu.VMEM((model, 2 * head), BF16),
            pltpu.VMEM(xn.shape, BF16),
            pltpu.VMEM(o.shape, BF16),
            dw,
            dw,
            dw,
            pltpu.SemaphoreType.DMA((3, 4)),
            pltpu.SemaphoreType.DMA((2,)),
            *spread_spec(),
            *fold_spec(count, 2 * head),
            deal,
            deal,
            deal,
            deal,
            pltpu.SemaphoreType.DMA((2,)),
            pltpu.SemaphoreType.DMA((2,)),
            pltpu.SemaphoreType.DMA,
        ],
        compiler_params=params(collective_id, 48),
    )(length, dh, a, x, gains, head_gains, trig, q_raw, k_raw, window, lse, pack, xn, o, *deps)


def after(value, *others):
    return pl.pallas_call(
        lambda *refs: None,
        out_shape=jax.ShapeDtypeStruct(value.shape, value.dtype),
        in_specs=[any_spec()] * (1 + len(others)),
        out_specs=any_spec(),
        input_output_aliases={0: 0},
    )(value, *others)


def scatter(member):
    return lax.psum_scatter(member, "wide", scatter_dimension=0, tiled=True)


def on_device(
    inputs, cotangent, lengths, norm_gains, head_gains, w_q, w_kv, w_o, w_gate_up, w_down
):
    core = lax.axis_index("section")
    narrow = lax.axis_index("narrow")
    n_narrow = lax.axis_size("narrow")
    is_zero = core == 0
    rows, model = inputs.shape[1], inputs.shape[2]
    block = w_q.shape[1]
    head_width = w_q.shape[2]
    n_wide = lax.axis_size("wide")
    hidden = w_down.shape[1]
    kv_part = w_kv.shape[2] // n_narrow

    def swap(value):
        return lax.ppermute(value, "section", [(0, 1), (1, 0)])

    def by_core(first, second):
        return jnp.where(is_zero, first, second)

    half = block // 2

    pad = -hidden % TILE
    kv_own = lax.dynamic_slice_in_dim(w_kv[0], narrow * kv_part, kv_part, 1)
    pack_width = 2 * head_width + kv_part
    gain_columns = jnp.zeros((block, GAIN_COLUMNS), BF16)
    gain_columns = lax.dynamic_update_slice(gain_columns, norm_gains[0].T, (0, 0))
    gain_columns = lax.dynamic_update_slice(gain_columns, head_gains[0].T, (0, 4))
    pack = jnp.concatenate([w_q[0], w_o[0].T, kv_own, gain_columns], axis=1)

    late = after(core.reshape(1), pack)[0]

    def half_of(side):
        gate_up = lax.dynamic_slice_in_dim(w_gate_up[0], side * half, half, 0)
        gate_up = jnp.pad(gate_up, ((0, 0), (0, 0), (0, pad))).reshape(half, -1)
        down = lax.dynamic_slice_in_dim(w_down[0].T, side * half, half, 0)
        return jnp.concatenate([gate_up, jnp.pad(down, ((0, 0), (0, pad)))], axis=1)

    keep, came = half_of(late), swap(half_of(1 - late))
    feed = by_core(keep, came), by_core(came, keep)
    padded = hidden + pad

    def gather(member):
        return lax.all_gather(member, ("wide", "section"), axis=0, tiled=True)

    both = gather(feed[0])
    feeds = [
        (both, both, padded),
        (gather(feed[1][:, : 2 * padded]), gather(feed[1][:, 2 * padded :]), padded),
    ]
    pack = lax.all_gather(pack, "wide", axis=0, tiled=True)
    packs, gain_packs = gather_pack(pack, pack_width, 6)

    def gains_of(section):
        columns = gain_packs[section].astype(F32)
        heads = columns.reshape(n_wide, block, -1)[:, : head_width // n_wide, 4:6]
        return columns[:, :4].T, heads.transpose(2, 0, 1).reshape(2, head_width)

    start = narrow * rows
    positions = start + jnp.arange(rows, dtype=jnp.int32)
    trig = tables(positions, head_width)
    length = lax.dynamic_index_in_dim(lengths[:, 0], core, 0, keepdims=False)

    x = lax.dynamic_index_in_dim(inputs, core, 0, keepdims=False)
    length_one = length.reshape(1)
    outs, kept, gains = [], [], []
    for section in range(2):
        layer_gains, head_gain = gains_of(section)
        gains.append((layer_gains, head_gain))
        h, xn, q_raw, k_raw, window, lse, o, a, *shared = attend(
            length_one, x, layer_gains, head_gain, trig, packs, head_width, section, 8 + section
        )
        w_up, w_down, _ = feeds[section]
        mid_rows, gu, act = feed_up(h, layer_gains[2:3], w_up, padded, (), 10 + section)
        kept.append(((a, x, q_raw, k_raw, window, lse), (h, mid_rows, gu, act), shared))
        if section == 0:
            x, f = feed_down(h, layer_gains[3:4], act, w_down, 12)
            outs.append(x)

    real = (positions < length).astype(F32)[:, None]
    dy = lax.dynamic_index_in_dim(cotangent, core, 0, keepdims=False).astype(F32) * real
    dxs, gain_grads = [None, None], [None, None]
    up_sums, down_sums, attention_sums = [None, None], [None, None], [None, None]
    extra = None
    for section in (1, 0):
        kept_a, (h, mid_rows, gu, act), (xn, o) = kept[section]
        layer_gains, head_gain = gains[section]
        w_up, w_down, _ = feeds[section]
        if section:
            out, dgu, d_down, dg3 = feed_turn(h, layer_gains[3:4], dy, act, w_down, gu, 13)
            outs.append(out)
        else:
            dgu, d_down, dg3 = feed_back_up(
                dy, f, layer_gains[3:4], gu, act, w_down, (extra, down_sums[1]), 14
            )
        down_sums[section] = scatter(d_down)
        dh, d_up, dg2 = feed_back_down(dy, h, layer_gains[2:3], dgu, mid_rows, w_up, 16 + section)
        up_sums[section] = scatter(d_up)
        dg23 = (dg2, dg3)
        a, x, q_raw, k_raw, window, lse = kept_a
        dx, extra, dg01, dhead = attend_back(
            length_one, dh, a, x, layer_gains, head_gain, trig, q_raw, k_raw, window, lse, packs, xn, o,
            () if section else (up_sums[1],), section, 18 + section,
        )
        dxs[section] = dx
        head_row = jnp.pad(dhead.reshape(1, -1), ((0, 0), (0, model - dhead.size)))
        gain_grads[section] = jnp.concatenate([dg01, *dg23, head_row, jnp.zeros((3, model), F32)])
        dy = dx
    outs = [after(out, extra) for out in outs]
    split = down_sums[1].shape[1]
    attention_sums = (scatter(extra), down_sums[0][:, split:])
    down_sums[0] = down_sums[0][:, :split]

    def own_section(first, second):
        came = swap(by_core(second, first))
        stays = by_core(first, second)
        return by_core(stays, came).astype(F32), by_core(came, stays).astype(F32)

    grad_gate_up = jnp.stack(own_section(*up_sums), axis=1)[:, :, :hidden]
    grad_down = jnp.concatenate(own_section(*down_sums), axis=1)[:, :hidden].T
    grad_q, grad_kv, grad_o = finish_attention(*attention_sums, grad_gate_up, head_width, 1)
    grad_o = grad_o.T
    gain_sums = sum_gains(jnp.concatenate(gain_grads), n_wide, 7)
    gain_sums = lax.dynamic_slice_in_dim(gain_sums, core * 8, 8, 0)
    wide = lax.axis_index("wide")
    grad_norm = lax.dynamic_slice_in_dim(gain_sums[:4], wide * block, block, 1)
    grad_head = gain_sums[4, : 2 * head_width].reshape(2, head_width)
    head_block = head_width // n_wide
    grad_head = lax.dynamic_slice_in_dim(grad_head, wide * head_block, head_block, 1)

    def by_section(first, second):
        stays, came = by_core(first, second), swap(by_core(second, first))
        return jnp.stack([by_core(stays, came), by_core(came, stays)])

    return (
        by_section(*outs)[None],
        by_section(*dxs)[None],
        grad_norm[None],
        grad_head[None],
        grad_q[None],
        grad_kv[None],
        grad_o[None],
        grad_gate_up[None],
        grad_down[None],
    )


def solution(mesh):
    return jax.shard_map(
        on_device,
        mesh=mesh,
        in_specs=(
            P(None, ("wide", "narrow"), None),
            P(None, ("wide", "narrow"), None),
            P(None, "wide"),
            P("section", None, "wide"),
            P("section", None, "wide"),
            P("section", "wide", "narrow"),
            P("section", "wide", None),
            P("section", "narrow", "wide"),
            P("section", "wide", None, "narrow"),
            P("section", "narrow", "wide"),
        ),
        out_specs=(
            P("section", None, ("wide", "narrow"), None),
            P("section", None, ("wide", "narrow"), None),
            P("section", None, "wide"),
            P("section", None, "wide"),
            P("section", "wide", "narrow"),
            P("section", "wide", None),
            P("section", "narrow", "wide"),
            P("section", "wide", None, "narrow"),
            P("section", "narrow", "wide"),
        ),
        check_vma=False,
    )
```

```python
import functools

import jax
import jax.numpy as jnp
from jax import lax
from jax.experimental import pallas as pl
from jax.experimental.pallas import tpu as pltpu
from jax.sharding import PartitionSpec as P

WINDOW = 512
EPSILON = 1e-06
NEGATIVE = -1e30
ROPE_BASE = 10000.0
MESH = pl.DeviceIdType.MESH
MIB = 2**20
GAIN_COLUMNS = 128
F32 = jnp.float32
BF16 = jnp.bfloat16


def dot(a, b, dims):
    return lax.dot_general(a, b, ((dims[0], dims[1]), ((), ())), preferred_element_type=F32)


def nn(a, b):
    return dot(a, b, ((1,), (0,)))


def nt(a, b):
    return dot(a, b, ((1,), (1,)))


def tn(a, b):
    return dot(a, b, ((0,), (0,)))


def normed(operand, gain_vec):
    return (
        operand
        * lax.rsqrt(jnp.mean(operand * operand, axis=-1, keepdims=True) + EPSILON)
        * gain_vec
    )


def geglu(gate, up):
    return jax.nn.gelu(gate, approximate=True) * up


def neighbours():
    me = lax.axis_index("narrow")
    return me, jnp.bitwise_xor(me, 1), jnp.bitwise_xor(me, 2)


def meet(nx, ny):
    barrier = pltpu.get_barrier_semaphore()
    for other in (nx, ny):
        pl.semaphore_signal(barrier, inc=1, device_id={"narrow": other}, device_id_type=MESH)
    pl.semaphore_wait(barrier, 2)


def remote(src, dst, send_sem, recv_sem, other):
    return pltpu.make_async_remote_copy(
        src_ref=src,
        dst_ref=dst,
        send_sem=send_sem,
        recv_sem=recv_sem,
        device_id={"narrow": other},
        device_id_type=MESH,
    )


def tables(positions, head_width):
    half_width = head_width // 2
    frequency = ROPE_BASE ** (-jnp.arange(half_width, dtype=F32) * (2.0 / head_width))
    angles = positions.astype(F32)[:, None] * frequency[None, :]
    return jnp.concatenate([jnp.cos(angles), jnp.sin(angles)], axis=1)


def rotate(operand, cosine, sine_table):
    half_width = operand.shape[-1] // 2
    front_half = operand[..., :half_width]
    back_half = operand[..., half_width:]
    return jnp.concatenate(
        [
            front_half * cosine - back_half * sine_table,
            back_half * cosine + front_half * sine_table,
        ],
        axis=-1,
    )


GELU_SCALE = 0.7978845608028654
GELU_CUBE = 0.044715


def vmem_spec():
    return pl.BlockSpec(memory_space=pltpu.VMEM)


def any_spec():
    return pl.BlockSpec(memory_space=pl.ANY)


def rows_of(block, count):
    return pl.ds(pl.multiple_of(block * count, count), count)


def columns_of(tile, width, offset=0):
    if isinstance(tile, int):
        return pl.ds(tile * width + offset, width)
    return pl.ds(pl.multiple_of(tile * width + offset, 128), width)


def inverse_rms(value):
    return lax.rsqrt(jnp.mean(value * value, axis=-1, keepdims=True) + EPSILON)


def normed_gradient(value, gain, grad):
    inverse = inverse_rms(value)
    unit = value * inverse
    scaled = grad * gain
    by_value = inverse * (scaled - unit * jnp.mean(scaled * unit, axis=-1, keepdims=True))
    return by_value, jnp.sum(grad * unit, axis=0, keepdims=True)


def halves_of(ref, count, base=0):
    half = count // 2

    def part(block, which):
        return ref.at[pl.ds(pl.multiple_of(base + block * count + which * half, half), half)]

    return part


class Spread:
    def __init__(self, part, send, recv):
        self.me, self.nx, self.ny = neighbours()
        self.far = jnp.bitwise_xor(self.me, 3)

        def copy(block, which, at, other):
            ref = part(block, which)
            return remote(ref, ref, send.at[at], recv.at[at], other)

        self.to_x1 = copy(self.me, 0, 0, self.nx)
        self.to_y2 = copy(self.me, 1, 1, self.ny)
        self.to_x2 = copy(self.me, 1, 2, self.nx)
        self.to_y1 = copy(self.me, 0, 3, self.ny)
        self.on_y = copy(self.nx, 0, 4, self.ny)
        self.on_x = copy(self.ny, 1, 5, self.nx)

    def start(self):
        for copy in (self.to_x1, self.to_y2, self.to_x2, self.to_y1):
            copy.start()

    def pass_on(self):
        self.to_x1.wait_recv()
        self.on_y.start()
        self.to_y2.wait_recv()
        self.on_x.start()

    def x_here(self):
        self.to_x2.wait_recv()

    def y_here(self):
        self.to_y1.wait_recv()

    def far_here(self):
        self.on_y.wait_recv()
        self.on_x.wait_recv()

    def all_here(self):
        self.x_here()
        self.y_here()
        self.far_here()

    def finish(self):
        for copy in (self.to_x1, self.to_y2, self.to_x2, self.to_y1, self.on_y, self.on_x):
            copy.wait_send()


class Fold:
    def __init__(self, part, land, passing, send, recv):
        self.me, self.nx, self.ny = neighbours()
        self.far = jnp.bitwise_xor(self.me, 3)
        self.part, self.land, self.passing = part, land, passing

        def copy(src, at, other):
            return remote(src, land.at[at], send.at[at], recv.at[at], other)

        self.far_x = copy(part(self.far, 0), 0, self.nx)
        self.far_y = copy(part(self.far, 1), 1, self.ny)
        self.near_x = copy(part(self.nx, 0), 2, self.nx)
        self.near_y = copy(part(self.ny, 1), 3, self.ny)
        self.on_y = copy(passing.at[0], 4, self.ny)
        self.on_x = copy(passing.at[1], 5, self.nx)

    def send_far(self):
        self.far_x.start()
        self.far_y.start()

    def send_near(self):
        self.near_x.start()
        self.near_y.start()

    def pass_on(self):
        self.far_x.wait_recv()
        self.passing[0] = (self.part(self.ny, 0)[...].astype(F32) + self.land[0].astype(F32)).astype(BF16)
        self.on_y.start()
        self.far_y.wait_recv()
        self.passing[1] = (self.part(self.nx, 1)[...].astype(F32) + self.land[1].astype(F32)).astype(BF16)
        self.on_x.start()

    def total(self, own):
        half = own.shape[0] // 2
        for copy in (self.near_x, self.near_y, self.on_y, self.on_x):
            copy.wait_recv()
        first = own[:half] + (self.land[2].astype(F32) + self.land[4].astype(F32))
        second = own[half:] + (self.land[3].astype(F32) + self.land[5].astype(F32))
        return jnp.concatenate([first, second], axis=0)

    def finish(self):
        for copy in (self.far_x, self.far_y, self.near_x, self.near_y, self.on_y, self.on_x):
            copy.wait_send()


class LineFold:
    def __init__(self, own, land, out, columns, send, recv):
        self.own, self.land, self.out, self.columns = own, land, out, columns
        self.send, self.recv = send, recv
        self.wides = own.shape[0]
        self.wide = lax.axis_index("wide")

    def place(self, way):
        return self.wide if way == 0 else self.wides - 1 - self.wide

    def copy(self, way, step):
        return pltpu.make_async_remote_copy(
            src_ref=self.out.at[self.slot(way, step), :, self.columns],
            dst_ref=self.land.at[way, step, :, self.columns],
            send_sem=self.send.at[way, step],
            recv_sem=self.recv.at[way, step],
            device_id={"wide": self.wide + 1 if way == 0 else self.wide - 1},
            device_id_type=MESH,
        )

    def slot(self, way, step):
        return jnp.clip(step - self.wide, 0, self.wides - 2) if way == 0 else step

    def sends(self, way, step):
        place = self.place(way)
        return (place <= step) & (place < self.wides - 1)

    def gets(self, way, step):
        place = self.place(way)
        return (place >= 1) & (place - 1 <= step)

    def step(self, step):
        for way in (0, 1):
            ahead = self.wides - 1 - step
            block = self.wide + ahead if way == 0 else self.wide - ahead
            block = jnp.clip(block, 0, self.wides - 1)
            begins = self.place(way) == 0

            @pl.when(self.sends(way, step) & begins)
            def _():
                self.out[self.slot(way, step), :, self.columns] = self.own[block, :, self.columns]
                self.copy(way, step).start()

            if step:

                @pl.when(self.sends(way, step) & jnp.logical_not(begins))
                def _():
                    self.copy(way, step - 1).wait_recv()
                    total = self.own[block, :, self.columns].astype(F32)
                    total = total + self.land[way, step - 1, :, self.columns].astype(F32)
                    self.out[self.slot(way, step), :, self.columns] = total.astype(BF16)
                    self.copy(way, step).start()

    def finish(self, result):
        last = self.wides - 2
        result[:, self.columns] = self.own[self.wide, :, self.columns]
        for way in (0, 1):

            @pl.when(self.gets(way, last))
            def _():
                self.copy(way, last).wait_recv()
                total = result[:, self.columns].astype(F32)
                total = total + self.land[way, last, :, self.columns].astype(F32)
                result[:, self.columns] = total.astype(BF16)

    def close(self):
        for step in range(self.wides - 1):
            for way in (0, 1):
                pl.when(self.sends(way, step))(self.copy(way, step).wait_send)


def line_spec(wides, block, columns, pieces):
    hops = pltpu.SemaphoreType.DMA((pieces, 2, wides - 1))
    return [
        pltpu.VMEM((wides, block, columns), BF16),
        pltpu.VMEM((2, wides - 1, block, columns), BF16),
        pltpu.VMEM((wides - 1, block, columns), BF16),
        pltpu.VMEM((block, columns), BF16),
        pltpu.SemaphoreType.DMA((wides + 1,)),
        hops,
        hops,
    ]


class LineSum:
    def __init__(self, src, dst, own, land, out, result, loads, send, recv):
        self.src, self.dst, self.own, self.result, self.loads = src, dst, own, result, loads
        pieces = send.shape[0]
        columns = own.shape[2]
        width = -(-columns // (128 * pieces)) * 128
        self.folds = [
            LineFold(own, land, out, pl.ds(first, min(width, columns - first)), send.at[p], recv.at[p])
            for p, first in enumerate(range(0, columns, width))
        ]
        self.steps = own.shape[0] - 1

    def load(self):
        wides, rows, columns = self.own.shape
        for w in range(wides):
            part = self.src.at[pl.ds(w * rows, rows), pl.ds(0, columns)]
            pltpu.make_async_copy(part, self.own.at[w], self.loads.at[w]).start()

    def begin(self):
        wides, rows, columns = self.own.shape
        for w in range(wides):
            part = self.src.at[pl.ds(w * rows, rows), pl.ds(0, columns)]
            pltpu.make_async_copy(part, self.own.at[w], self.loads.at[w]).wait()
        for fold in self.folds:
            fold.step(0)

    def step(self, step, piece):
        self.folds[piece].step(step)

    def end(self):
        for fold in self.folds:
            fold.finish(self.result)
        copy = pltpu.make_async_copy(self.result, self.dst, self.loads.at[self.own.shape[0]])
        copy.start()
        for fold in self.folds:
            fold.close()
        copy.wait()


class Deal:
    def __init__(self, src, place, send, recv):
        me, nx, ny = neighbours()
        far = jnp.bitwise_xor(me, 3)
        self.copies = [
            remote(src(other), place(me), send.at[at], recv.at[at], other)
            for at, other in enumerate((far, nx, ny))
        ]

    def start(self):
        for copy in self.copies:
            copy.start()

    def here(self):
        for copy in self.copies:
            copy.wait_recv()

    def finish(self):
        for copy in self.copies:
            copy.wait_send()


def greet(*others):
    barrier = pltpu.get_barrier_semaphore()
    for other in others:
        pl.semaphore_signal(barrier, inc=1, device_id=other, device_id_type=MESH)
    return lambda: pl.semaphore_wait(barrier, len(others))


def spread_spec():
    return [pltpu.SemaphoreType.DMA((6,)), pltpu.SemaphoreType.DMA((6,))]


def fold_spec(count, width):
    return [
        pltpu.VMEM((6, count // 2, width), BF16),
        pltpu.VMEM((2, count // 2, width), BF16),
        pltpu.SemaphoreType.DMA((6,)),
        pltpu.SemaphoreType.DMA((6,)),
    ]


def params(collective_id, mib):
    return pltpu.CompilerParams(
        collective_id=collective_id, has_side_effects=True, vmem_limit_bytes=mib * MIB
    )


TILE = 256


def up_kernel(h_ref, gain_ref, w_ref, *refs):
    sharing = len(refs) > 11
    if sharing:
        xn_ref, o_ref, rows_out, gu_out, act_out, xn_out, o_out, *refs = refs
        rows, w, gu, act, load, store, send, recv, *share_refs = refs
        share = Share(xn_ref, o_ref, *share_refs)
    else:
        rows_out, gu_out, act_out, rows, w, gu, act, load, store, send, recv = refs
    count = h_ref.shape[0]
    hidden = act.shape[1]
    weights = pltpu.make_async_copy(w_ref.at[:, pl.ds(0, 2 * hidden)], w, load)
    weights.start()
    me, nx, ny = neighbours()
    met = greet({"narrow": nx}, {"narrow": ny}, {"narrow": jnp.bitwise_xor(me, 3)})
    value = h_ref[...]
    rows[rows_of(me, count), :] = (value * inverse_rms(value) * gain_ref[...]).astype(BF16)
    spread = Spread(halves_of(rows, count), send, recv)
    met()
    spread.start()
    weights.wait()

    def one(block, at):
        here = rows_of(block, count)

        def tile(j):
            left = rows[here, :]
            gate = nn(left, w[:, columns_of(j, TILE)])
            up = nn(left, w[:, columns_of(j, TILE, hidden)])
            inner = jnp.tanh(GELU_SCALE * (gate + GELU_CUBE * (gate * gate * gate)))
            gu[here, columns_of(j, TILE)] = gate.astype(BF16)
            gu[here, columns_of(j, TILE, hidden)] = up.astype(BF16)
            act[here, columns_of(j, TILE)] = (0.5 * gate * (1.0 + inner) * up).astype(BF16)

        for j in range(hidden // TILE):
            tile(j)
        copies = [
            pltpu.make_async_copy(ref.at[here], out.at[here], store.at[k, at])
            for k, (ref, out) in enumerate(((gu, gu_out), (act, act_out), (rows, rows_out)))
        ]
        for copy in copies:
            copy.start()
        return copies

    copies = one(me, 0)
    spread.pass_on()
    if sharing:
        share.start_rows()
        share.start_deal()
    spread.x_here()
    copies += one(nx, 1)
    spread.y_here()
    copies += one(ny, 2)
    spread.far_here()
    if sharing:
        share.spread.pass_on()
    copies += one(spread.far, 3)
    spread.finish()
    if sharing:
        share.all_here()
        share.finish()
        xn, o, loads = share_refs[:3]
        copies += [pltpu.make_async_copy(xn, xn_out, loads.at[2]), pltpu.make_async_copy(o, o_out, loads.at[3])]
        for copy in copies[-2:]:
            copy.start()
    for copy in copies:
        copy.wait()


def feed_up(h, gain, w_gu, hidden, shared, collective_id):
    count, model = h.shape
    total = 4 * count
    shapes = [(total, model), (total, 2 * hidden), (total, hidden)]
    shapes = [jax.ShapeDtypeStruct(shape, BF16) for shape in shapes]
    if shared:
        shapes += share_shapes(*shared)
    return pl.pallas_call(
        up_kernel,
        out_shape=shapes,
        in_specs=[vmem_spec(), vmem_spec(), any_spec()] + [vmem_spec()] * len(shared),
        out_specs=[any_spec()] * len(shapes),
        scratch_shapes=[
            pltpu.VMEM((total, model), BF16),
            pltpu.VMEM((model, 2 * hidden), BF16),
            pltpu.VMEM((total, 2 * hidden), BF16),
            pltpu.VMEM((total, hidden), BF16),
            pltpu.SemaphoreType.DMA,
            pltpu.SemaphoreType.DMA((3, 4)),
            *spread_spec(),
            *(share_spec(count, model, shared[1].shape[1] // 4) if shared else []),
        ],
        compiler_params=params(collective_id, 60),
    )(h, gain, w_gu, *shared)


def down_kernel(
    h_ref, gain_ref, act_ref, w_ref, x_out, f_out, act, w, parts, load, land, passing, send, recv
):
    count, model = h_ref.shape
    me, nx, ny = neighbours()
    met = greet({"narrow": nx}, {"narrow": ny})
    far = jnp.bitwise_xor(me, 3)
    first = w_ref.shape[1] - w.shape[1]
    weights = pltpu.make_async_copy(w_ref.at[:, pl.ds(first, w.shape[1])], w, load.at[0])
    weights.start()
    arrivals = []
    for at, block in enumerate((far, nx, ny, me)):
        here = rows_of(block, count)
        arrivals.append(pltpu.make_async_copy(act_ref.at[here], act.at[here], load.at[1 + at]))
        arrivals[-1].start()
    fold = Fold(halves_of(parts, count), land, passing, send, recv)
    weights.wait()
    met()

    def one(block, at):
        arrivals[at].wait()
        return nt(act[rows_of(block, count), :], w[...])

    parts[rows_of(far, count), :] = one(far, 0).astype(BF16)
    fold.send_far()
    parts[rows_of(nx, count), :] = one(nx, 1).astype(BF16)
    parts[rows_of(ny, count), :] = one(ny, 2).astype(BF16)
    fold.send_near()
    f_out[...] = one(me, 3)
    fold.pass_on()
    total = fold.total(f_out[...])
    f_out[...] = total
    x_out[...] = (h_ref[...] + total * inverse_rms(total) * gain_ref[...]).astype(BF16)
    fold.finish()


def feed_down(h, gain, act, w_dt, collective_id):
    count, model = h.shape
    return pl.pallas_call(
        down_kernel,
        out_shape=[
            jax.ShapeDtypeStruct((count, model), BF16),
            jax.ShapeDtypeStruct((count, model), F32),
        ],
        in_specs=[vmem_spec(), vmem_spec(), any_spec(), any_spec()],
        out_specs=[vmem_spec(), vmem_spec()],
        scratch_shapes=[
            pltpu.VMEM(act.shape, BF16),
            pltpu.VMEM((model, act.shape[1]), BF16),
            pltpu.VMEM((4 * count, model), BF16),
            pltpu.SemaphoreType.DMA((5,)),
            *fold_spec(count, model),
        ],
        compiler_params=params(collective_id, 60),
    )(h, gain, act, w_dt)


def swap_sum(make, tiles, ours, theirs, came, send, recv, out, out_sems, between=None):
    other = {"section": 1 - lax.axis_index("section")}
    sends = []
    for at, (first, width) in enumerate(tiles):
        columns = pl.ds(first, width)
        theirs[:, columns] = make(False, first, width).astype(BF16)
        copy = pltpu.make_async_remote_copy(
            src_ref=theirs.at[:, columns],
            dst_ref=came.at[:, columns],
            send_sem=send.at[at],
            recv_sem=recv.at[at],
            device_id=other,
            device_id_type=MESH,
        )
        copy.start()
        sends.append(copy)
    if between is not None:
        between()
    stores = []
    for at, (first, width) in enumerate(tiles):
        columns = pl.ds(first, width)
        own = make(True, first, width)
        sends[at].wait_recv()
        ours[:, columns] = (own + came[:, columns].astype(F32)).astype(BF16)
        copy = pltpu.make_async_copy(ours.at[:, columns], out.at[:, columns], out_sems.at[at])
        copy.start()
        stores.append(copy)
    return sends, stores


def column_tiles(width):
    return [(first, min(2 * TILE, width - first)) for first in range(0, width, 2 * TILE)]


def gate_up_gradient(df, here, w, gu, hidden):
    for j in range(hidden // TILE):
        dact = nn(df[here, :], w[:, columns_of(j, TILE)])
        gate = gu[here, columns_of(j, TILE)].astype(F32)
        up = gu[here, columns_of(j, TILE, hidden)].astype(F32)
        square = gate * gate
        inner = jnp.tanh(GELU_SCALE * gate * (1.0 + GELU_CUBE * square))
        half = 0.5 * (1.0 + inner)
        slope = half + 0.5 * GELU_SCALE * gate * (1.0 - inner * inner) * (
            1.0 + 3.0 * GELU_CUBE * square
        )
        gu[here, columns_of(j, TILE)] = (dact * up * slope).astype(BF16)
        gu[here, columns_of(j, TILE, hidden)] = (dact * gate * half).astype(BF16)


def back_up_kernel(dy_ref, f_ref, gain_ref, gu_ref, act_ref, w_ref, *refs):
    if len(refs) == 19:
        extra_ref, _, *refs = refs
    else:
        extra_ref = None
    (
        dgu_out, dw_out, dgain_out, df, gu, act, w, ours, theirs, came,
        load, store, send, recv, swap_send, swap_recv, out_sems,
    ) = refs
    if extra_ref is not None:
        first = ours.shape[1]
        extra = pltpu.make_async_copy(
            extra_ref, dw_out.at[:, pl.ds(first, extra_ref.shape[1])], load.at[0, 1]
        )
        extra.start()
    count, model = dy_ref.shape
    hidden = act.shape[1]
    me, nx, ny = neighbours()
    core = lax.axis_index("section")
    met = greet({"narrow": nx}, {"narrow": ny}, {"section": 1 - core})
    far = jnp.bitwise_xor(me, 3)
    start = w_ref.shape[1] - hidden
    weights = pltpu.make_async_copy(w_ref.at[:, pl.ds(start, hidden)], w, load.at[0, 0])
    weights.start()
    arrivals = []
    for at, block in enumerate((me, nx, ny, far)):
        here = rows_of(block, count)
        pair = [
            pltpu.make_async_copy(gu_ref.at[here], gu.at[here], load.at[1, at]),
            pltpu.make_async_copy(act_ref.at[here], act.at[here], load.at[2, at]),
        ]
        for copy in pair:
            copy.start()
        arrivals.append(pair)
    dy = dy_ref[...].astype(BF16).astype(F32)
    by_value, by_gain = normed_gradient(f_ref[...], gain_ref[...], dy)
    df[rows_of(me, count), :] = by_value.astype(BF16)
    spread = Spread(halves_of(df, count), send, recv)
    met()
    spread.start()
    dgain_out[...] = by_gain
    weights.wait()

    def one(block, at):
        here = rows_of(block, count)
        for copy in arrivals[at]:
            copy.wait()

        gate_up_gradient(df, here, w, gu, hidden)
        copy = pltpu.make_async_copy(gu.at[here], dgu_out.at[here], store.at[at])
        copy.start()
        return copy

    copies = [one(me, 0)]
    spread.pass_on()
    spread.x_here()
    copies.append(one(nx, 1))
    spread.y_here()
    copies.append(one(ny, 2))
    spread.far_here()
    copies.append(one(far, 3))

    def make(mine, first, width):
        side = core if mine else 1 - core
        start = pl.multiple_of(side * (hidden // 2) + first, 128)
        return tn(df[...], act[:, pl.ds(start, width)])

    sends, stores = swap_sum(
        make, column_tiles(hidden // 2), ours, theirs, came, swap_send, swap_recv, dw_out, out_sems
    )
    spread.finish()
    for copy in sends:
        copy.wait_send()
    for copy in copies + stores:
        copy.wait()
    if extra_ref is not None:
        extra.wait()


def turn_kernel(
    h_ref, gain_ref, dy_ref, act_ref, w_ref, gu_ref, x_out, dgu_out, dw_out, dgain_out,
    act, w, parts, df, gu, ours, theirs, came, load, store, land, passing, fold_send, fold_recv, send, recv,
    swap_send, swap_recv, out_sems,
):
    count, model = h_ref.shape
    hidden = act.shape[1]
    me, nx, ny = neighbours()
    core = lax.axis_index("section")
    far = jnp.bitwise_xor(me, 3)
    met = greet({"narrow": nx}, {"narrow": ny}, {"section": 1 - core})
    first = w_ref.shape[1] - hidden
    weights = pltpu.make_async_copy(w_ref.at[:, pl.ds(first, hidden)], w, load.at[0, 0])
    weights.start()
    blocks = (far, nx, ny, me)
    for at, block in enumerate(blocks):
        here = rows_of(block, count)
        pltpu.make_async_copy(act_ref.at[here], act.at[here], load.at[1, at]).start()
    for at, block in enumerate(blocks):
        here = rows_of(block, count)
        pltpu.make_async_copy(gu_ref.at[here], gu.at[here], load.at[2, at]).start()

    def here_now(row, at):
        here = rows_of(blocks[at], count)
        src, dst = ((act_ref, act), (gu_ref, gu))[row - 1]
        pltpu.make_async_copy(src.at[here], dst.at[here], load.at[row, at]).wait()
        return here

    fold = Fold(halves_of(parts, count), land, passing, fold_send, fold_recv)
    weights.wait()
    met()

    def part(at):
        here = here_now(1, at)
        return here, nt(act[here, :], w[...])

    here, value = part(0)
    parts[here, :] = value.astype(BF16)
    fold.send_far()
    for at in (1, 2):
        here, value = part(at)
        parts[here, :] = value.astype(BF16)
    fold.send_near()
    _, value = part(3)
    fold.pass_on()
    f = fold.total(value)
    gain = gain_ref[...]
    by_value, by_gain = normed_gradient(f, gain, dy_ref[...])
    df[rows_of(me, count), :] = by_value.astype(BF16)
    spread = Spread(halves_of(df, count), send, recv)
    spread.start()
    dgain_out[...] = by_gain
    x_out[...] = (h_ref[...] + f * inverse_rms(f) * gain).astype(BF16)

    def one(at):
        here = here_now(2, at)
        gate_up_gradient(df, here, w, gu, hidden)
        copy = pltpu.make_async_copy(gu.at[here], dgu_out.at[here], store.at[at])
        copy.start()
        return copy

    copies = [one(3)]
    spread.pass_on()
    spread.x_here()
    copies.append(one(1))
    spread.y_here()
    copies.append(one(2))
    spread.far_here()
    copies.append(one(0))

    def make(mine, first, width):
        side = core if mine else 1 - core
        start = pl.multiple_of(side * (hidden // 2) + first, 128)
        return tn(df[...], act[:, pl.ds(start, width)])

    sends, stores = swap_sum(
        make, column_tiles(hidden // 2), ours, theirs, came, swap_send, swap_recv, dw_out, out_sems
    )
    spread.finish()
    fold.finish()
    for copy in sends:
        copy.wait_send()
    for copy in copies + stores:
        copy.wait()


def feed_turn(h, gain, dy, act, w_dt, gu, collective_id):
    count, model = h.shape
    total, hidden = act.shape
    tiles = pltpu.SemaphoreType.DMA((len(column_tiles(hidden // 2)),))
    dw = pltpu.VMEM((model, hidden // 2), BF16)
    return pl.pallas_call(
        turn_kernel,
        out_shape=[
            jax.ShapeDtypeStruct((count, model), BF16),
            jax.ShapeDtypeStruct(gu.shape, BF16),
            jax.ShapeDtypeStruct((model, hidden // 2), BF16),
            jax.ShapeDtypeStruct((1, model), F32),
        ],
        in_specs=[vmem_spec()] * 3 + [any_spec()] * 3,
        out_specs=[vmem_spec(), any_spec(), any_spec(), vmem_spec()],
        scratch_shapes=[
            pltpu.VMEM(act.shape, BF16),
            pltpu.VMEM((model, hidden), BF16),
            pltpu.VMEM((total, model), BF16),
            pltpu.VMEM((total, model), BF16),
            pltpu.VMEM(gu.shape, BF16),
            dw,
            dw,
            dw,
            pltpu.SemaphoreType.DMA((3, 4)),
            pltpu.SemaphoreType.DMA((4,)),
            *fold_spec(count, model),
            *spread_spec(),
            tiles,
            tiles,
            tiles,
        ],
        compiler_params=params(collective_id, 60),
    )(h, gain, dy, act, w_dt, gu)


def feed_back_up(dy, f, gain, gu, act, w_dt, extra, collective_id):
    count, model = dy.shape
    total, hidden = act.shape
    tiles = len(column_tiles(hidden // 2))
    extras = () if extra is None else extra
    return pl.pallas_call(
        back_up_kernel,
        out_shape=[
            jax.ShapeDtypeStruct(gu.shape, BF16),
            jax.ShapeDtypeStruct((model, hidden // 2 + sum(e.shape[1] for e in extras[:1])), BF16),
            jax.ShapeDtypeStruct((1, model), F32),
        ],
        in_specs=[vmem_spec()] * 3 + [any_spec()] * (3 + len(extras)),
        out_specs=[any_spec(), any_spec(), vmem_spec()],
        scratch_shapes=[
            pltpu.VMEM((total, model), BF16),
            pltpu.VMEM(gu.shape, BF16),
            pltpu.VMEM(act.shape, BF16),
            pltpu.VMEM((model, hidden), BF16),
            pltpu.VMEM((model, hidden // 2), BF16),
            pltpu.VMEM((model, hidden // 2), BF16),
            pltpu.VMEM((model, hidden // 2), BF16),
            pltpu.SemaphoreType.DMA((3, 4)),
            pltpu.SemaphoreType.DMA((4,)),
            *spread_spec(),
            pltpu.SemaphoreType.DMA((tiles,)),
            pltpu.SemaphoreType.DMA((tiles,)),
            pltpu.SemaphoreType.DMA((tiles,)),
        ],
        compiler_params=params(collective_id, 60),
    )(dy, f, gain, gu, act, w_dt, *extras)


def back_down_kernel(
    dy_ref, h_ref, gain_ref, dgu_ref, rows_ref, w_ref, dh_out, dw_out, dgain_out,
    dgu, rows, w, parts, ours, theirs, came, load, land, passing, send, recv, swap_send, swap_recv, out_sems,
):
    count, model = dy_ref.shape
    hidden = dgu.shape[1] // 2
    me, nx, ny = neighbours()
    core = lax.axis_index("section")
    far = jnp.bitwise_xor(me, 3)
    met = greet({"narrow": nx}, {"narrow": ny}, {"section": 1 - core})
    weights = pltpu.make_async_copy(w_ref.at[:, pl.ds(0, 2 * hidden)], w, load.at[0])
    weights.start()
    arrivals = []
    for at, block in enumerate((far, nx, ny, me)):
        here = rows_of(block, count)
        arrivals.append(pltpu.make_async_copy(dgu_ref.at[here], dgu.at[here], load.at[1 + at]))
        arrivals[-1].start()
    kept = pltpu.make_async_copy(rows_ref, rows, load.at[5])
    kept.start()
    fold = Fold(halves_of(parts, count), land, passing, send, recv)
    weights.wait()
    met()

    def one(block, at, out, here):
        arrivals[at].wait()
        out[here, :] = nt(dgu[rows_of(block, count), :], w[...]).astype(out.dtype)

    one(far, 0, parts, rows_of(far, count))
    fold.send_far()
    one(nx, 1, parts, rows_of(nx, count))
    one(ny, 2, parts, rows_of(ny, count))
    fold.send_near()
    one(me, 3, dh_out, pl.ds(0, count))
    fold.pass_on()
    kept.wait()

    def make(mine, first, width):
        side = core if mine else 1 - core
        start = pl.multiple_of(side * hidden + first, 128)
        return tn(rows[...], dgu[:, pl.ds(start, width)])

    sends, stores = swap_sum(
        make, column_tiles(hidden), ours, theirs, came, swap_send, swap_recv, dw_out, out_sems
    )
    total = fold.total(dh_out[...])
    by_value, by_gain = normed_gradient(h_ref[...], gain_ref[...], total)
    dh_out[...] = dy_ref[...].astype(BF16).astype(F32) + by_value
    dgain_out[...] = by_gain
    fold.finish()
    for copy in sends:
        copy.wait_send()
    for copy in stores:
        copy.wait()


def feed_back_down(dy, h, gain, dgu, rows, w_gu, collective_id):
    count, model = dy.shape
    total, hidden = dgu.shape[0], dgu.shape[1] // 2
    tiles = len(column_tiles(hidden))
    return pl.pallas_call(
        back_down_kernel,
        out_shape=[
            jax.ShapeDtypeStruct((count, model), F32),
            jax.ShapeDtypeStruct((model, hidden), BF16),
            jax.ShapeDtypeStruct((1, model), F32),
        ],
        in_specs=[vmem_spec()] * 3 + [any_spec()] * 3,
        out_specs=[vmem_spec(), any_spec(), vmem_spec()],
        scratch_shapes=[
            pltpu.VMEM(dgu.shape, BF16),
            pltpu.VMEM(rows.shape, BF16),
            pltpu.VMEM((model, 2 * hidden), BF16),
            pltpu.VMEM((total, model), BF16),
            pltpu.VMEM((model, hidden), BF16),
            pltpu.VMEM((model, hidden), BF16),
            pltpu.VMEM((model, hidden), BF16),
            pltpu.SemaphoreType.DMA((6,)),
            *fold_spec(count, model),
            pltpu.SemaphoreType.DMA((tiles,)),
            pltpu.SemaphoreType.DMA((tiles,)),
            pltpu.SemaphoreType.DMA((tiles,)),
        ],
        compiler_params=params(collective_id, 60),
    )(dy, h, gain, dgu, rows, w_gu)


def pack_kernel(*refs):
    *p_refs, o_ref, g_ref, local, send, recv, peer_send, peer_recv = refs
    model, width = o_ref.shape[2:]
    half = model // 2
    rest = g_ref.shape[2]
    core = lax.axis_index("section")
    me, nx, ny = neighbours()
    met = greet({"narrow": nx}, {"narrow": ny}, {"section": 1 - core})
    rows = p_refs[0].shape[0]

    def owns(run):
        wides = model // rows
        for at in range(wides):
            for distance, p_ref in enumerate(p_refs, -(len(p_refs) // 2)):
                wide = at - distance
                if not 0 <= wide < wides:
                    continue
                place = pl.ds(at * rows, rows)
                both = [
                    (p_ref.at[:, pl.ds(0, width)], o_ref.at[core, me, place], local.at[0, at]),
                    (p_ref.at[:, pl.ds(width, rest)], g_ref.at[core, place], local.at[1, at]),
                ]
                for src, dst, sem in both:
                    copy = pltpu.make_async_copy(src, dst, sem)
                    if wides == 1:
                        run(copy)()
                    else:
                        pl.when(lax.axis_index("wide") == wide)(run(copy))

    owns(lambda copy: copy.start)
    spread = Spread(lambda block, which: o_ref.at[core, block, pl.ds(which * half, half)], send, recv)
    owns(lambda copy: copy.wait)
    met()
    spread.start()
    copies = []

    def across(ref):
        copy = pltpu.make_async_remote_copy(
            src_ref=ref,
            dst_ref=ref,
            send_sem=peer_send.at[len(copies)],
            recv_sem=peer_recv.at[len(copies)],
            device_id={"section": 1 - core},
            device_id_type=MESH,
        )
        copy.start()
        copies.append(copy)

    across(g_ref.at[core])
    across(o_ref.at[core, me])
    spread.pass_on()
    spread.x_here()
    across(o_ref.at[core, nx])
    spread.y_here()
    across(o_ref.at[core, ny])
    spread.far_here()
    across(o_ref.at[core, spread.far])
    for copy in copies:
        copy.wait_recv()
    spread.finish()
    for copy in copies:
        copy.wait_send()


def gather_pack(packs, model, width, collective_id):
    pack = packs[0]
    return pl.pallas_call(
        pack_kernel,
        out_shape=[
            jax.ShapeDtypeStruct((2, 4, model, width), pack.dtype),
            jax.ShapeDtypeStruct((2, model, pack.shape[1] - width), pack.dtype),
        ],
        in_specs=[any_spec()] * len(packs),
        out_specs=[vmem_spec()] * 2,
        scratch_shapes=[
            pltpu.SemaphoreType.DMA((2, model // pack.shape[0])),
            *spread_spec(),
            pltpu.SemaphoreType.DMA((5,)),
            pltpu.SemaphoreType.DMA((5,)),
        ],
        compiler_params=params(collective_id, 32),
    )(*packs)


def finish_kernel(
    zero_ref, one_ref, early_ref, dep_ref, q_out, kv_out, o_out, came, kv, send, recv, kv_send, kv_recv
):
    core = lax.axis_index("section")
    me, nx, ny = neighbours()
    others = (nx, ny, jnp.bitwise_xor(me, 3))
    met = greet({"section": 1 - core}, *[{"narrow": other} for other in others])
    head = q_out.shape[1]
    first = core == 0
    by_qkv = jnp.where(first, zero_ref[...], early_ref[...])
    kv[me] = by_qkv[:, head:]
    met()
    across = pltpu.make_async_remote_copy(
        src_ref=zero_ref,
        dst_ref=came,
        send_sem=send,
        recv_sem=recv,
        device_id={"section": 1 - core},
        device_id_type=MESH,
    )
    across.start()
    copies = []
    for at, other in enumerate(others):
        copies.append(remote(kv.at[me], kv.at[me], kv_send.at[at], kv_recv.at[at], other))
        copies[-1].start()
    q_out[...] = by_qkv[:, :head].astype(F32)
    across.wait_recv()
    o_out[...] = jnp.where(first, came[:, :head], one_ref[:, :head]).astype(F32)
    for copy in copies:
        copy.wait_recv()
    width = kv.shape[2]
    for n in range(4):
        kv_out[:, n * width : (n + 1) * width] = kv[n].astype(F32)
    across.wait_send()
    for copy in copies:
        copy.wait_send()


def finish_attention(zero, one, early, dep, head, collective_id):
    block, width = zero.shape
    return pl.pallas_call(
        finish_kernel,
        out_shape=[
            jax.ShapeDtypeStruct((block, head), F32),
            jax.ShapeDtypeStruct((block, 4 * (width - head)), F32),
            jax.ShapeDtypeStruct((block, head), F32),
        ],
        in_specs=[vmem_spec()] * 3 + [any_spec()],
        out_specs=[vmem_spec()] * 3,
        scratch_shapes=[
            pltpu.VMEM((block, width), BF16),
            pltpu.VMEM((4, block, width - head), BF16),
            pltpu.SemaphoreType.DMA,
            pltpu.SemaphoreType.DMA,
            pltpu.SemaphoreType.DMA((3,)),
            pltpu.SemaphoreType.DMA((3,)),
        ],
        compiler_params=params(collective_id, 16),
    )(zero, one, early, dep)


def pair_kernel(zero_ref, one_ref, came_zero_ref, came_one_ref, out_ref, flag_ref):
    hidden = out_ref.shape[2]
    first = lax.axis_index("section") == 0
    keep = jnp.where(first, zero_ref[:, :hidden], one_ref[:, :hidden])
    came = jnp.where(first, came_zero_ref[:, :hidden], came_one_ref[:, :hidden])
    out_ref[:, 0, :] = jnp.where(first, keep, came).astype(F32)
    out_ref[:, 1, :] = jnp.where(first, came, keep).astype(F32)
    flag_ref[...] = jnp.zeros_like(flag_ref)


def pair_up(zero, one, came_zero, came_one, hidden):
    return pl.pallas_call(
        pair_kernel,
        out_shape=[
            jax.ShapeDtypeStruct((zero.shape[0], 2, hidden), F32),
            jax.ShapeDtypeStruct((8, 128), F32),
        ],
        in_specs=[vmem_spec()] * 4,
        out_specs=[vmem_spec()] * 2,
        compiler_params=pltpu.CompilerParams(vmem_limit_bytes=40 * MIB),
    )(zero, one, came_zero, came_one)


class Share:
    def __init__(self, xn_ref, o_ref, xn, o, loads, spread_send, spread_recv, deal_send, deal_recv):
        count, head = xn_ref.shape[0], o.shape[1]
        me = lax.axis_index("narrow")
        self.loads = [
            pltpu.make_async_copy(xn_ref, xn.at[rows_of(me, count)], loads.at[0]),
            pltpu.make_async_copy(o_ref.at[:, columns_of(me, head)], o.at[rows_of(me, count)], loads.at[1]),
        ]
        self.spread = Spread(halves_of(xn, count), spread_send, spread_recv)
        self.deal = Deal(
            lambda other: o_ref.at[:, columns_of(other, head)],
            lambda mine: o.at[rows_of(mine, count)],
            deal_send,
            deal_recv,
        )

    def start_rows(self):
        self.loads[0].start()
        self.loads[0].wait()
        self.spread.start()

    def start_deal(self):
        self.loads[1].start()
        self.deal.start()

    def all_here(self):
        self.spread.all_here()
        self.deal.here()

    def finish(self):
        self.spread.finish()
        self.deal.finish()
        self.loads[1].wait()


def share_spec(count, model, head):
    return [
        pltpu.VMEM((4 * count, model), BF16),
        pltpu.VMEM((4 * count, head), BF16),
        pltpu.SemaphoreType.DMA((4,)),
        *spread_spec(),
        pltpu.SemaphoreType.DMA((3,)),
        pltpu.SemaphoreType.DMA((3,)),
    ]


def share_shapes(xn, o):
    total = 4 * xn.shape[0]
    return [
        jax.ShapeDtypeStruct((total, xn.shape[1]), BF16),
        jax.ShapeDtypeStruct((total, o.shape[1] // 4), BF16),
    ]


def gain_stages():
    wides = lax.axis_size("wide")
    core, wide = lax.axis_index("section"), lax.axis_index("wide")
    me, nx, ny = neighbours()
    return [
        [{"narrow": nx}, {"narrow": ny}, {"narrow": jnp.bitwise_xor(me, 3)}],
        [{"section": 1 - core}],
        [{"wide": lax.rem(wide + step, wides)} for step in range(1, wides)],
    ]


class GainSum:
    def __init__(self, land, total, send, recv):
        self.land, self.total, self.send, self.recv = land, total, send, recv
        self.copies = []
        self.waiting = []

    def start(self, stage):
        for other in gain_stages()[stage]:
            at = len(self.copies)
            copy = pltpu.make_async_remote_copy(
                src_ref=self.total.at[stage],
                dst_ref=self.land.at[at],
                send_sem=self.send.at[at],
                recv_sem=self.recv.at[at],
                device_id=other,
                device_id_type=MESH,
            )
            copy.start()
            self.copies.append(copy)
            self.waiting.append(at)

    def add(self, stage):
        value = self.total[stage]
        for at in self.waiting:
            self.copies[at].wait_recv()
            value = value + self.land[at]
        self.waiting = []
        self.total[stage + 1] = value

    def close(self):
        for copy in self.copies:
            copy.wait_send()


def gain_spec(wides, shape):
    return [
        pltpu.VMEM((wides + 3, *shape), F32),
        pltpu.VMEM((4, *shape), F32),
        pltpu.SemaphoreType.DMA((wides + 3,)),
        pltpu.SemaphoreType.DMA((wides + 3,)),
    ]


def turn_back(grad, cosine, sine_table):
    half = grad.shape[1] // 2
    front, back = grad[:, :half], grad[:, half:]
    return jnp.concatenate(
        [front * cosine + back * sine_table, back * cosine - front * sine_table], axis=1
    )


def pack_loads(pack_ref, layer, head, wq, wot, wkv, sems):
    kv_part = wkv.shape[1] // 4
    loads = []
    for at, (w, first, width) in enumerate(
        ((wq, 0, head), (wot, head, head), (wkv, 2 * head, kv_part))
    ):
        loads.append(
            [
                pltpu.make_async_copy(
                    pack_ref.at[layer, n, :, pl.ds(first, width)], w.at[:, pl.ds(n * width, width)], sems.at[at, n]
                )
                for n in range(4)
            ]
        )
    return loads


def start_all(copies):
    for copy in copies:
        copy.start()


def wait_all(copies):
    for copy in copies:
        copy.wait()


def window_mask(me, count, window, length):
    rows_at = me * count + lax.broadcasted_iota(jnp.int32, (count, 1), 0)
    cols_at = me * count - WINDOW + lax.broadcasted_iota(jnp.int32, (1, window), 1)
    return (
        (cols_at <= rows_at)
        & (rows_at - cols_at < WINDOW)
        & (cols_at >= 0)
        & ((cols_at < length) | (cols_at == rows_at))
    )


def attend_kernel(layer, length_ref, x_ref, gains_ref, head_ref, trig_ref, pack_ref, *refs):
    (
        h_out, xn_out, q_out, k_out, win_out, lse_out, o_out, a_out, *refs
    ) = refs
    sharing = len(refs) > 9
    if sharing:
        xn_all_out, o_all_out, *refs = refs
    kv, wq, wot, wkv, load, send, recv, *share_refs = refs
    count, model = x_ref.shape
    head = k_out.shape[1]
    heads = q_out.shape[1] // head
    me, nx, ny = neighbours()
    met = greet({"narrow": nx}, {"narrow": ny}, {"narrow": jnp.bitwise_xor(me, 3)})
    q_loads, out_loads, kv_loads = pack_loads(pack_ref, layer, head, wq, wot, wkv, load)
    start_all(kv_loads + q_loads + out_loads)
    scaling = head ** (-0.5)
    cosine, sine_table = trig_ref[:, : head // 2], trig_ref[:, head // 2 :]
    x = x_ref[...].astype(F32)
    xn_out[...] = (x * inverse_rms(x) * gains_ref[0:1, :]).astype(BF16)
    kv[pl.ds(0, WINDOW), :] = jnp.zeros((WINDOW, 2 * head), BF16)
    wait_all(kv_loads)
    raw = nn(xn_out[...], wkv[...])
    k_raw = raw[:, :head]
    k_out[...] = k_raw
    k_rot = rotate(k_raw * inverse_rms(k_raw) * head_ref[1:2, :], cosine, sine_table)
    here = pl.ds(pl.multiple_of(WINDOW + me * count, count), count)
    kv[here, :head] = k_rot.astype(BF16)
    kv[here, head:] = raw[:, head:].astype(BF16)
    spread = Spread(halves_of(kv, count, WINDOW), send, recv)
    met()
    spread.start()
    if sharing:
        share = Share(xn_out, o_out, *share_refs)
    wait_all(q_loads)
    q_out[...] = nn(xn_out[...], wq[...])
    spread.pass_on()
    if sharing:
        share.start_rows()
    spread.all_here()
    window = win_out.shape[0]
    win_out[...] = kv[pl.ds(pl.multiple_of(me * count, count), window), :]
    visible = window_mask(me, count, window, length_ref[0])
    k_win, v_win = win_out[:, :head], win_out[:, head:]
    q_gain = head_ref[0:1, :]

    def one_head(i):
        columns = columns_of(i, head)
        q_raw = q_out[:, columns]
        qr = rotate(q_raw * inverse_rms(q_raw) * q_gain, cosine, sine_table).astype(BF16)
        scores = jnp.where(visible, nt(qr, k_win) * scaling, NEGATIVE)
        most = jnp.max(scores, axis=-1, keepdims=True)
        exponent = jnp.exp(scores - most)
        total = jnp.sum(exponent, axis=-1, keepdims=True)
        lse_out[i] = most + jnp.log(total)
        o_out[:, columns] = nn((exponent / total).astype(BF16), v_win).astype(BF16)

    for i in range(heads):
        one_head(i)
    if sharing:
        share.start_deal()
        share.spread.pass_on()
    wait_all(out_loads)
    a = nt(o_out[...], wot[...])
    a_out[...] = a
    h_out[...] = x_ref[...].astype(F32) + a * inverse_rms(a) * gains_ref[1:2, :]
    spread.finish()
    if sharing:
        share.all_here()
        share.finish()
        xn, o, loads = share_refs[:3]
        stores = [
            pltpu.make_async_copy(xn, xn_all_out, loads.at[2]),
            pltpu.make_async_copy(o, o_all_out, loads.at[3]),
        ]
        start_all(stores)
        wait_all(stores)


def attend(length, x, gains, head_gains, trig, pack, head, layer, collective_id):
    count, model = x.shape
    kv_width = 2 * head
    width = 4 * head
    window = count + WINDOW
    sharing = True
    xn_shape = jax.ShapeDtypeStruct((count, model), BF16)
    o_shape = jax.ShapeDtypeStruct((count, width), BF16)
    shapes = [
        jax.ShapeDtypeStruct((count, model), F32),
        xn_shape,
        jax.ShapeDtypeStruct((count, width), F32),
        jax.ShapeDtypeStruct((count, head), F32),
        jax.ShapeDtypeStruct((window, kv_width), BF16),
        jax.ShapeDtypeStruct((4, count, 1), F32),
        o_shape,
        jax.ShapeDtypeStruct((count, model), F32),
    ]
    outs = [vmem_spec()] * 8
    if sharing:
        shapes += share_shapes(xn_shape, o_shape)
        outs += [any_spec()] * 2
    return pl.pallas_call(
        functools.partial(attend_kernel, layer),
        out_shape=shapes,
        in_specs=[pl.BlockSpec(memory_space=pltpu.SMEM)] + [vmem_spec()] * 4 + [any_spec()],
        out_specs=outs,
        scratch_shapes=[
            pltpu.VMEM((4 * count + WINDOW, kv_width), BF16),
            pltpu.VMEM((model, width), BF16),
            pltpu.VMEM((model, width), BF16),
            pltpu.VMEM((model, kv_width), BF16),
            pltpu.SemaphoreType.DMA((3, 4)),
            *spread_spec(),
            *(share_spec(count, model, head) if sharing else []),
        ],
        compiler_params=params(collective_id, 40),
    )(length, x, gains, head_gains, trig, pack)


def attend_back_kernel(
    layer, length_ref, dh_ref, a_ref, x_ref, gains_ref, head_ref, trig_ref, q_ref, k_ref, win_ref, lse_ref,
    pack_ref, xn_ref, o_ref, *refs
):
    if layer == 0:
        block_ref, lined_ref, *refs = refs
        block_out, lined_out, came_out, small_out = refs[4:8]
        refs = refs[:4] + refs[8:]
        gain_refs, line_refs = refs[36:40], refs[40:]
        refs = refs[:36]
    (
    dx_out, dw_out, dgain_out, dhead_out,
    da, do, dq, dk, dv, parts, dq_all, dkv, dkv_all, wq, wot, wkv, xn, o, ours, theirs, came,
    pack_load, load, send, recv, land, passing, fold_send, fold_recv, q_send, q_recv, kv_send, kv_recv, swap_send, swap_recv, out_sem,
    ) = refs
    count = dh_ref.shape[0]
    head = k_ref.shape[1]
    heads = q_ref.shape[1] // head
    kv_part = dkv_all.shape[1]
    me, nx, ny = neighbours()
    core = lax.axis_index("section")
    far = jnp.bitwise_xor(me, 3)
    lined = layer == 0 and len(line_refs) > 0
    if layer == 0:
        met = greet(*sum(gain_stages(), []))
        sums = GainSum(*gain_refs)
    else:
        met = greet({"narrow": nx}, {"narrow": ny}, {"narrow": far}, {"section": 1 - core})
    if lined:
        line = LineSum(lined_ref, lined_out, *line_refs[:7])
        small = LineSum(ours, small_out, *line_refs[7:14])
        came_line, came_send, came_recv, came_store = line_refs[14:]
        line.load()
    q_loads, out_loads, kv_loads = pack_loads(pack_ref, layer, head, wq, wot, wkv, pack_load)
    loads = [
        pltpu.make_async_copy(src, dst, load.at[at])
        for at, (src, dst) in enumerate(((xn_ref, xn), (o_ref, o)))
    ]
    start_all(out_loads + q_loads + kv_loads + loads)
    here = rows_of(me, count)
    scaling = head ** (-0.5)
    cosine, sine_table = trig_ref[:, : head // 2], trig_ref[:, head // 2 :]

    dh = dh_ref[...]
    by_value, dg1 = normed_gradient(a_ref[...], gains_ref[1:2, :], dh)
    da[here, :] = by_value.astype(BF16)
    dgain_out[1:2, :] = dg1
    spread = Spread(halves_of(da, count), send, recv)
    met()
    spread.start()
    if lined:
        line.begin()
    wait_all(out_loads)
    do[...] = nn(da[here, :], wot[...]).astype(BF16)

    visible = window_mask(me, count, win_ref.shape[0], length_ref[0])
    k_win, v_win = win_ref[:, :head], win_ref[:, head:]
    dk[...] = jnp.zeros_like(dk)
    dv[...] = jnp.zeros_like(dv)
    dhead_out[...] = jnp.zeros_like(dhead_out)
    q_gain, k_gain = head_ref[0:1, :], head_ref[1:2, :]

    def one_head(i):
        columns = columns_of(i, head)
        raw = q_ref[:, columns]
        inverse = inverse_rms(raw)
        unit = raw * inverse
        qr = rotate(unit * q_gain, cosine, sine_table).astype(BF16)
        scores = jnp.where(visible, nt(qr, k_win) * scaling, NEGATIVE)
        probs = jnp.exp(scores - lse_ref[i])
        do_head = do[:, columns]
        dp = nt(do_head, v_win)
        ds = (probs * (dp - jnp.sum(probs * dp, axis=-1, keepdims=True))).astype(BF16)
        dk[...] += tn(ds, qr)
        dv[...] += tn(probs.astype(BF16), do_head)
        grad = turn_back(nn(ds, k_win) * scaling, cosine, sine_table)
        scaled = grad * q_gain
        dq_raw = inverse * (scaled - unit * jnp.mean(scaled * unit, axis=-1, keepdims=True))
        dq[:, columns] = dq_raw.astype(BF16)
        dhead_out[0:1, :] += jnp.sum(grad * unit, axis=0, keepdims=True)

    for i in range(heads):
        one_head(i)
    if lined:
        line.step(1, 0)
    parts[...] = jnp.zeros_like(parts)
    window = pl.ds(pl.multiple_of(me * count, count), win_ref.shape[0])
    parts[window, :head] = (dk[...] * scaling).astype(BF16)
    parts[window, head:] = dv[...].astype(BF16)
    fold = Fold(halves_of(parts, count, WINDOW), land, passing, fold_send, fold_recv)
    fold.send_far()
    fold.send_near()
    deal_q = Deal(
        lambda other: dq.at[:, columns_of(other, head)],
        lambda mine: dq_all.at[rows_of(mine, count)],
        q_send,
        q_recv,
    )
    deal_q.start()
    dq_all[here, :] = dq[:, columns_of(me, head)]
    spread.pass_on()
    wait_all(q_loads)
    dx_out[...] = nt(dq[...], wq[...])
    fold.pass_on()
    spread.all_here()
    wait_all(loads)
    first = core == 0
    swaps = []

    def exchange(at, columns, a, b):
        ours[:, columns] = jnp.where(first, a, b).astype(BF16)
        theirs[:, columns] = jnp.where(first, b, a).astype(BF16)
        copy = pltpu.make_async_remote_copy(
            src_ref=theirs.at[:, columns],
            dst_ref=came.at[:, columns],
            send_sem=swap_send.at[at],
            recv_sem=swap_recv.at[at],
            device_id={"section": 1 - core},
            device_id_type=MESH,
        )
        copy.start()
        swaps.append(copy)

    by_out = tn(da[...], o[...])
    deal_q.here()
    exchange(0, pl.ds(0, head), tn(xn[...], dq_all[...]), by_out)
    own = jnp.concatenate([dk[WINDOW:, :] * scaling, dv[WINDOW:, :]], axis=1)
    total = fold.total(own)
    grad = turn_back(total[:, :head], cosine, sine_table)
    dk_raw, dk_gain = normed_gradient(k_ref[...], k_gain, grad)
    dhead_out[1:2, :] = dk_gain
    dkv[:, :head] = dk_raw.astype(BF16)
    dkv[:, head:] = total[:, head:].astype(BF16)
    deal_kv = Deal(
        lambda other: dkv.at[:, columns_of(other, kv_part)],
        lambda mine: dkv_all.at[rows_of(mine, count)],
        kv_send,
        kv_recv,
    )
    deal_kv.start()
    dkv_all[here, :] = dkv[:, columns_of(me, kv_part)]
    wait_all(kv_loads)
    dxn = dx_out[...] + nt(dkv[...], wkv[...])
    by_value, dg0 = normed_gradient(x_ref[...].astype(F32), gains_ref[0:1, :], dxn)
    dx_out[...] = dh_ref[...] + by_value
    dgain_out[0:1, :] = dg0
    if lined:
        line.step(1, 1)
    if layer == 0:
        own_total = sums.total.at[0]
        own_total[...] = block_ref[...]
        own_total[0:2, :] = dgain_out[...]
        own_total[4:5, :head] = dhead_out[0:1, :]
        own_total[4:5, head : 2 * head] = dhead_out[1:2, :]
        sums.start(0)

    deal_kv.here()
    by_kv = tn(xn[...], dkv_all[...])
    if layer == 0:
        sums.add(0)
        sums.start(1)
    exchange(1, pl.ds(head, kv_part), by_kv, jnp.zeros_like(by_kv))
    for copy in swaps:
        copy.wait_recv()
    ours[...] = (ours[...].astype(F32) + came[...].astype(F32)).astype(BF16)
    out = pltpu.make_async_copy(ours, dw_out, out_sem)
    out.start()
    if layer == 0:
        sums.add(1)
        sums.start(2)
    if lined:
        small.load()
        for step in range(2, line.steps):
            for piece in (0, 1):
                line.step(step, piece)
        small.begin()
        line.end()
        cross = pltpu.make_async_remote_copy(
            src_ref=line.result,
            dst_ref=came_line,
            send_sem=came_send,
            recv_sem=came_recv,
            device_id={"section": 1 - core},
            device_id_type=MESH,
        )
        cross.start()
        for step in range(1, small.steps):
            for piece in range(len(small.folds)):
                small.step(step, piece)
        cross.wait_recv()
        keep = pltpu.make_async_copy(came_line, came_out, came_store)
        keep.start()
        small.end()
        keep.wait()
        cross.wait_send()
    if layer == 0:
        sums.add(2)
        block_out[...] = sums.total[3]
        sums.close()
    spread.finish()
    fold.finish()
    deal_q.finish()
    deal_kv.finish()
    for copy in swaps:
        copy.wait_send()
    out.wait()


def attend_back(length, dh, a, x, gains, head_gains, trig, q_raw, k_raw, window, lse, pack, xn, o, deps, layer, collective_id):
    count, model = dh.shape
    head = k_raw.shape[1]
    width = q_raw.shape[1]
    kv_part = pack.shape[3] - 2 * head
    if layer == 0:
        wides = lax.axis_size("wide")
        block, lined = deps
        rows = model // wides
    deal = pltpu.SemaphoreType.DMA((3,))
    dw = pltpu.VMEM((model, head + kv_part), BF16)
    return pl.pallas_call(
        functools.partial(attend_back_kernel, layer),
        out_shape=[
            jax.ShapeDtypeStruct((count, model), F32),
            jax.ShapeDtypeStruct((model, head + kv_part), BF16),
            jax.ShapeDtypeStruct((2, model), F32),
            jax.ShapeDtypeStruct((2, head), F32),
            *(
                [
                    jax.ShapeDtypeStruct(block.shape, F32),
                    jax.ShapeDtypeStruct((rows, lined.shape[1]), BF16),
                    jax.ShapeDtypeStruct((rows, lined.shape[1]), BF16),
                    jax.ShapeDtypeStruct((rows, head + kv_part), BF16),
                ]
                if layer == 0
                else []
            ),
        ],
        in_specs=[pl.BlockSpec(memory_space=pltpu.SMEM)] + [vmem_spec()] * 10 + [any_spec()] * 3 + ([vmem_spec(), any_spec()] if layer == 0 else []),
        out_specs=[vmem_spec(), any_spec(), vmem_spec(), vmem_spec()]
        + ([vmem_spec()] + [any_spec()] * 3 if layer == 0 else []),
        scratch_shapes=[
            pltpu.VMEM((4 * count, model), BF16),
            pltpu.VMEM((count, width), BF16),
            pltpu.VMEM((count, width), BF16),
            pltpu.VMEM((window.shape[0], head), F32),
            pltpu.VMEM((window.shape[0], head), F32),
            pltpu.VMEM((4 * count + WINDOW, 2 * head), BF16),
            pltpu.VMEM((4 * count, head), BF16),
            pltpu.VMEM((count, 2 * head), BF16),
            pltpu.VMEM((4 * count, kv_part), BF16),
            pltpu.VMEM((model, width), BF16),
            pltpu.VMEM((model, width), BF16),
            pltpu.VMEM((model, 2 * head), BF16),
            pltpu.VMEM(xn.shape, BF16),
            pltpu.VMEM(o.shape, BF16),
            dw,
            dw,
            dw,
            pltpu.SemaphoreType.DMA((3, 4)),
            pltpu.SemaphoreType.DMA((2,)),
            *spread_spec(),
            *fold_spec(count, 2 * head),
            deal,
            deal,
            deal,
            deal,
            pltpu.SemaphoreType.DMA((2,)),
            pltpu.SemaphoreType.DMA((2,)),
            pltpu.SemaphoreType.DMA,
            *(gain_spec(wides, block.shape) if layer == 0 else []),
            *(
                [
                    *line_spec(wides, rows, lined.shape[1], 2),
                    *line_spec(wides, rows, head + kv_part, 2),
                    pltpu.VMEM((rows, lined.shape[1]), BF16),
                    pltpu.SemaphoreType.DMA,
                    pltpu.SemaphoreType.DMA,
                    pltpu.SemaphoreType.DMA,
                ]
                if layer == 0 and rows % 16 == 0
                else []
            ),
        ],
        compiler_params=params(collective_id, 56 if layer == 0 else 48),
    )(length, dh, a, x, gains, head_gains, trig, q_raw, k_raw, window, lse, pack, xn, o, *deps)


def after(value, *others):
    return pl.pallas_call(
        lambda *refs: None,
        out_shape=jax.ShapeDtypeStruct(value.shape, value.dtype),
        in_specs=[any_spec()] * (1 + len(others)),
        out_specs=any_spec(),
        input_output_aliases={0: 0},
    )(value, *others)


def scatter(member):
    return lax.psum_scatter(member, "wide", scatter_dimension=0, tiled=True)


def on_device(
    inputs, cotangent, lengths, norm_gains, head_gains, w_q, w_kv, w_o, w_gate_up, w_down
):
    core = lax.axis_index("section")
    narrow = lax.axis_index("narrow")
    n_narrow = lax.axis_size("narrow")
    is_zero = core == 0
    rows, model = inputs.shape[1], inputs.shape[2]
    block = w_q.shape[1]
    head_width = w_q.shape[2]
    n_wide = lax.axis_size("wide")
    hidden = w_down.shape[1]
    kv_part = w_kv.shape[2] // n_narrow

    def swap(value):
        return lax.ppermute(value, "section", [(0, 1), (1, 0)])

    def by_core(first, second):
        return jnp.where(is_zero, first, second)

    half = block // 2

    pad = -hidden % TILE
    kv_own = lax.dynamic_slice_in_dim(w_kv[0], narrow * kv_part, kv_part, 1)
    pack_width = 2 * head_width + kv_part
    gain_columns = jnp.zeros((block, GAIN_COLUMNS), BF16)
    gain_columns = lax.dynamic_update_slice(gain_columns, norm_gains[0].T, (0, 0))
    gain_columns = lax.dynamic_update_slice(gain_columns, head_gains[0].T, (0, 4))
    pack = jnp.concatenate([w_q[0], w_o[0].T, kv_own, gain_columns], axis=1)

    late = after(core.reshape(1), pack)[0]
    pack = (lax.all_gather(pack, "wide", axis=0, tiled=True),)

    def half_of(side):
        gate_up = lax.dynamic_slice_in_dim(w_gate_up[0], side * half, half, 0)
        gate_up = jnp.pad(gate_up, ((0, 0), (0, 0), (0, pad))).reshape(half, -1)
        down = lax.dynamic_slice_in_dim(w_down[0].T, side * half, half, 0)
        return jnp.concatenate([gate_up, jnp.pad(down, ((0, 0), (0, pad)))], axis=1)

    keep, came = half_of(late), swap(half_of(1 - late))
    feed = by_core(keep, came), by_core(came, keep)
    padded = hidden + pad

    def gather(member):
        return lax.all_gather(member, ("wide", "section"), axis=0, tiled=True)

    both = gather(feed[0])
    feeds = [
        (both, both, padded),
        (gather(feed[1][:, : 2 * padded]), gather(feed[1][:, 2 * padded :]), padded),
    ]
    packs, gain_packs = gather_pack(pack, model, pack_width, 6)

    def gains_of(section):
        columns = gain_packs[section].astype(F32)
        heads = columns.reshape(n_wide, block, -1)[:, : head_width // n_wide, 4:6]
        return columns[:, :4].T, heads.transpose(2, 0, 1).reshape(2, head_width)

    start = narrow * rows
    positions = start + jnp.arange(rows, dtype=jnp.int32)
    trig = tables(positions, head_width)
    length = lax.dynamic_index_in_dim(lengths[:, 0], core, 0, keepdims=False)

    x = lax.dynamic_index_in_dim(inputs, core, 0, keepdims=False)
    length_one = length.reshape(1)
    outs, kept, gains = [], [], []
    for section in range(2):
        layer_gains, head_gain = gains_of(section)
        gains.append((layer_gains, head_gain))
        h, xn, q_raw, k_raw, window, lse, o, a, *shared = attend(
            length_one, x, layer_gains, head_gain, trig, packs, head_width, section, 8 + section
        )
        w_up, w_down, _ = feeds[section]
        mid_rows, gu, act = feed_up(h, layer_gains[2:3], w_up, padded, (), 10 + section)
        kept.append(((a, x, q_raw, k_raw, window, lse), (h, mid_rows, gu, act), shared))
        if section == 0:
            x, f = feed_down(h, layer_gains[3:4], act, w_down, 12)
            outs.append(x)

    def by_section(first, second):
        stays, came = by_core(first, second), swap(by_core(second, first))
        return jnp.stack([by_core(stays, came), by_core(came, stays)])

    real = (positions < length).astype(F32)[:, None]
    dy = lax.dynamic_index_in_dim(cotangent, core, 0, keepdims=False).astype(F32) * real
    dxs, gain_grads = [None, None], [None, None]
    up_sums, down_sums, attention_sums = [None, None], [None, None], [None, None]
    extra = None
    for section in (1, 0):
        kept_a, (h, mid_rows, gu, act), (xn, o) = kept[section]
        layer_gains, head_gain = gains[section]
        w_up, w_down, _ = feeds[section]
        if section:
            out, dgu, d_down, dg3 = feed_turn(h, layer_gains[3:4], dy, act, w_down, gu, 13)
            outs.append(out)
        else:
            dgu, d_down, dg3 = feed_back_up(
                dy, f, layer_gains[3:4], gu, act, w_down, (extra, down_sums[1]), 14
            )
        down_sums[section] = scatter(d_down)
        dh, d_up, dg2 = feed_back_down(dy, h, layer_gains[2:3], dgu, mid_rows, w_up, 16 + section)
        if section or block % 16:
            up_sums[section] = scatter(d_up)
        a, x, q_raw, k_raw, window, lse = kept_a
        if section == 0:
            zeros = jnp.zeros((2, model), F32)
            gain_grads[0] = jnp.concatenate([zeros, dg2, dg3, zeros, zeros])
            section_out = by_section(*outs)
            deps = (jnp.concatenate(gain_grads), after(d_up, up_sums[1], section_out))
        dx, extra, dg01, dhead, *more = attend_back(
            length_one, dh, a, x, layer_gains, head_gain, trig, q_raw, k_raw, window, lse, packs, xn, o,
            () if section else deps, section, 18 + section,
        )
        dxs[section] = dx
        if section:
            head_row = jnp.pad(dhead.reshape(1, -1), ((0, 0), (0, model - dhead.size)))
            gain_grads[1] = jnp.concatenate([dg01, dg2, dg3, head_row, jnp.zeros((3, model), F32)])
        else:
            gain_sums, up_lined, came_up, attention_lined = more
            if block % 16 == 0:
                up_sums[0] = up_lined
            else:
                came_up = swap(up_sums[0])
        dy = dx
    split = down_sums[1].shape[1]
    attention_zero = scatter(extra) if block % 16 else attention_lined
    attention_sums = (attention_zero, down_sums[0][:, split:])
    down_sums[0] = down_sums[0][:, :split]

    def own_section(first, second):
        came = swap(by_core(second, first))
        stays = by_core(first, second)
        return by_core(stays, came).astype(F32), by_core(came, stays).astype(F32)

    grad_gate_up, flag = pair_up(*up_sums, came_up, swap(up_sums[1]), hidden)
    grad_down = jnp.concatenate(own_section(*down_sums), axis=1)[:, :hidden].T
    grad_q, grad_kv, grad_o = finish_attention(
        *attention_sums, swap(attention_sums[1]), flag, head_width, 1
    )
    grad_o = grad_o.T
    gain_sums = lax.dynamic_slice_in_dim(gain_sums, core * 8, 8, 0)
    wide = lax.axis_index("wide")
    grad_norm = lax.dynamic_slice_in_dim(gain_sums[:4], wide * block, block, 1)
    grad_head = gain_sums[4, : 2 * head_width].reshape(2, head_width)
    head_block = head_width // n_wide
    grad_head = lax.dynamic_slice_in_dim(grad_head, wide * head_block, head_block, 1)

    return (
        section_out[None],
        by_section(*dxs)[None],
        grad_norm[None],
        grad_head[None],
        grad_q[None],
        grad_kv[None],
        grad_o[None],
        grad_gate_up[None],
        grad_down[None],
    )


def solution(mesh):
    return jax.shard_map(
        on_device,
        mesh=mesh,
        in_specs=(
            P(None, ("wide", "narrow"), None),
            P(None, ("wide", "narrow"), None),
            P(None, "wide"),
            P("section", None, "wide"),
            P("section", None, "wide"),
            P("section", "wide", "narrow"),
            P("section", "wide", None),
            P("section", "narrow", "wide"),
            P("section", "wide", None, "narrow"),
            P("section", "narrow", "wide"),
        ),
        out_specs=(
            P("section", None, ("wide", "narrow"), None),
            P("section", None, ("wide", "narrow"), None),
            P("section", None, "wide"),
            P("section", None, "wide"),
            P("section", "wide", "narrow"),
            P("section", "wide", None),
            P("section", "narrow", "wide"),
            P("section", "wide", None, "narrow"),
            P("section", "narrow", "wide"),
        ),
        check_vma=False,
    )
```

```python
import functools

import jax
import jax.numpy as jnp
from jax import lax
from jax.experimental import pallas as pl
from jax.experimental.pallas import tpu as pltpu
from jax.sharding import PartitionSpec as P

WINDOW = 512
EPSILON = 1e-06
NEGATIVE = -1e30
ROPE_BASE = 10000.0
MESH = pl.DeviceIdType.MESH
MIB = 2**20
GAIN_ROWS = 16
F32 = jnp.float32
BF16 = jnp.bfloat16


def dot(a, b, dims):
    return lax.dot_general(a, b, ((dims[0], dims[1]), ((), ())), preferred_element_type=F32)


def nn(a, b):
    return dot(a, b, ((1,), (0,)))


def nt(a, b):
    return dot(a, b, ((1,), (1,)))


def tn(a, b):
    return dot(a, b, ((0,), (0,)))


def normed(operand, gain_vec):
    return (
        operand
        * lax.rsqrt(jnp.mean(operand * operand, axis=-1, keepdims=True) + EPSILON)
        * gain_vec
    )


def geglu(gate, up):
    return jax.nn.gelu(gate, approximate=True) * up


def neighbours():
    me = lax.axis_index("narrow")
    return me, jnp.bitwise_xor(me, 1), jnp.bitwise_xor(me, 2)


def meet(nx, ny):
    barrier = pltpu.get_barrier_semaphore()
    for other in (nx, ny):
        pl.semaphore_signal(barrier, inc=1, device_id={"narrow": other}, device_id_type=MESH)
    pl.semaphore_wait(barrier, 2)


def remote(src, dst, send_sem, recv_sem, other):
    return pltpu.make_async_remote_copy(
        src_ref=src,
        dst_ref=dst,
        send_sem=send_sem,
        recv_sem=recv_sem,
        device_id={"narrow": other},
        device_id_type=MESH,
    )


def tables(positions, head_width):
    half_width = head_width // 2
    frequency = ROPE_BASE ** (-jnp.arange(half_width, dtype=F32) * (2.0 / head_width))
    angles = positions.astype(F32)[:, None] * frequency[None, :]
    return jnp.concatenate([jnp.cos(angles), jnp.sin(angles)], axis=1)


def rotate(operand, cosine, sine_table):
    half_width = operand.shape[-1] // 2
    front_half = operand[..., :half_width]
    back_half = operand[..., half_width:]
    return jnp.concatenate(
        [
            front_half * cosine - back_half * sine_table,
            back_half * cosine + front_half * sine_table,
        ],
        axis=-1,
    )


GELU_SCALE = 0.7978845608028654
GELU_CUBE = 0.044715


def vmem_spec():
    return pl.BlockSpec(memory_space=pltpu.VMEM)


def any_spec():
    return pl.BlockSpec(memory_space=pl.ANY)


def rows_of(block, count):
    return pl.ds(pl.multiple_of(block * count, count), count)


def columns_of(tile, width, offset=0):
    if isinstance(tile, int):
        return pl.ds(tile * width + offset, width)
    return pl.ds(pl.multiple_of(tile * width + offset, 128), width)


def inverse_rms(value):
    return lax.rsqrt(jnp.mean(value * value, axis=-1, keepdims=True) + EPSILON)


def normed_gradient(value, gain, grad):
    inverse = inverse_rms(value)
    unit = value * inverse
    scaled = grad * gain
    by_value = inverse * (scaled - unit * jnp.mean(scaled * unit, axis=-1, keepdims=True))
    return by_value, jnp.sum(grad * unit, axis=0, keepdims=True)


def halves_of(ref, count, base=0):
    half = count // 2

    def part(block, which):
        return ref.at[pl.ds(pl.multiple_of(base + block * count + which * half, half), half)]

    return part


class Spread:
    def __init__(self, part, send, recv):
        self.me, self.nx, self.ny = neighbours()
        self.far = jnp.bitwise_xor(self.me, 3)

        def copy(block, which, at, other):
            ref = part(block, which)
            return remote(ref, ref, send.at[at], recv.at[at], other)

        self.to_x1 = copy(self.me, 0, 0, self.nx)
        self.to_y2 = copy(self.me, 1, 1, self.ny)
        self.to_x2 = copy(self.me, 1, 2, self.nx)
        self.to_y1 = copy(self.me, 0, 3, self.ny)
        self.on_y = copy(self.nx, 0, 4, self.ny)
        self.on_x = copy(self.ny, 1, 5, self.nx)

    def start(self):
        for copy in (self.to_x1, self.to_y2, self.to_x2, self.to_y1):
            copy.start()

    def pass_on(self):
        self.to_x1.wait_recv()
        self.on_y.start()
        self.to_y2.wait_recv()
        self.on_x.start()

    def x_here(self):
        self.to_x2.wait_recv()

    def y_here(self):
        self.to_y1.wait_recv()

    def far_here(self):
        self.on_y.wait_recv()
        self.on_x.wait_recv()

    def all_here(self):
        self.x_here()
        self.y_here()
        self.far_here()

    def finish(self):
        for copy in (self.to_x1, self.to_y2, self.to_x2, self.to_y1, self.on_y, self.on_x):
            copy.wait_send()


class Fold:
    def __init__(self, part, land, passing, send, recv):
        self.me, self.nx, self.ny = neighbours()
        self.far = jnp.bitwise_xor(self.me, 3)
        self.part, self.land, self.passing = part, land, passing

        def copy(src, at, other):
            return remote(src, land.at[at], send.at[at], recv.at[at], other)

        self.far_x = copy(part(self.far, 0), 0, self.nx)
        self.far_y = copy(part(self.far, 1), 1, self.ny)
        self.near_x = copy(part(self.nx, 0), 2, self.nx)
        self.near_y = copy(part(self.ny, 1), 3, self.ny)
        self.on_y = copy(passing.at[0], 4, self.ny)
        self.on_x = copy(passing.at[1], 5, self.nx)

    def send_far(self):
        self.far_x.start()
        self.far_y.start()

    def send_near(self):
        self.near_x.start()
        self.near_y.start()

    def pass_on(self):
        self.far_x.wait_recv()
        self.passing[0] = (self.part(self.ny, 0)[...].astype(F32) + self.land[0].astype(F32)).astype(BF16)
        self.on_y.start()
        self.far_y.wait_recv()
        self.passing[1] = (self.part(self.nx, 1)[...].astype(F32) + self.land[1].astype(F32)).astype(BF16)
        self.on_x.start()

    def total(self, own):
        half = own.shape[0] // 2
        for copy in (self.near_x, self.near_y, self.on_y, self.on_x):
            copy.wait_recv()
        first = own[:half] + (self.land[2].astype(F32) + self.land[4].astype(F32))
        second = own[half:] + (self.land[3].astype(F32) + self.land[5].astype(F32))
        return jnp.concatenate([first, second], axis=0)

    def finish(self):
        for copy in (self.far_x, self.far_y, self.near_x, self.near_y, self.on_y, self.on_x):
            copy.wait_send()


class LineFold:
    def __init__(self, own, land, out, columns, send, recv):
        self.own, self.land, self.out, self.columns = own, land, out, columns
        self.send, self.recv = send, recv
        self.wides = own.shape[0]
        self.wide = lax.axis_index("wide")

    def place(self, way):
        return self.wide if way == 0 else self.wides - 1 - self.wide

    def copy(self, way, step):
        return pltpu.make_async_remote_copy(
            src_ref=self.out.at[self.slot(way, step), :, self.columns],
            dst_ref=self.land.at[way, step, :, self.columns],
            send_sem=self.send.at[way, step],
            recv_sem=self.recv.at[way, step],
            device_id={"wide": self.wide + 1 if way == 0 else self.wide - 1},
            device_id_type=MESH,
        )

    def slot(self, way, step):
        return jnp.clip(step - self.wide, 0, self.wides - 2) if way == 0 else step

    def sends(self, way, step):
        place = self.place(way)
        return (place <= step) & (place < self.wides - 1)

    def gets(self, way, step):
        place = self.place(way)
        return (place >= 1) & (place - 1 <= step)

    def step(self, step):
        for way in (0, 1):
            ahead = self.wides - 1 - step
            block = self.wide + ahead if way == 0 else self.wide - ahead
            block = jnp.clip(block, 0, self.wides - 1)
            begins = self.place(way) == 0

            @pl.when(self.sends(way, step) & begins)
            def _():
                self.out[self.slot(way, step), :, self.columns] = self.own[block, :, self.columns]
                self.copy(way, step).start()

            if step:

                @pl.when(self.sends(way, step) & jnp.logical_not(begins))
                def _():
                    self.copy(way, step - 1).wait_recv()
                    total = self.own[block, :, self.columns].astype(F32)
                    total = total + self.land[way, step - 1, :, self.columns].astype(F32)
                    self.out[self.slot(way, step), :, self.columns] = total.astype(BF16)
                    self.copy(way, step).start()

    def finish(self, result):
        last = self.wides - 2
        result[:, self.columns] = self.own[self.wide, :, self.columns]
        for way in (0, 1):

            @pl.when(self.gets(way, last))
            def _():
                self.copy(way, last).wait_recv()
                total = result[:, self.columns].astype(F32)
                total = total + self.land[way, last, :, self.columns].astype(F32)
                result[:, self.columns] = total.astype(BF16)

    def close(self):
        for step in range(self.wides - 1):
            for way in (0, 1):
                pl.when(self.sends(way, step))(self.copy(way, step).wait_send)


def line_spec(wides, block, columns, pieces):
    hops = pltpu.SemaphoreType.DMA((pieces, 2, wides - 1))
    return [
        pltpu.VMEM((wides, block, columns), BF16),
        pltpu.VMEM((2, wides - 1, block, columns), BF16),
        pltpu.VMEM((wides - 1, block, columns), BF16),
        pltpu.VMEM((block, columns), BF16),
        pltpu.SemaphoreType.DMA((wides + 1,)),
        hops,
        hops,
    ]


class LineSum:
    def __init__(self, src, dst, own, land, out, result, loads, send, recv):
        self.src, self.dst, self.own, self.result, self.loads = src, dst, own, result, loads
        pieces = send.shape[0]
        columns = own.shape[2]
        width = -(-columns // (128 * pieces)) * 128
        self.folds = [
            LineFold(own, land, out, pl.ds(first, min(width, columns - first)), send.at[p], recv.at[p])
            for p, first in enumerate(range(0, columns, width))
        ]
        self.steps = own.shape[0] - 1

    def load(self):
        wides, rows, columns = self.own.shape
        for w in range(wides):
            part = self.src.at[pl.ds(w * rows, rows), pl.ds(0, columns)]
            pltpu.make_async_copy(part, self.own.at[w], self.loads.at[w]).start()

    def begin(self):
        wides, rows, columns = self.own.shape
        for w in range(wides):
            part = self.src.at[pl.ds(w * rows, rows), pl.ds(0, columns)]
            pltpu.make_async_copy(part, self.own.at[w], self.loads.at[w]).wait()
        for fold in self.folds:
            fold.step(0)

    def step(self, step, piece):
        self.folds[piece].step(step)

    def end(self):
        for fold in self.folds:
            fold.finish(self.result)
        if self.dst is not None:
            copy = pltpu.make_async_copy(self.result, self.dst, self.loads.at[self.own.shape[0]])
            copy.start()
        for fold in self.folds:
            fold.close()
        if self.dst is not None:
            copy.wait()


class Deal:
    def __init__(self, src, place, send, recv):
        me, nx, ny = neighbours()
        far = jnp.bitwise_xor(me, 3)
        self.copies = [
            remote(src(other), place(me), send.at[at], recv.at[at], other)
            for at, other in enumerate((far, nx, ny))
        ]

    def start(self):
        for copy in self.copies:
            copy.start()

    def here(self):
        for copy in self.copies:
            copy.wait_recv()

    def finish(self):
        for copy in self.copies:
            copy.wait_send()


def greet(*others):
    barrier = pltpu.get_barrier_semaphore()
    for other in others:
        pl.semaphore_signal(barrier, inc=1, device_id=other, device_id_type=MESH)
    return lambda: pl.semaphore_wait(barrier, len(others))


def spread_spec():
    return [pltpu.SemaphoreType.DMA((6,)), pltpu.SemaphoreType.DMA((6,))]


def fold_spec(count, width):
    return [
        pltpu.VMEM((6, count // 2, width), BF16),
        pltpu.VMEM((2, count // 2, width), BF16),
        pltpu.SemaphoreType.DMA((6,)),
        pltpu.SemaphoreType.DMA((6,)),
    ]


def params(collective_id, mib):
    return pltpu.CompilerParams(
        collective_id=collective_id, has_side_effects=True, vmem_limit_bytes=mib * MIB
    )


TILE = 256


def up_kernel(h_ref, gain_ref, w_ref, *refs):
    sharing = len(refs) > 11
    if sharing:
        xn_ref, o_ref, rows_out, gu_out, act_out, xn_out, o_out, *refs = refs
        rows, w, gu, act, load, store, send, recv, *share_refs = refs
        share = Share(xn_ref, o_ref, *share_refs)
    else:
        rows_out, gu_out, act_out, rows, w, gu, act, load, store, send, recv = refs
    count = h_ref.shape[0]
    hidden = act.shape[1]
    weights = pltpu.make_async_copy(w_ref.at[:, pl.ds(0, 2 * hidden)], w, load)
    weights.start()
    me, nx, ny = neighbours()
    met = greet({"narrow": nx}, {"narrow": ny}, {"narrow": jnp.bitwise_xor(me, 3)})
    value = h_ref[...]
    rows[rows_of(me, count), :] = (value * inverse_rms(value) * gain_ref[...]).astype(BF16)
    spread = Spread(halves_of(rows, count), send, recv)
    met()
    spread.start()
    weights.wait()

    def one(block, at):
        here = rows_of(block, count)

        def tile(j):
            left = rows[here, :]
            gate = nn(left, w[:, columns_of(j, TILE)])
            up = nn(left, w[:, columns_of(j, TILE, hidden)])
            inner = jnp.tanh(GELU_SCALE * (gate + GELU_CUBE * (gate * gate * gate)))
            gu[here, columns_of(j, TILE)] = gate.astype(BF16)
            gu[here, columns_of(j, TILE, hidden)] = up.astype(BF16)
            act[here, columns_of(j, TILE)] = (0.5 * gate * (1.0 + inner) * up).astype(BF16)

        for j in range(hidden // TILE):
            tile(j)
        copies = [
            pltpu.make_async_copy(ref.at[here], out.at[here], store.at[k, at])
            for k, (ref, out) in enumerate(((gu, gu_out), (act, act_out), (rows, rows_out)))
        ]
        for copy in copies:
            copy.start()
        return copies

    copies = one(me, 0)
    spread.pass_on()
    if sharing:
        share.start_rows()
        share.start_deal()
    spread.x_here()
    copies += one(nx, 1)
    spread.y_here()
    copies += one(ny, 2)
    spread.far_here()
    if sharing:
        share.spread.pass_on()
    copies += one(spread.far, 3)
    spread.finish()
    if sharing:
        share.all_here()
        share.finish()
        xn, o, loads = share_refs[:3]
        copies += [pltpu.make_async_copy(xn, xn_out, loads.at[2]), pltpu.make_async_copy(o, o_out, loads.at[3])]
        for copy in copies[-2:]:
            copy.start()
    for copy in copies:
        copy.wait()


def feed_up(h, gain, w_gu, hidden, shared, collective_id):
    count, model = h.shape
    total = 4 * count
    shapes = [(total, model), (total, 2 * hidden), (total, hidden)]
    shapes = [jax.ShapeDtypeStruct(shape, BF16) for shape in shapes]
    if shared:
        shapes += share_shapes(*shared)
    return pl.pallas_call(
        up_kernel,
        out_shape=shapes,
        in_specs=[vmem_spec(), vmem_spec(), any_spec()] + [vmem_spec()] * len(shared),
        out_specs=[any_spec()] * len(shapes),
        scratch_shapes=[
            pltpu.VMEM((total, model), BF16),
            pltpu.VMEM((model, 2 * hidden), BF16),
            pltpu.VMEM((total, 2 * hidden), BF16),
            pltpu.VMEM((total, hidden), BF16),
            pltpu.SemaphoreType.DMA,
            pltpu.SemaphoreType.DMA((3, 4)),
            *spread_spec(),
            *(share_spec(count, model, shared[1].shape[1] // 4) if shared else []),
        ],
        compiler_params=params(collective_id, 60),
    )(h, gain, w_gu, *shared)


def down_kernel(
    h_ref, gain_ref, act_ref, w_ref, x_out, f_out, act, w, parts, load, land, passing, send, recv
):
    count, model = h_ref.shape
    me, nx, ny = neighbours()
    met = greet({"narrow": nx}, {"narrow": ny})
    far = jnp.bitwise_xor(me, 3)
    first = w_ref.shape[1] - w.shape[1]
    weights = pltpu.make_async_copy(w_ref.at[:, pl.ds(first, w.shape[1])], w, load.at[0])
    weights.start()
    arrivals = []
    for at, block in enumerate((far, nx, ny, me)):
        here = rows_of(block, count)
        arrivals.append(pltpu.make_async_copy(act_ref.at[here], act.at[here], load.at[1 + at]))
        arrivals[-1].start()
    fold = Fold(halves_of(parts, count), land, passing, send, recv)
    weights.wait()
    met()

    def one(block, at):
        arrivals[at].wait()
        return nt(act[rows_of(block, count), :], w[...])

    parts[rows_of(far, count), :] = one(far, 0).astype(BF16)
    fold.send_far()
    parts[rows_of(nx, count), :] = one(nx, 1).astype(BF16)
    parts[rows_of(ny, count), :] = one(ny, 2).astype(BF16)
    fold.send_near()
    f_out[...] = one(me, 3)
    fold.pass_on()
    total = fold.total(f_out[...])
    f_out[...] = total
    x_out[...] = (h_ref[...] + total * inverse_rms(total) * gain_ref[...]).astype(BF16)
    fold.finish()


def feed_down(h, gain, act, w_dt, collective_id):
    count, model = h.shape
    return pl.pallas_call(
        down_kernel,
        out_shape=[
            jax.ShapeDtypeStruct((count, model), BF16),
            jax.ShapeDtypeStruct((count, model), F32),
        ],
        in_specs=[vmem_spec(), vmem_spec(), any_spec(), any_spec()],
        out_specs=[vmem_spec(), vmem_spec()],
        scratch_shapes=[
            pltpu.VMEM(act.shape, BF16),
            pltpu.VMEM((model, act.shape[1]), BF16),
            pltpu.VMEM((4 * count, model), BF16),
            pltpu.SemaphoreType.DMA((5,)),
            *fold_spec(count, model),
        ],
        compiler_params=params(collective_id, 60),
    )(h, gain, act, w_dt)


def swap_sum(make, tiles, ours, theirs, came, send, recv, out, out_sems, between=None):
    other = {"section": 1 - lax.axis_index("section")}
    sends = []
    for at, (first, width) in enumerate(tiles):
        columns = pl.ds(first, width)
        theirs[:, columns] = make(False, first, width).astype(BF16)
        copy = pltpu.make_async_remote_copy(
            src_ref=theirs.at[:, columns],
            dst_ref=came.at[:, columns],
            send_sem=send.at[at],
            recv_sem=recv.at[at],
            device_id=other,
            device_id_type=MESH,
        )
        copy.start()
        sends.append(copy)
    if between is not None:
        between()
    stores = []
    for at, (first, width) in enumerate(tiles):
        columns = pl.ds(first, width)
        own = make(True, first, width)
        sends[at].wait_recv()
        ours[:, columns] = (own + came[:, columns].astype(F32)).astype(BF16)
        copy = pltpu.make_async_copy(ours.at[:, columns], out.at[:, columns], out_sems.at[at])
        copy.start()
        stores.append(copy)
    return sends, stores


def column_tiles(width):
    return [(first, min(2 * TILE, width - first)) for first in range(0, width, 2 * TILE)]


def gate_up_gradient(df, here, w, gu, hidden):
    for j in range(hidden // TILE):
        dact = nn(df[here, :], w[:, columns_of(j, TILE)])
        gate = gu[here, columns_of(j, TILE)].astype(F32)
        up = gu[here, columns_of(j, TILE, hidden)].astype(F32)
        square = gate * gate
        inner = jnp.tanh(GELU_SCALE * gate * (1.0 + GELU_CUBE * square))
        half = 0.5 * (1.0 + inner)
        slope = half + 0.5 * GELU_SCALE * gate * (1.0 - inner * inner) * (
            1.0 + 3.0 * GELU_CUBE * square
        )
        gu[here, columns_of(j, TILE)] = (dact * up * slope).astype(BF16)
        gu[here, columns_of(j, TILE, hidden)] = (dact * gate * half).astype(BF16)


def back_up_kernel(dy_ref, f_ref, gain_ref, gu_ref, act_ref, w_ref, *refs):
    if len(refs) == 18:
        refs = refs[1:]
    if len(refs) == 19:
        extra_ref, _, *refs = refs
    else:
        extra_ref = None
    (
        dgu_out, dw_out, dgain_out, df, gu, act, w, ours, theirs, came,
        load, store, send, recv, swap_send, swap_recv, out_sems,
    ) = refs
    if extra_ref is not None:
        first = ours.shape[1]
        extra = pltpu.make_async_copy(
            extra_ref, dw_out.at[:, pl.ds(first, extra_ref.shape[1])], load.at[0, 1]
        )
        extra.start()
    count, model = dy_ref.shape
    hidden = act.shape[1]
    me, nx, ny = neighbours()
    core = lax.axis_index("section")
    met = greet({"narrow": nx}, {"narrow": ny}, {"section": 1 - core})
    far = jnp.bitwise_xor(me, 3)
    start = w_ref.shape[1] - hidden
    weights = pltpu.make_async_copy(w_ref.at[:, pl.ds(start, hidden)], w, load.at[0, 0])
    weights.start()
    arrivals = []
    for at, block in enumerate((me, nx, ny, far)):
        here = rows_of(block, count)
        pair = [
            pltpu.make_async_copy(gu_ref.at[here], gu.at[here], load.at[1, at]),
            pltpu.make_async_copy(act_ref.at[here], act.at[here], load.at[2, at]),
        ]
        for copy in pair:
            copy.start()
        arrivals.append(pair)
    dy = dy_ref[...].astype(BF16).astype(F32)
    by_value, by_gain = normed_gradient(f_ref[...], gain_ref[...], dy)
    df[rows_of(me, count), :] = by_value.astype(BF16)
    spread = Spread(halves_of(df, count), send, recv)
    met()
    spread.start()
    dgain_out[...] = by_gain
    weights.wait()

    def one(block, at):
        here = rows_of(block, count)
        for copy in arrivals[at]:
            copy.wait()

        gate_up_gradient(df, here, w, gu, hidden)
        copy = pltpu.make_async_copy(gu.at[here], dgu_out.at[here], store.at[at])
        copy.start()
        return copy

    copies = [one(me, 0)]
    spread.pass_on()
    spread.x_here()
    copies.append(one(nx, 1))
    spread.y_here()
    copies.append(one(ny, 2))
    spread.far_here()
    copies.append(one(far, 3))

    def make(mine, first, width):
        side = core if mine else 1 - core
        start = pl.multiple_of(side * (hidden // 2) + first, 128)
        return tn(df[...], act[:, pl.ds(start, width)])

    sends, stores = swap_sum(
        make, column_tiles(hidden // 2), ours, theirs, came, swap_send, swap_recv, dw_out, out_sems
    )
    spread.finish()
    for copy in sends:
        copy.wait_send()
    for copy in copies + stores:
        copy.wait()
    if extra_ref is not None:
        extra.wait()


def turn_kernel(
    h_ref, gain_ref, dy_ref, act_ref, w_ref, gu_ref, x_out, dgu_out, dw_out, dgain_out,
    act, w, parts, df, gu, ours, theirs, came, load, store, land, passing, fold_send, fold_recv, send, recv,
    swap_send, swap_recv, out_sems,
):
    count, model = h_ref.shape
    hidden = act.shape[1]
    me, nx, ny = neighbours()
    core = lax.axis_index("section")
    far = jnp.bitwise_xor(me, 3)
    met = greet({"narrow": nx}, {"narrow": ny}, {"section": 1 - core})
    first = w_ref.shape[1] - hidden
    weights = pltpu.make_async_copy(w_ref.at[:, pl.ds(first, hidden)], w, load.at[0, 0])
    weights.start()
    blocks = (far, nx, ny, me)
    for at, block in enumerate(blocks):
        here = rows_of(block, count)
        pltpu.make_async_copy(act_ref.at[here], act.at[here], load.at[1, at]).start()
    for at, block in enumerate(blocks):
        here = rows_of(block, count)
        pltpu.make_async_copy(gu_ref.at[here], gu.at[here], load.at[2, at]).start()

    def here_now(row, at):
        here = rows_of(blocks[at], count)
        src, dst = ((act_ref, act), (gu_ref, gu))[row - 1]
        pltpu.make_async_copy(src.at[here], dst.at[here], load.at[row, at]).wait()
        return here

    fold = Fold(halves_of(parts, count), land, passing, fold_send, fold_recv)
    weights.wait()
    met()

    def part(at):
        here = here_now(1, at)
        return here, nt(act[here, :], w[...])

    here, value = part(0)
    parts[here, :] = value.astype(BF16)
    fold.send_far()
    for at in (1, 2):
        here, value = part(at)
        parts[here, :] = value.astype(BF16)
    fold.send_near()
    _, value = part(3)
    fold.pass_on()
    f = fold.total(value)
    gain = gain_ref[...]
    by_value, by_gain = normed_gradient(f, gain, dy_ref[...])
    df[rows_of(me, count), :] = by_value.astype(BF16)
    spread = Spread(halves_of(df, count), send, recv)
    spread.start()
    dgain_out[...] = by_gain
    x_out[...] = (h_ref[...] + f * inverse_rms(f) * gain).astype(BF16)

    def one(at):
        here = here_now(2, at)
        gate_up_gradient(df, here, w, gu, hidden)
        copy = pltpu.make_async_copy(gu.at[here], dgu_out.at[here], store.at[at])
        copy.start()
        return copy

    copies = [one(3)]
    spread.pass_on()
    spread.x_here()
    copies.append(one(1))
    spread.y_here()
    copies.append(one(2))
    spread.far_here()
    copies.append(one(0))

    def make(mine, first, width):
        side = core if mine else 1 - core
        start = pl.multiple_of(side * (hidden // 2) + first, 128)
        return tn(df[...], act[:, pl.ds(start, width)])

    sends, stores = swap_sum(
        make, column_tiles(hidden // 2), ours, theirs, came, swap_send, swap_recv, dw_out, out_sems
    )
    spread.finish()
    fold.finish()
    for copy in sends:
        copy.wait_send()
    for copy in copies + stores:
        copy.wait()


def feed_turn(h, gain, dy, act, w_dt, gu, collective_id):
    count, model = h.shape
    total, hidden = act.shape
    tiles = pltpu.SemaphoreType.DMA((len(column_tiles(hidden // 2)),))
    dw = pltpu.VMEM((model, hidden // 2), BF16)
    return pl.pallas_call(
        turn_kernel,
        out_shape=[
            jax.ShapeDtypeStruct((count, model), BF16),
            jax.ShapeDtypeStruct(gu.shape, BF16),
            jax.ShapeDtypeStruct((model, hidden // 2), BF16),
            jax.ShapeDtypeStruct((1, model), F32),
        ],
        in_specs=[vmem_spec()] * 3 + [any_spec()] * 3,
        out_specs=[vmem_spec(), any_spec(), any_spec(), vmem_spec()],
        scratch_shapes=[
            pltpu.VMEM(act.shape, BF16),
            pltpu.VMEM((model, hidden), BF16),
            pltpu.VMEM((total, model), BF16),
            pltpu.VMEM((total, model), BF16),
            pltpu.VMEM(gu.shape, BF16),
            dw,
            dw,
            dw,
            pltpu.SemaphoreType.DMA((3, 4)),
            pltpu.SemaphoreType.DMA((4,)),
            *fold_spec(count, model),
            *spread_spec(),
            tiles,
            tiles,
            tiles,
        ],
        compiler_params=params(collective_id, 60),
    )(h, gain, dy, act, w_dt, gu)


def feed_back_up(dy, f, gain, gu, act, w_dt, extra, collective_id):
    count, model = dy.shape
    total, hidden = act.shape
    tiles = len(column_tiles(hidden // 2))
    extras = extra
    return pl.pallas_call(
        back_up_kernel,
        out_shape=[
            jax.ShapeDtypeStruct(gu.shape, BF16),
            jax.ShapeDtypeStruct((model, hidden // 2 + sum(e.shape[1] for e in extras[:-1])), BF16),
            jax.ShapeDtypeStruct((1, model), F32),
        ],
        in_specs=[vmem_spec()] * 3 + [any_spec()] * (3 + len(extras)),
        out_specs=[any_spec(), any_spec(), vmem_spec()],
        scratch_shapes=[
            pltpu.VMEM((total, model), BF16),
            pltpu.VMEM(gu.shape, BF16),
            pltpu.VMEM(act.shape, BF16),
            pltpu.VMEM((model, hidden), BF16),
            pltpu.VMEM((model, hidden // 2), BF16),
            pltpu.VMEM((model, hidden // 2), BF16),
            pltpu.VMEM((model, hidden // 2), BF16),
            pltpu.SemaphoreType.DMA((3, 4)),
            pltpu.SemaphoreType.DMA((4,)),
            *spread_spec(),
            pltpu.SemaphoreType.DMA((tiles,)),
            pltpu.SemaphoreType.DMA((tiles,)),
            pltpu.SemaphoreType.DMA((tiles,)),
        ],
        compiler_params=params(collective_id, 60),
    )(dy, f, gain, gu, act, w_dt, *extras)


def back_down_kernel(
    dy_ref, h_ref, gain_ref, dgu_ref, rows_ref, w_ref, dh_out, dw_out, dgain_out,
    dgu, rows, w, parts, ours, theirs, came, load, land, passing, send, recv, swap_send, swap_recv, out_sems,
):
    count, model = dy_ref.shape
    hidden = dgu.shape[1] // 2
    me, nx, ny = neighbours()
    core = lax.axis_index("section")
    far = jnp.bitwise_xor(me, 3)
    met = greet({"narrow": nx}, {"narrow": ny}, {"section": 1 - core})
    weights = pltpu.make_async_copy(w_ref.at[:, pl.ds(0, 2 * hidden)], w, load.at[0])
    weights.start()
    arrivals = []
    for at, block in enumerate((far, nx, ny, me)):
        here = rows_of(block, count)
        arrivals.append(pltpu.make_async_copy(dgu_ref.at[here], dgu.at[here], load.at[1 + at]))
        arrivals[-1].start()
    kept = pltpu.make_async_copy(rows_ref, rows, load.at[5])
    kept.start()
    fold = Fold(halves_of(parts, count), land, passing, send, recv)
    weights.wait()
    met()

    def one(block, at, out, here):
        arrivals[at].wait()
        out[here, :] = nt(dgu[rows_of(block, count), :], w[...]).astype(out.dtype)

    one(far, 0, parts, rows_of(far, count))
    fold.send_far()
    one(nx, 1, parts, rows_of(nx, count))
    one(ny, 2, parts, rows_of(ny, count))
    fold.send_near()
    one(me, 3, dh_out, pl.ds(0, count))
    fold.pass_on()
    kept.wait()

    def make(mine, first, width):
        side = core if mine else 1 - core
        start = pl.multiple_of(side * hidden + first, 128)
        return tn(rows[...], dgu[:, pl.ds(start, width)])

    sends, stores = swap_sum(
        make, column_tiles(hidden), ours, theirs, came, swap_send, swap_recv, dw_out, out_sems
    )
    total = fold.total(dh_out[...])
    by_value, by_gain = normed_gradient(h_ref[...], gain_ref[...], total)
    dh_out[...] = dy_ref[...].astype(BF16).astype(F32) + by_value
    dgain_out[...] = by_gain
    fold.finish()
    for copy in sends:
        copy.wait_send()
    for copy in stores:
        copy.wait()


def feed_back_down(dy, h, gain, dgu, rows, w_gu, collective_id):
    count, model = dy.shape
    total, hidden = dgu.shape[0], dgu.shape[1] // 2
    tiles = len(column_tiles(hidden))
    return pl.pallas_call(
        back_down_kernel,
        out_shape=[
            jax.ShapeDtypeStruct((count, model), F32),
            jax.ShapeDtypeStruct((model, hidden), BF16),
            jax.ShapeDtypeStruct((1, model), F32),
        ],
        in_specs=[vmem_spec()] * 3 + [any_spec()] * 3,
        out_specs=[vmem_spec(), any_spec(), vmem_spec()],
        scratch_shapes=[
            pltpu.VMEM(dgu.shape, BF16),
            pltpu.VMEM(rows.shape, BF16),
            pltpu.VMEM((model, 2 * hidden), BF16),
            pltpu.VMEM((total, model), BF16),
            pltpu.VMEM((model, hidden), BF16),
            pltpu.VMEM((model, hidden), BF16),
            pltpu.VMEM((model, hidden), BF16),
            pltpu.SemaphoreType.DMA((6,)),
            *fold_spec(count, model),
            pltpu.SemaphoreType.DMA((tiles,)),
            pltpu.SemaphoreType.DMA((tiles,)),
            pltpu.SemaphoreType.DMA((tiles,)),
        ],
        compiler_params=params(collective_id, 60),
    )(dy, h, gain, dgu, rows, w_gu)


def pack_kernel(p_ref, o_ref, g_ref, local, send, recv, peer_send, peer_recv):
    model, width = o_ref.shape[2:]
    half = model // 2
    wides, extra = g_ref.shape[1:3]
    rows = model // wides
    core = lax.axis_index("section")
    me, nx, ny = neighbours()
    met = greet({"narrow": nx}, {"narrow": ny}, {"section": 1 - core})
    whole = p_ref.shape[0] == model
    owns = []
    if whole:
        owns.append(pltpu.make_async_copy(p_ref, o_ref.at[core, me], local.at[0, 0]))
    else:
        for w in range(wides):
            first = w * (rows + extra)
            place = o_ref.at[core, me, pl.ds(w * rows, rows)]
            owns.append(pltpu.make_async_copy(p_ref.at[pl.ds(first, rows)], place, local.at[0, w]))
            part = p_ref.at[pl.ds(first + rows, extra)]
            owns.append(pltpu.make_async_copy(part, g_ref.at[core, w], local.at[1, w]))
    start_all(owns)
    spread = Spread(lambda block, which: o_ref.at[core, block, pl.ds(which * half, half)], send, recv)
    wait_all(owns)
    met()
    spread.start()
    copies = []

    def across(ref):
        copy = pltpu.make_async_remote_copy(
            src_ref=ref,
            dst_ref=ref,
            send_sem=peer_send.at[len(copies)],
            recv_sem=peer_recv.at[len(copies)],
            device_id={"section": 1 - core},
            device_id_type=MESH,
        )
        copy.start()
        copies.append(copy)

    if not whole:
        across(g_ref.at[core])
    across(o_ref.at[core, me])
    spread.pass_on()
    spread.x_here()
    across(o_ref.at[core, nx])
    spread.y_here()
    across(o_ref.at[core, ny])
    spread.far_here()
    across(o_ref.at[core, spread.far])
    for copy in copies:
        copy.wait_recv()
    spread.finish()
    for copy in copies:
        copy.wait_send()


def gather_pack(pack, model, wides, collective_id):
    width = pack.shape[1]
    return pl.pallas_call(
        pack_kernel,
        out_shape=[
            jax.ShapeDtypeStruct((2, 4, model, width), pack.dtype),
            jax.ShapeDtypeStruct((2, wides, GAIN_ROWS, width), pack.dtype),
        ],
        in_specs=[any_spec()],
        out_specs=[vmem_spec()] * 2,
        scratch_shapes=[
            pltpu.SemaphoreType.DMA((2, wides)),
            *spread_spec(),
            pltpu.SemaphoreType.DMA((5,)),
            pltpu.SemaphoreType.DMA((5,)),
        ],
        compiler_params=params(collective_id, 32),
    )(pack)


def finish_kernel(
    zero_ref, one_ref, early_ref, dep_ref, q_out, kv_out, o_out, came, kv, send, recv, kv_send, kv_recv
):
    core = lax.axis_index("section")
    me, nx, ny = neighbours()
    others = (nx, ny, jnp.bitwise_xor(me, 3))
    met = greet({"section": 1 - core}, *[{"narrow": other} for other in others])
    head = q_out.shape[1]
    first = core == 0
    by_qkv = jnp.where(first, zero_ref[...], early_ref[...])
    kv[me] = by_qkv[:, head:]
    met()
    across = pltpu.make_async_remote_copy(
        src_ref=zero_ref,
        dst_ref=came,
        send_sem=send,
        recv_sem=recv,
        device_id={"section": 1 - core},
        device_id_type=MESH,
    )
    across.start()
    copies = []
    for at, other in enumerate(others):
        copies.append(remote(kv.at[me], kv.at[me], kv_send.at[at], kv_recv.at[at], other))
        copies[-1].start()
    q_out[...] = by_qkv[:, :head].astype(F32)
    across.wait_recv()
    o_out[...] = jnp.where(first, came[:, :head], one_ref[:, :head]).astype(F32)
    for copy in copies:
        copy.wait_recv()
    width = kv.shape[2]
    for n in range(4):
        kv_out[:, n * width : (n + 1) * width] = kv[n].astype(F32)
    across.wait_send()
    for copy in copies:
        copy.wait_send()


def finish_attention(zero, one, early, dep, head, collective_id):
    block, width = zero.shape
    return pl.pallas_call(
        finish_kernel,
        out_shape=[
            jax.ShapeDtypeStruct((block, head), F32),
            jax.ShapeDtypeStruct((block, 4 * (width - head)), F32),
            jax.ShapeDtypeStruct((block, head), F32),
        ],
        in_specs=[vmem_spec()] * 3 + [any_spec()],
        out_specs=[vmem_spec()] * 3,
        scratch_shapes=[
            pltpu.VMEM((block, width), BF16),
            pltpu.VMEM((4, block, width - head), BF16),
            pltpu.SemaphoreType.DMA,
            pltpu.SemaphoreType.DMA,
            pltpu.SemaphoreType.DMA((3,)),
            pltpu.SemaphoreType.DMA((3,)),
        ],
        compiler_params=params(collective_id, 16),
    )(zero, one, early, dep)


def pair_kernel(zero_ref, one_ref, came_zero_ref, came_one_ref, out_ref, flag_ref):
    hidden = out_ref.shape[2]
    first = lax.axis_index("section") == 0
    keep = jnp.where(first, zero_ref[:, :hidden], one_ref[:, :hidden])
    came = jnp.where(first, came_zero_ref[:, :hidden], came_one_ref[:, :hidden])
    out_ref[:, 0, :] = jnp.where(first, keep, came).astype(F32)
    out_ref[:, 1, :] = jnp.where(first, came, keep).astype(F32)
    flag_ref[...] = jnp.zeros_like(flag_ref)


def pair_up(zero, one, came_zero, came_one, hidden):
    return pl.pallas_call(
        pair_kernel,
        out_shape=[
            jax.ShapeDtypeStruct((zero.shape[0], 2, hidden), F32),
            jax.ShapeDtypeStruct((8, 128), F32),
        ],
        in_specs=[vmem_spec()] * 4,
        out_specs=[vmem_spec()] * 2,
        compiler_params=pltpu.CompilerParams(vmem_limit_bytes=40 * MIB),
    )(zero, one, came_zero, came_one)


class Share:
    def __init__(self, xn_ref, o_ref, xn, o, loads, spread_send, spread_recv, deal_send, deal_recv):
        count, head = xn_ref.shape[0], o.shape[1]
        me = lax.axis_index("narrow")
        self.loads = [
            pltpu.make_async_copy(xn_ref, xn.at[rows_of(me, count)], loads.at[0]),
            pltpu.make_async_copy(o_ref.at[:, columns_of(me, head)], o.at[rows_of(me, count)], loads.at[1]),
        ]
        self.spread = Spread(halves_of(xn, count), spread_send, spread_recv)
        self.deal = Deal(
            lambda other: o_ref.at[:, columns_of(other, head)],
            lambda mine: o.at[rows_of(mine, count)],
            deal_send,
            deal_recv,
        )

    def start_rows(self):
        self.loads[0].start()
        self.loads[0].wait()
        self.spread.start()

    def start_deal(self):
        self.loads[1].start()
        self.deal.start()

    def all_here(self):
        self.spread.all_here()
        self.deal.here()

    def finish(self):
        self.spread.finish()
        self.deal.finish()
        self.loads[1].wait()


def share_spec(count, model, head):
    return [
        pltpu.VMEM((4 * count, model), BF16),
        pltpu.VMEM((4 * count, head), BF16),
        pltpu.SemaphoreType.DMA((4,)),
        *spread_spec(),
        pltpu.SemaphoreType.DMA((3,)),
        pltpu.SemaphoreType.DMA((3,)),
    ]


def share_shapes(xn, o):
    total = 4 * xn.shape[0]
    return [
        jax.ShapeDtypeStruct((total, xn.shape[1]), BF16),
        jax.ShapeDtypeStruct((total, o.shape[1] // 4), BF16),
    ]


def gain_stages():
    wides = lax.axis_size("wide")
    core, wide = lax.axis_index("section"), lax.axis_index("wide")
    me, nx, ny = neighbours()
    return [
        [{"narrow": nx}, {"narrow": ny}, {"narrow": jnp.bitwise_xor(me, 3)}],
        [{"section": 1 - core}],
        [{"wide": lax.rem(wide + step, wides)} for step in range(1, wides)],
    ]


class GainSum:
    def __init__(self, land, total, send, recv):
        self.land, self.total, self.send, self.recv = land, total, send, recv
        self.copies = []
        self.waiting = []

    def start(self, stage):
        for other in gain_stages()[stage]:
            at = len(self.copies)
            copy = pltpu.make_async_remote_copy(
                src_ref=self.total.at[stage],
                dst_ref=self.land.at[at],
                send_sem=self.send.at[at],
                recv_sem=self.recv.at[at],
                device_id=other,
                device_id_type=MESH,
            )
            copy.start()
            self.copies.append(copy)
            self.waiting.append(at)

    def add(self, stage):
        value = self.total[stage]
        for at in self.waiting:
            self.copies[at].wait_recv()
            value = value + self.land[at]
        self.waiting = []
        self.total[stage + 1] = value

    def close(self):
        for copy in self.copies:
            copy.wait_send()


def gain_spec(wides, shape):
    return [
        pltpu.VMEM((wides + 3, *shape), F32),
        pltpu.VMEM((4, *shape), F32),
        pltpu.SemaphoreType.DMA((wides + 3,)),
        pltpu.SemaphoreType.DMA((wides + 3,)),
    ]


def turn_back(grad, cosine, sine_table):
    half = grad.shape[1] // 2
    front, back = grad[:, :half], grad[:, half:]
    return jnp.concatenate(
        [front * cosine + back * sine_table, back * cosine - front * sine_table], axis=1
    )


def pack_loads(pack_ref, layer, head, wq, wot, wkv, sems):
    kv_part = wkv.shape[1] // 4
    loads = []
    for at, (w, first, width) in enumerate(
        ((wq, 0, head), (wot, head, head), (wkv, 2 * head, kv_part))
    ):
        loads.append(
            [
                pltpu.make_async_copy(
                    pack_ref.at[layer, n, :, pl.ds(first, width)], w.at[:, pl.ds(n * width, width)], sems.at[at, n]
                )
                for n in range(4)
            ]
        )
    return loads


def start_all(copies):
    for copy in copies:
        copy.start()


def wait_all(copies):
    for copy in copies:
        copy.wait()


def window_mask(me, count, window, length):
    rows_at = me * count + lax.broadcasted_iota(jnp.int32, (count, 1), 0)
    cols_at = me * count - WINDOW + lax.broadcasted_iota(jnp.int32, (1, window), 1)
    return (
        (cols_at <= rows_at)
        & (rows_at - cols_at < WINDOW)
        & (cols_at >= 0)
        & ((cols_at < length) | (cols_at == rows_at))
    )


def attend_kernel(layer, length_ref, x_ref, gains_ref, head_ref, trig_ref, pack_ref, *refs):
    (
        h_out, xn_out, q_out, k_out, win_out, lse_out, o_out, a_out, *refs
    ) = refs
    sharing = len(refs) > 9
    if sharing:
        xn_all_out, o_all_out, *refs = refs
    kv, wq, wot, wkv, load, send, recv, *share_refs = refs
    count, model = x_ref.shape
    head = k_out.shape[1]
    heads = q_out.shape[1] // head
    me, nx, ny = neighbours()
    met = greet({"narrow": nx}, {"narrow": ny}, {"narrow": jnp.bitwise_xor(me, 3)})
    q_loads, out_loads, kv_loads = pack_loads(pack_ref, layer, head, wq, wot, wkv, load)
    start_all(kv_loads + q_loads + out_loads)
    scaling = head ** (-0.5)
    cosine, sine_table = trig_ref[:, : head // 2], trig_ref[:, head // 2 :]
    x = x_ref[...].astype(F32)
    xn_out[...] = (x * inverse_rms(x) * gains_ref[0:1, :]).astype(BF16)
    kv[pl.ds(0, WINDOW), :] = jnp.zeros((WINDOW, 2 * head), BF16)
    wait_all(kv_loads)
    raw = nn(xn_out[...], wkv[...])
    k_raw = raw[:, :head]
    k_out[...] = k_raw
    k_rot = rotate(k_raw * inverse_rms(k_raw) * head_ref[1:2, :], cosine, sine_table)
    here = pl.ds(pl.multiple_of(WINDOW + me * count, count), count)
    kv[here, :head] = k_rot.astype(BF16)
    kv[here, head:] = raw[:, head:].astype(BF16)
    spread = Spread(halves_of(kv, count, WINDOW), send, recv)
    met()
    spread.start()
    if sharing:
        share = Share(xn_out, o_out, *share_refs)
    wait_all(q_loads)
    q_out[...] = nn(xn_out[...], wq[...])
    spread.pass_on()
    if sharing:
        share.start_rows()
    spread.all_here()
    window = win_out.shape[0]
    win_out[...] = kv[pl.ds(pl.multiple_of(me * count, count), window), :]
    visible = window_mask(me, count, window, length_ref[0])
    k_win, v_win = win_out[:, :head], win_out[:, head:]
    q_gain = head_ref[0:1, :]

    def one_head(i):
        columns = columns_of(i, head)
        q_raw = q_out[:, columns]
        qr = rotate(q_raw * inverse_rms(q_raw) * q_gain, cosine, sine_table).astype(BF16)
        scores = jnp.where(visible, nt(qr, k_win) * scaling, NEGATIVE)
        most = jnp.max(scores, axis=-1, keepdims=True)
        exponent = jnp.exp(scores - most)
        total = jnp.sum(exponent, axis=-1, keepdims=True)
        lse_out[i] = most + jnp.log(total)
        o_out[:, columns] = nn((exponent / total).astype(BF16), v_win).astype(BF16)

    for i in range(heads):
        one_head(i)
    if sharing:
        share.start_deal()
        share.spread.pass_on()
    wait_all(out_loads)
    a = nt(o_out[...], wot[...])
    a_out[...] = a
    h_out[...] = x_ref[...].astype(F32) + a * inverse_rms(a) * gains_ref[1:2, :]
    spread.finish()
    if sharing:
        share.all_here()
        share.finish()
        xn, o, loads = share_refs[:3]
        stores = [
            pltpu.make_async_copy(xn, xn_all_out, loads.at[2]),
            pltpu.make_async_copy(o, o_all_out, loads.at[3]),
        ]
        start_all(stores)
        wait_all(stores)


def attend(length, x, gains, head_gains, trig, pack, head, layer, collective_id):
    count, model = x.shape
    kv_width = 2 * head
    width = 4 * head
    window = count + WINDOW
    sharing = True
    xn_shape = jax.ShapeDtypeStruct((count, model), BF16)
    o_shape = jax.ShapeDtypeStruct((count, width), BF16)
    shapes = [
        jax.ShapeDtypeStruct((count, model), F32),
        xn_shape,
        jax.ShapeDtypeStruct((count, width), F32),
        jax.ShapeDtypeStruct((count, head), F32),
        jax.ShapeDtypeStruct((window, kv_width), BF16),
        jax.ShapeDtypeStruct((4, count, 1), F32),
        o_shape,
        jax.ShapeDtypeStruct((count, model), F32),
    ]
    outs = [vmem_spec()] * 8
    if sharing:
        shapes += share_shapes(xn_shape, o_shape)
        outs += [any_spec()] * 2
    return pl.pallas_call(
        functools.partial(attend_kernel, layer),
        out_shape=shapes,
        in_specs=[pl.BlockSpec(memory_space=pltpu.SMEM)] + [vmem_spec()] * 4 + [any_spec()],
        out_specs=outs,
        scratch_shapes=[
            pltpu.VMEM((4 * count + WINDOW, kv_width), BF16),
            pltpu.VMEM((model, width), BF16),
            pltpu.VMEM((model, width), BF16),
            pltpu.VMEM((model, kv_width), BF16),
            pltpu.SemaphoreType.DMA((3, 4)),
            *spread_spec(),
            *(share_spec(count, model, head) if sharing else []),
        ],
        compiler_params=params(collective_id, 40),
    )(length, x, gains, head_gains, trig, pack)


def attend_back_kernel(
    layer, length_ref, dh_ref, a_ref, x_ref, gains_ref, head_ref, trig_ref, q_ref, k_ref, win_ref, lse_ref,
    pack_ref, xn_ref, o_ref, *refs
):
    if layer == 0:
        block_ref, dx_one_ref, lined_ref, early_ref, *refs = refs
        block_out, both_out, lined_out, came_out, q_out, kv_out, o_out = refs[4:11]
        refs = refs[:4] + refs[11:]
        gain_refs, (dx_give, dx_send, dx_recv), line_refs = refs[36:40], refs[40:43], refs[43:]
        refs = refs[:36]
    (
    dx_out, dw_out, dgain_out, dhead_out,
    da, do, dq, dk, dv, parts, dq_all, dkv, dkv_all, wq, wot, wkv, xn, o, ours, theirs, came,
    pack_load, load, send, recv, land, passing, fold_send, fold_recv, q_send, q_recv, kv_send, kv_recv, swap_send, swap_recv, out_sem,
    ) = refs
    count = dh_ref.shape[0]
    head = k_ref.shape[1]
    heads = q_ref.shape[1] // head
    kv_part = dkv_all.shape[1]
    me, nx, ny = neighbours()
    core = lax.axis_index("section")
    far = jnp.bitwise_xor(me, 3)
    lined = layer == 0 and len(line_refs) > 0
    if layer == 0:
        met = greet(*sum(gain_stages(), []))
        sums = GainSum(*gain_refs)
    else:
        met = greet({"narrow": nx}, {"narrow": ny}, {"narrow": far}, {"section": 1 - core})
    if lined:
        line = LineSum(lined_ref, lined_out, *line_refs[:7])
        early = LineSum(early_ref, None, *line_refs[7:14])
        late = LineSum(ours, None, *line_refs[14:21])
        came_line, came_store, came_early, came_late, kv_all, cross_send, cross_recv, narrow_send, narrow_recv = (
            line_refs[21:]
        )

        def across(at, src, dst):
            return pltpu.make_async_remote_copy(
                src_ref=src,
                dst_ref=dst,
                send_sem=cross_send.at[at],
                recv_sem=cross_recv.at[at],
                device_id={"section": 1 - core},
                device_id_type=MESH,
            )

        early.load()
        line.load()
    q_loads, out_loads, kv_loads = pack_loads(pack_ref, layer, head, wq, wot, wkv, pack_load)
    loads = [
        pltpu.make_async_copy(src, dst, load.at[at])
        for at, (src, dst) in enumerate(((xn_ref, xn), (o_ref, o)))
    ]
    start_all(out_loads + q_loads + kv_loads + loads)
    here = rows_of(me, count)
    scaling = head ** (-0.5)
    cosine, sine_table = trig_ref[:, : head // 2], trig_ref[:, head // 2 :]

    dh = dh_ref[...]
    by_value, dg1 = normed_gradient(a_ref[...], gains_ref[1:2, :], dh)
    da[here, :] = by_value.astype(BF16)
    dgain_out[1:2, :] = dg1
    spread = Spread(halves_of(da, count), send, recv)
    met()
    spread.start()
    if lined:
        early.begin()
        line.begin()
    wait_all(out_loads)
    do[...] = nn(da[here, :], wot[...]).astype(BF16)

    visible = window_mask(me, count, win_ref.shape[0], length_ref[0])
    k_win, v_win = win_ref[:, :head], win_ref[:, head:]
    dk[...] = jnp.zeros_like(dk)
    dv[...] = jnp.zeros_like(dv)
    dhead_out[...] = jnp.zeros_like(dhead_out)
    q_gain, k_gain = head_ref[0:1, :], head_ref[1:2, :]

    def one_head(i):
        columns = columns_of(i, head)
        raw = q_ref[:, columns]
        inverse = inverse_rms(raw)
        unit = raw * inverse
        qr = rotate(unit * q_gain, cosine, sine_table).astype(BF16)
        scores = jnp.where(visible, nt(qr, k_win) * scaling, NEGATIVE)
        probs = jnp.exp(scores - lse_ref[i])
        do_head = do[:, columns]
        dp = nt(do_head, v_win)
        ds = (probs * (dp - jnp.sum(probs * dp, axis=-1, keepdims=True))).astype(BF16)
        dk[...] += tn(ds, qr)
        dv[...] += tn(probs.astype(BF16), do_head)
        grad = turn_back(nn(ds, k_win) * scaling, cosine, sine_table)
        scaled = grad * q_gain
        dq_raw = inverse * (scaled - unit * jnp.mean(scaled * unit, axis=-1, keepdims=True))
        dq[:, columns] = dq_raw.astype(BF16)
        dhead_out[0:1, :] += jnp.sum(grad * unit, axis=0, keepdims=True)

    for i in range(heads):
        one_head(i)
    parts[...] = jnp.zeros_like(parts)
    window = pl.ds(pl.multiple_of(me * count, count), win_ref.shape[0])
    parts[window, :head] = (dk[...] * scaling).astype(BF16)
    parts[window, head:] = dv[...].astype(BF16)
    fold = Fold(halves_of(parts, count, WINDOW), land, passing, fold_send, fold_recv)
    fold.send_far()
    fold.send_near()
    deal_q = Deal(
        lambda other: dq.at[:, columns_of(other, head)],
        lambda mine: dq_all.at[rows_of(mine, count)],
        q_send,
        q_recv,
    )
    deal_q.start()
    dq_all[here, :] = dq[:, columns_of(me, head)]
    spread.pass_on()
    if lined:
        early.step(1, 0)
        line.step(1, 0)
    wait_all(q_loads)
    dx_out[...] = nt(dq[...], wq[...])
    fold.pass_on()
    spread.all_here()
    wait_all(loads)
    first = core == 0
    swaps = []

    def exchange(at, columns, a, b):
        ours[:, columns] = jnp.where(first, a, b).astype(BF16)
        theirs[:, columns] = jnp.where(first, b, a).astype(BF16)
        copy = pltpu.make_async_remote_copy(
            src_ref=theirs.at[:, columns],
            dst_ref=came.at[:, columns],
            send_sem=swap_send.at[at],
            recv_sem=swap_recv.at[at],
            device_id={"section": 1 - core},
            device_id_type=MESH,
        )
        copy.start()
        swaps.append(copy)

    if lined:
        line.step(1, 1)
    by_out = tn(da[...], o[...])
    deal_q.here()
    exchange(0, pl.ds(0, head), tn(xn[...], dq_all[...]), by_out)
    own = jnp.concatenate([dk[WINDOW:, :] * scaling, dv[WINDOW:, :]], axis=1)
    total = fold.total(own)
    grad = turn_back(total[:, :head], cosine, sine_table)
    dk_raw, dk_gain = normed_gradient(k_ref[...], k_gain, grad)
    dhead_out[1:2, :] = dk_gain
    dkv[:, :head] = dk_raw.astype(BF16)
    dkv[:, head:] = total[:, head:].astype(BF16)
    deal_kv = Deal(
        lambda other: dkv.at[:, columns_of(other, kv_part)],
        lambda mine: dkv_all.at[rows_of(mine, count)],
        kv_send,
        kv_recv,
    )
    deal_kv.start()
    dkv_all[here, :] = dkv[:, columns_of(me, kv_part)]
    wait_all(kv_loads)
    dxn = dx_out[...] + nt(dkv[...], wkv[...])
    by_value, dg0 = normed_gradient(x_ref[...].astype(F32), gains_ref[0:1, :], dxn)
    dx_out[...] = dh_ref[...] + by_value
    dgain_out[0:1, :] = dg0
    if layer == 0:
        zero = core == 0
        both_out[core] = jnp.where(zero, dx_out[...], dx_one_ref[...])
        dx_give[...] = jnp.where(zero, dx_one_ref[...], dx_out[...])
        dx_copy = pltpu.make_async_remote_copy(
            src_ref=dx_give,
            dst_ref=both_out.at[core],
            send_sem=dx_send,
            recv_sem=dx_recv,
            device_id={"section": 1 - core},
            device_id_type=MESH,
        )
        dx_copy.start()
    if lined:
        line.step(2, 0)
        for step in range(2, early.steps):
            early.step(step, 0)
    if layer == 0:
        own_total = sums.total.at[0]
        own_total[...] = block_ref[...]
        own_total[0:2, :] = dgain_out[...]
        own_total[4:5, :head] = dhead_out[0:1, :]
        own_total[4:5, head : 2 * head] = dhead_out[1:2, :]
        sums.start(0)

    deal_kv.here()
    by_kv = tn(xn[...], dkv_all[...])
    if layer == 0:
        sums.add(0)
        sums.start(1)
    exchange(1, pl.ds(head, kv_part), by_kv, jnp.zeros_like(by_kv))
    for copy in swaps:
        copy.wait_recv()
    ours[...] = (ours[...].astype(F32) + came[...].astype(F32)).astype(BF16)
    out = pltpu.make_async_copy(ours, dw_out, out_sem)
    out.start()
    if layer == 0:
        sums.add(1)
        sums.start(2)
    if lined:
        late.load()
        late.begin()
        for step in range(2, line.steps):
            if step > 2:
                line.step(step, 0)
            late.step(step - 1, 0)
            line.step(step, 1)
        early.end()
        crosses = [across(0, early.result, came_early)]
        crosses[0].start()
        late.step(late.steps - 1, 0)
        late.end()
        crosses.append(across(1, late.result, came_late))
        crosses[1].start()
        crosses[0].wait_recv()
        by_qkv = jnp.where(zero, late.result[...], came_early[...])
        kv_all[me] = by_qkv[:, head:]
        narrows = [
            remote(kv_all.at[me], kv_all.at[me], narrow_send.at[at], narrow_recv.at[at], other)
            for at, other in enumerate((nx, ny, far))
        ]
        start_all(narrows)
        q_out[...] = by_qkv[:, :head].astype(F32)
        crosses[1].wait_recv()
        o_out[...] = jnp.where(zero, came_late[:, :head], early.result[:, :head]).astype(F32)
        for copy in narrows:
            copy.wait_recv()
        for n in range(4):
            kv_out[:, n * kv_part : (n + 1) * kv_part] = kv_all[n].astype(F32)
        line.end()
        crosses.append(across(2, line.result, came_line))
        crosses[2].start()
        crosses[2].wait_recv()
        keep = pltpu.make_async_copy(came_line, came_out, came_store)
        keep.start()
        for copy in crosses + narrows:
            copy.wait_send()
        keep.wait()
    if layer == 0:
        dx_copy.wait_recv()
        dx_copy.wait_send()
    if layer == 0:
        sums.add(2)
        block_out[...] = sums.total[3]
        sums.close()
    spread.finish()
    fold.finish()
    deal_q.finish()
    deal_kv.finish()
    for copy in swaps:
        copy.wait_send()
    out.wait()


def attend_back(length, dh, a, x, gains, head_gains, trig, q_raw, k_raw, window, lse, pack, xn, o, deps, layer, collective_id):
    count, model = dh.shape
    head = k_raw.shape[1]
    width = q_raw.shape[1]
    kv_part = pack.shape[3] - 2 * head
    if layer == 0:
        wides = lax.axis_size("wide")
        block, dx_one, lined, early = deps
        rows = model // wides
    deal = pltpu.SemaphoreType.DMA((3,))
    dw = pltpu.VMEM((model, head + kv_part), BF16)
    return pl.pallas_call(
        functools.partial(attend_back_kernel, layer),
        out_shape=[
            jax.ShapeDtypeStruct((count, model), F32),
            jax.ShapeDtypeStruct((model, head + kv_part), BF16),
            jax.ShapeDtypeStruct((2, model), F32),
            jax.ShapeDtypeStruct((2, head), F32),
            *(
                [
                    jax.ShapeDtypeStruct(block.shape, F32),
                    jax.ShapeDtypeStruct((2, count, model), F32),
                    jax.ShapeDtypeStruct((rows, lined.shape[1]), BF16),
                    jax.ShapeDtypeStruct((rows, lined.shape[1]), BF16),
                    jax.ShapeDtypeStruct((rows, head), F32),
                    jax.ShapeDtypeStruct((rows, 4 * kv_part), F32),
                    jax.ShapeDtypeStruct((rows, head), F32),
                ]
                if layer == 0
                else []
            ),
        ],
        in_specs=[pl.BlockSpec(memory_space=pltpu.SMEM)] + [vmem_spec()] * 10 + [any_spec()] * 3 + ([vmem_spec()] * 2 + [any_spec()] * 2 if layer == 0 else []),
        out_specs=[vmem_spec(), any_spec(), vmem_spec(), vmem_spec()]
        + ([vmem_spec()] * 2 + [any_spec()] * 2 + [vmem_spec()] * 3 if layer == 0 else []),
        scratch_shapes=[
            pltpu.VMEM((4 * count, model), BF16),
            pltpu.VMEM((count, width), BF16),
            pltpu.VMEM((count, width), BF16),
            pltpu.VMEM((window.shape[0], head), F32),
            pltpu.VMEM((window.shape[0], head), F32),
            pltpu.VMEM((4 * count + WINDOW, 2 * head), BF16),
            pltpu.VMEM((4 * count, head), BF16),
            pltpu.VMEM((count, 2 * head), BF16),
            pltpu.VMEM((4 * count, kv_part), BF16),
            pltpu.VMEM((model, width), BF16),
            pltpu.VMEM((model, width), BF16),
            pltpu.VMEM((model, 2 * head), BF16),
            pltpu.VMEM(xn.shape, BF16),
            pltpu.VMEM(o.shape, BF16),
            dw,
            dw,
            dw,
            pltpu.SemaphoreType.DMA((3, 4)),
            pltpu.SemaphoreType.DMA((2,)),
            *spread_spec(),
            *fold_spec(count, 2 * head),
            deal,
            deal,
            deal,
            deal,
            pltpu.SemaphoreType.DMA((2,)),
            pltpu.SemaphoreType.DMA((2,)),
            pltpu.SemaphoreType.DMA,
            *(
                [
                    *gain_spec(wides, block.shape),
                    pltpu.VMEM((count, model), F32),
                    pltpu.SemaphoreType.DMA,
                    pltpu.SemaphoreType.DMA,
                ]
                if layer == 0
                else []
            ),
            *(
                [
                    *line_spec(wides, rows, lined.shape[1], 2),
                    *line_spec(wides, rows, head + kv_part, 1),
                    *line_spec(wides, rows, head + kv_part, 1),
                    pltpu.VMEM((rows, lined.shape[1]), BF16),
                    pltpu.SemaphoreType.DMA,
                    pltpu.VMEM((rows, head + kv_part), BF16),
                    pltpu.VMEM((rows, head + kv_part), BF16),
                    pltpu.VMEM((4, rows, kv_part), BF16),
                    pltpu.SemaphoreType.DMA((3,)),
                    pltpu.SemaphoreType.DMA((3,)),
                    pltpu.SemaphoreType.DMA((3,)),
                    pltpu.SemaphoreType.DMA((3,)),
                ]
                if layer == 0 and rows % 16 == 0
                else []
            ),
        ],
        compiler_params=params(collective_id, 60 if layer == 0 else 48),
    )(length, dh, a, x, gains, head_gains, trig, q_raw, k_raw, window, lse, pack, xn, o, *deps)


def after(value, *others):
    return pl.pallas_call(
        lambda *refs: None,
        out_shape=jax.ShapeDtypeStruct(value.shape, value.dtype),
        in_specs=[any_spec()] * (1 + len(others)),
        out_specs=any_spec(),
        input_output_aliases={0: 0},
    )(value, *others)


def scatter(member):
    return lax.psum_scatter(member, "wide", scatter_dimension=0, tiled=True)


def on_device(
    inputs, cotangent, lengths, norm_gains, head_gains, w_q, w_kv, w_o, w_gate_up, w_down
):
    core = lax.axis_index("section")
    narrow = lax.axis_index("narrow")
    n_narrow = lax.axis_size("narrow")
    is_zero = core == 0
    rows, model = inputs.shape[1], inputs.shape[2]
    block = w_q.shape[1]
    head_width = w_q.shape[2]
    n_wide = lax.axis_size("wide")
    hidden = w_down.shape[1]
    kv_part = w_kv.shape[2] // n_narrow

    def swap(value):
        return lax.ppermute(value, "section", [(0, 1), (1, 0)])

    def by_core(first, second):
        return jnp.where(is_zero, first, second)

    half = block // 2

    pad = -hidden % TILE
    kv_own = lax.dynamic_slice_in_dim(w_kv[0], narrow * kv_part, kv_part, 1)
    pack_width = 2 * head_width + kv_part
    pack = [w_q[0], w_o[0].T, kv_own]
    pack = jnp.concatenate(pack, axis=1)
    if block % 16 == 0:
        gain_rows = jnp.zeros((GAIN_ROWS, pack_width), BF16)
        gain_rows = lax.dynamic_update_slice(gain_rows, norm_gains[0], (0, 0))
        gain_rows = lax.dynamic_update_slice(gain_rows, head_gains[0], (4, 0))
        pack = jnp.concatenate([pack, gain_rows], axis=0)
    late = after(core.reshape(1), pack)[0]
    pack = lax.all_gather(pack, "wide", axis=0, tiled=True)

    def half_of(side):
        gate_up = lax.dynamic_slice_in_dim(w_gate_up[0], side * half, half, 0)
        gate_up = jnp.pad(gate_up, ((0, 0), (0, 0), (0, pad))).reshape(half, -1)
        down = lax.dynamic_slice_in_dim(w_down[0].T, side * half, half, 0)
        return jnp.concatenate([gate_up, jnp.pad(down, ((0, 0), (0, pad)))], axis=1)

    keep, came = half_of(late), swap(half_of(1 - late))
    feed = by_core(keep, came), by_core(came, keep)
    padded = hidden + pad

    def gather(member):
        return lax.all_gather(member, ("wide", "section"), axis=0, tiled=True)

    both = gather(feed[0])
    feeds = [
        (both, both, padded),
        (gather(feed[1][:, : 2 * padded]), gather(feed[1][:, 2 * padded :]), padded),
    ]
    packs, gain_packs = gather_pack(pack, model, n_wide, 6)
    if block % 16:
        norm_own = lax.all_gather(norm_gains[0], "wide", axis=1, tiled=True)
        head_own = lax.all_gather(head_gains[0], "wide", axis=1, tiled=True)
        norm_came, head_came = swap(norm_own), swap(head_own)

    def gains_of(section):
        if block % 16:
            mine = core == section
            norm_part = jnp.where(mine, norm_own, norm_came)
            head_part = jnp.where(mine, head_own, head_came)
        else:
            tail = gain_packs[section]
            norm_part = tail[:, :4, :block].transpose(1, 0, 2).reshape(4, model)
            head_part = tail[:, 4:6, : head_width // n_wide].transpose(1, 0, 2).reshape(2, head_width)
        return norm_part.astype(F32), head_part.astype(F32)

    start = narrow * rows
    positions = start + jnp.arange(rows, dtype=jnp.int32)
    trig = tables(positions, head_width)
    length = lax.dynamic_index_in_dim(lengths[:, 0], core, 0, keepdims=False)

    x = lax.dynamic_index_in_dim(inputs, core, 0, keepdims=False)
    length_one = length.reshape(1)
    outs, kept, gains = [], [], []
    for section in range(2):
        layer_gains, head_gain = gains_of(section)
        gains.append((layer_gains, head_gain))
        h, xn, q_raw, k_raw, window, lse, o, a, *shared = attend(
            length_one, x, layer_gains, head_gain, trig, packs, head_width, section, 8 + section
        )
        w_up, w_down, _ = feeds[section]
        mid_rows, gu, act = feed_up(h, layer_gains[2:3], w_up, padded, (), 10 + section)
        kept.append(((a, x, q_raw, k_raw, window, lse), (h, mid_rows, gu, act), shared))
        if section == 0:
            x, f = feed_down(h, layer_gains[3:4], act, w_down, 12)
            outs.append(x)

    def by_section(first, second):
        stays, came = by_core(first, second), swap(by_core(second, first))
        return jnp.stack([by_core(stays, came), by_core(came, stays)])

    real = (positions < length).astype(F32)[:, None]
    dy = lax.dynamic_index_in_dim(cotangent, core, 0, keepdims=False).astype(F32) * real
    dxs, gain_grads = [None, None], [None, None]
    up_sums, down_sums, attention_sums = [None, None], [None, None], [None, None]
    extra = None
    for section in (1, 0):
        kept_a, (h, mid_rows, gu, act), (xn, o) = kept[section]
        layer_gains, head_gain = gains[section]
        w_up, w_down, _ = feeds[section]
        if section:
            out, dgu, d_down, dg3 = feed_turn(h, layer_gains[3:4], dy, act, w_down, gu, 13)
            outs.append(out)
        else:
            dgu, d_down, dg3 = feed_back_up(
                dy, f, layer_gains[3:4], gu, act, w_down,
                (extra, down_sums[1]) if block % 16 else (down_sums[1],), 14,
            )
        down_sums[section] = scatter(d_down)
        dh, d_up, dg2 = feed_back_down(dy, h, layer_gains[2:3], dgu, mid_rows, w_up, 16 + section)
        if section or block % 16:
            up_sums[section] = scatter(d_up)
        a, x, q_raw, k_raw, window, lse = kept_a
        if section == 0:
            zeros = jnp.zeros((2, model), F32)
            gain_grads[0] = jnp.concatenate([zeros, dg2, dg3, zeros, zeros])
            section_out = by_section(*outs)
            lined = after(d_up, up_sums[1], section_out)
            deps = (jnp.concatenate(gain_grads), dxs[1], lined, extra)
        dx, extra, dg01, dhead, *more = attend_back(
            length_one, dh, a, x, layer_gains, head_gain, trig, q_raw, k_raw, window, lse, packs, xn, o,
            () if section else deps, section, 18 + section,
        )
        dxs[section] = dx
        if section:
            head_row = jnp.pad(dhead.reshape(1, -1), ((0, 0), (0, model - dhead.size)))
            gain_grads[1] = jnp.concatenate([dg01, dg2, dg3, head_row, jnp.zeros((3, model), F32)])
        else:
            gain_sums, input_grad, up_lined, came_up, grad_q, grad_kv, grad_o = more
            if block % 16 == 0:
                up_sums[0] = up_lined
            else:
                came_up = swap(up_sums[0])
        dy = dx
    def own_section(first, second):
        came = swap(by_core(second, first))
        stays = by_core(first, second)
        return by_core(stays, came).astype(F32), by_core(came, stays).astype(F32)

    if block % 16:
        split = down_sums[1].shape[1]
        attention_sums = (scatter(extra), down_sums[0][:, split:])
        down_sums[0] = down_sums[0][:, :split]
        grad_q, grad_kv, grad_o = finish_attention(
            *attention_sums, swap(attention_sums[1]), up_sums[0], head_width, 2
        )
    grad_o = grad_o.T
    grad_gate_up, _ = pair_up(*up_sums, came_up, swap(up_sums[1]), hidden)
    down_sums[0] = after(down_sums[0], gain_sums)
    grad_down = jnp.concatenate(own_section(*down_sums), axis=1)[:, :hidden].T
    gain_sums = lax.dynamic_slice_in_dim(gain_sums, core * 8, 8, 0)
    wide = lax.axis_index("wide")
    grad_norm = lax.dynamic_slice_in_dim(gain_sums[:4], wide * block, block, 1)
    grad_head = gain_sums[4, : 2 * head_width].reshape(2, head_width)
    head_block = head_width // n_wide
    grad_head = lax.dynamic_slice_in_dim(grad_head, wide * head_block, head_block, 1)

    return (
        section_out[None],
        input_grad[None],
        grad_norm[None],
        grad_head[None],
        grad_q[None],
        grad_kv[None],
        grad_o[None],
        grad_gate_up[None],
        grad_down[None],
    )


def solution(mesh):
    return jax.shard_map(
        on_device,
        mesh=mesh,
        in_specs=(
            P(None, ("wide", "narrow"), None),
            P(None, ("wide", "narrow"), None),
            P(None, "wide"),
            P("section", None, "wide"),
            P("section", None, "wide"),
            P("section", "wide", "narrow"),
            P("section", "wide", None),
            P("section", "narrow", "wide"),
            P("section", "wide", None, "narrow"),
            P("section", "narrow", "wide"),
        ),
        out_specs=(
            P("section", None, ("wide", "narrow"), None),
            P("section", None, ("wide", "narrow"), None),
            P("section", None, "wide"),
            P("section", None, "wide"),
            P("section", "wide", "narrow"),
            P("section", "wide", None),
            P("section", "narrow", "wide"),
            P("section", "wide", None, "narrow"),
            P("section", "narrow", "wide"),
        ),
        check_vma=False,
    )
```

```python
import functools

import jax
import jax.numpy as jnp
from jax import lax
from jax.experimental import pallas as pl
from jax.experimental.pallas import tpu as pltpu
from jax.sharding import PartitionSpec as P

WINDOW = 512
EPSILON = 1e-06
NEGATIVE = -1e30
ROPE_BASE = 10000.0
MESH = pl.DeviceIdType.MESH
MIB = 2**20
GAIN_ROWS = 16
F32 = jnp.float32
BF16 = jnp.bfloat16


def dot(a, b, dims):
    return lax.dot_general(a, b, ((dims[0], dims[1]), ((), ())), preferred_element_type=F32)


def nn(a, b):
    return dot(a, b, ((1,), (0,)))


def nt(a, b):
    return dot(a, b, ((1,), (1,)))


def tn(a, b):
    return dot(a, b, ((0,), (0,)))


def normed(operand, gain_vec):
    return (
        operand
        * lax.rsqrt(jnp.mean(operand * operand, axis=-1, keepdims=True) + EPSILON)
        * gain_vec
    )


def geglu(gate, up):
    return jax.nn.gelu(gate, approximate=True) * up


def neighbours():
    me = lax.axis_index("narrow")
    return me, jnp.bitwise_xor(me, 1), jnp.bitwise_xor(me, 2)


def meet(nx, ny):
    barrier = pltpu.get_barrier_semaphore()
    for other in (nx, ny):
        pl.semaphore_signal(barrier, inc=1, device_id={"narrow": other}, device_id_type=MESH)
    pl.semaphore_wait(barrier, 2)


def remote(src, dst, send_sem, recv_sem, other):
    return pltpu.make_async_remote_copy(
        src_ref=src,
        dst_ref=dst,
        send_sem=send_sem,
        recv_sem=recv_sem,
        device_id={"narrow": other},
        device_id_type=MESH,
    )


def tables(positions, head_width):
    half_width = head_width // 2
    frequency = ROPE_BASE ** (-jnp.arange(half_width, dtype=F32) * (2.0 / head_width))
    angles = positions.astype(F32)[:, None] * frequency[None, :]
    return jnp.concatenate([jnp.cos(angles), jnp.sin(angles)], axis=1)


def rotate(operand, cosine, sine_table):
    half_width = operand.shape[-1] // 2
    front_half = operand[..., :half_width]
    back_half = operand[..., half_width:]
    return jnp.concatenate(
        [
            front_half * cosine - back_half * sine_table,
            back_half * cosine + front_half * sine_table,
        ],
        axis=-1,
    )


GELU_SCALE = 0.7978845608028654
GELU_CUBE = 0.044715


def vmem_spec():
    return pl.BlockSpec(memory_space=pltpu.VMEM)


def any_spec():
    return pl.BlockSpec(memory_space=pl.ANY)


def rows_of(block, count):
    return pl.ds(pl.multiple_of(block * count, count), count)


def columns_of(tile, width, offset=0):
    if isinstance(tile, int):
        return pl.ds(tile * width + offset, width)
    return pl.ds(pl.multiple_of(tile * width + offset, 128), width)


def inverse_rms(value):
    return lax.rsqrt(jnp.mean(value * value, axis=-1, keepdims=True) + EPSILON)


def normed_gradient(value, gain, grad):
    inverse = inverse_rms(value)
    unit = value * inverse
    scaled = grad * gain
    by_value = inverse * (scaled - unit * jnp.mean(scaled * unit, axis=-1, keepdims=True))
    return by_value, jnp.sum(grad * unit, axis=0, keepdims=True)


def halves_of(ref, count, base=0):
    half = count // 2

    def part(block, which):
        return ref.at[pl.ds(pl.multiple_of(base + block * count + which * half, half), half)]

    return part


class Spread:
    def __init__(self, part, send, recv):
        self.me, self.nx, self.ny = neighbours()
        self.far = jnp.bitwise_xor(self.me, 3)

        def copy(block, which, at, other):
            ref = part(block, which)
            return remote(ref, ref, send.at[at], recv.at[at], other)

        self.to_x1 = copy(self.me, 0, 0, self.nx)
        self.to_y2 = copy(self.me, 1, 1, self.ny)
        self.to_x2 = copy(self.me, 1, 2, self.nx)
        self.to_y1 = copy(self.me, 0, 3, self.ny)
        self.on_y = copy(self.nx, 0, 4, self.ny)
        self.on_x = copy(self.ny, 1, 5, self.nx)

    def start(self):
        for copy in (self.to_x1, self.to_y2, self.to_x2, self.to_y1):
            copy.start()

    def pass_on(self):
        self.to_x1.wait_recv()
        self.on_y.start()
        self.to_y2.wait_recv()
        self.on_x.start()

    def x_here(self):
        self.to_x2.wait_recv()

    def y_here(self):
        self.to_y1.wait_recv()

    def far_here(self):
        self.on_y.wait_recv()
        self.on_x.wait_recv()

    def all_here(self):
        self.x_here()
        self.y_here()
        self.far_here()

    def finish(self):
        for copy in (self.to_x1, self.to_y2, self.to_x2, self.to_y1, self.on_y, self.on_x):
            copy.wait_send()


class Fold:
    def __init__(self, part, land, passing, send, recv):
        self.me, self.nx, self.ny = neighbours()
        self.far = jnp.bitwise_xor(self.me, 3)
        self.part, self.land, self.passing = part, land, passing

        def copy(src, at, other):
            return remote(src, land.at[at], send.at[at], recv.at[at], other)

        self.far_x = copy(part(self.far, 0), 0, self.nx)
        self.far_y = copy(part(self.far, 1), 1, self.ny)
        self.near_x = copy(part(self.nx, 0), 2, self.nx)
        self.near_y = copy(part(self.ny, 1), 3, self.ny)
        self.on_y = copy(passing.at[0], 4, self.ny)
        self.on_x = copy(passing.at[1], 5, self.nx)

    def send_far(self):
        self.far_x.start()
        self.far_y.start()

    def send_near(self):
        self.near_x.start()
        self.near_y.start()

    def pass_on(self):
        self.far_x.wait_recv()
        self.passing[0] = (self.part(self.ny, 0)[...].astype(F32) + self.land[0].astype(F32)).astype(BF16)
        self.on_y.start()
        self.far_y.wait_recv()
        self.passing[1] = (self.part(self.nx, 1)[...].astype(F32) + self.land[1].astype(F32)).astype(BF16)
        self.on_x.start()

    def total(self, own):
        half = own.shape[0] // 2
        for copy in (self.near_x, self.near_y, self.on_y, self.on_x):
            copy.wait_recv()
        first = own[:half] + (self.land[2].astype(F32) + self.land[4].astype(F32))
        second = own[half:] + (self.land[3].astype(F32) + self.land[5].astype(F32))
        return jnp.concatenate([first, second], axis=0)

    def finish(self):
        for copy in (self.far_x, self.far_y, self.near_x, self.near_y, self.on_y, self.on_x):
            copy.wait_send()


class LineFold:
    def __init__(self, own, land, out, columns, send, recv):
        self.own, self.land, self.out, self.columns = own, land, out, columns
        self.send, self.recv = send, recv
        self.wides = own.shape[0]
        self.wide = lax.axis_index("wide")

    def place(self, way):
        return self.wide if way == 0 else self.wides - 1 - self.wide

    def copy(self, way, step):
        return pltpu.make_async_remote_copy(
            src_ref=self.out.at[self.slot(way, step), :, self.columns],
            dst_ref=self.land.at[way, step, :, self.columns],
            send_sem=self.send.at[way, step],
            recv_sem=self.recv.at[way, step],
            device_id={"wide": self.wide + 1 if way == 0 else self.wide - 1},
            device_id_type=MESH,
        )

    def slot(self, way, step):
        return jnp.clip(step - self.wide, 0, self.wides - 2) if way == 0 else step

    def sends(self, way, step):
        place = self.place(way)
        return (place <= step) & (place < self.wides - 1)

    def gets(self, way, step):
        place = self.place(way)
        return (place >= 1) & (place - 1 <= step)

    def step(self, step):
        for way in (0, 1):
            ahead = self.wides - 1 - step
            block = self.wide + ahead if way == 0 else self.wide - ahead
            block = jnp.clip(block, 0, self.wides - 1)
            begins = self.place(way) == 0

            @pl.when(self.sends(way, step) & begins)
            def _():
                self.out[self.slot(way, step), :, self.columns] = self.own[block, :, self.columns]
                self.copy(way, step).start()

            if step:

                @pl.when(self.sends(way, step) & jnp.logical_not(begins))
                def _():
                    self.copy(way, step - 1).wait_recv()
                    total = self.own[block, :, self.columns].astype(F32)
                    total = total + self.land[way, step - 1, :, self.columns].astype(F32)
                    self.out[self.slot(way, step), :, self.columns] = total.astype(BF16)
                    self.copy(way, step).start()

    def finish(self, result):
        last = self.wides - 2
        result[:, self.columns] = self.own[self.wide, :, self.columns]
        for way in (0, 1):

            @pl.when(self.gets(way, last))
            def _():
                self.copy(way, last).wait_recv()
                total = result[:, self.columns].astype(F32)
                total = total + self.land[way, last, :, self.columns].astype(F32)
                result[:, self.columns] = total.astype(BF16)

    def close(self):
        for step in range(self.wides - 1):
            for way in (0, 1):
                pl.when(self.sends(way, step))(self.copy(way, step).wait_send)


def line_spec(wides, block, columns, pieces):
    hops = pltpu.SemaphoreType.DMA((pieces, 2, wides - 1))
    return [
        pltpu.VMEM((wides, block, columns), BF16),
        pltpu.VMEM((2, wides - 1, block, columns), BF16),
        pltpu.VMEM((wides - 1, block, columns), BF16),
        pltpu.VMEM((block, columns), BF16),
        pltpu.SemaphoreType.DMA((wides + 1,)),
        hops,
        hops,
    ]


class LineSum:
    def __init__(self, src, dst, own, land, out, result, loads, send, recv):
        self.src, self.dst, self.own, self.result, self.loads = src, dst, own, result, loads
        pieces = send.shape[0]
        columns = own.shape[2]
        width = -(-columns // (128 * pieces)) * 128
        self.folds = [
            LineFold(own, land, out, pl.ds(first, min(width, columns - first)), send.at[p], recv.at[p])
            for p, first in enumerate(range(0, columns, width))
        ]
        self.steps = own.shape[0] - 1

    def load(self):
        wides, rows, columns = self.own.shape
        for w in range(wides):
            part = self.src.at[pl.ds(w * rows, rows), pl.ds(0, columns)]
            pltpu.make_async_copy(part, self.own.at[w], self.loads.at[w]).start()

    def begin(self):
        wides, rows, columns = self.own.shape
        for w in range(wides):
            part = self.src.at[pl.ds(w * rows, rows), pl.ds(0, columns)]
            pltpu.make_async_copy(part, self.own.at[w], self.loads.at[w]).wait()
        for fold in self.folds:
            fold.step(0)

    def step(self, step, piece):
        self.folds[piece].step(step)

    def end(self):
        for fold in self.folds:
            fold.finish(self.result)
        if self.dst is not None:
            copy = pltpu.make_async_copy(self.result, self.dst, self.loads.at[self.own.shape[0]])
            copy.start()
        for fold in self.folds:
            fold.close()
        if self.dst is not None:
            copy.wait()


class Deal:
    def __init__(self, src, place, send, recv):
        me, nx, ny = neighbours()
        far = jnp.bitwise_xor(me, 3)
        self.copies = [
            remote(src(other), place(me), send.at[at], recv.at[at], other)
            for at, other in enumerate((far, nx, ny))
        ]

    def start(self):
        for copy in self.copies:
            copy.start()

    def here(self):
        for copy in self.copies:
            copy.wait_recv()

    def finish(self):
        for copy in self.copies:
            copy.wait_send()


def greet(*others):
    barrier = pltpu.get_barrier_semaphore()
    for other in others:
        pl.semaphore_signal(barrier, inc=1, device_id=other, device_id_type=MESH)
    return lambda: pl.semaphore_wait(barrier, len(others))


def spread_spec():
    return [pltpu.SemaphoreType.DMA((6,)), pltpu.SemaphoreType.DMA((6,))]


def fold_spec(count, width):
    return [
        pltpu.VMEM((6, count // 2, width), BF16),
        pltpu.VMEM((2, count // 2, width), BF16),
        pltpu.SemaphoreType.DMA((6,)),
        pltpu.SemaphoreType.DMA((6,)),
    ]


def params(collective_id, mib):
    return pltpu.CompilerParams(
        collective_id=collective_id, has_side_effects=True, vmem_limit_bytes=mib * MIB
    )


TILE = 256


def up_kernel(h_ref, gain_ref, w_ref, *refs):
    sharing = len(refs) > 11
    if sharing:
        xn_ref, o_ref, rows_out, gu_out, act_out, xn_out, o_out, *refs = refs
        rows, w, gu, act, load, store, send, recv, *share_refs = refs
        share = Share(xn_ref, o_ref, *share_refs)
    else:
        rows_out, gu_out, act_out, rows, w, gu, act, load, store, send, recv = refs
    count = h_ref.shape[0]
    hidden = act.shape[1]
    weights = pltpu.make_async_copy(w_ref.at[:, pl.ds(0, 2 * hidden)], w, load)
    weights.start()
    me, nx, ny = neighbours()
    met = greet({"narrow": nx}, {"narrow": ny}, {"narrow": jnp.bitwise_xor(me, 3)})
    value = h_ref[...]
    rows[rows_of(me, count), :] = (value * inverse_rms(value) * gain_ref[...]).astype(BF16)
    spread = Spread(halves_of(rows, count), send, recv)
    met()
    spread.start()
    weights.wait()

    def one(block, at):
        here = rows_of(block, count)

        def tile(j):
            left = rows[here, :]
            gate = nn(left, w[:, columns_of(j, TILE)])
            up = nn(left, w[:, columns_of(j, TILE, hidden)])
            inner = jnp.tanh(GELU_SCALE * (gate + GELU_CUBE * (gate * gate * gate)))
            gu[here, columns_of(j, TILE)] = gate.astype(BF16)
            gu[here, columns_of(j, TILE, hidden)] = up.astype(BF16)
            act[here, columns_of(j, TILE)] = (0.5 * gate * (1.0 + inner) * up).astype(BF16)

        for j in range(hidden // TILE):
            tile(j)
        copies = [
            pltpu.make_async_copy(ref.at[here], out.at[here], store.at[k, at])
            for k, (ref, out) in enumerate(((gu, gu_out), (act, act_out), (rows, rows_out)))
        ]
        for copy in copies:
            copy.start()
        return copies

    copies = one(me, 0)
    spread.pass_on()
    if sharing:
        share.start_rows()
        share.start_deal()
    spread.x_here()
    copies += one(nx, 1)
    spread.y_here()
    copies += one(ny, 2)
    spread.far_here()
    if sharing:
        share.spread.pass_on()
    copies += one(spread.far, 3)
    spread.finish()
    if sharing:
        share.all_here()
        share.finish()
        xn, o, loads = share_refs[:3]
        copies += [pltpu.make_async_copy(xn, xn_out, loads.at[2]), pltpu.make_async_copy(o, o_out, loads.at[3])]
        for copy in copies[-2:]:
            copy.start()
    for copy in copies:
        copy.wait()


def feed_up(h, gain, w_gu, hidden, shared, collective_id):
    count, model = h.shape
    total = 4 * count
    shapes = [(total, model), (total, 2 * hidden), (total, hidden)]
    shapes = [jax.ShapeDtypeStruct(shape, BF16) for shape in shapes]
    if shared:
        shapes += share_shapes(*shared)
    return pl.pallas_call(
        up_kernel,
        out_shape=shapes,
        in_specs=[vmem_spec(), vmem_spec(), any_spec()] + [vmem_spec()] * len(shared),
        out_specs=[any_spec()] * len(shapes),
        scratch_shapes=[
            pltpu.VMEM((total, model), BF16),
            pltpu.VMEM((model, 2 * hidden), BF16),
            pltpu.VMEM((total, 2 * hidden), BF16),
            pltpu.VMEM((total, hidden), BF16),
            pltpu.SemaphoreType.DMA,
            pltpu.SemaphoreType.DMA((3, 4)),
            *spread_spec(),
            *(share_spec(count, model, shared[1].shape[1] // 4) if shared else []),
        ],
        compiler_params=params(collective_id, 60),
    )(h, gain, w_gu, *shared)


def down_kernel(
    h_ref, gain_ref, act_ref, w_ref, x_out, f_out, act, w, parts, load, land, passing, send, recv
):
    count, model = h_ref.shape
    me, nx, ny = neighbours()
    met = greet({"narrow": nx}, {"narrow": ny})
    far = jnp.bitwise_xor(me, 3)
    first = w_ref.shape[1] - w.shape[1]
    weights = pltpu.make_async_copy(w_ref.at[:, pl.ds(first, w.shape[1])], w, load.at[0])
    weights.start()
    arrivals = []
    for at, block in enumerate((far, nx, ny, me)):
        here = rows_of(block, count)
        arrivals.append(pltpu.make_async_copy(act_ref.at[here], act.at[here], load.at[1 + at]))
        arrivals[-1].start()
    fold = Fold(halves_of(parts, count), land, passing, send, recv)
    weights.wait()
    met()

    def one(block, at):
        arrivals[at].wait()
        return nt(act[rows_of(block, count), :], w[...])

    parts[rows_of(far, count), :] = one(far, 0).astype(BF16)
    fold.send_far()
    parts[rows_of(nx, count), :] = one(nx, 1).astype(BF16)
    parts[rows_of(ny, count), :] = one(ny, 2).astype(BF16)
    fold.send_near()
    f_out[...] = one(me, 3)
    fold.pass_on()
    total = fold.total(f_out[...])
    f_out[...] = total
    x_out[...] = (h_ref[...] + total * inverse_rms(total) * gain_ref[...]).astype(BF16)
    fold.finish()


def feed_down(h, gain, act, w_dt, collective_id):
    count, model = h.shape
    return pl.pallas_call(
        down_kernel,
        out_shape=[
            jax.ShapeDtypeStruct((count, model), BF16),
            jax.ShapeDtypeStruct((count, model), F32),
        ],
        in_specs=[vmem_spec(), vmem_spec(), any_spec(), any_spec()],
        out_specs=[vmem_spec(), vmem_spec()],
        scratch_shapes=[
            pltpu.VMEM(act.shape, BF16),
            pltpu.VMEM((model, act.shape[1]), BF16),
            pltpu.VMEM((4 * count, model), BF16),
            pltpu.SemaphoreType.DMA((5,)),
            *fold_spec(count, model),
        ],
        compiler_params=params(collective_id, 60),
    )(h, gain, act, w_dt)


def swap_sum(make, tiles, ours, theirs, came, send, recv, out, out_sems, between=None):
    other = {"section": 1 - lax.axis_index("section")}
    sends = []
    for at, (first, width) in enumerate(tiles):
        columns = pl.ds(first, width)
        theirs[:, columns] = make(False, first, width).astype(BF16)
        copy = pltpu.make_async_remote_copy(
            src_ref=theirs.at[:, columns],
            dst_ref=came.at[:, columns],
            send_sem=send.at[at],
            recv_sem=recv.at[at],
            device_id=other,
            device_id_type=MESH,
        )
        copy.start()
        sends.append(copy)
    if between is not None:
        between()
    stores = []
    for at, (first, width) in enumerate(tiles):
        columns = pl.ds(first, width)
        own = make(True, first, width)
        sends[at].wait_recv()
        ours[:, columns] = (own + came[:, columns].astype(F32)).astype(BF16)
        copy = pltpu.make_async_copy(ours.at[:, columns], out.at[:, columns], out_sems.at[at])
        copy.start()
        stores.append(copy)
    return sends, stores


def column_tiles(width):
    return [(first, min(2 * TILE, width - first)) for first in range(0, width, 2 * TILE)]


def gate_up_gradient(df, here, w, gu, hidden):
    for j in range(hidden // TILE):
        dact = nn(df[here, :], w[:, columns_of(j, TILE)])
        gate = gu[here, columns_of(j, TILE)].astype(F32)
        up = gu[here, columns_of(j, TILE, hidden)].astype(F32)
        square = gate * gate
        inner = jnp.tanh(GELU_SCALE * gate * (1.0 + GELU_CUBE * square))
        half = 0.5 * (1.0 + inner)
        slope = half + 0.5 * GELU_SCALE * gate * (1.0 - inner * inner) * (
            1.0 + 3.0 * GELU_CUBE * square
        )
        gu[here, columns_of(j, TILE)] = (dact * up * slope).astype(BF16)
        gu[here, columns_of(j, TILE, hidden)] = (dact * gate * half).astype(BF16)


def back_up_kernel(dy_ref, f_ref, gain_ref, gu_ref, act_ref, w_ref, *refs):
    if len(refs) == 18:
        refs = refs[1:]
    if len(refs) == 19:
        extra_ref, _, *refs = refs
    else:
        extra_ref = None
    (
        dgu_out, dw_out, dgain_out, df, gu, act, w, ours, theirs, came,
        load, store, send, recv, swap_send, swap_recv, out_sems,
    ) = refs
    if extra_ref is not None:
        first = ours.shape[1]
        extra = pltpu.make_async_copy(
            extra_ref, dw_out.at[:, pl.ds(first, extra_ref.shape[1])], load.at[0, 1]
        )
        extra.start()
    count, model = dy_ref.shape
    hidden = act.shape[1]
    me, nx, ny = neighbours()
    core = lax.axis_index("section")
    met = greet({"narrow": nx}, {"narrow": ny}, {"section": 1 - core})
    far = jnp.bitwise_xor(me, 3)
    start = w_ref.shape[1] - hidden
    weights = pltpu.make_async_copy(w_ref.at[:, pl.ds(start, hidden)], w, load.at[0, 0])
    weights.start()
    arrivals = []
    for at, block in enumerate((me, nx, ny, far)):
        here = rows_of(block, count)
        pair = [
            pltpu.make_async_copy(gu_ref.at[here], gu.at[here], load.at[1, at]),
            pltpu.make_async_copy(act_ref.at[here], act.at[here], load.at[2, at]),
        ]
        for copy in pair:
            copy.start()
        arrivals.append(pair)
    dy = dy_ref[...].astype(BF16).astype(F32)
    by_value, by_gain = normed_gradient(f_ref[...], gain_ref[...], dy)
    df[rows_of(me, count), :] = by_value.astype(BF16)
    spread = Spread(halves_of(df, count), send, recv)
    met()
    spread.start()
    dgain_out[...] = by_gain
    weights.wait()

    def one(block, at):
        here = rows_of(block, count)
        for copy in arrivals[at]:
            copy.wait()

        gate_up_gradient(df, here, w, gu, hidden)
        copy = pltpu.make_async_copy(gu.at[here], dgu_out.at[here], store.at[at])
        copy.start()
        return copy

    copies = [one(me, 0)]
    spread.pass_on()
    spread.x_here()
    copies.append(one(nx, 1))
    spread.y_here()
    copies.append(one(ny, 2))
    spread.far_here()
    copies.append(one(far, 3))

    def make(mine, first, width):
        side = core if mine else 1 - core
        start = pl.multiple_of(side * (hidden // 2) + first, 128)
        return tn(df[...], act[:, pl.ds(start, width)])

    sends, stores = swap_sum(
        make, column_tiles(hidden // 2), ours, theirs, came, swap_send, swap_recv, dw_out, out_sems
    )
    spread.finish()
    for copy in sends:
        copy.wait_send()
    for copy in copies + stores:
        copy.wait()
    if extra_ref is not None:
        extra.wait()


def turn_kernel(
    h_ref, gain_ref, dy_ref, act_ref, w_ref, gu_ref, x_out, dgu_out, dw_out, dgain_out,
    act, w, parts, df, gu, ours, theirs, came, load, store, land, passing, fold_send, fold_recv, send, recv,
    swap_send, swap_recv, out_sems,
):
    count, model = h_ref.shape
    hidden = act.shape[1]
    me, nx, ny = neighbours()
    core = lax.axis_index("section")
    far = jnp.bitwise_xor(me, 3)
    met = greet({"narrow": nx}, {"narrow": ny}, {"section": 1 - core})
    first = w_ref.shape[1] - hidden
    weights = pltpu.make_async_copy(w_ref.at[:, pl.ds(first, hidden)], w, load.at[0, 0])
    weights.start()
    blocks = (far, nx, ny, me)
    for at, block in enumerate(blocks):
        here = rows_of(block, count)
        pltpu.make_async_copy(act_ref.at[here], act.at[here], load.at[1, at]).start()
    for at, block in enumerate(blocks):
        here = rows_of(block, count)
        pltpu.make_async_copy(gu_ref.at[here], gu.at[here], load.at[2, at]).start()

    def here_now(row, at):
        here = rows_of(blocks[at], count)
        src, dst = ((act_ref, act), (gu_ref, gu))[row - 1]
        pltpu.make_async_copy(src.at[here], dst.at[here], load.at[row, at]).wait()
        return here

    fold = Fold(halves_of(parts, count), land, passing, fold_send, fold_recv)
    weights.wait()
    met()

    def part(at):
        here = here_now(1, at)
        return here, nt(act[here, :], w[...])

    here, value = part(0)
    parts[here, :] = value.astype(BF16)
    fold.send_far()
    for at in (1, 2):
        here, value = part(at)
        parts[here, :] = value.astype(BF16)
    fold.send_near()
    _, value = part(3)
    fold.pass_on()
    f = fold.total(value)
    gain = gain_ref[...]
    by_value, by_gain = normed_gradient(f, gain, dy_ref[...])
    df[rows_of(me, count), :] = by_value.astype(BF16)
    spread = Spread(halves_of(df, count), send, recv)
    spread.start()
    dgain_out[...] = by_gain
    x_out[...] = (h_ref[...] + f * inverse_rms(f) * gain).astype(BF16)

    def one(at):
        here = here_now(2, at)
        gate_up_gradient(df, here, w, gu, hidden)
        copy = pltpu.make_async_copy(gu.at[here], dgu_out.at[here], store.at[at])
        copy.start()
        return copy

    copies = [one(3)]
    spread.pass_on()
    spread.x_here()
    copies.append(one(1))
    spread.y_here()
    copies.append(one(2))
    spread.far_here()
    copies.append(one(0))

    def make(mine, first, width):
        side = core if mine else 1 - core
        start = pl.multiple_of(side * (hidden // 2) + first, 128)
        return tn(df[...], act[:, pl.ds(start, width)])

    sends, stores = swap_sum(
        make, column_tiles(hidden // 2), ours, theirs, came, swap_send, swap_recv, dw_out, out_sems
    )
    spread.finish()
    fold.finish()
    for copy in sends:
        copy.wait_send()
    for copy in copies + stores:
        copy.wait()


def feed_turn(h, gain, dy, act, w_dt, gu, collective_id):
    count, model = h.shape
    total, hidden = act.shape
    tiles = pltpu.SemaphoreType.DMA((len(column_tiles(hidden // 2)),))
    dw = pltpu.VMEM((model, hidden // 2), BF16)
    return pl.pallas_call(
        turn_kernel,
        out_shape=[
            jax.ShapeDtypeStruct((count, model), BF16),
            jax.ShapeDtypeStruct(gu.shape, BF16),
            jax.ShapeDtypeStruct((model, hidden // 2), BF16),
            jax.ShapeDtypeStruct((1, model), F32),
        ],
        in_specs=[vmem_spec()] * 3 + [any_spec()] * 3,
        out_specs=[vmem_spec(), any_spec(), any_spec(), vmem_spec()],
        scratch_shapes=[
            pltpu.VMEM(act.shape, BF16),
            pltpu.VMEM((model, hidden), BF16),
            pltpu.VMEM((total, model), BF16),
            pltpu.VMEM((total, model), BF16),
            pltpu.VMEM(gu.shape, BF16),
            dw,
            dw,
            dw,
            pltpu.SemaphoreType.DMA((3, 4)),
            pltpu.SemaphoreType.DMA((4,)),
            *fold_spec(count, model),
            *spread_spec(),
            tiles,
            tiles,
            tiles,
        ],
        compiler_params=params(collective_id, 60),
    )(h, gain, dy, act, w_dt, gu)


def feed_back_up(dy, f, gain, gu, act, w_dt, extra, collective_id):
    count, model = dy.shape
    total, hidden = act.shape
    tiles = len(column_tiles(hidden // 2))
    extras = extra
    return pl.pallas_call(
        back_up_kernel,
        out_shape=[
            jax.ShapeDtypeStruct(gu.shape, BF16),
            jax.ShapeDtypeStruct((model, hidden // 2 + sum(e.shape[1] for e in extras[:-1])), BF16),
            jax.ShapeDtypeStruct((1, model), F32),
        ],
        in_specs=[vmem_spec()] * 3 + [any_spec()] * (3 + len(extras)),
        out_specs=[any_spec(), any_spec(), vmem_spec()],
        scratch_shapes=[
            pltpu.VMEM((total, model), BF16),
            pltpu.VMEM(gu.shape, BF16),
            pltpu.VMEM(act.shape, BF16),
            pltpu.VMEM((model, hidden), BF16),
            pltpu.VMEM((model, hidden // 2), BF16),
            pltpu.VMEM((model, hidden // 2), BF16),
            pltpu.VMEM((model, hidden // 2), BF16),
            pltpu.SemaphoreType.DMA((3, 4)),
            pltpu.SemaphoreType.DMA((4,)),
            *spread_spec(),
            pltpu.SemaphoreType.DMA((tiles,)),
            pltpu.SemaphoreType.DMA((tiles,)),
            pltpu.SemaphoreType.DMA((tiles,)),
        ],
        compiler_params=params(collective_id, 60),
    )(dy, f, gain, gu, act, w_dt, *extras)


def back_down_kernel(
    dy_ref, h_ref, gain_ref, dgu_ref, rows_ref, w_ref, dh_out, dw_out, dgain_out,
    dgu, rows, w, parts, ours, theirs, came, load, land, passing, send, recv, swap_send, swap_recv, out_sems,
):
    count, model = dy_ref.shape
    hidden = dgu.shape[1] // 2
    me, nx, ny = neighbours()
    core = lax.axis_index("section")
    far = jnp.bitwise_xor(me, 3)
    met = greet({"narrow": nx}, {"narrow": ny}, {"section": 1 - core})
    weights = pltpu.make_async_copy(w_ref.at[:, pl.ds(0, 2 * hidden)], w, load.at[0])
    weights.start()
    arrivals = []
    for at, block in enumerate((far, nx, ny, me)):
        here = rows_of(block, count)
        arrivals.append(pltpu.make_async_copy(dgu_ref.at[here], dgu.at[here], load.at[1 + at]))
        arrivals[-1].start()
    kept = pltpu.make_async_copy(rows_ref, rows, load.at[5])
    kept.start()
    fold = Fold(halves_of(parts, count), land, passing, send, recv)
    weights.wait()
    met()

    def one(block, at, out, here):
        arrivals[at].wait()
        out[here, :] = nt(dgu[rows_of(block, count), :], w[...]).astype(out.dtype)

    one(far, 0, parts, rows_of(far, count))
    fold.send_far()
    one(nx, 1, parts, rows_of(nx, count))
    one(ny, 2, parts, rows_of(ny, count))
    fold.send_near()
    one(me, 3, dh_out, pl.ds(0, count))
    fold.pass_on()
    kept.wait()

    def make(mine, first, width):
        side = core if mine else 1 - core
        start = pl.multiple_of(side * hidden + first, 128)
        return tn(rows[...], dgu[:, pl.ds(start, width)])

    sends, stores = swap_sum(
        make, column_tiles(hidden), ours, theirs, came, swap_send, swap_recv, dw_out, out_sems
    )
    total = fold.total(dh_out[...])
    by_value, by_gain = normed_gradient(h_ref[...], gain_ref[...], total)
    dh_out[...] = dy_ref[...].astype(BF16).astype(F32) + by_value
    dgain_out[...] = by_gain
    fold.finish()
    for copy in sends:
        copy.wait_send()
    for copy in stores:
        copy.wait()


def feed_back_down(dy, h, gain, dgu, rows, w_gu, collective_id):
    count, model = dy.shape
    total, hidden = dgu.shape[0], dgu.shape[1] // 2
    tiles = len(column_tiles(hidden))
    return pl.pallas_call(
        back_down_kernel,
        out_shape=[
            jax.ShapeDtypeStruct((count, model), F32),
            jax.ShapeDtypeStruct((model, hidden), BF16),
            jax.ShapeDtypeStruct((1, model), F32),
        ],
        in_specs=[vmem_spec()] * 3 + [any_spec()] * 3,
        out_specs=[vmem_spec(), any_spec(), vmem_spec()],
        scratch_shapes=[
            pltpu.VMEM(dgu.shape, BF16),
            pltpu.VMEM(rows.shape, BF16),
            pltpu.VMEM((model, 2 * hidden), BF16),
            pltpu.VMEM((total, model), BF16),
            pltpu.VMEM((model, hidden), BF16),
            pltpu.VMEM((model, hidden), BF16),
            pltpu.VMEM((model, hidden), BF16),
            pltpu.SemaphoreType.DMA((6,)),
            *fold_spec(count, model),
            pltpu.SemaphoreType.DMA((tiles,)),
            pltpu.SemaphoreType.DMA((tiles,)),
            pltpu.SemaphoreType.DMA((tiles,)),
        ],
        compiler_params=params(collective_id, 60),
    )(dy, h, gain, dgu, rows, w_gu)


def pack_kernel(p_ref, o_ref, g_ref, local, send, recv, peer_send, peer_recv):
    model, width = o_ref.shape[2:]
    half = model // 2
    wides, extra = g_ref.shape[1:3]
    rows = model // wides
    core = lax.axis_index("section")
    me, nx, ny = neighbours()
    met = greet({"narrow": nx}, {"narrow": ny}, {"section": 1 - core})
    whole = p_ref.shape[0] == model
    owns = []
    if whole:
        owns.append(pltpu.make_async_copy(p_ref, o_ref.at[core, me], local.at[0, 0]))
    else:
        for w in range(wides):
            first = w * (rows + extra)
            place = o_ref.at[core, me, pl.ds(w * rows, rows)]
            owns.append(pltpu.make_async_copy(p_ref.at[pl.ds(first, rows)], place, local.at[0, w]))
            part = p_ref.at[pl.ds(first + rows, extra)]
            owns.append(pltpu.make_async_copy(part, g_ref.at[core, w], local.at[1, w]))
    start_all(owns)
    spread = Spread(lambda block, which: o_ref.at[core, block, pl.ds(which * half, half)], send, recv)
    wait_all(owns)
    met()
    spread.start()
    copies = []

    def across(ref):
        copy = pltpu.make_async_remote_copy(
            src_ref=ref,
            dst_ref=ref,
            send_sem=peer_send.at[len(copies)],
            recv_sem=peer_recv.at[len(copies)],
            device_id={"section": 1 - core},
            device_id_type=MESH,
        )
        copy.start()
        copies.append(copy)

    if not whole:
        across(g_ref.at[core])
    across(o_ref.at[core, me])
    spread.pass_on()
    spread.x_here()
    across(o_ref.at[core, nx])
    spread.y_here()
    across(o_ref.at[core, ny])
    spread.far_here()
    across(o_ref.at[core, spread.far])
    for copy in copies:
        copy.wait_recv()
    spread.finish()
    for copy in copies:
        copy.wait_send()


def gather_pack(pack, model, wides, collective_id):
    width = pack.shape[1]
    return pl.pallas_call(
        pack_kernel,
        out_shape=[
            jax.ShapeDtypeStruct((2, 4, model, width), pack.dtype),
            jax.ShapeDtypeStruct((2, wides, GAIN_ROWS, width), pack.dtype),
        ],
        in_specs=[any_spec()],
        out_specs=[vmem_spec()] * 2,
        scratch_shapes=[
            pltpu.SemaphoreType.DMA((2, wides)),
            *spread_spec(),
            pltpu.SemaphoreType.DMA((5,)),
            pltpu.SemaphoreType.DMA((5,)),
        ],
        compiler_params=params(collective_id, 32),
    )(pack)


def finish_kernel(
    zero_ref, one_ref, early_ref, dep_ref, q_out, kv_out, o_out, came, kv, send, recv, kv_send, kv_recv
):
    core = lax.axis_index("section")
    me, nx, ny = neighbours()
    others = (nx, ny, jnp.bitwise_xor(me, 3))
    met = greet({"section": 1 - core}, *[{"narrow": other} for other in others])
    head = q_out.shape[1]
    first = core == 0
    by_qkv = jnp.where(first, zero_ref[...], early_ref[...])
    kv[me] = by_qkv[:, head:]
    met()
    across = pltpu.make_async_remote_copy(
        src_ref=zero_ref,
        dst_ref=came,
        send_sem=send,
        recv_sem=recv,
        device_id={"section": 1 - core},
        device_id_type=MESH,
    )
    across.start()
    copies = []
    for at, other in enumerate(others):
        copies.append(remote(kv.at[me], kv.at[me], kv_send.at[at], kv_recv.at[at], other))
        copies[-1].start()
    q_out[...] = by_qkv[:, :head].astype(F32)
    across.wait_recv()
    o_out[...] = jnp.where(first, came[:, :head], one_ref[:, :head]).astype(F32)
    for copy in copies:
        copy.wait_recv()
    width = kv.shape[2]
    for n in range(4):
        kv_out[:, n * width : (n + 1) * width] = kv[n].astype(F32)
    across.wait_send()
    for copy in copies:
        copy.wait_send()


def finish_attention(zero, one, early, dep, head, collective_id):
    block, width = zero.shape
    return pl.pallas_call(
        finish_kernel,
        out_shape=[
            jax.ShapeDtypeStruct((block, head), F32),
            jax.ShapeDtypeStruct((block, 4 * (width - head)), F32),
            jax.ShapeDtypeStruct((block, head), F32),
        ],
        in_specs=[vmem_spec()] * 3 + [any_spec()],
        out_specs=[vmem_spec()] * 3,
        scratch_shapes=[
            pltpu.VMEM((block, width), BF16),
            pltpu.VMEM((4, block, width - head), BF16),
            pltpu.SemaphoreType.DMA,
            pltpu.SemaphoreType.DMA,
            pltpu.SemaphoreType.DMA((3,)),
            pltpu.SemaphoreType.DMA((3,)),
        ],
        compiler_params=params(collective_id, 16),
    )(zero, one, early, dep)


def pair_kernel(zero_ref, one_ref, came_zero_ref, came_one_ref, out_ref, flag_ref):
    hidden = out_ref.shape[2]
    first = lax.axis_index("section") == 0
    keep = jnp.where(first, zero_ref[:, :hidden], one_ref[:, :hidden])
    came = jnp.where(first, came_zero_ref[:, :hidden], came_one_ref[:, :hidden])
    out_ref[:, 0, :] = jnp.where(first, keep, came).astype(F32)
    out_ref[:, 1, :] = jnp.where(first, came, keep).astype(F32)
    flag_ref[...] = jnp.zeros_like(flag_ref)


def pair_up(zero, one, came_zero, came_one, hidden):
    return pl.pallas_call(
        pair_kernel,
        out_shape=[
            jax.ShapeDtypeStruct((zero.shape[0], 2, hidden), F32),
            jax.ShapeDtypeStruct((8, 128), F32),
        ],
        in_specs=[vmem_spec()] * 4,
        out_specs=[vmem_spec()] * 2,
        compiler_params=pltpu.CompilerParams(vmem_limit_bytes=40 * MIB),
    )(zero, one, came_zero, came_one)


class Share:
    def __init__(self, xn_ref, o_ref, xn, o, loads, spread_send, spread_recv, deal_send, deal_recv):
        count, head = xn_ref.shape[0], o.shape[1]
        me = lax.axis_index("narrow")
        self.loads = [
            pltpu.make_async_copy(xn_ref, xn.at[rows_of(me, count)], loads.at[0]),
            pltpu.make_async_copy(o_ref.at[:, columns_of(me, head)], o.at[rows_of(me, count)], loads.at[1]),
        ]
        self.spread = Spread(halves_of(xn, count), spread_send, spread_recv)
        self.deal = Deal(
            lambda other: o_ref.at[:, columns_of(other, head)],
            lambda mine: o.at[rows_of(mine, count)],
            deal_send,
            deal_recv,
        )

    def start_rows(self):
        self.loads[0].start()
        self.loads[0].wait()
        self.spread.start()

    def start_deal(self):
        self.loads[1].start()
        self.deal.start()

    def all_here(self):
        self.spread.all_here()
        self.deal.here()

    def finish(self):
        self.spread.finish()
        self.deal.finish()
        self.loads[1].wait()


def share_spec(count, model, head):
    return [
        pltpu.VMEM((4 * count, model), BF16),
        pltpu.VMEM((4 * count, head), BF16),
        pltpu.SemaphoreType.DMA((4,)),
        *spread_spec(),
        pltpu.SemaphoreType.DMA((3,)),
        pltpu.SemaphoreType.DMA((3,)),
    ]


def share_shapes(xn, o):
    total = 4 * xn.shape[0]
    return [
        jax.ShapeDtypeStruct((total, xn.shape[1]), BF16),
        jax.ShapeDtypeStruct((total, o.shape[1] // 4), BF16),
    ]


def gain_stages():
    wides = lax.axis_size("wide")
    core, wide = lax.axis_index("section"), lax.axis_index("wide")
    me, nx, ny = neighbours()
    return [
        [{"narrow": nx}, {"narrow": ny}, {"narrow": jnp.bitwise_xor(me, 3)}],
        [{"section": 1 - core}],
        [{"wide": lax.rem(wide + step, wides)} for step in range(1, wides)],
    ]


class GainSum:
    def __init__(self, land, total, send, recv):
        self.land, self.total, self.send, self.recv = land, total, send, recv
        self.copies = []
        self.waiting = []

    def start(self, stage):
        for other in gain_stages()[stage]:
            at = len(self.copies)
            copy = pltpu.make_async_remote_copy(
                src_ref=self.total.at[stage],
                dst_ref=self.land.at[at],
                send_sem=self.send.at[at],
                recv_sem=self.recv.at[at],
                device_id=other,
                device_id_type=MESH,
            )
            copy.start()
            self.copies.append(copy)
            self.waiting.append(at)

    def add(self, stage):
        value = self.total[stage]
        for at in self.waiting:
            self.copies[at].wait_recv()
            value = value + self.land[at]
        self.waiting = []
        self.total[stage + 1] = value

    def close(self):
        for copy in self.copies:
            copy.wait_send()


def gain_spec(wides, shape):
    return [
        pltpu.VMEM((wides + 3, *shape), F32),
        pltpu.VMEM((4, *shape), F32),
        pltpu.SemaphoreType.DMA((wides + 3,)),
        pltpu.SemaphoreType.DMA((wides + 3,)),
    ]


def trade_kernel(keep_ref, give_ref, zero_ref, one_ref, came, send, recv):
    core = lax.axis_index("section")
    met = greet({"section": 1 - core})
    met()
    copy = pltpu.make_async_remote_copy(
        src_ref=give_ref,
        dst_ref=came,
        send_sem=send,
        recv_sem=recv,
        device_id={"section": 1 - core},
        device_id_type=MESH,
    )
    copy.start()

    @pl.when(core == 0)
    def _():
        zero_ref[...] = keep_ref[...]

    @pl.when(core == 1)
    def _():
        one_ref[...] = keep_ref[...]

    copy.wait_recv()

    @pl.when(core == 0)
    def _():
        one_ref[...] = came[...]

    @pl.when(core == 1)
    def _():
        zero_ref[...] = came[...]

    copy.wait_send()


def trade(keep, give, collective_id):
    shape = jax.ShapeDtypeStruct(keep.shape, keep.dtype)
    return pl.pallas_call(
        trade_kernel,
        out_shape=[shape, shape],
        in_specs=[vmem_spec()] * 2,
        out_specs=[vmem_spec()] * 2,
        scratch_shapes=[
            pltpu.VMEM(keep.shape, keep.dtype),
            pltpu.SemaphoreType.DMA,
            pltpu.SemaphoreType.DMA,
        ],
        compiler_params=params(collective_id, 16),
    )(keep, give)


def turn_back(grad, cosine, sine_table):
    half = grad.shape[1] // 2
    front, back = grad[:, :half], grad[:, half:]
    return jnp.concatenate(
        [front * cosine + back * sine_table, back * cosine - front * sine_table], axis=1
    )


def pack_loads(pack_ref, layer, head, wq, wot, wkv, sems):
    kv_part = wkv.shape[1] // 4
    loads = []
    for at, (w, first, width) in enumerate(
        ((wq, 0, head), (wot, head, head), (wkv, 2 * head, kv_part))
    ):
        loads.append(
            [
                pltpu.make_async_copy(
                    pack_ref.at[layer, n, :, pl.ds(first, width)], w.at[:, pl.ds(n * width, width)], sems.at[at, n]
                )
                for n in range(4)
            ]
        )
    return loads


def start_all(copies):
    for copy in copies:
        copy.start()


def wait_all(copies):
    for copy in copies:
        copy.wait()


def window_mask(me, count, window, length):
    rows_at = me * count + lax.broadcasted_iota(jnp.int32, (count, 1), 0)
    cols_at = me * count - WINDOW + lax.broadcasted_iota(jnp.int32, (1, window), 1)
    return (
        (cols_at <= rows_at)
        & (rows_at - cols_at < WINDOW)
        & (cols_at >= 0)
        & ((cols_at < length) | (cols_at == rows_at))
    )


def attend_kernel(layer, length_ref, x_ref, gains_ref, head_ref, trig_ref, pack_ref, *refs):
    (
        h_out, xn_out, q_out, k_out, win_out, lse_out, o_out, a_out, *refs
    ) = refs
    sharing = len(refs) > 9
    if sharing:
        xn_all_out, o_all_out, *refs = refs
    kv, wq, wot, wkv, load, send, recv, *share_refs = refs
    count, model = x_ref.shape
    head = k_out.shape[1]
    heads = q_out.shape[1] // head
    me, nx, ny = neighbours()
    met = greet({"narrow": nx}, {"narrow": ny}, {"narrow": jnp.bitwise_xor(me, 3)})
    q_loads, out_loads, kv_loads = pack_loads(pack_ref, layer, head, wq, wot, wkv, load)
    start_all(kv_loads + q_loads + out_loads)
    scaling = head ** (-0.5)
    cosine, sine_table = trig_ref[:, : head // 2], trig_ref[:, head // 2 :]
    x = x_ref[...].astype(F32)
    xn_out[...] = (x * inverse_rms(x) * gains_ref[0:1, :]).astype(BF16)
    kv[pl.ds(0, WINDOW), :] = jnp.zeros((WINDOW, 2 * head), BF16)
    wait_all(kv_loads)
    raw = nn(xn_out[...], wkv[...])
    k_raw = raw[:, :head]
    k_out[...] = k_raw
    k_rot = rotate(k_raw * inverse_rms(k_raw) * head_ref[1:2, :], cosine, sine_table)
    here = pl.ds(pl.multiple_of(WINDOW + me * count, count), count)
    kv[here, :head] = k_rot.astype(BF16)
    kv[here, head:] = raw[:, head:].astype(BF16)
    spread = Spread(halves_of(kv, count, WINDOW), send, recv)
    met()
    spread.start()
    if sharing:
        share = Share(xn_out, o_out, *share_refs)
    wait_all(q_loads)
    q_out[...] = nn(xn_out[...], wq[...])
    spread.pass_on()
    if sharing:
        share.start_rows()
    spread.all_here()
    window = win_out.shape[0]
    win_out[...] = kv[pl.ds(pl.multiple_of(me * count, count), window), :]
    visible = window_mask(me, count, window, length_ref[0])
    k_win, v_win = win_out[:, :head], win_out[:, head:]
    q_gain = head_ref[0:1, :]

    def one_head(i):
        columns = columns_of(i, head)
        q_raw = q_out[:, columns]
        qr = rotate(q_raw * inverse_rms(q_raw) * q_gain, cosine, sine_table).astype(BF16)
        scores = jnp.where(visible, nt(qr, k_win) * scaling, NEGATIVE)
        most = jnp.max(scores, axis=-1, keepdims=True)
        exponent = jnp.exp(scores - most)
        total = jnp.sum(exponent, axis=-1, keepdims=True)
        lse_out[i] = most + jnp.log(total)
        o_out[:, columns] = nn((exponent / total).astype(BF16), v_win).astype(BF16)

    for i in range(heads):
        one_head(i)
    if sharing:
        share.start_deal()
        share.spread.pass_on()
    wait_all(out_loads)
    a = nt(o_out[...], wot[...])
    a_out[...] = a
    h_out[...] = x_ref[...].astype(F32) + a * inverse_rms(a) * gains_ref[1:2, :]
    spread.finish()
    if sharing:
        share.all_here()
        share.finish()
        xn, o, loads = share_refs[:3]
        stores = [
            pltpu.make_async_copy(xn, xn_all_out, loads.at[2]),
            pltpu.make_async_copy(o, o_all_out, loads.at[3]),
        ]
        start_all(stores)
        wait_all(stores)


def attend(length, x, gains, head_gains, trig, pack, head, layer, collective_id):
    count, model = x.shape
    kv_width = 2 * head
    width = 4 * head
    window = count + WINDOW
    sharing = True
    xn_shape = jax.ShapeDtypeStruct((count, model), BF16)
    o_shape = jax.ShapeDtypeStruct((count, width), BF16)
    shapes = [
        jax.ShapeDtypeStruct((count, model), F32),
        xn_shape,
        jax.ShapeDtypeStruct((count, width), F32),
        jax.ShapeDtypeStruct((count, head), F32),
        jax.ShapeDtypeStruct((window, kv_width), BF16),
        jax.ShapeDtypeStruct((4, count, 1), F32),
        o_shape,
        jax.ShapeDtypeStruct((count, model), F32),
    ]
    outs = [vmem_spec()] * 8
    if sharing:
        shapes += share_shapes(xn_shape, o_shape)
        outs += [any_spec()] * 2
    return pl.pallas_call(
        functools.partial(attend_kernel, layer),
        out_shape=shapes,
        in_specs=[pl.BlockSpec(memory_space=pltpu.SMEM)] + [vmem_spec()] * 4 + [any_spec()],
        out_specs=outs,
        scratch_shapes=[
            pltpu.VMEM((4 * count + WINDOW, kv_width), BF16),
            pltpu.VMEM((model, width), BF16),
            pltpu.VMEM((model, width), BF16),
            pltpu.VMEM((model, kv_width), BF16),
            pltpu.SemaphoreType.DMA((3, 4)),
            *spread_spec(),
            *(share_spec(count, model, head) if sharing else []),
        ],
        compiler_params=params(collective_id, 40),
    )(length, x, gains, head_gains, trig, pack)


def attend_back_kernel(
    layer, length_ref, dh_ref, a_ref, x_ref, gains_ref, head_ref, trig_ref, q_ref, k_ref, win_ref, lse_ref,
    pack_ref, xn_ref, o_ref, *refs
):
    if layer == 0:
        block_ref, dx_one_ref, lined_ref, early_ref, *refs = refs
        block_out, both_out, lined_out, came_out, q_out, kv_out, o_out = refs[4:11]
        refs = refs[:4] + refs[11:]
        gain_refs, (dx_give, dx_send, dx_recv), line_refs = refs[36:40], refs[40:43], refs[43:]
        refs = refs[:36]
    (
    dx_out, dw_out, dgain_out, dhead_out,
    da, do, dq, dk, dv, parts, dq_all, dkv, dkv_all, wq, wot, wkv, xn, o, ours, theirs, came,
    pack_load, load, send, recv, land, passing, fold_send, fold_recv, q_send, q_recv, kv_send, kv_recv, swap_send, swap_recv, out_sem,
    ) = refs
    count = dh_ref.shape[0]
    head = k_ref.shape[1]
    heads = q_ref.shape[1] // head
    kv_part = dkv_all.shape[1]
    me, nx, ny = neighbours()
    core = lax.axis_index("section")
    far = jnp.bitwise_xor(me, 3)
    lined = layer == 0 and len(line_refs) > 0
    if layer == 0:
        met = greet(*sum(gain_stages(), []))
        sums = GainSum(*gain_refs)
    else:
        met = greet({"narrow": nx}, {"narrow": ny}, {"narrow": far}, {"section": 1 - core})
    if lined:
        line = LineSum(lined_ref, lined_out, *line_refs[:7])
        early = LineSum(early_ref, None, *line_refs[7:14])
        late = LineSum(ours, None, *line_refs[14:21])
        came_line, came_store, came_early, came_late, kv_all, cross_send, cross_recv, narrow_send, narrow_recv = (
            line_refs[21:]
        )

        def across(at, src, dst):
            return pltpu.make_async_remote_copy(
                src_ref=src,
                dst_ref=dst,
                send_sem=cross_send.at[at],
                recv_sem=cross_recv.at[at],
                device_id={"section": 1 - core},
                device_id_type=MESH,
            )

        early.load()
        line.load()
    q_loads, out_loads, kv_loads = pack_loads(pack_ref, layer, head, wq, wot, wkv, pack_load)
    loads = [
        pltpu.make_async_copy(src, dst, load.at[at])
        for at, (src, dst) in enumerate(((xn_ref, xn), (o_ref, o)))
    ]
    start_all(out_loads + q_loads + kv_loads + loads)
    here = rows_of(me, count)
    scaling = head ** (-0.5)
    cosine, sine_table = trig_ref[:, : head // 2], trig_ref[:, head // 2 :]

    dh = dh_ref[...]
    by_value, dg1 = normed_gradient(a_ref[...], gains_ref[1:2, :], dh)
    da[here, :] = by_value.astype(BF16)
    dgain_out[1:2, :] = dg1
    spread = Spread(halves_of(da, count), send, recv)
    met()
    spread.start()
    if lined:
        early.begin()
        line.begin()
    wait_all(out_loads)
    do[...] = nn(da[here, :], wot[...]).astype(BF16)

    visible = window_mask(me, count, win_ref.shape[0], length_ref[0])
    k_win, v_win = win_ref[:, :head], win_ref[:, head:]
    dk[...] = jnp.zeros_like(dk)
    dv[...] = jnp.zeros_like(dv)
    dhead_out[...] = jnp.zeros_like(dhead_out)
    q_gain, k_gain = head_ref[0:1, :], head_ref[1:2, :]

    def one_head(i):
        columns = columns_of(i, head)
        raw = q_ref[:, columns]
        inverse = inverse_rms(raw)
        unit = raw * inverse
        qr = rotate(unit * q_gain, cosine, sine_table).astype(BF16)
        scores = jnp.where(visible, nt(qr, k_win) * scaling, NEGATIVE)
        probs = jnp.exp(scores - lse_ref[i])
        do_head = do[:, columns]
        dp = nt(do_head, v_win)
        ds = (probs * (dp - jnp.sum(probs * dp, axis=-1, keepdims=True))).astype(BF16)
        dk[...] += tn(ds, qr)
        dv[...] += tn(probs.astype(BF16), do_head)
        grad = turn_back(nn(ds, k_win) * scaling, cosine, sine_table)
        scaled = grad * q_gain
        dq_raw = inverse * (scaled - unit * jnp.mean(scaled * unit, axis=-1, keepdims=True))
        dq[:, columns] = dq_raw.astype(BF16)
        dhead_out[0:1, :] += jnp.sum(grad * unit, axis=0, keepdims=True)

    for i in range(heads):
        one_head(i)
    parts[...] = jnp.zeros_like(parts)
    window = pl.ds(pl.multiple_of(me * count, count), win_ref.shape[0])
    parts[window, :head] = (dk[...] * scaling).astype(BF16)
    parts[window, head:] = dv[...].astype(BF16)
    fold = Fold(halves_of(parts, count, WINDOW), land, passing, fold_send, fold_recv)
    fold.send_far()
    fold.send_near()
    deal_q = Deal(
        lambda other: dq.at[:, columns_of(other, head)],
        lambda mine: dq_all.at[rows_of(mine, count)],
        q_send,
        q_recv,
    )
    deal_q.start()
    dq_all[here, :] = dq[:, columns_of(me, head)]
    spread.pass_on()
    if lined:
        early.step(1, 0)
        line.step(1, 0)
    wait_all(q_loads)
    dx_out[...] = nt(dq[...], wq[...])
    fold.pass_on()
    spread.all_here()
    wait_all(loads)
    first = core == 0
    swaps = []

    def exchange(at, columns, a, b):
        ours[:, columns] = jnp.where(first, a, b).astype(BF16)
        theirs[:, columns] = jnp.where(first, b, a).astype(BF16)
        copy = pltpu.make_async_remote_copy(
            src_ref=theirs.at[:, columns],
            dst_ref=came.at[:, columns],
            send_sem=swap_send.at[at],
            recv_sem=swap_recv.at[at],
            device_id={"section": 1 - core},
            device_id_type=MESH,
        )
        copy.start()
        swaps.append(copy)

    if lined:
        line.step(1, 1)
    by_out = tn(da[...], o[...])
    deal_q.here()
    exchange(0, pl.ds(0, head), tn(xn[...], dq_all[...]), by_out)
    own = jnp.concatenate([dk[WINDOW:, :] * scaling, dv[WINDOW:, :]], axis=1)
    total = fold.total(own)
    grad = turn_back(total[:, :head], cosine, sine_table)
    dk_raw, dk_gain = normed_gradient(k_ref[...], k_gain, grad)
    dhead_out[1:2, :] = dk_gain
    dkv[:, :head] = dk_raw.astype(BF16)
    dkv[:, head:] = total[:, head:].astype(BF16)
    deal_kv = Deal(
        lambda other: dkv.at[:, columns_of(other, kv_part)],
        lambda mine: dkv_all.at[rows_of(mine, count)],
        kv_send,
        kv_recv,
    )
    deal_kv.start()
    dkv_all[here, :] = dkv[:, columns_of(me, kv_part)]
    wait_all(kv_loads)
    dxn = dx_out[...] + nt(dkv[...], wkv[...])
    by_value, dg0 = normed_gradient(x_ref[...].astype(F32), gains_ref[0:1, :], dxn)
    dx_out[...] = dh_ref[...] + by_value
    dgain_out[0:1, :] = dg0
    if layer == 0:
        zero = core == 0
        both_out[core] = jnp.where(zero, dx_out[...], dx_one_ref[...])
        dx_give[...] = jnp.where(zero, dx_one_ref[...], dx_out[...])
        dx_copy = pltpu.make_async_remote_copy(
            src_ref=dx_give,
            dst_ref=both_out.at[core],
            send_sem=dx_send,
            recv_sem=dx_recv,
            device_id={"section": 1 - core},
            device_id_type=MESH,
        )
        dx_copy.start()
    if lined:
        line.step(2, 0)
        for step in range(2, early.steps):
            early.step(step, 0)
    if layer == 0:
        own_total = sums.total.at[0]
        own_total[...] = block_ref[...]
        own_total[0:2, :] = dgain_out[...]
        own_total[4:5, :head] = dhead_out[0:1, :]
        own_total[4:5, head : 2 * head] = dhead_out[1:2, :]
        sums.start(0)

    deal_kv.here()
    by_kv = tn(xn[...], dkv_all[...])
    if layer == 0:
        sums.add(0)
        sums.start(1)
    exchange(1, pl.ds(head, kv_part), by_kv, jnp.zeros_like(by_kv))
    for copy in swaps:
        copy.wait_recv()
    ours[...] = (ours[...].astype(F32) + came[...].astype(F32)).astype(BF16)
    out = pltpu.make_async_copy(ours, dw_out, out_sem)
    out.start()
    if layer == 0:
        sums.add(1)
        sums.start(2)
    if lined:
        late.load()
        late.begin()
        for step in range(2, line.steps):
            if step > 2:
                line.step(step, 0)
            late.step(step - 1, 0)
            line.step(step, 1)
        early.end()
        crosses = [across(0, early.result, came_early)]
        crosses[0].start()
        late.step(late.steps - 1, 0)
        late.end()
        crosses.append(across(1, late.result, came_late))
        crosses[1].start()
        crosses[0].wait_recv()
        by_qkv = jnp.where(zero, late.result[...], came_early[...])
        kv_all[me] = by_qkv[:, head:]
        narrows = [
            remote(kv_all.at[me], kv_all.at[me], narrow_send.at[at], narrow_recv.at[at], other)
            for at, other in enumerate((nx, ny, far))
        ]
        start_all(narrows)
        q_out[...] = by_qkv[:, :head].astype(F32)
        crosses[1].wait_recv()
        o_out[...] = jnp.where(zero, came_late[:, :head], early.result[:, :head]).astype(F32)
        for copy in narrows:
            copy.wait_recv()
        for n in range(4):
            kv_out[:, n * kv_part : (n + 1) * kv_part] = kv_all[n].astype(F32)
        line.end()
        crosses.append(across(2, line.result, came_line))
        crosses[2].start()
        crosses[2].wait_recv()
        keep = pltpu.make_async_copy(came_line, came_out, came_store)
        keep.start()
        for copy in crosses + narrows:
            copy.wait_send()
        keep.wait()
    if layer == 0:
        dx_copy.wait_recv()
        dx_copy.wait_send()
    if layer == 0:
        sums.add(2)
        block_out[...] = sums.total[3]
        sums.close()
    spread.finish()
    fold.finish()
    deal_q.finish()
    deal_kv.finish()
    for copy in swaps:
        copy.wait_send()
    out.wait()


def attend_back(length, dh, a, x, gains, head_gains, trig, q_raw, k_raw, window, lse, pack, xn, o, deps, layer, collective_id):
    count, model = dh.shape
    head = k_raw.shape[1]
    width = q_raw.shape[1]
    kv_part = pack.shape[3] - 2 * head
    if layer == 0:
        wides = lax.axis_size("wide")
        block, dx_one, lined, early = deps
        rows = model // wides
    deal = pltpu.SemaphoreType.DMA((3,))
    dw = pltpu.VMEM((model, head + kv_part), BF16)
    return pl.pallas_call(
        functools.partial(attend_back_kernel, layer),
        out_shape=[
            jax.ShapeDtypeStruct((count, model), F32),
            jax.ShapeDtypeStruct((model, head + kv_part), BF16),
            jax.ShapeDtypeStruct((2, model), F32),
            jax.ShapeDtypeStruct((2, head), F32),
            *(
                [
                    jax.ShapeDtypeStruct(block.shape, F32),
                    jax.ShapeDtypeStruct((2, count, model), F32),
                    jax.ShapeDtypeStruct((rows, lined.shape[1]), BF16),
                    jax.ShapeDtypeStruct((rows, lined.shape[1]), BF16),
                    jax.ShapeDtypeStruct((rows, head), F32),
                    jax.ShapeDtypeStruct((rows, 4 * kv_part), F32),
                    jax.ShapeDtypeStruct((rows, head), F32),
                ]
                if layer == 0
                else []
            ),
        ],
        in_specs=[pl.BlockSpec(memory_space=pltpu.SMEM)] + [vmem_spec()] * 10 + [any_spec()] * 3 + ([vmem_spec()] * 2 + [any_spec()] * 2 if layer == 0 else []),
        out_specs=[vmem_spec(), any_spec(), vmem_spec(), vmem_spec()]
        + ([vmem_spec()] * 2 + [any_spec()] * 2 + [vmem_spec()] * 3 if layer == 0 else []),
        scratch_shapes=[
            pltpu.VMEM((4 * count, model), BF16),
            pltpu.VMEM((count, width), BF16),
            pltpu.VMEM((count, width), BF16),
            pltpu.VMEM((window.shape[0], head), F32),
            pltpu.VMEM((window.shape[0], head), F32),
            pltpu.VMEM((4 * count + WINDOW, 2 * head), BF16),
            pltpu.VMEM((4 * count, head), BF16),
            pltpu.VMEM((count, 2 * head), BF16),
            pltpu.VMEM((4 * count, kv_part), BF16),
            pltpu.VMEM((model, width), BF16),
            pltpu.VMEM((model, width), BF16),
            pltpu.VMEM((model, 2 * head), BF16),
            pltpu.VMEM(xn.shape, BF16),
            pltpu.VMEM(o.shape, BF16),
            dw,
            dw,
            dw,
            pltpu.SemaphoreType.DMA((3, 4)),
            pltpu.SemaphoreType.DMA((2,)),
            *spread_spec(),
            *fold_spec(count, 2 * head),
            deal,
            deal,
            deal,
            deal,
            pltpu.SemaphoreType.DMA((2,)),
            pltpu.SemaphoreType.DMA((2,)),
            pltpu.SemaphoreType.DMA,
            *(
                [
                    *gain_spec(wides, block.shape),
                    pltpu.VMEM((count, model), F32),
                    pltpu.SemaphoreType.DMA,
                    pltpu.SemaphoreType.DMA,
                ]
                if layer == 0
                else []
            ),
            *(
                [
                    *line_spec(wides, rows, lined.shape[1], 2),
                    *line_spec(wides, rows, head + kv_part, 1),
                    *line_spec(wides, rows, head + kv_part, 1),
                    pltpu.VMEM((rows, lined.shape[1]), BF16),
                    pltpu.SemaphoreType.DMA,
                    pltpu.VMEM((rows, head + kv_part), BF16),
                    pltpu.VMEM((rows, head + kv_part), BF16),
                    pltpu.VMEM((4, rows, kv_part), BF16),
                    pltpu.SemaphoreType.DMA((3,)),
                    pltpu.SemaphoreType.DMA((3,)),
                    pltpu.SemaphoreType.DMA((3,)),
                    pltpu.SemaphoreType.DMA((3,)),
                ]
                if layer == 0 and rows % 16 == 0
                else []
            ),
        ],
        compiler_params=params(collective_id, 60 if layer == 0 else 48),
    )(length, dh, a, x, gains, head_gains, trig, q_raw, k_raw, window, lse, pack, xn, o, *deps)


def after(value, *others):
    return pl.pallas_call(
        lambda *refs: None,
        out_shape=jax.ShapeDtypeStruct(value.shape, value.dtype),
        in_specs=[any_spec()] * (1 + len(others)),
        out_specs=any_spec(),
        input_output_aliases={0: 0},
    )(value, *others)


def scatter(member):
    return lax.psum_scatter(member, "wide", scatter_dimension=0, tiled=True)


def on_device(
    inputs, cotangent, lengths, norm_gains, head_gains, w_q, w_kv, w_o, w_gate_up, w_down
):
    core = lax.axis_index("section")
    narrow = lax.axis_index("narrow")
    n_narrow = lax.axis_size("narrow")
    is_zero = core == 0
    rows, model = inputs.shape[1], inputs.shape[2]
    block = w_q.shape[1]
    head_width = w_q.shape[2]
    n_wide = lax.axis_size("wide")
    hidden = w_down.shape[1]
    kv_part = w_kv.shape[2] // n_narrow

    def swap(value):
        return lax.ppermute(value, "section", [(0, 1), (1, 0)])

    def by_core(first, second):
        return jnp.where(is_zero, first, second)

    half = block // 2

    pad = -hidden % TILE
    kv_own = lax.dynamic_slice_in_dim(w_kv[0], narrow * kv_part, kv_part, 1)
    pack_width = 2 * head_width + kv_part
    pack = [w_q[0], w_o[0].T, kv_own]
    pack = jnp.concatenate(pack, axis=1)
    if block % 16 == 0:
        gain_rows = jnp.zeros((GAIN_ROWS, pack_width), BF16)
        gain_rows = lax.dynamic_update_slice(gain_rows, norm_gains[0], (0, 0))
        gain_rows = lax.dynamic_update_slice(gain_rows, head_gains[0], (4, 0))
        pack = jnp.concatenate([pack, gain_rows], axis=0)
    late = after(core.reshape(1), pack)[0]
    pack = lax.all_gather(pack, "wide", axis=0, tiled=True)

    def half_of(side):
        gate_up = lax.dynamic_slice_in_dim(w_gate_up[0], side * half, half, 0)
        gate_up = jnp.pad(gate_up, ((0, 0), (0, 0), (0, pad))).reshape(half, -1)
        down = lax.dynamic_slice_in_dim(w_down[0].T, side * half, half, 0)
        return jnp.concatenate([gate_up, jnp.pad(down, ((0, 0), (0, pad)))], axis=1)

    feed = trade(half_of(late), half_of(1 - late), 7)
    padded = hidden + pad

    def gather(member):
        return lax.all_gather(member, ("wide", "section"), axis=0, tiled=True)

    both = gather(feed[0])
    feeds = [
        (both, both, padded),
        (gather(feed[1][:, : 2 * padded]), gather(feed[1][:, 2 * padded :]), padded),
    ]
    packs, gain_packs = gather_pack(pack, model, n_wide, 6)
    if block % 16:
        norm_own = lax.all_gather(norm_gains[0], "wide", axis=1, tiled=True)
        head_own = lax.all_gather(head_gains[0], "wide", axis=1, tiled=True)
        norm_came, head_came = swap(norm_own), swap(head_own)

    def gains_of(section):
        if block % 16:
            mine = core == section
            norm_part = jnp.where(mine, norm_own, norm_came)
            head_part = jnp.where(mine, head_own, head_came)
        else:
            tail = gain_packs[section]
            norm_part = tail[:, :4, :block].transpose(1, 0, 2).reshape(4, model)
            head_part = tail[:, 4:6, : head_width // n_wide].transpose(1, 0, 2).reshape(2, head_width)
        return norm_part.astype(F32), head_part.astype(F32)

    start = narrow * rows
    positions = start + jnp.arange(rows, dtype=jnp.int32)
    trig = tables(positions, head_width)
    length = lax.dynamic_index_in_dim(lengths[:, 0], core, 0, keepdims=False)

    x = lax.dynamic_index_in_dim(inputs, core, 0, keepdims=False)
    length_one = length.reshape(1)
    outs, kept, gains = [], [], []
    for section in range(2):
        layer_gains, head_gain = gains_of(section)
        gains.append((layer_gains, head_gain))
        h, xn, q_raw, k_raw, window, lse, o, a, *shared = attend(
            length_one, x, layer_gains, head_gain, trig, packs, head_width, section, 8 + section
        )
        w_up, w_down, _ = feeds[section]
        mid_rows, gu, act = feed_up(h, layer_gains[2:3], w_up, padded, (), 10 + section)
        kept.append(((a, x, q_raw, k_raw, window, lse), (h, mid_rows, gu, act), shared))
        if section == 0:
            x, f = feed_down(h, layer_gains[3:4], act, w_down, 12)
            outs.append(x)

    def by_section(first, second):
        stays, came = by_core(first, second), swap(by_core(second, first))
        return jnp.stack([by_core(stays, came), by_core(came, stays)])

    real = (positions < length).astype(F32)[:, None]
    dy = lax.dynamic_index_in_dim(cotangent, core, 0, keepdims=False).astype(F32) * real
    dxs, gain_grads = [None, None], [None, None]
    up_sums, down_sums, attention_sums = [None, None], [None, None], [None, None]
    extra = None
    for section in (1, 0):
        kept_a, (h, mid_rows, gu, act), (xn, o) = kept[section]
        layer_gains, head_gain = gains[section]
        w_up, w_down, _ = feeds[section]
        if section:
            out, dgu, d_down, dg3 = feed_turn(h, layer_gains[3:4], dy, act, w_down, gu, 13)
            outs.append(out)
        else:
            dgu, d_down, dg3 = feed_back_up(
                dy, f, layer_gains[3:4], gu, act, w_down,
                (extra, down_sums[1]) if block % 16 else (down_sums[1],), 14,
            )
        down_sums[section] = scatter(d_down)
        dh, d_up, dg2 = feed_back_down(dy, h, layer_gains[2:3], dgu, mid_rows, w_up, 16 + section)
        if section or block % 16:
            up_sums[section] = scatter(d_up)
        a, x, q_raw, k_raw, window, lse = kept_a
        if section == 0:
            zeros = jnp.zeros((2, model), F32)
            gain_grads[0] = jnp.concatenate([zeros, dg2, dg3, zeros, zeros])
            section_out = by_section(*outs)
            lined = after(d_up, up_sums[1], section_out)
            deps = (jnp.concatenate(gain_grads), dxs[1], lined, extra)
        dx, extra, dg01, dhead, *more = attend_back(
            length_one, dh, a, x, layer_gains, head_gain, trig, q_raw, k_raw, window, lse, packs, xn, o,
            () if section else deps, section, 18 + section,
        )
        dxs[section] = dx
        if section:
            head_row = jnp.pad(dhead.reshape(1, -1), ((0, 0), (0, model - dhead.size)))
            gain_grads[1] = jnp.concatenate([dg01, dg2, dg3, head_row, jnp.zeros((3, model), F32)])
        else:
            gain_sums, input_grad, up_lined, came_up, grad_q, grad_kv, grad_o = more
            if block % 16 == 0:
                up_sums[0] = up_lined
            else:
                came_up = swap(up_sums[0])
        dy = dx
    def own_section(first, second):
        came = swap(by_core(second, first))
        stays = by_core(first, second)
        return by_core(stays, came).astype(F32), by_core(came, stays).astype(F32)

    if block % 16:
        split = down_sums[1].shape[1]
        attention_sums = (scatter(extra), down_sums[0][:, split:])
        down_sums[0] = down_sums[0][:, :split]
        grad_q, grad_kv, grad_o = finish_attention(
            *attention_sums, swap(attention_sums[1]), up_sums[0], head_width, 2
        )
    grad_o = grad_o.T
    grad_gate_up, _ = pair_up(*up_sums, came_up, swap(up_sums[1]), hidden)
    down_sums[0] = after(down_sums[0], gain_sums)
    grad_down = jnp.concatenate(own_section(*down_sums), axis=1)[:, :hidden].T
    gain_sums = lax.dynamic_slice_in_dim(gain_sums, core * 8, 8, 0)
    wide = lax.axis_index("wide")
    grad_norm = lax.dynamic_slice_in_dim(gain_sums[:4], wide * block, block, 1)
    grad_head = gain_sums[4, : 2 * head_width].reshape(2, head_width)
    head_block = head_width // n_wide
    grad_head = lax.dynamic_slice_in_dim(grad_head, wide * head_block, head_block, 1)

    return (
        section_out[None],
        input_grad[None],
        grad_norm[None],
        grad_head[None],
        grad_q[None],
        grad_kv[None],
        grad_o[None],
        grad_gate_up[None],
        grad_down[None],
    )


def solution(mesh):
    return jax.shard_map(
        on_device,
        mesh=mesh,
        in_specs=(
            P(None, ("wide", "narrow"), None),
            P(None, ("wide", "narrow"), None),
            P(None, "wide"),
            P("section", None, "wide"),
            P("section", None, "wide"),
            P("section", "wide", "narrow"),
            P("section", "wide", None),
            P("section", "narrow", "wide"),
            P("section", "wide", None, "narrow"),
            P("section", "narrow", "wide"),
        ),
        out_specs=(
            P("section", None, ("wide", "narrow"), None),
            P("section", None, ("wide", "narrow"), None),
            P("section", None, "wide"),
            P("section", None, "wide"),
            P("section", "wide", "narrow"),
            P("section", "wide", None),
            P("section", "narrow", "wide"),
            P("section", "wide", None, "narrow"),
            P("section", "narrow", "wide"),
        ),
        check_vma=False,
    )
```

```python
import functools

import jax
import jax.numpy as jnp
from jax import lax
from jax.experimental import pallas as pl
from jax.experimental.pallas import tpu as pltpu
from jax.sharding import PartitionSpec as P

WINDOW = 512
EPSILON = 1e-06
NEGATIVE = -1e30
ROPE_BASE = 10000.0
MESH = pl.DeviceIdType.MESH
MIB = 2**20
GAIN_ROWS = 16
F32 = jnp.float32
BF16 = jnp.bfloat16


def dot(a, b, dims):
    return lax.dot_general(a, b, ((dims[0], dims[1]), ((), ())), preferred_element_type=F32)


def nn(a, b):
    return dot(a, b, ((1,), (0,)))


def nt(a, b):
    return dot(a, b, ((1,), (1,)))


def tn(a, b):
    return dot(a, b, ((0,), (0,)))


def normed(operand, gain_vec):
    return (
        operand
        * lax.rsqrt(jnp.mean(operand * operand, axis=-1, keepdims=True) + EPSILON)
        * gain_vec
    )


def geglu(gate, up):
    return jax.nn.gelu(gate, approximate=True) * up


def neighbours():
    me = lax.axis_index("narrow")
    return me, jnp.bitwise_xor(me, 1), jnp.bitwise_xor(me, 2)


def meet(nx, ny):
    barrier = pltpu.get_barrier_semaphore()
    for other in (nx, ny):
        pl.semaphore_signal(barrier, inc=1, device_id={"narrow": other}, device_id_type=MESH)
    pl.semaphore_wait(barrier, 2)


def remote(src, dst, send_sem, recv_sem, other):
    return pltpu.make_async_remote_copy(
        src_ref=src,
        dst_ref=dst,
        send_sem=send_sem,
        recv_sem=recv_sem,
        device_id={"narrow": other},
        device_id_type=MESH,
    )


def tables(positions, head_width):
    half_width = head_width // 2
    frequency = ROPE_BASE ** (-jnp.arange(half_width, dtype=F32) * (2.0 / head_width))
    angles = positions.astype(F32)[:, None] * frequency[None, :]
    return jnp.concatenate([jnp.cos(angles), jnp.sin(angles)], axis=1)


def rotate(operand, cosine, sine_table):
    half_width = operand.shape[-1] // 2
    front_half = operand[..., :half_width]
    back_half = operand[..., half_width:]
    return jnp.concatenate(
        [
            front_half * cosine - back_half * sine_table,
            back_half * cosine + front_half * sine_table,
        ],
        axis=-1,
    )


GELU_SCALE = 0.7978845608028654
GELU_CUBE = 0.044715


def vmem_spec():
    return pl.BlockSpec(memory_space=pltpu.VMEM)


def any_spec():
    return pl.BlockSpec(memory_space=pl.ANY)


def rows_of(block, count):
    return pl.ds(pl.multiple_of(block * count, count), count)


def columns_of(tile, width, offset=0):
    if isinstance(tile, int):
        return pl.ds(tile * width + offset, width)
    return pl.ds(pl.multiple_of(tile * width + offset, 128), width)


def inverse_rms(value):
    return lax.rsqrt(jnp.mean(value * value, axis=-1, keepdims=True) + EPSILON)


def normed_gradient(value, gain, grad):
    inverse = inverse_rms(value)
    unit = value * inverse
    scaled = grad * gain
    by_value = inverse * (scaled - unit * jnp.mean(scaled * unit, axis=-1, keepdims=True))
    return by_value, jnp.sum(grad * unit, axis=0, keepdims=True)


def halves_of(ref, count, base=0):
    half = count // 2

    def part(block, which):
        return ref.at[pl.ds(pl.multiple_of(base + block * count + which * half, half), half)]

    return part


class Spread:
    def __init__(self, part, send, recv):
        self.me, self.nx, self.ny = neighbours()
        self.far = jnp.bitwise_xor(self.me, 3)

        def copy(block, which, at, other):
            ref = part(block, which)
            return remote(ref, ref, send.at[at], recv.at[at], other)

        self.to_x1 = copy(self.me, 0, 0, self.nx)
        self.to_y2 = copy(self.me, 1, 1, self.ny)
        self.to_x2 = copy(self.me, 1, 2, self.nx)
        self.to_y1 = copy(self.me, 0, 3, self.ny)
        self.on_y = copy(self.nx, 0, 4, self.ny)
        self.on_x = copy(self.ny, 1, 5, self.nx)

    def start(self):
        for copy in (self.to_x1, self.to_y2, self.to_x2, self.to_y1):
            copy.start()

    def pass_on(self):
        self.to_x1.wait_recv()
        self.on_y.start()
        self.to_y2.wait_recv()
        self.on_x.start()

    def x_here(self):
        self.to_x2.wait_recv()

    def y_here(self):
        self.to_y1.wait_recv()

    def far_here(self):
        self.on_y.wait_recv()
        self.on_x.wait_recv()

    def all_here(self):
        self.x_here()
        self.y_here()
        self.far_here()

    def finish(self):
        for copy in (self.to_x1, self.to_y2, self.to_x2, self.to_y1, self.on_y, self.on_x):
            copy.wait_send()


class Fold:
    def __init__(self, part, land, passing, send, recv):
        self.me, self.nx, self.ny = neighbours()
        self.far = jnp.bitwise_xor(self.me, 3)
        self.part, self.land, self.passing = part, land, passing

        def copy(src, at, other):
            return remote(src, land.at[at], send.at[at], recv.at[at], other)

        self.far_x = copy(part(self.far, 0), 0, self.nx)
        self.far_y = copy(part(self.far, 1), 1, self.ny)
        self.near_x = copy(part(self.nx, 0), 2, self.nx)
        self.near_y = copy(part(self.ny, 1), 3, self.ny)
        self.on_y = copy(passing.at[0], 4, self.ny)
        self.on_x = copy(passing.at[1], 5, self.nx)

    def send_far(self):
        self.far_x.start()
        self.far_y.start()

    def send_near(self):
        self.near_x.start()
        self.near_y.start()

    def pass_on(self):
        self.far_x.wait_recv()
        self.passing[0] = (self.part(self.ny, 0)[...].astype(F32) + self.land[0].astype(F32)).astype(BF16)
        self.on_y.start()
        self.far_y.wait_recv()
        self.passing[1] = (self.part(self.nx, 1)[...].astype(F32) + self.land[1].astype(F32)).astype(BF16)
        self.on_x.start()

    def total(self, own):
        half = own.shape[0] // 2
        for copy in (self.near_x, self.near_y, self.on_y, self.on_x):
            copy.wait_recv()
        first = own[:half] + (self.land[2].astype(F32) + self.land[4].astype(F32))
        second = own[half:] + (self.land[3].astype(F32) + self.land[5].astype(F32))
        return jnp.concatenate([first, second], axis=0)

    def finish(self):
        for copy in (self.far_x, self.far_y, self.near_x, self.near_y, self.on_y, self.on_x):
            copy.wait_send()


class LineFold:
    def __init__(self, own, land, out, columns, send, recv):
        self.own, self.land, self.out, self.columns = own, land, out, columns
        self.send, self.recv = send, recv
        self.wides = own.shape[0]
        self.wide = lax.axis_index("wide")

    def place(self, way):
        return self.wide if way == 0 else self.wides - 1 - self.wide

    def copy(self, way, step):
        return pltpu.make_async_remote_copy(
            src_ref=self.out.at[self.slot(way, step), :, self.columns],
            dst_ref=self.land.at[way, step, :, self.columns],
            send_sem=self.send.at[way, step],
            recv_sem=self.recv.at[way, step],
            device_id={"wide": self.wide + 1 if way == 0 else self.wide - 1},
            device_id_type=MESH,
        )

    def slot(self, way, step):
        return jnp.clip(step - self.wide, 0, self.wides - 2) if way == 0 else step

    def sends(self, way, step):
        place = self.place(way)
        return (place <= step) & (place < self.wides - 1)

    def gets(self, way, step):
        place = self.place(way)
        return (place >= 1) & (place - 1 <= step)

    def step(self, step):
        for way in (0, 1):
            ahead = self.wides - 1 - step
            block = self.wide + ahead if way == 0 else self.wide - ahead
            block = jnp.clip(block, 0, self.wides - 1)
            begins = self.place(way) == 0

            @pl.when(self.sends(way, step) & begins)
            def _():
                self.out[self.slot(way, step), :, self.columns] = self.own[block, :, self.columns]
                self.copy(way, step).start()

            if step:

                @pl.when(self.sends(way, step) & jnp.logical_not(begins))
                def _():
                    self.copy(way, step - 1).wait_recv()
                    total = self.own[block, :, self.columns].astype(F32)
                    total = total + self.land[way, step - 1, :, self.columns].astype(F32)
                    self.out[self.slot(way, step), :, self.columns] = total.astype(BF16)
                    self.copy(way, step).start()

    def finish(self, result):
        last = self.wides - 2
        result[:, self.columns] = self.own[self.wide, :, self.columns]
        for way in (0, 1):

            @pl.when(self.gets(way, last))
            def _():
                self.copy(way, last).wait_recv()
                total = result[:, self.columns].astype(F32)
                total = total + self.land[way, last, :, self.columns].astype(F32)
                result[:, self.columns] = total.astype(BF16)

    def close(self):
        for step in range(self.wides - 1):
            for way in (0, 1):
                pl.when(self.sends(way, step))(self.copy(way, step).wait_send)


def line_spec(wides, block, columns, pieces):
    hops = pltpu.SemaphoreType.DMA((pieces, 2, wides - 1))
    return [
        pltpu.VMEM((wides, block, columns), BF16),
        pltpu.VMEM((2, wides - 1, block, columns), BF16),
        pltpu.VMEM((wides - 1, block, columns), BF16),
        pltpu.VMEM((block, columns), BF16),
        pltpu.SemaphoreType.DMA((wides + 1,)),
        hops,
        hops,
    ]


class LineSum:
    def __init__(self, src, dst, own, land, out, result, loads, send, recv):
        self.src, self.dst, self.own, self.result, self.loads = src, dst, own, result, loads
        pieces = send.shape[0]
        columns = own.shape[2]
        width = -(-columns // (128 * pieces)) * 128
        self.folds = [
            LineFold(own, land, out, pl.ds(first, min(width, columns - first)), send.at[p], recv.at[p])
            for p, first in enumerate(range(0, columns, width))
        ]
        self.steps = own.shape[0] - 1

    def load(self):
        wides, rows, columns = self.own.shape
        for w in range(wides):
            part = self.src.at[pl.ds(w * rows, rows), pl.ds(0, columns)]
            pltpu.make_async_copy(part, self.own.at[w], self.loads.at[w]).start()

    def begin(self):
        wides, rows, columns = self.own.shape
        for w in range(wides):
            part = self.src.at[pl.ds(w * rows, rows), pl.ds(0, columns)]
            pltpu.make_async_copy(part, self.own.at[w], self.loads.at[w]).wait()
        for fold in self.folds:
            fold.step(0)

    def step(self, step, piece):
        self.folds[piece].step(step)

    def end(self, done=0):
        for fold in self.folds[done:]:
            fold.finish(self.result)
        if self.dst is not None:
            copy = pltpu.make_async_copy(self.result, self.dst, self.loads.at[self.own.shape[0]])
            copy.start()
        for fold in self.folds:
            fold.close()
        if self.dst is not None:
            copy.wait()


class Deal:
    def __init__(self, src, place, send, recv):
        me, nx, ny = neighbours()
        far = jnp.bitwise_xor(me, 3)
        self.copies = [
            remote(src(other), place(me), send.at[at], recv.at[at], other)
            for at, other in enumerate((far, nx, ny))
        ]

    def start(self):
        for copy in self.copies:
            copy.start()

    def here(self):
        for copy in self.copies:
            copy.wait_recv()

    def finish(self):
        for copy in self.copies:
            copy.wait_send()


def greet(*others):
    barrier = pltpu.get_barrier_semaphore()
    for other in others:
        pl.semaphore_signal(barrier, inc=1, device_id=other, device_id_type=MESH)
    return lambda: pl.semaphore_wait(barrier, len(others))


def spread_spec():
    return [pltpu.SemaphoreType.DMA((6,)), pltpu.SemaphoreType.DMA((6,))]


def fold_spec(count, width):
    return [
        pltpu.VMEM((6, count // 2, width), BF16),
        pltpu.VMEM((2, count // 2, width), BF16),
        pltpu.SemaphoreType.DMA((6,)),
        pltpu.SemaphoreType.DMA((6,)),
    ]


def params(collective_id, mib):
    return pltpu.CompilerParams(
        collective_id=collective_id, has_side_effects=True, vmem_limit_bytes=mib * MIB
    )


TILE = 256


def up_kernel(h_ref, gain_ref, w_ref, *refs):
    sharing = len(refs) > 11
    if sharing:
        xn_ref, o_ref, rows_out, gu_out, act_out, xn_out, o_out, *refs = refs
        rows, w, gu, act, load, store, send, recv, *share_refs = refs
        share = Share(xn_ref, o_ref, *share_refs)
    else:
        rows_out, gu_out, act_out, rows, w, gu, act, load, store, send, recv = refs
    count = h_ref.shape[0]
    hidden = act.shape[1]
    weights = pltpu.make_async_copy(w_ref.at[:, pl.ds(0, 2 * hidden)], w, load)
    weights.start()
    me, nx, ny = neighbours()
    met = greet({"narrow": nx}, {"narrow": ny}, {"narrow": jnp.bitwise_xor(me, 3)})
    value = h_ref[...]
    rows[rows_of(me, count), :] = (value * inverse_rms(value) * gain_ref[...]).astype(BF16)
    spread = Spread(halves_of(rows, count), send, recv)
    met()
    spread.start()
    weights.wait()

    def one(block, at):
        here = rows_of(block, count)

        def tile(j):
            left = rows[here, :]
            gate = nn(left, w[:, columns_of(j, TILE)])
            up = nn(left, w[:, columns_of(j, TILE, hidden)])
            inner = jnp.tanh(GELU_SCALE * (gate + GELU_CUBE * (gate * gate * gate)))
            gu[here, columns_of(j, TILE)] = gate.astype(BF16)
            gu[here, columns_of(j, TILE, hidden)] = up.astype(BF16)
            act[here, columns_of(j, TILE)] = (0.5 * gate * (1.0 + inner) * up).astype(BF16)

        for j in range(hidden // TILE):
            tile(j)
        copies = [
            pltpu.make_async_copy(ref.at[here], out.at[here], store.at[k, at])
            for k, (ref, out) in enumerate(((gu, gu_out), (act, act_out), (rows, rows_out)))
        ]
        for copy in copies:
            copy.start()
        return copies

    copies = one(me, 0)
    spread.pass_on()
    if sharing:
        share.start_rows()
        share.start_deal()
    spread.x_here()
    copies += one(nx, 1)
    spread.y_here()
    copies += one(ny, 2)
    spread.far_here()
    if sharing:
        share.spread.pass_on()
    copies += one(spread.far, 3)
    spread.finish()
    if sharing:
        share.all_here()
        share.finish()
        xn, o, loads = share_refs[:3]
        copies += [pltpu.make_async_copy(xn, xn_out, loads.at[2]), pltpu.make_async_copy(o, o_out, loads.at[3])]
        for copy in copies[-2:]:
            copy.start()
    for copy in copies:
        copy.wait()


def feed_up(h, gain, w_gu, hidden, shared, collective_id):
    count, model = h.shape
    total = 4 * count
    shapes = [(total, model), (total, 2 * hidden), (total, hidden)]
    shapes = [jax.ShapeDtypeStruct(shape, BF16) for shape in shapes]
    if shared:
        shapes += share_shapes(*shared)
    return pl.pallas_call(
        up_kernel,
        out_shape=shapes,
        in_specs=[vmem_spec(), vmem_spec(), any_spec()] + [vmem_spec()] * len(shared),
        out_specs=[any_spec()] * len(shapes),
        scratch_shapes=[
            pltpu.VMEM((total, model), BF16),
            pltpu.VMEM((model, 2 * hidden), BF16),
            pltpu.VMEM((total, 2 * hidden), BF16),
            pltpu.VMEM((total, hidden), BF16),
            pltpu.SemaphoreType.DMA,
            pltpu.SemaphoreType.DMA((3, 4)),
            *spread_spec(),
            *(share_spec(count, model, shared[1].shape[1] // 4) if shared else []),
        ],
        compiler_params=params(collective_id, 60),
    )(h, gain, w_gu, *shared)


def down_kernel(
    h_ref, gain_ref, act_ref, w_ref, x_out, f_out, act, w, parts, load, land, passing, send, recv
):
    count, model = h_ref.shape
    me, nx, ny = neighbours()
    met = greet({"narrow": nx}, {"narrow": ny})
    far = jnp.bitwise_xor(me, 3)
    first = w_ref.shape[1] - w.shape[1]
    weights = pltpu.make_async_copy(w_ref.at[:, pl.ds(first, w.shape[1])], w, load.at[0])
    weights.start()
    arrivals = []
    for at, block in enumerate((far, nx, ny, me)):
        here = rows_of(block, count)
        arrivals.append(pltpu.make_async_copy(act_ref.at[here], act.at[here], load.at[1 + at]))
        arrivals[-1].start()
    fold = Fold(halves_of(parts, count), land, passing, send, recv)
    weights.wait()
    met()

    def one(block, at):
        arrivals[at].wait()
        return nt(act[rows_of(block, count), :], w[...])

    parts[rows_of(far, count), :] = one(far, 0).astype(BF16)
    fold.send_far()
    parts[rows_of(nx, count), :] = one(nx, 1).astype(BF16)
    parts[rows_of(ny, count), :] = one(ny, 2).astype(BF16)
    fold.send_near()
    f_out[...] = one(me, 3)
    fold.pass_on()
    total = fold.total(f_out[...])
    f_out[...] = total
    x_out[...] = (h_ref[...] + total * inverse_rms(total) * gain_ref[...]).astype(BF16)
    fold.finish()


def feed_down(h, gain, act, w_dt, collective_id):
    count, model = h.shape
    return pl.pallas_call(
        down_kernel,
        out_shape=[
            jax.ShapeDtypeStruct((count, model), BF16),
            jax.ShapeDtypeStruct((count, model), F32),
        ],
        in_specs=[vmem_spec(), vmem_spec(), any_spec(), any_spec()],
        out_specs=[vmem_spec(), vmem_spec()],
        scratch_shapes=[
            pltpu.VMEM(act.shape, BF16),
            pltpu.VMEM((model, act.shape[1]), BF16),
            pltpu.VMEM((4 * count, model), BF16),
            pltpu.SemaphoreType.DMA((5,)),
            *fold_spec(count, model),
        ],
        compiler_params=params(collective_id, 60),
    )(h, gain, act, w_dt)


def swap_sum(make, tiles, ours, theirs, came, send, recv, out, out_sems, between=None):
    other = {"section": 1 - lax.axis_index("section")}
    sends = []
    for at, (first, width) in enumerate(tiles):
        columns = pl.ds(first, width)
        theirs[:, columns] = make(False, first, width).astype(BF16)
        copy = pltpu.make_async_remote_copy(
            src_ref=theirs.at[:, columns],
            dst_ref=came.at[:, columns],
            send_sem=send.at[at],
            recv_sem=recv.at[at],
            device_id=other,
            device_id_type=MESH,
        )
        copy.start()
        sends.append(copy)
    if between is not None:
        between()
    stores = []
    for at, (first, width) in enumerate(tiles):
        columns = pl.ds(first, width)
        own = make(True, first, width)
        sends[at].wait_recv()
        ours[:, columns] = (own + came[:, columns].astype(F32)).astype(BF16)
        copy = pltpu.make_async_copy(ours.at[:, columns], out.at[:, columns], out_sems.at[at])
        copy.start()
        stores.append(copy)
    return sends, stores


def column_tiles(width):
    return [(first, min(2 * TILE, width - first)) for first in range(0, width, 2 * TILE)]


def gate_up_gradient(df, here, w, gu, hidden):
    for j in range(hidden // TILE):
        dact = nn(df[here, :], w[:, columns_of(j, TILE)])
        gate = gu[here, columns_of(j, TILE)].astype(F32)
        up = gu[here, columns_of(j, TILE, hidden)].astype(F32)
        square = gate * gate
        inner = jnp.tanh(GELU_SCALE * gate * (1.0 + GELU_CUBE * square))
        half = 0.5 * (1.0 + inner)
        slope = half + 0.5 * GELU_SCALE * gate * (1.0 - inner * inner) * (
            1.0 + 3.0 * GELU_CUBE * square
        )
        gu[here, columns_of(j, TILE)] = (dact * up * slope).astype(BF16)
        gu[here, columns_of(j, TILE, hidden)] = (dact * gate * half).astype(BF16)


def back_up_kernel(dy_ref, f_ref, gain_ref, gu_ref, act_ref, w_ref, *refs):
    if len(refs) == 18:
        refs = refs[1:]
    if len(refs) == 19:
        extra_ref, _, *refs = refs
    else:
        extra_ref = None
    (
        dgu_out, dw_out, dgain_out, df, gu, act, w, ours, theirs, came,
        load, store, send, recv, swap_send, swap_recv, out_sems,
    ) = refs
    if extra_ref is not None:
        first = ours.shape[1]
        extra = pltpu.make_async_copy(
            extra_ref, dw_out.at[:, pl.ds(first, extra_ref.shape[1])], load.at[0, 1]
        )
        extra.start()
    count, model = dy_ref.shape
    hidden = act.shape[1]
    me, nx, ny = neighbours()
    core = lax.axis_index("section")
    met = greet({"narrow": nx}, {"narrow": ny}, {"section": 1 - core})
    far = jnp.bitwise_xor(me, 3)
    start = w_ref.shape[1] - hidden
    weights = pltpu.make_async_copy(w_ref.at[:, pl.ds(start, hidden)], w, load.at[0, 0])
    weights.start()
    arrivals = []
    for at, block in enumerate((me, nx, ny, far)):
        here = rows_of(block, count)
        pair = [
            pltpu.make_async_copy(gu_ref.at[here], gu.at[here], load.at[1, at]),
            pltpu.make_async_copy(act_ref.at[here], act.at[here], load.at[2, at]),
        ]
        for copy in pair:
            copy.start()
        arrivals.append(pair)
    dy = dy_ref[...].astype(BF16).astype(F32)
    by_value, by_gain = normed_gradient(f_ref[...], gain_ref[...], dy)
    df[rows_of(me, count), :] = by_value.astype(BF16)
    spread = Spread(halves_of(df, count), send, recv)
    met()
    spread.start()
    dgain_out[...] = by_gain
    weights.wait()

    def one(block, at):
        here = rows_of(block, count)
        for copy in arrivals[at]:
            copy.wait()

        gate_up_gradient(df, here, w, gu, hidden)
        copy = pltpu.make_async_copy(gu.at[here], dgu_out.at[here], store.at[at])
        copy.start()
        return copy

    copies = [one(me, 0)]
    spread.pass_on()
    spread.x_here()
    copies.append(one(nx, 1))
    spread.y_here()
    copies.append(one(ny, 2))
    spread.far_here()
    copies.append(one(far, 3))

    def make(mine, first, width):
        side = core if mine else 1 - core
        start = pl.multiple_of(side * (hidden // 2) + first, 128)
        return tn(df[...], act[:, pl.ds(start, width)])

    sends, stores = swap_sum(
        make, column_tiles(hidden // 2), ours, theirs, came, swap_send, swap_recv, dw_out, out_sems
    )
    spread.finish()
    for copy in sends:
        copy.wait_send()
    for copy in copies + stores:
        copy.wait()
    if extra_ref is not None:
        extra.wait()


def turn_kernel(
    h_ref, gain_ref, dy_ref, act_ref, w_ref, gu_ref, x_out, dgu_out, dw_out, dgain_out,
    act, w, parts, df, gu, ours, theirs, came, load, store, land, passing, fold_send, fold_recv, send, recv,
    swap_send, swap_recv, out_sems,
):
    count, model = h_ref.shape
    hidden = act.shape[1]
    me, nx, ny = neighbours()
    core = lax.axis_index("section")
    far = jnp.bitwise_xor(me, 3)
    met = greet({"narrow": nx}, {"narrow": ny}, {"section": 1 - core})
    first = w_ref.shape[1] - hidden
    weights = pltpu.make_async_copy(w_ref.at[:, pl.ds(first, hidden)], w, load.at[0, 0])
    weights.start()
    blocks = (far, nx, ny, me)
    for at, block in enumerate(blocks):
        here = rows_of(block, count)
        pltpu.make_async_copy(act_ref.at[here], act.at[here], load.at[1, at]).start()
    for at, block in enumerate(blocks):
        here = rows_of(block, count)
        pltpu.make_async_copy(gu_ref.at[here], gu.at[here], load.at[2, at]).start()

    def here_now(row, at):
        here = rows_of(blocks[at], count)
        src, dst = ((act_ref, act), (gu_ref, gu))[row - 1]
        pltpu.make_async_copy(src.at[here], dst.at[here], load.at[row, at]).wait()
        return here

    fold = Fold(halves_of(parts, count), land, passing, fold_send, fold_recv)
    weights.wait()
    met()

    def part(at):
        here = here_now(1, at)
        return here, nt(act[here, :], w[...])

    here, value = part(0)
    parts[here, :] = value.astype(BF16)
    fold.send_far()
    for at in (1, 2):
        here, value = part(at)
        parts[here, :] = value.astype(BF16)
    fold.send_near()
    _, value = part(3)
    fold.pass_on()
    f = fold.total(value)
    gain = gain_ref[...]
    by_value, by_gain = normed_gradient(f, gain, dy_ref[...])
    df[rows_of(me, count), :] = by_value.astype(BF16)
    spread = Spread(halves_of(df, count), send, recv)
    spread.start()
    dgain_out[...] = by_gain
    x_out[...] = (h_ref[...] + f * inverse_rms(f) * gain).astype(BF16)

    def one(at):
        here = here_now(2, at)
        gate_up_gradient(df, here, w, gu, hidden)
        copy = pltpu.make_async_copy(gu.at[here], dgu_out.at[here], store.at[at])
        copy.start()
        return copy

    copies = [one(3)]
    spread.pass_on()
    spread.x_here()
    copies.append(one(1))
    spread.y_here()
    copies.append(one(2))
    spread.far_here()
    copies.append(one(0))

    def make(mine, first, width):
        side = core if mine else 1 - core
        start = pl.multiple_of(side * (hidden // 2) + first, 128)
        return tn(df[...], act[:, pl.ds(start, width)])

    sends, stores = swap_sum(
        make, column_tiles(hidden // 2), ours, theirs, came, swap_send, swap_recv, dw_out, out_sems
    )
    spread.finish()
    fold.finish()
    for copy in sends:
        copy.wait_send()
    for copy in copies + stores:
        copy.wait()


def feed_turn(h, gain, dy, act, w_dt, gu, collective_id):
    count, model = h.shape
    total, hidden = act.shape
    tiles = pltpu.SemaphoreType.DMA((len(column_tiles(hidden // 2)),))
    dw = pltpu.VMEM((model, hidden // 2), BF16)
    return pl.pallas_call(
        turn_kernel,
        out_shape=[
            jax.ShapeDtypeStruct((count, model), BF16),
            jax.ShapeDtypeStruct(gu.shape, BF16),
            jax.ShapeDtypeStruct((model, hidden // 2), BF16),
            jax.ShapeDtypeStruct((1, model), F32),
        ],
        in_specs=[vmem_spec()] * 3 + [any_spec()] * 3,
        out_specs=[vmem_spec(), any_spec(), any_spec(), vmem_spec()],
        scratch_shapes=[
            pltpu.VMEM(act.shape, BF16),
            pltpu.VMEM((model, hidden), BF16),
            pltpu.VMEM((total, model), BF16),
            pltpu.VMEM((total, model), BF16),
            pltpu.VMEM(gu.shape, BF16),
            dw,
            dw,
            dw,
            pltpu.SemaphoreType.DMA((3, 4)),
            pltpu.SemaphoreType.DMA((4,)),
            *fold_spec(count, model),
            *spread_spec(),
            tiles,
            tiles,
            tiles,
        ],
        compiler_params=params(collective_id, 60),
    )(h, gain, dy, act, w_dt, gu)


def feed_back_up(dy, f, gain, gu, act, w_dt, extra, collective_id):
    count, model = dy.shape
    total, hidden = act.shape
    tiles = len(column_tiles(hidden // 2))
    extras = extra
    return pl.pallas_call(
        back_up_kernel,
        out_shape=[
            jax.ShapeDtypeStruct(gu.shape, BF16),
            jax.ShapeDtypeStruct((model, hidden // 2 + sum(e.shape[1] for e in extras[:-1])), BF16),
            jax.ShapeDtypeStruct((1, model), F32),
        ],
        in_specs=[vmem_spec()] * 3 + [any_spec()] * (3 + len(extras)),
        out_specs=[any_spec(), any_spec(), vmem_spec()],
        scratch_shapes=[
            pltpu.VMEM((total, model), BF16),
            pltpu.VMEM(gu.shape, BF16),
            pltpu.VMEM(act.shape, BF16),
            pltpu.VMEM((model, hidden), BF16),
            pltpu.VMEM((model, hidden // 2), BF16),
            pltpu.VMEM((model, hidden // 2), BF16),
            pltpu.VMEM((model, hidden // 2), BF16),
            pltpu.SemaphoreType.DMA((3, 4)),
            pltpu.SemaphoreType.DMA((4,)),
            *spread_spec(),
            pltpu.SemaphoreType.DMA((tiles,)),
            pltpu.SemaphoreType.DMA((tiles,)),
            pltpu.SemaphoreType.DMA((tiles,)),
        ],
        compiler_params=params(collective_id, 60),
    )(dy, f, gain, gu, act, w_dt, *extras)


def back_down_kernel(
    dy_ref, h_ref, gain_ref, dgu_ref, rows_ref, w_ref, dh_out, dw_out, dgain_out,
    dgu, rows, w, parts, ours, theirs, came, load, land, passing, send, recv, swap_send, swap_recv, out_sems,
):
    count, model = dy_ref.shape
    hidden = dgu.shape[1] // 2
    me, nx, ny = neighbours()
    core = lax.axis_index("section")
    far = jnp.bitwise_xor(me, 3)
    met = greet({"narrow": nx}, {"narrow": ny}, {"section": 1 - core})
    weights = pltpu.make_async_copy(w_ref.at[:, pl.ds(0, 2 * hidden)], w, load.at[0])
    weights.start()
    arrivals = []
    for at, block in enumerate((far, nx, ny, me)):
        here = rows_of(block, count)
        arrivals.append(pltpu.make_async_copy(dgu_ref.at[here], dgu.at[here], load.at[1 + at]))
        arrivals[-1].start()
    kept = pltpu.make_async_copy(rows_ref, rows, load.at[5])
    kept.start()
    fold = Fold(halves_of(parts, count), land, passing, send, recv)
    weights.wait()
    met()

    def one(block, at, out, here):
        arrivals[at].wait()
        out[here, :] = nt(dgu[rows_of(block, count), :], w[...]).astype(out.dtype)

    one(far, 0, parts, rows_of(far, count))
    fold.send_far()
    one(nx, 1, parts, rows_of(nx, count))
    one(ny, 2, parts, rows_of(ny, count))
    fold.send_near()
    one(me, 3, dh_out, pl.ds(0, count))
    fold.pass_on()
    kept.wait()

    def make(mine, first, width):
        side = core if mine else 1 - core
        start = pl.multiple_of(side * hidden + first, 128)
        return tn(rows[...], dgu[:, pl.ds(start, width)])

    sends, stores = swap_sum(
        make, column_tiles(hidden), ours, theirs, came, swap_send, swap_recv, dw_out, out_sems
    )
    total = fold.total(dh_out[...])
    by_value, by_gain = normed_gradient(h_ref[...], gain_ref[...], total)
    dh_out[...] = dy_ref[...].astype(BF16).astype(F32) + by_value
    dgain_out[...] = by_gain
    fold.finish()
    for copy in sends:
        copy.wait_send()
    for copy in stores:
        copy.wait()


def feed_back_down(dy, h, gain, dgu, rows, w_gu, collective_id):
    count, model = dy.shape
    total, hidden = dgu.shape[0], dgu.shape[1] // 2
    tiles = len(column_tiles(hidden))
    return pl.pallas_call(
        back_down_kernel,
        out_shape=[
            jax.ShapeDtypeStruct((count, model), F32),
            jax.ShapeDtypeStruct((model, hidden), BF16),
            jax.ShapeDtypeStruct((1, model), F32),
        ],
        in_specs=[vmem_spec()] * 3 + [any_spec()] * 3,
        out_specs=[vmem_spec(), any_spec(), vmem_spec()],
        scratch_shapes=[
            pltpu.VMEM(dgu.shape, BF16),
            pltpu.VMEM(rows.shape, BF16),
            pltpu.VMEM((model, 2 * hidden), BF16),
            pltpu.VMEM((total, model), BF16),
            pltpu.VMEM((model, hidden), BF16),
            pltpu.VMEM((model, hidden), BF16),
            pltpu.VMEM((model, hidden), BF16),
            pltpu.SemaphoreType.DMA((6,)),
            *fold_spec(count, model),
            pltpu.SemaphoreType.DMA((tiles,)),
            pltpu.SemaphoreType.DMA((tiles,)),
            pltpu.SemaphoreType.DMA((tiles,)),
        ],
        compiler_params=params(collective_id, 60),
    )(dy, h, gain, dgu, rows, w_gu)


def pack_kernel(p_ref, o_ref, g_ref, local, send, recv, peer_send, peer_recv):
    model, width = o_ref.shape[2:]
    half = model // 2
    wides, extra = g_ref.shape[1:3]
    rows = model // wides
    core = lax.axis_index("section")
    me, nx, ny = neighbours()
    met = greet({"narrow": nx}, {"narrow": ny}, {"section": 1 - core})
    whole = p_ref.shape[0] == model
    owns = []
    if whole:
        owns.append(pltpu.make_async_copy(p_ref, o_ref.at[core, me], local.at[0, 0]))
    else:
        for w in range(wides):
            first = w * (rows + extra)
            place = o_ref.at[core, me, pl.ds(w * rows, rows)]
            owns.append(pltpu.make_async_copy(p_ref.at[pl.ds(first, rows)], place, local.at[0, w]))
            part = p_ref.at[pl.ds(first + rows, extra)]
            owns.append(pltpu.make_async_copy(part, g_ref.at[core, w], local.at[1, w]))
    start_all(owns)
    spread = Spread(lambda block, which: o_ref.at[core, block, pl.ds(which * half, half)], send, recv)
    wait_all(owns)
    met()
    spread.start()
    copies = []

    def across(ref):
        copy = pltpu.make_async_remote_copy(
            src_ref=ref,
            dst_ref=ref,
            send_sem=peer_send.at[len(copies)],
            recv_sem=peer_recv.at[len(copies)],
            device_id={"section": 1 - core},
            device_id_type=MESH,
        )
        copy.start()
        copies.append(copy)

    if not whole:
        across(g_ref.at[core])
    across(o_ref.at[core, me])
    spread.pass_on()
    spread.x_here()
    across(o_ref.at[core, nx])
    spread.y_here()
    across(o_ref.at[core, ny])
    spread.far_here()
    across(o_ref.at[core, spread.far])
    for copy in copies:
        copy.wait_recv()
    spread.finish()
    for copy in copies:
        copy.wait_send()


def gather_pack(pack, model, wides, collective_id):
    width = pack.shape[1]
    return pl.pallas_call(
        pack_kernel,
        out_shape=[
            jax.ShapeDtypeStruct((2, 4, model, width), pack.dtype),
            jax.ShapeDtypeStruct((2, wides, GAIN_ROWS, width), pack.dtype),
        ],
        in_specs=[any_spec()],
        out_specs=[vmem_spec()] * 2,
        scratch_shapes=[
            pltpu.SemaphoreType.DMA((2, wides)),
            *spread_spec(),
            pltpu.SemaphoreType.DMA((5,)),
            pltpu.SemaphoreType.DMA((5,)),
        ],
        compiler_params=params(collective_id, 32),
    )(pack)


def finish_kernel(
    zero_ref, one_ref, early_ref, dep_ref, q_out, kv_out, o_out, came, kv, send, recv, kv_send, kv_recv
):
    core = lax.axis_index("section")
    me, nx, ny = neighbours()
    others = (nx, ny, jnp.bitwise_xor(me, 3))
    met = greet({"section": 1 - core}, *[{"narrow": other} for other in others])
    head = q_out.shape[1]
    first = core == 0
    by_qkv = jnp.where(first, zero_ref[...], early_ref[...])
    kv[me] = by_qkv[:, head:]
    met()
    across = pltpu.make_async_remote_copy(
        src_ref=zero_ref,
        dst_ref=came,
        send_sem=send,
        recv_sem=recv,
        device_id={"section": 1 - core},
        device_id_type=MESH,
    )
    across.start()
    copies = []
    for at, other in enumerate(others):
        copies.append(remote(kv.at[me], kv.at[me], kv_send.at[at], kv_recv.at[at], other))
        copies[-1].start()
    q_out[...] = by_qkv[:, :head].astype(F32)
    across.wait_recv()
    o_out[...] = jnp.where(first, came[:, :head], one_ref[:, :head]).astype(F32)
    for copy in copies:
        copy.wait_recv()
    width = kv.shape[2]
    for n in range(4):
        kv_out[:, n * width : (n + 1) * width] = kv[n].astype(F32)
    across.wait_send()
    for copy in copies:
        copy.wait_send()


def finish_attention(zero, one, early, dep, head, collective_id):
    block, width = zero.shape
    return pl.pallas_call(
        finish_kernel,
        out_shape=[
            jax.ShapeDtypeStruct((block, head), F32),
            jax.ShapeDtypeStruct((block, 4 * (width - head)), F32),
            jax.ShapeDtypeStruct((block, head), F32),
        ],
        in_specs=[vmem_spec()] * 3 + [any_spec()],
        out_specs=[vmem_spec()] * 3,
        scratch_shapes=[
            pltpu.VMEM((block, width), BF16),
            pltpu.VMEM((4, block, width - head), BF16),
            pltpu.SemaphoreType.DMA,
            pltpu.SemaphoreType.DMA,
            pltpu.SemaphoreType.DMA((3,)),
            pltpu.SemaphoreType.DMA((3,)),
        ],
        compiler_params=params(collective_id, 16),
    )(zero, one, early, dep)


def pair_kernel(zero_ref, one_ref, came_zero_ref, came_one_ref, out_ref, flag_ref):
    hidden = out_ref.shape[2]
    first = lax.axis_index("section") == 0
    keep = jnp.where(first, zero_ref[:, :hidden], one_ref[:, :hidden])
    came = jnp.where(first, came_zero_ref[:, :hidden], came_one_ref[:, :hidden])
    out_ref[:, 0, :] = jnp.where(first, keep, came).astype(F32)
    out_ref[:, 1, :] = jnp.where(first, came, keep).astype(F32)
    flag_ref[...] = jnp.zeros_like(flag_ref)


def pair_up(zero, one, came_zero, came_one, hidden):
    return pl.pallas_call(
        pair_kernel,
        out_shape=[
            jax.ShapeDtypeStruct((zero.shape[0], 2, hidden), F32),
            jax.ShapeDtypeStruct((8, 128), F32),
        ],
        in_specs=[vmem_spec()] * 4,
        out_specs=[vmem_spec()] * 2,
        compiler_params=pltpu.CompilerParams(vmem_limit_bytes=40 * MIB),
    )(zero, one, came_zero, came_one)


class Share:
    def __init__(self, xn_ref, o_ref, xn, o, loads, spread_send, spread_recv, deal_send, deal_recv):
        count, head = xn_ref.shape[0], o.shape[1]
        me = lax.axis_index("narrow")
        self.loads = [
            pltpu.make_async_copy(xn_ref, xn.at[rows_of(me, count)], loads.at[0]),
            pltpu.make_async_copy(o_ref.at[:, columns_of(me, head)], o.at[rows_of(me, count)], loads.at[1]),
        ]
        self.spread = Spread(halves_of(xn, count), spread_send, spread_recv)
        self.deal = Deal(
            lambda other: o_ref.at[:, columns_of(other, head)],
            lambda mine: o.at[rows_of(mine, count)],
            deal_send,
            deal_recv,
        )

    def start_rows(self):
        self.loads[0].start()
        self.loads[0].wait()
        self.spread.start()

    def start_deal(self):
        self.loads[1].start()
        self.deal.start()

    def all_here(self):
        self.spread.all_here()
        self.deal.here()

    def finish(self):
        self.spread.finish()
        self.deal.finish()
        self.loads[1].wait()


def share_spec(count, model, head):
    return [
        pltpu.VMEM((4 * count, model), BF16),
        pltpu.VMEM((4 * count, head), BF16),
        pltpu.SemaphoreType.DMA((4,)),
        *spread_spec(),
        pltpu.SemaphoreType.DMA((3,)),
        pltpu.SemaphoreType.DMA((3,)),
    ]


def share_shapes(xn, o):
    total = 4 * xn.shape[0]
    return [
        jax.ShapeDtypeStruct((total, xn.shape[1]), BF16),
        jax.ShapeDtypeStruct((total, o.shape[1] // 4), BF16),
    ]


def gain_stages():
    wides = lax.axis_size("wide")
    core, wide = lax.axis_index("section"), lax.axis_index("wide")
    me, nx, ny = neighbours()
    return [
        [{"narrow": nx}, {"narrow": ny}, {"narrow": jnp.bitwise_xor(me, 3)}],
        [{"section": 1 - core}],
        [{"wide": lax.rem(wide + step, wides)} for step in range(1, wides)],
    ]


class GainSum:
    def __init__(self, land, total, send, recv):
        self.land, self.total, self.send, self.recv = land, total, send, recv
        self.copies = []
        self.waiting = []

    def start(self, stage):
        for other in gain_stages()[stage]:
            at = len(self.copies)
            copy = pltpu.make_async_remote_copy(
                src_ref=self.total.at[stage],
                dst_ref=self.land.at[at],
                send_sem=self.send.at[at],
                recv_sem=self.recv.at[at],
                device_id=other,
                device_id_type=MESH,
            )
            copy.start()
            self.copies.append(copy)
            self.waiting.append(at)

    def add(self, stage):
        value = self.total[stage]
        for at in self.waiting:
            self.copies[at].wait_recv()
            value = value + self.land[at]
        self.waiting = []
        self.total[stage + 1] = value

    def close(self):
        for copy in self.copies:
            copy.wait_send()


def gain_spec(wides, shape):
    return [
        pltpu.VMEM((wides + 3, *shape), F32),
        pltpu.VMEM((4, *shape), F32),
        pltpu.SemaphoreType.DMA((wides + 3,)),
        pltpu.SemaphoreType.DMA((wides + 3,)),
    ]


def trade_kernel(keep_ref, give_ref, zero_ref, one_ref, came, send, recv):
    core = lax.axis_index("section")
    met = greet({"section": 1 - core})
    met()
    copy = pltpu.make_async_remote_copy(
        src_ref=give_ref,
        dst_ref=came,
        send_sem=send,
        recv_sem=recv,
        device_id={"section": 1 - core},
        device_id_type=MESH,
    )
    copy.start()

    @pl.when(core == 0)
    def _():
        zero_ref[...] = keep_ref[...]

    @pl.when(core == 1)
    def _():
        one_ref[...] = keep_ref[...]

    copy.wait_recv()

    @pl.when(core == 0)
    def _():
        one_ref[...] = came[...]

    @pl.when(core == 1)
    def _():
        zero_ref[...] = came[...]

    copy.wait_send()


def trade(keep, give, collective_id):
    shape = jax.ShapeDtypeStruct(keep.shape, keep.dtype)
    return pl.pallas_call(
        trade_kernel,
        out_shape=[shape, shape],
        in_specs=[vmem_spec()] * 2,
        out_specs=[vmem_spec()] * 2,
        scratch_shapes=[
            pltpu.VMEM(keep.shape, keep.dtype),
            pltpu.SemaphoreType.DMA,
            pltpu.SemaphoreType.DMA,
        ],
        compiler_params=params(collective_id, 16),
    )(keep, give)


def turn_back(grad, cosine, sine_table):
    half = grad.shape[1] // 2
    front, back = grad[:, :half], grad[:, half:]
    return jnp.concatenate(
        [front * cosine + back * sine_table, back * cosine - front * sine_table], axis=1
    )


def pack_loads(pack_ref, layer, head, wq, wot, wkv, sems):
    kv_part = wkv.shape[1] // 4
    loads = []
    for at, (w, first, width) in enumerate(
        ((wq, 0, head), (wot, head, head), (wkv, 2 * head, kv_part))
    ):
        loads.append(
            [
                pltpu.make_async_copy(
                    pack_ref.at[layer, n, :, pl.ds(first, width)], w.at[:, pl.ds(n * width, width)], sems.at[at, n]
                )
                for n in range(4)
            ]
        )
    return loads


def start_all(copies):
    for copy in copies:
        copy.start()


def wait_all(copies):
    for copy in copies:
        copy.wait()


def window_mask(me, count, window, length):
    rows_at = me * count + lax.broadcasted_iota(jnp.int32, (count, 1), 0)
    cols_at = me * count - WINDOW + lax.broadcasted_iota(jnp.int32, (1, window), 1)
    return (
        (cols_at <= rows_at)
        & (rows_at - cols_at < WINDOW)
        & (cols_at >= 0)
        & ((cols_at < length) | (cols_at == rows_at))
    )


def attend_kernel(layer, length_ref, x_ref, gains_ref, head_ref, trig_ref, pack_ref, *refs):
    (
        h_out, xn_out, q_out, k_out, win_out, lse_out, o_out, a_out, *refs
    ) = refs
    sharing = len(refs) > 9
    if sharing:
        xn_all_out, o_all_out, *refs = refs
    kv, wq, wot, wkv, load, send, recv, *share_refs = refs
    count, model = x_ref.shape
    head = k_out.shape[1]
    heads = q_out.shape[1] // head
    me, nx, ny = neighbours()
    met = greet({"narrow": nx}, {"narrow": ny}, {"narrow": jnp.bitwise_xor(me, 3)})
    q_loads, out_loads, kv_loads = pack_loads(pack_ref, layer, head, wq, wot, wkv, load)
    start_all(kv_loads + q_loads + out_loads)
    scaling = head ** (-0.5)
    cosine, sine_table = trig_ref[:, : head // 2], trig_ref[:, head // 2 :]
    x = x_ref[...].astype(F32)
    xn_out[...] = (x * inverse_rms(x) * gains_ref[0:1, :]).astype(BF16)
    kv[pl.ds(0, WINDOW), :] = jnp.zeros((WINDOW, 2 * head), BF16)
    wait_all(kv_loads)
    raw = nn(xn_out[...], wkv[...])
    k_raw = raw[:, :head]
    k_out[...] = k_raw
    k_rot = rotate(k_raw * inverse_rms(k_raw) * head_ref[1:2, :], cosine, sine_table)
    here = pl.ds(pl.multiple_of(WINDOW + me * count, count), count)
    kv[here, :head] = k_rot.astype(BF16)
    kv[here, head:] = raw[:, head:].astype(BF16)
    spread = Spread(halves_of(kv, count, WINDOW), send, recv)
    met()
    spread.start()
    if sharing:
        share = Share(xn_out, o_out, *share_refs)
    wait_all(q_loads)
    q_out[...] = nn(xn_out[...], wq[...])
    spread.pass_on()
    if sharing:
        share.start_rows()
    spread.all_here()
    window = win_out.shape[0]
    win_out[...] = kv[pl.ds(pl.multiple_of(me * count, count), window), :]
    visible = window_mask(me, count, window, length_ref[0])
    k_win, v_win = win_out[:, :head], win_out[:, head:]
    q_gain = head_ref[0:1, :]

    def one_head(i):
        columns = columns_of(i, head)
        q_raw = q_out[:, columns]
        qr = rotate(q_raw * inverse_rms(q_raw) * q_gain, cosine, sine_table).astype(BF16)
        scores = jnp.where(visible, nt(qr, k_win) * scaling, NEGATIVE)
        most = jnp.max(scores, axis=-1, keepdims=True)
        exponent = jnp.exp(scores - most)
        total = jnp.sum(exponent, axis=-1, keepdims=True)
        lse_out[i] = most + jnp.log(total)
        o_out[:, columns] = nn((exponent / total).astype(BF16), v_win).astype(BF16)

    for i in range(heads):
        one_head(i)
    if sharing:
        share.start_deal()
        share.spread.pass_on()
    wait_all(out_loads)
    a = nt(o_out[...], wot[...])
    a_out[...] = a
    h_out[...] = x_ref[...].astype(F32) + a * inverse_rms(a) * gains_ref[1:2, :]
    spread.finish()
    if sharing:
        share.all_here()
        share.finish()
        xn, o, loads = share_refs[:3]
        stores = [
            pltpu.make_async_copy(xn, xn_all_out, loads.at[2]),
            pltpu.make_async_copy(o, o_all_out, loads.at[3]),
        ]
        start_all(stores)
        wait_all(stores)


def attend(length, x, gains, head_gains, trig, pack, head, layer, collective_id):
    count, model = x.shape
    kv_width = 2 * head
    width = 4 * head
    window = count + WINDOW
    sharing = True
    xn_shape = jax.ShapeDtypeStruct((count, model), BF16)
    o_shape = jax.ShapeDtypeStruct((count, width), BF16)
    shapes = [
        jax.ShapeDtypeStruct((count, model), F32),
        xn_shape,
        jax.ShapeDtypeStruct((count, width), F32),
        jax.ShapeDtypeStruct((count, head), F32),
        jax.ShapeDtypeStruct((window, kv_width), BF16),
        jax.ShapeDtypeStruct((4, count, 1), F32),
        o_shape,
        jax.ShapeDtypeStruct((count, model), F32),
    ]
    outs = [vmem_spec()] * 8
    if sharing:
        shapes += share_shapes(xn_shape, o_shape)
        outs += [any_spec()] * 2
    return pl.pallas_call(
        functools.partial(attend_kernel, layer),
        out_shape=shapes,
        in_specs=[pl.BlockSpec(memory_space=pltpu.SMEM)] + [vmem_spec()] * 4 + [any_spec()],
        out_specs=outs,
        scratch_shapes=[
            pltpu.VMEM((4 * count + WINDOW, kv_width), BF16),
            pltpu.VMEM((model, width), BF16),
            pltpu.VMEM((model, width), BF16),
            pltpu.VMEM((model, kv_width), BF16),
            pltpu.SemaphoreType.DMA((3, 4)),
            *spread_spec(),
            *(share_spec(count, model, head) if sharing else []),
        ],
        compiler_params=params(collective_id, 40),
    )(length, x, gains, head_gains, trig, pack)


def attend_back_kernel(
    layer, length_ref, dh_ref, a_ref, x_ref, gains_ref, head_ref, trig_ref, q_ref, k_ref, win_ref, lse_ref,
    pack_ref, xn_ref, o_ref, *refs
):
    if layer == 0:
        block_ref, dx_one_ref, lined_ref, early_ref, *refs = refs
        block_out, both_out, lined_out, came_out, q_out, kv_out, o_out = refs[4:11]
        refs = refs[:4] + refs[11:]
        gain_refs, (dx_give, dx_send, dx_recv), line_refs = refs[36:40], refs[40:43], refs[43:]
        refs = refs[:36]
    (
    dx_out, dw_out, dgain_out, dhead_out,
    da, do, dq, dk, dv, parts, dq_all, dkv, dkv_all, wq, wot, wkv, xn, o, ours, theirs, came,
    pack_load, load, send, recv, land, passing, fold_send, fold_recv, q_send, q_recv, kv_send, kv_recv, swap_send, swap_recv, out_sem,
    ) = refs
    count = dh_ref.shape[0]
    head = k_ref.shape[1]
    heads = q_ref.shape[1] // head
    kv_part = dkv_all.shape[1]
    me, nx, ny = neighbours()
    core = lax.axis_index("section")
    far = jnp.bitwise_xor(me, 3)
    lined = layer == 0 and len(line_refs) > 0
    if layer == 0:
        met = greet(*sum(gain_stages(), []))
        sums = GainSum(*gain_refs)
    else:
        met = greet({"narrow": nx}, {"narrow": ny}, {"narrow": far}, {"section": 1 - core})
    if lined:
        line = LineSum(lined_ref, lined_out, *line_refs[:7])
        early = LineSum(early_ref, None, *line_refs[7:14])
        late = LineSum(ours, None, *line_refs[14:21])
        came_line, came_store, came_early, came_late, kv_all, cross_send, cross_recv, narrow_send, narrow_recv = (
            line_refs[21:]
        )

        def across(at, src, dst):
            return pltpu.make_async_remote_copy(
                src_ref=src,
                dst_ref=dst,
                send_sem=cross_send.at[at],
                recv_sem=cross_recv.at[at],
                device_id={"section": 1 - core},
                device_id_type=MESH,
            )

        early.load()
        line.load()
    q_loads, out_loads, kv_loads = pack_loads(pack_ref, layer, head, wq, wot, wkv, pack_load)
    loads = [
        pltpu.make_async_copy(src, dst, load.at[at])
        for at, (src, dst) in enumerate(((xn_ref, xn), (o_ref, o)))
    ]
    start_all(out_loads + q_loads + kv_loads + loads)
    here = rows_of(me, count)
    scaling = head ** (-0.5)
    cosine, sine_table = trig_ref[:, : head // 2], trig_ref[:, head // 2 :]

    dh = dh_ref[...]
    by_value, dg1 = normed_gradient(a_ref[...], gains_ref[1:2, :], dh)
    da[here, :] = by_value.astype(BF16)
    dgain_out[1:2, :] = dg1
    spread = Spread(halves_of(da, count), send, recv)
    met()
    spread.start()
    if lined:
        early.begin()
        line.begin()
    wait_all(out_loads)
    do[...] = nn(da[here, :], wot[...]).astype(BF16)

    visible = window_mask(me, count, win_ref.shape[0], length_ref[0])
    k_win, v_win = win_ref[:, :head], win_ref[:, head:]
    dk[...] = jnp.zeros_like(dk)
    dv[...] = jnp.zeros_like(dv)
    dhead_out[...] = jnp.zeros_like(dhead_out)
    q_gain, k_gain = head_ref[0:1, :], head_ref[1:2, :]

    def one_head(i):
        columns = columns_of(i, head)
        raw = q_ref[:, columns]
        inverse = inverse_rms(raw)
        unit = raw * inverse
        qr = rotate(unit * q_gain, cosine, sine_table).astype(BF16)
        scores = jnp.where(visible, nt(qr, k_win) * scaling, NEGATIVE)
        probs = jnp.exp(scores - lse_ref[i])
        do_head = do[:, columns]
        dp = nt(do_head, v_win)
        ds = (probs * (dp - jnp.sum(probs * dp, axis=-1, keepdims=True))).astype(BF16)
        dk[...] += tn(ds, qr)
        dv[...] += tn(probs.astype(BF16), do_head)
        grad = turn_back(nn(ds, k_win) * scaling, cosine, sine_table)
        scaled = grad * q_gain
        dq_raw = inverse * (scaled - unit * jnp.mean(scaled * unit, axis=-1, keepdims=True))
        dq[:, columns] = dq_raw.astype(BF16)
        dhead_out[0:1, :] += jnp.sum(grad * unit, axis=0, keepdims=True)

    for i in range(heads):
        one_head(i)
    parts[...] = jnp.zeros_like(parts)
    window = pl.ds(pl.multiple_of(me * count, count), win_ref.shape[0])
    parts[window, :head] = (dk[...] * scaling).astype(BF16)
    parts[window, head:] = dv[...].astype(BF16)
    fold = Fold(halves_of(parts, count, WINDOW), land, passing, fold_send, fold_recv)
    fold.send_far()
    fold.send_near()
    deal_q = Deal(
        lambda other: dq.at[:, columns_of(other, head)],
        lambda mine: dq_all.at[rows_of(mine, count)],
        q_send,
        q_recv,
    )
    deal_q.start()
    dq_all[here, :] = dq[:, columns_of(me, head)]
    spread.pass_on()
    if lined:
        early.step(1, 0)
        line.step(1, 0)
    wait_all(q_loads)
    dx_out[...] = nt(dq[...], wq[...])
    fold.pass_on()
    spread.all_here()
    wait_all(loads)
    first = core == 0
    swaps = []

    def exchange(at, columns, a, b):
        ours[:, columns] = jnp.where(first, a, b).astype(BF16)
        theirs[:, columns] = jnp.where(first, b, a).astype(BF16)
        copy = pltpu.make_async_remote_copy(
            src_ref=theirs.at[:, columns],
            dst_ref=came.at[:, columns],
            send_sem=swap_send.at[at],
            recv_sem=swap_recv.at[at],
            device_id={"section": 1 - core},
            device_id_type=MESH,
        )
        copy.start()
        swaps.append(copy)

    if lined:
        line.step(1, 1)
    by_out = tn(da[...], o[...])
    deal_q.here()
    exchange(0, pl.ds(0, head), tn(xn[...], dq_all[...]), by_out)
    own = jnp.concatenate([dk[WINDOW:, :] * scaling, dv[WINDOW:, :]], axis=1)
    total = fold.total(own)
    grad = turn_back(total[:, :head], cosine, sine_table)
    dk_raw, dk_gain = normed_gradient(k_ref[...], k_gain, grad)
    dhead_out[1:2, :] = dk_gain
    dkv[:, :head] = dk_raw.astype(BF16)
    dkv[:, head:] = total[:, head:].astype(BF16)
    deal_kv = Deal(
        lambda other: dkv.at[:, columns_of(other, kv_part)],
        lambda mine: dkv_all.at[rows_of(mine, count)],
        kv_send,
        kv_recv,
    )
    deal_kv.start()
    dkv_all[here, :] = dkv[:, columns_of(me, kv_part)]
    wait_all(kv_loads)
    dxn = dx_out[...] + nt(dkv[...], wkv[...])
    by_value, dg0 = normed_gradient(x_ref[...].astype(F32), gains_ref[0:1, :], dxn)
    dx_out[...] = dh_ref[...] + by_value
    dgain_out[0:1, :] = dg0
    if layer == 0:
        zero = core == 0
        both_out[core] = jnp.where(zero, dx_out[...], dx_one_ref[...])
        dx_give[...] = jnp.where(zero, dx_one_ref[...], dx_out[...])
        dx_copy = pltpu.make_async_remote_copy(
            src_ref=dx_give,
            dst_ref=both_out.at[core],
            send_sem=dx_send,
            recv_sem=dx_recv,
            device_id={"section": 1 - core},
            device_id_type=MESH,
        )
        dx_copy.start()
    if lined:
        line.step(2, 0)
        for step in range(2, early.steps):
            early.step(step, 0)
    if layer == 0:
        own_total = sums.total.at[0]
        own_total[...] = block_ref[...]
        own_total[0:2, :] = dgain_out[...]
        own_total[4:5, :head] = dhead_out[0:1, :]
        own_total[4:5, head : 2 * head] = dhead_out[1:2, :]
        sums.start(0)

    deal_kv.here()
    by_kv = tn(xn[...], dkv_all[...])
    if layer == 0:
        sums.add(0)
        sums.start(1)
    exchange(1, pl.ds(head, kv_part), by_kv, jnp.zeros_like(by_kv))
    for copy in swaps:
        copy.wait_recv()
    ours[...] = (ours[...].astype(F32) + came[...].astype(F32)).astype(BF16)
    out = pltpu.make_async_copy(ours, dw_out, out_sem)
    out.start()
    if layer == 0:
        sums.add(1)
        sums.start(2)
    if lined:
        late.load()
        late.begin()
        for step in range(2, line.steps):
            if step > 2:
                line.step(step, 0)
            late.step(step - 1, 0)
            line.step(step, 1)
        early.end()
        crosses = [across(0, early.result, came_early)]
        crosses[0].start()
        late.step(late.steps - 1, 0)
        line.folds[0].finish(line.result)
        half = line.folds[0].columns
        crosses.append(across(1, line.result.at[:, half], came_line.at[:, half]))
        crosses[1].start()
        late.end()
        crosses.append(across(2, late.result, came_late))
        crosses[2].start()
        crosses[0].wait_recv()
        by_qkv = jnp.where(zero, late.result[...], came_early[...])
        kv_all[me] = by_qkv[:, head:]
        narrows = [
            remote(kv_all.at[me], kv_all.at[me], narrow_send.at[at], narrow_recv.at[at], other)
            for at, other in enumerate((nx, ny, far))
        ]
        start_all(narrows)
        q_out[...] = by_qkv[:, :head].astype(F32)
        crosses[2].wait_recv()
        o_out[...] = jnp.where(zero, came_late[:, :head], early.result[:, :head]).astype(F32)
        for copy in narrows:
            copy.wait_recv()
        for n in range(4):
            kv_out[:, n * kv_part : (n + 1) * kv_part] = kv_all[n].astype(F32)
        rest = line.folds[1].columns
        line.folds[1].finish(line.result)
        crosses.append(across(3, line.result.at[:, rest], came_line.at[:, rest]))
        crosses[3].start()
        line.end(2)
        crosses[1].wait_recv()
        crosses[3].wait_recv()
        keep = pltpu.make_async_copy(came_line, came_out, came_store)
        keep.start()
        for copy in crosses + narrows:
            copy.wait_send()
        keep.wait()
    if layer == 0:
        dx_copy.wait_recv()
        dx_copy.wait_send()
    if layer == 0:
        sums.add(2)
        block_out[...] = sums.total[3]
        sums.close()
    spread.finish()
    fold.finish()
    deal_q.finish()
    deal_kv.finish()
    for copy in swaps:
        copy.wait_send()
    out.wait()


def attend_back(length, dh, a, x, gains, head_gains, trig, q_raw, k_raw, window, lse, pack, xn, o, deps, layer, collective_id):
    count, model = dh.shape
    head = k_raw.shape[1]
    width = q_raw.shape[1]
    kv_part = pack.shape[3] - 2 * head
    if layer == 0:
        wides = lax.axis_size("wide")
        block, dx_one, lined, early = deps
        rows = model // wides
    deal = pltpu.SemaphoreType.DMA((3,))
    dw = pltpu.VMEM((model, head + kv_part), BF16)
    return pl.pallas_call(
        functools.partial(attend_back_kernel, layer),
        out_shape=[
            jax.ShapeDtypeStruct((count, model), F32),
            jax.ShapeDtypeStruct((model, head + kv_part), BF16),
            jax.ShapeDtypeStruct((2, model), F32),
            jax.ShapeDtypeStruct((2, head), F32),
            *(
                [
                    jax.ShapeDtypeStruct(block.shape, F32),
                    jax.ShapeDtypeStruct((2, count, model), F32),
                    jax.ShapeDtypeStruct((rows, lined.shape[1]), BF16),
                    jax.ShapeDtypeStruct((rows, lined.shape[1]), BF16),
                    jax.ShapeDtypeStruct((rows, head), F32),
                    jax.ShapeDtypeStruct((rows, 4 * kv_part), F32),
                    jax.ShapeDtypeStruct((rows, head), F32),
                ]
                if layer == 0
                else []
            ),
        ],
        in_specs=[pl.BlockSpec(memory_space=pltpu.SMEM)] + [vmem_spec()] * 10 + [any_spec()] * 3 + ([vmem_spec()] * 2 + [any_spec()] * 2 if layer == 0 else []),
        out_specs=[vmem_spec(), any_spec(), vmem_spec(), vmem_spec()]
        + ([vmem_spec()] * 2 + [any_spec()] * 2 + [vmem_spec()] * 3 if layer == 0 else []),
        scratch_shapes=[
            pltpu.VMEM((4 * count, model), BF16),
            pltpu.VMEM((count, width), BF16),
            pltpu.VMEM((count, width), BF16),
            pltpu.VMEM((window.shape[0], head), F32),
            pltpu.VMEM((window.shape[0], head), F32),
            pltpu.VMEM((4 * count + WINDOW, 2 * head), BF16),
            pltpu.VMEM((4 * count, head), BF16),
            pltpu.VMEM((count, 2 * head), BF16),
            pltpu.VMEM((4 * count, kv_part), BF16),
            pltpu.VMEM((model, width), BF16),
            pltpu.VMEM((model, width), BF16),
            pltpu.VMEM((model, 2 * head), BF16),
            pltpu.VMEM(xn.shape, BF16),
            pltpu.VMEM(o.shape, BF16),
            dw,
            dw,
            dw,
            pltpu.SemaphoreType.DMA((3, 4)),
            pltpu.SemaphoreType.DMA((2,)),
            *spread_spec(),
            *fold_spec(count, 2 * head),
            deal,
            deal,
            deal,
            deal,
            pltpu.SemaphoreType.DMA((2,)),
            pltpu.SemaphoreType.DMA((2,)),
            pltpu.SemaphoreType.DMA,
            *(
                [
                    *gain_spec(wides, block.shape),
                    pltpu.VMEM((count, model), F32),
                    pltpu.SemaphoreType.DMA,
                    pltpu.SemaphoreType.DMA,
                ]
                if layer == 0
                else []
            ),
            *(
                [
                    *line_spec(wides, rows, lined.shape[1], 2),
                    *line_spec(wides, rows, head + kv_part, 1),
                    *line_spec(wides, rows, head + kv_part, 1),
                    pltpu.VMEM((rows, lined.shape[1]), BF16),
                    pltpu.SemaphoreType.DMA,
                    pltpu.VMEM((rows, head + kv_part), BF16),
                    pltpu.VMEM((rows, head + kv_part), BF16),
                    pltpu.VMEM((4, rows, kv_part), BF16),
                    pltpu.SemaphoreType.DMA((4,)),
                    pltpu.SemaphoreType.DMA((4,)),
                    pltpu.SemaphoreType.DMA((3,)),
                    pltpu.SemaphoreType.DMA((3,)),
                ]
                if layer == 0 and rows % 16 == 0
                else []
            ),
        ],
        compiler_params=params(collective_id, 60 if layer == 0 else 48),
    )(length, dh, a, x, gains, head_gains, trig, q_raw, k_raw, window, lse, pack, xn, o, *deps)


def after(value, *others):
    return pl.pallas_call(
        lambda *refs: None,
        out_shape=jax.ShapeDtypeStruct(value.shape, value.dtype),
        in_specs=[any_spec()] * (1 + len(others)),
        out_specs=any_spec(),
        input_output_aliases={0: 0},
    )(value, *others)


def scatter(member):
    return lax.psum_scatter(member, "wide", scatter_dimension=0, tiled=True)


def on_device(
    inputs, cotangent, lengths, norm_gains, head_gains, w_q, w_kv, w_o, w_gate_up, w_down
):
    core = lax.axis_index("section")
    narrow = lax.axis_index("narrow")
    n_narrow = lax.axis_size("narrow")
    is_zero = core == 0
    rows, model = inputs.shape[1], inputs.shape[2]
    block = w_q.shape[1]
    head_width = w_q.shape[2]
    n_wide = lax.axis_size("wide")
    hidden = w_down.shape[1]
    kv_part = w_kv.shape[2] // n_narrow

    def swap(value):
        return lax.ppermute(value, "section", [(0, 1), (1, 0)])

    def by_core(first, second):
        return jnp.where(is_zero, first, second)

    half = block // 2

    pad = -hidden % TILE
    kv_own = lax.dynamic_slice_in_dim(w_kv[0], narrow * kv_part, kv_part, 1)
    pack_width = 2 * head_width + kv_part
    pack = [w_q[0], w_o[0].T, kv_own]
    pack = jnp.concatenate(pack, axis=1)
    if block % 16 == 0:
        norm_rows = jnp.pad(norm_gains[0], ((0, 0), (0, pack_width - block)))
        head_rows = jnp.pad(head_gains[0], ((0, GAIN_ROWS - 6), (0, pack_width - head_width // n_wide)))
        pack = jnp.concatenate([pack, norm_rows, head_rows], axis=0)
    late = after(core.reshape(1), pack)[0]
    pack = lax.all_gather(pack, "wide", axis=0, tiled=True)

    def half_of(side):
        gate_up = lax.dynamic_slice_in_dim(w_gate_up[0], side * half, half, 0)
        gate_up = jnp.pad(gate_up, ((0, 0), (0, 0), (0, pad))).reshape(half, -1)
        down = lax.dynamic_slice_in_dim(w_down[0].T, side * half, half, 0)
        return jnp.concatenate([gate_up, jnp.pad(down, ((0, 0), (0, pad)))], axis=1)

    feed = trade(half_of(late), half_of(1 - late), 7)
    padded = hidden + pad

    def gather(member):
        return lax.all_gather(member, ("wide", "section"), axis=0, tiled=True)

    both = gather(feed[0])
    feeds = [
        (both, both, padded),
        (gather(feed[1][:, : 2 * padded]), gather(feed[1][:, 2 * padded :]), padded),
    ]
    packs, gain_packs = gather_pack(pack, model, n_wide, 6)
    if block % 16:
        norm_own = lax.all_gather(norm_gains[0], "wide", axis=1, tiled=True)
        head_own = lax.all_gather(head_gains[0], "wide", axis=1, tiled=True)
        norm_came, head_came = swap(norm_own), swap(head_own)

    def gains_of(section):
        if block % 16:
            mine = core == section
            norm_part = jnp.where(mine, norm_own, norm_came)
            head_part = jnp.where(mine, head_own, head_came)
        else:
            tail = gain_packs[section]
            norm_part = tail[:, :4, :block].transpose(1, 0, 2).reshape(4, model)
            head_part = tail[:, 4:6, : head_width // n_wide].transpose(1, 0, 2).reshape(2, head_width)
        return norm_part.astype(F32), head_part.astype(F32)

    start = narrow * rows
    positions = start + jnp.arange(rows, dtype=jnp.int32)
    trig = tables(positions, head_width)
    length = lax.dynamic_index_in_dim(lengths[:, 0], core, 0, keepdims=False)

    x = lax.dynamic_index_in_dim(inputs, core, 0, keepdims=False)
    length_one = length.reshape(1)
    outs, kept, gains = [], [], []
    for section in range(2):
        layer_gains, head_gain = gains_of(section)
        gains.append((layer_gains, head_gain))
        h, xn, q_raw, k_raw, window, lse, o, a, *shared = attend(
            length_one, x, layer_gains, head_gain, trig, packs, head_width, section, 8 + section
        )
        w_up, w_down, _ = feeds[section]
        mid_rows, gu, act = feed_up(h, layer_gains[2:3], w_up, padded, (), 10 + section)
        kept.append(((a, x, q_raw, k_raw, window, lse), (h, mid_rows, gu, act), shared))
        if section == 0:
            x, f = feed_down(h, layer_gains[3:4], act, w_down, 12)
            outs.append(x)

    def by_section(first, second):
        stays, came = by_core(first, second), swap(by_core(second, first))
        return jnp.stack([by_core(stays, came), by_core(came, stays)])

    real = (positions < length).astype(F32)[:, None]
    dy = lax.dynamic_index_in_dim(cotangent, core, 0, keepdims=False).astype(F32) * real
    dxs, gain_grads = [None, None], [None, None]
    up_sums, down_sums, attention_sums = [None, None], [None, None], [None, None]
    extra = None
    for section in (1, 0):
        kept_a, (h, mid_rows, gu, act), (xn, o) = kept[section]
        layer_gains, head_gain = gains[section]
        w_up, w_down, _ = feeds[section]
        if section:
            out, dgu, d_down, dg3 = feed_turn(h, layer_gains[3:4], dy, act, w_down, gu, 13)
            outs.append(out)
        else:
            dgu, d_down, dg3 = feed_back_up(
                dy, f, layer_gains[3:4], gu, act, w_down,
                (extra, down_sums[1]) if block % 16 else (down_sums[1],), 14,
            )
        down_sums[section] = scatter(d_down)
        dh, d_up, dg2 = feed_back_down(dy, h, layer_gains[2:3], dgu, mid_rows, w_up, 16 + section)
        if section or block % 16:
            up_sums[section] = scatter(d_up)
        a, x, q_raw, k_raw, window, lse = kept_a
        if section == 0:
            zeros = jnp.zeros((2, model), F32)
            gain_grads[0] = jnp.concatenate([zeros, dg2, dg3, zeros, zeros])
            section_out = by_section(*outs)
            lined = after(d_up, up_sums[1], section_out)
            deps = (jnp.concatenate(gain_grads), dxs[1], lined, extra)
        dx, extra, dg01, dhead, *more = attend_back(
            length_one, dh, a, x, layer_gains, head_gain, trig, q_raw, k_raw, window, lse, packs, xn, o,
            () if section else deps, section, 18 + section,
        )
        dxs[section] = dx
        if section:
            head_row = jnp.pad(dhead.reshape(1, -1), ((0, 0), (0, model - dhead.size)))
            gain_grads[1] = jnp.concatenate([dg01, dg2, dg3, head_row, jnp.zeros((3, model), F32)])
        else:
            gain_sums, input_grad, up_lined, came_up, grad_q, grad_kv, grad_o = more
            if block % 16 == 0:
                up_sums[0] = up_lined
            else:
                came_up = swap(up_sums[0])
        dy = dx
    def own_section(first, second):
        came = swap(by_core(second, first))
        stays = by_core(first, second)
        return by_core(stays, came).astype(F32), by_core(came, stays).astype(F32)

    if block % 16:
        split = down_sums[1].shape[1]
        attention_sums = (scatter(extra), down_sums[0][:, split:])
        down_sums[0] = down_sums[0][:, :split]
        grad_q, grad_kv, grad_o = finish_attention(
            *attention_sums, swap(attention_sums[1]), up_sums[0], head_width, 2
        )
    grad_o = grad_o.T
    grad_gate_up, _ = pair_up(*up_sums, came_up, swap(up_sums[1]), hidden)
    down_sums[0] = after(down_sums[0], gain_sums)
    grad_down = jnp.concatenate(own_section(*down_sums), axis=1)[:, :hidden].T
    gain_sums = lax.dynamic_slice_in_dim(gain_sums, core * 8, 8, 0)
    wide = lax.axis_index("wide")
    grad_norm = lax.dynamic_slice_in_dim(gain_sums[:4], wide * block, block, 1)
    grad_head = gain_sums[4, : 2 * head_width].reshape(2, head_width)
    head_block = head_width // n_wide
    grad_head = lax.dynamic_slice_in_dim(grad_head, wide * head_block, head_block, 1)

    return (
        section_out[None],
        input_grad[None],
        grad_norm[None],
        grad_head[None],
        grad_q[None],
        grad_kv[None],
        grad_o[None],
        grad_gate_up[None],
        grad_down[None],
    )


def solution(mesh):
    return jax.shard_map(
        on_device,
        mesh=mesh,
        in_specs=(
            P(None, ("wide", "narrow"), None),
            P(None, ("wide", "narrow"), None),
            P(None, "wide"),
            P("section", None, "wide"),
            P("section", None, "wide"),
            P("section", "wide", "narrow"),
            P("section", "wide", None),
            P("section", "narrow", "wide"),
            P("section", "wide", None, "narrow"),
            P("section", "narrow", "wide"),
        ),
        out_specs=(
            P("section", None, ("wide", "narrow"), None),
            P("section", None, ("wide", "narrow"), None),
            P("section", None, "wide"),
            P("section", None, "wide"),
            P("section", "wide", "narrow"),
            P("section", "wide", None),
            P("section", "narrow", "wide"),
            P("section", "wide", None, "narrow"),
            P("section", "narrow", "wide"),
        ),
        check_vma=False,
    )
```

```python
import functools

import jax
import jax.numpy as jnp
from jax import lax
from jax.experimental import pallas as pl
from jax.experimental.pallas import tpu as pltpu
from jax.sharding import PartitionSpec as P

WINDOW = 512
EPSILON = 1e-06
NEGATIVE = -1e30
ROPE_BASE = 10000.0
MESH = pl.DeviceIdType.MESH
MIB = 2**20
GAIN_ROWS = 16
F32 = jnp.float32
BF16 = jnp.bfloat16


def dot(a, b, dims):
    return lax.dot_general(a, b, ((dims[0], dims[1]), ((), ())), preferred_element_type=F32)


def nn(a, b):
    return dot(a, b, ((1,), (0,)))


def nt(a, b):
    return dot(a, b, ((1,), (1,)))


def tn(a, b):
    return dot(a, b, ((0,), (0,)))


def normed(operand, gain_vec):
    return (
        operand
        * lax.rsqrt(jnp.mean(operand * operand, axis=-1, keepdims=True) + EPSILON)
        * gain_vec
    )


def geglu(gate, up):
    return jax.nn.gelu(gate, approximate=True) * up


def neighbours():
    me = lax.axis_index("narrow")
    return me, jnp.bitwise_xor(me, 1), jnp.bitwise_xor(me, 2)


def meet(nx, ny):
    barrier = pltpu.get_barrier_semaphore()
    for other in (nx, ny):
        pl.semaphore_signal(barrier, inc=1, device_id={"narrow": other}, device_id_type=MESH)
    pl.semaphore_wait(barrier, 2)


def remote(src, dst, send_sem, recv_sem, other):
    return pltpu.make_async_remote_copy(
        src_ref=src,
        dst_ref=dst,
        send_sem=send_sem,
        recv_sem=recv_sem,
        device_id={"narrow": other},
        device_id_type=MESH,
    )


def tables(positions, head_width):
    half_width = head_width // 2
    frequency = ROPE_BASE ** (-jnp.arange(half_width, dtype=F32) * (2.0 / head_width))
    angles = positions.astype(F32)[:, None] * frequency[None, :]
    return jnp.concatenate([jnp.cos(angles), jnp.sin(angles)], axis=1)


def rotate(operand, cosine, sine_table):
    half_width = operand.shape[-1] // 2
    front_half = operand[..., :half_width]
    back_half = operand[..., half_width:]
    return jnp.concatenate(
        [
            front_half * cosine - back_half * sine_table,
            back_half * cosine + front_half * sine_table,
        ],
        axis=-1,
    )


GELU_SCALE = 0.7978845608028654
GELU_CUBE = 0.044715


def vmem_spec():
    return pl.BlockSpec(memory_space=pltpu.VMEM)


def any_spec():
    return pl.BlockSpec(memory_space=pl.ANY)


def rows_of(block, count):
    return pl.ds(pl.multiple_of(block * count, count), count)


def columns_of(tile, width, offset=0):
    if isinstance(tile, int):
        return pl.ds(tile * width + offset, width)
    return pl.ds(pl.multiple_of(tile * width + offset, 128), width)


def inverse_rms(value):
    return lax.rsqrt(jnp.mean(value * value, axis=-1, keepdims=True) + EPSILON)


def normed_gradient(value, gain, grad):
    inverse = inverse_rms(value)
    unit = value * inverse
    scaled = grad * gain
    by_value = inverse * (scaled - unit * jnp.mean(scaled * unit, axis=-1, keepdims=True))
    return by_value, jnp.sum(grad * unit, axis=0, keepdims=True)


def halves_of(ref, count, base=0):
    half = count // 2

    def part(block, which):
        return ref.at[pl.ds(pl.multiple_of(base + block * count + which * half, half), half)]

    return part


class Spread:
    def __init__(self, part, send, recv):
        self.me, self.nx, self.ny = neighbours()
        self.far = jnp.bitwise_xor(self.me, 3)

        def copy(block, which, at, other):
            ref = part(block, which)
            return remote(ref, ref, send.at[at], recv.at[at], other)

        self.to_x1 = copy(self.me, 0, 0, self.nx)
        self.to_y2 = copy(self.me, 1, 1, self.ny)
        self.to_x2 = copy(self.me, 1, 2, self.nx)
        self.to_y1 = copy(self.me, 0, 3, self.ny)
        self.on_y = copy(self.nx, 0, 4, self.ny)
        self.on_x = copy(self.ny, 1, 5, self.nx)

    def start(self):
        for copy in (self.to_x1, self.to_y2, self.to_x2, self.to_y1):
            copy.start()

    def pass_on(self):
        self.to_x1.wait_recv()
        self.on_y.start()
        self.to_y2.wait_recv()
        self.on_x.start()

    def x_here(self):
        self.to_x2.wait_recv()

    def y_here(self):
        self.to_y1.wait_recv()

    def far_here(self):
        self.on_y.wait_recv()
        self.on_x.wait_recv()

    def all_here(self):
        self.x_here()
        self.y_here()
        self.far_here()

    def finish(self):
        for copy in (self.to_x1, self.to_y2, self.to_x2, self.to_y1, self.on_y, self.on_x):
            copy.wait_send()


class Fold:
    def __init__(self, part, land, passing, send, recv):
        self.me, self.nx, self.ny = neighbours()
        self.far = jnp.bitwise_xor(self.me, 3)
        self.part, self.land, self.passing = part, land, passing

        def copy(src, at, other):
            return remote(src, land.at[at], send.at[at], recv.at[at], other)

        self.far_x = copy(part(self.far, 0), 0, self.nx)
        self.far_y = copy(part(self.far, 1), 1, self.ny)
        self.near_x = copy(part(self.nx, 0), 2, self.nx)
        self.near_y = copy(part(self.ny, 1), 3, self.ny)
        self.on_y = copy(passing.at[0], 4, self.ny)
        self.on_x = copy(passing.at[1], 5, self.nx)

    def send_far(self):
        self.far_x.start()
        self.far_y.start()

    def send_near(self):
        self.near_x.start()
        self.near_y.start()

    def pass_on(self):
        self.far_x.wait_recv()
        self.passing[0] = (self.part(self.ny, 0)[...].astype(F32) + self.land[0].astype(F32)).astype(BF16)
        self.on_y.start()
        self.far_y.wait_recv()
        self.passing[1] = (self.part(self.nx, 1)[...].astype(F32) + self.land[1].astype(F32)).astype(BF16)
        self.on_x.start()

    def total(self, own):
        half = own.shape[0] // 2
        for copy in (self.near_x, self.near_y, self.on_y, self.on_x):
            copy.wait_recv()
        first = own[:half] + (self.land[2].astype(F32) + self.land[4].astype(F32))
        second = own[half:] + (self.land[3].astype(F32) + self.land[5].astype(F32))
        return jnp.concatenate([first, second], axis=0)

    def finish(self):
        for copy in (self.far_x, self.far_y, self.near_x, self.near_y, self.on_y, self.on_x):
            copy.wait_send()


class LineFold:
    def __init__(self, own, land, out, columns, send, recv):
        self.own, self.land, self.out, self.columns = own, land, out, columns
        self.send, self.recv = send, recv
        self.wides = own.shape[0]
        self.wide = lax.axis_index("wide")

    def place(self, way):
        return self.wide if way == 0 else self.wides - 1 - self.wide

    def copy(self, way, step):
        return pltpu.make_async_remote_copy(
            src_ref=self.out.at[self.slot(way, step), :, self.columns],
            dst_ref=self.land.at[way, step, :, self.columns],
            send_sem=self.send.at[way, step],
            recv_sem=self.recv.at[way, step],
            device_id={"wide": self.wide + 1 if way == 0 else self.wide - 1},
            device_id_type=MESH,
        )

    def slot(self, way, step):
        return jnp.clip(step - self.wide, 0, self.wides - 2) if way == 0 else step

    def sends(self, way, step):
        place = self.place(way)
        return (place <= step) & (place < self.wides - 1)

    def gets(self, way, step):
        place = self.place(way)
        return (place >= 1) & (place - 1 <= step)

    def step(self, step):
        for way in (0, 1):
            ahead = self.wides - 1 - step
            block = self.wide + ahead if way == 0 else self.wide - ahead
            block = jnp.clip(block, 0, self.wides - 1)
            begins = self.place(way) == 0

            @pl.when(self.sends(way, step) & begins)
            def _():
                self.out[self.slot(way, step), :, self.columns] = self.own[block, :, self.columns]
                self.copy(way, step).start()

            if step:

                @pl.when(self.sends(way, step) & jnp.logical_not(begins))
                def _():
                    self.copy(way, step - 1).wait_recv()
                    total = self.own[block, :, self.columns].astype(F32)
                    total = total + self.land[way, step - 1, :, self.columns].astype(F32)
                    self.out[self.slot(way, step), :, self.columns] = total.astype(BF16)
                    self.copy(way, step).start()

    def finish(self, result):
        last = self.wides - 2
        result[:, self.columns] = self.own[self.wide, :, self.columns]
        for way in (0, 1):

            @pl.when(self.gets(way, last))
            def _():
                self.copy(way, last).wait_recv()
                total = result[:, self.columns].astype(F32)
                total = total + self.land[way, last, :, self.columns].astype(F32)
                result[:, self.columns] = total.astype(BF16)

    def close(self):
        for step in range(self.wides - 1):
            for way in (0, 1):
                pl.when(self.sends(way, step))(self.copy(way, step).wait_send)


def line_spec(wides, block, columns, pieces):
    hops = pltpu.SemaphoreType.DMA((pieces, 2, wides - 1))
    return [
        pltpu.VMEM((wides, block, columns), BF16),
        pltpu.VMEM((2, wides - 1, block, columns), BF16),
        pltpu.VMEM((wides - 1, block, columns), BF16),
        pltpu.VMEM((block, columns), BF16),
        pltpu.SemaphoreType.DMA((wides + 1,)),
        hops,
        hops,
    ]


class LineSum:
    def __init__(self, src, dst, own, land, out, result, loads, send, recv):
        self.src, self.dst, self.own, self.result, self.loads = src, dst, own, result, loads
        pieces = send.shape[0]
        columns = own.shape[2]
        width = -(-columns // (128 * pieces)) * 128
        self.folds = [
            LineFold(own, land, out, pl.ds(first, min(width, columns - first)), send.at[p], recv.at[p])
            for p, first in enumerate(range(0, columns, width))
        ]
        self.steps = own.shape[0] - 1

    def load(self):
        wides, rows, columns = self.own.shape
        for w in range(wides):
            part = self.src.at[pl.ds(w * rows, rows), pl.ds(0, columns)]
            pltpu.make_async_copy(part, self.own.at[w], self.loads.at[w]).start()

    def begin(self):
        wides, rows, columns = self.own.shape
        for w in range(wides):
            part = self.src.at[pl.ds(w * rows, rows), pl.ds(0, columns)]
            pltpu.make_async_copy(part, self.own.at[w], self.loads.at[w]).wait()
        for fold in self.folds:
            fold.step(0)

    def step(self, step, piece):
        self.folds[piece].step(step)

    def end(self, done=0):
        for fold in self.folds[done:]:
            fold.finish(self.result)
        if self.dst is not None:
            copy = pltpu.make_async_copy(self.result, self.dst, self.loads.at[self.own.shape[0]])
            copy.start()
        for fold in self.folds:
            fold.close()
        if self.dst is not None:
            copy.wait()


class Deal:
    def __init__(self, src, place, send, recv):
        me, nx, ny = neighbours()
        far = jnp.bitwise_xor(me, 3)
        self.copies = [
            remote(src(other), place(me), send.at[at], recv.at[at], other)
            for at, other in enumerate((far, nx, ny))
        ]

    def start(self):
        for copy in self.copies:
            copy.start()

    def here(self):
        for copy in self.copies:
            copy.wait_recv()

    def finish(self):
        for copy in self.copies:
            copy.wait_send()


def greet(*others):
    barrier = pltpu.get_barrier_semaphore()
    for other in others:
        pl.semaphore_signal(barrier, inc=1, device_id=other, device_id_type=MESH)
    return lambda: pl.semaphore_wait(barrier, len(others))


def spread_spec():
    return [pltpu.SemaphoreType.DMA((6,)), pltpu.SemaphoreType.DMA((6,))]


def fold_spec(count, width):
    return [
        pltpu.VMEM((6, count // 2, width), BF16),
        pltpu.VMEM((2, count // 2, width), BF16),
        pltpu.SemaphoreType.DMA((6,)),
        pltpu.SemaphoreType.DMA((6,)),
    ]


def params(collective_id, mib):
    return pltpu.CompilerParams(
        collective_id=collective_id, has_side_effects=True, vmem_limit_bytes=mib * MIB
    )


TILE = 256


def up_kernel(h_ref, gain_ref, w_ref, *refs):
    sharing = len(refs) > 11
    if sharing:
        xn_ref, o_ref, rows_out, gu_out, act_out, xn_out, o_out, *refs = refs
        rows, w, gu, act, load, store, send, recv, *share_refs = refs
        share = Share(xn_ref, o_ref, *share_refs)
    else:
        rows_out, gu_out, act_out, rows, w, gu, act, load, store, send, recv = refs
    count = h_ref.shape[0]
    hidden = act.shape[1]
    weights = pltpu.make_async_copy(w_ref.at[:, pl.ds(0, 2 * hidden)], w, load)
    weights.start()
    me, nx, ny = neighbours()
    met = greet({"narrow": nx}, {"narrow": ny}, {"narrow": jnp.bitwise_xor(me, 3)})
    value = h_ref[...]
    rows[rows_of(me, count), :] = (value * inverse_rms(value) * gain_ref[...]).astype(BF16)
    spread = Spread(halves_of(rows, count), send, recv)
    met()
    spread.start()
    weights.wait()

    def one(block, at):
        here = rows_of(block, count)

        def tile(j):
            left = rows[here, :]
            gate = nn(left, w[:, columns_of(j, TILE)])
            up = nn(left, w[:, columns_of(j, TILE, hidden)])
            inner = jnp.tanh(GELU_SCALE * (gate + GELU_CUBE * (gate * gate * gate)))
            gu[here, columns_of(j, TILE)] = gate.astype(BF16)
            gu[here, columns_of(j, TILE, hidden)] = up.astype(BF16)
            act[here, columns_of(j, TILE)] = (0.5 * gate * (1.0 + inner) * up).astype(BF16)

        for j in range(hidden // TILE):
            tile(j)
        copies = [
            pltpu.make_async_copy(ref.at[here], out.at[here], store.at[k, at])
            for k, (ref, out) in enumerate(((gu, gu_out), (act, act_out), (rows, rows_out)))
        ]
        for copy in copies:
            copy.start()
        return copies

    copies = one(me, 0)
    spread.pass_on()
    if sharing:
        share.start_rows()
        share.start_deal()
    spread.x_here()
    copies += one(nx, 1)
    spread.y_here()
    copies += one(ny, 2)
    spread.far_here()
    if sharing:
        share.spread.pass_on()
    copies += one(spread.far, 3)
    spread.finish()
    if sharing:
        share.all_here()
        share.finish()
        xn, o, loads = share_refs[:3]
        copies += [pltpu.make_async_copy(xn, xn_out, loads.at[2]), pltpu.make_async_copy(o, o_out, loads.at[3])]
        for copy in copies[-2:]:
            copy.start()
    for copy in copies:
        copy.wait()


def feed_up(h, gain, w_gu, hidden, shared, collective_id):
    count, model = h.shape
    total = 4 * count
    shapes = [(total, model), (total, 2 * hidden), (total, hidden)]
    shapes = [jax.ShapeDtypeStruct(shape, BF16) for shape in shapes]
    if shared:
        shapes += share_shapes(*shared)
    return pl.pallas_call(
        up_kernel,
        out_shape=shapes,
        in_specs=[vmem_spec(), vmem_spec(), any_spec()] + [vmem_spec()] * len(shared),
        out_specs=[any_spec()] * len(shapes),
        scratch_shapes=[
            pltpu.VMEM((total, model), BF16),
            pltpu.VMEM((model, 2 * hidden), BF16),
            pltpu.VMEM((total, 2 * hidden), BF16),
            pltpu.VMEM((total, hidden), BF16),
            pltpu.SemaphoreType.DMA,
            pltpu.SemaphoreType.DMA((3, 4)),
            *spread_spec(),
            *(share_spec(count, model, shared[1].shape[1] // 4) if shared else []),
        ],
        compiler_params=params(collective_id, 60),
    )(h, gain, w_gu, *shared)


def down_kernel(
    h_ref, gain_ref, act_ref, w_ref, x_out, f_out, act, w, parts, load, land, passing, send, recv
):
    count, model = h_ref.shape
    me, nx, ny = neighbours()
    met = greet({"narrow": nx}, {"narrow": ny})
    far = jnp.bitwise_xor(me, 3)
    first = w_ref.shape[1] - w.shape[1]
    weights = pltpu.make_async_copy(w_ref.at[:, pl.ds(first, w.shape[1])], w, load.at[0])
    weights.start()
    arrivals = []
    for at, block in enumerate((far, nx, ny, me)):
        here = rows_of(block, count)
        arrivals.append(pltpu.make_async_copy(act_ref.at[here], act.at[here], load.at[1 + at]))
        arrivals[-1].start()
    fold = Fold(halves_of(parts, count), land, passing, send, recv)
    weights.wait()
    met()

    def one(block, at):
        arrivals[at].wait()
        return nt(act[rows_of(block, count), :], w[...])

    parts[rows_of(far, count), :] = one(far, 0).astype(BF16)
    fold.send_far()
    parts[rows_of(nx, count), :] = one(nx, 1).astype(BF16)
    parts[rows_of(ny, count), :] = one(ny, 2).astype(BF16)
    fold.send_near()
    f_out[...] = one(me, 3)
    fold.pass_on()
    total = fold.total(f_out[...])
    f_out[...] = total
    x_out[...] = (h_ref[...] + total * inverse_rms(total) * gain_ref[...]).astype(BF16)
    fold.finish()


def feed_down(h, gain, act, w_dt, collective_id):
    count, model = h.shape
    return pl.pallas_call(
        down_kernel,
        out_shape=[
            jax.ShapeDtypeStruct((count, model), BF16),
            jax.ShapeDtypeStruct((count, model), F32),
        ],
        in_specs=[vmem_spec(), vmem_spec(), any_spec(), any_spec()],
        out_specs=[vmem_spec(), vmem_spec()],
        scratch_shapes=[
            pltpu.VMEM(act.shape, BF16),
            pltpu.VMEM((model, act.shape[1]), BF16),
            pltpu.VMEM((4 * count, model), BF16),
            pltpu.SemaphoreType.DMA((5,)),
            *fold_spec(count, model),
        ],
        compiler_params=params(collective_id, 60),
    )(h, gain, act, w_dt)


def swap_sum(make, tiles, ours, theirs, came, send, recv, out, out_sems, between=None):
    other = {"section": 1 - lax.axis_index("section")}
    sends = []
    for at, (first, width) in enumerate(tiles):
        columns = pl.ds(first, width)
        theirs[:, columns] = make(False, first, width).astype(BF16)
        copy = pltpu.make_async_remote_copy(
            src_ref=theirs.at[:, columns],
            dst_ref=came.at[:, columns],
            send_sem=send.at[at],
            recv_sem=recv.at[at],
            device_id=other,
            device_id_type=MESH,
        )
        copy.start()
        sends.append(copy)
    if between is not None:
        between()
    stores = []
    for at, (first, width) in enumerate(tiles):
        columns = pl.ds(first, width)
        own = make(True, first, width)
        sends[at].wait_recv()
        ours[:, columns] = (own + came[:, columns].astype(F32)).astype(BF16)
        copy = pltpu.make_async_copy(ours.at[:, columns], out.at[:, columns], out_sems.at[at])
        copy.start()
        stores.append(copy)
    return sends, stores


def column_tiles(width):
    return [(first, min(2 * TILE, width - first)) for first in range(0, width, 2 * TILE)]


def gate_up_gradient(df, here, w, gu, hidden):
    for j in range(hidden // TILE):
        dact = nn(df[here, :], w[:, columns_of(j, TILE)])
        gate = gu[here, columns_of(j, TILE)].astype(F32)
        up = gu[here, columns_of(j, TILE, hidden)].astype(F32)
        square = gate * gate
        inner = jnp.tanh(GELU_SCALE * gate * (1.0 + GELU_CUBE * square))
        half = 0.5 * (1.0 + inner)
        slope = half + 0.5 * GELU_SCALE * gate * (1.0 - inner * inner) * (
            1.0 + 3.0 * GELU_CUBE * square
        )
        gu[here, columns_of(j, TILE)] = (dact * up * slope).astype(BF16)
        gu[here, columns_of(j, TILE, hidden)] = (dact * gate * half).astype(BF16)


def back_up_kernel(dy_ref, f_ref, gain_ref, gu_ref, act_ref, w_ref, *refs):
    if len(refs) == 18:
        refs = refs[1:]
    if len(refs) == 19:
        extra_ref, _, *refs = refs
    else:
        extra_ref = None
    (
        dgu_out, dw_out, dgain_out, df, gu, act, w, ours, theirs, came,
        load, store, send, recv, swap_send, swap_recv, out_sems,
    ) = refs
    if extra_ref is not None:
        first = ours.shape[1]
        extra = pltpu.make_async_copy(
            extra_ref, dw_out.at[:, pl.ds(first, extra_ref.shape[1])], load.at[0, 1]
        )
        extra.start()
    count, model = dy_ref.shape
    hidden = act.shape[1]
    me, nx, ny = neighbours()
    core = lax.axis_index("section")
    met = greet({"narrow": nx}, {"narrow": ny}, {"section": 1 - core})
    far = jnp.bitwise_xor(me, 3)
    start = w_ref.shape[1] - hidden
    weights = pltpu.make_async_copy(w_ref.at[:, pl.ds(start, hidden)], w, load.at[0, 0])
    weights.start()
    arrivals = []
    for at, block in enumerate((me, nx, ny, far)):
        here = rows_of(block, count)
        pair = [
            pltpu.make_async_copy(gu_ref.at[here], gu.at[here], load.at[1, at]),
            pltpu.make_async_copy(act_ref.at[here], act.at[here], load.at[2, at]),
        ]
        for copy in pair:
            copy.start()
        arrivals.append(pair)
    dy = dy_ref[...].astype(BF16).astype(F32)
    by_value, by_gain = normed_gradient(f_ref[...], gain_ref[...], dy)
    df[rows_of(me, count), :] = by_value.astype(BF16)
    spread = Spread(halves_of(df, count), send, recv)
    met()
    spread.start()
    dgain_out[...] = by_gain
    weights.wait()

    def one(block, at):
        here = rows_of(block, count)
        for copy in arrivals[at]:
            copy.wait()

        gate_up_gradient(df, here, w, gu, hidden)
        copy = pltpu.make_async_copy(gu.at[here], dgu_out.at[here], store.at[at])
        copy.start()
        return copy

    copies = [one(me, 0)]
    spread.pass_on()
    spread.x_here()
    copies.append(one(nx, 1))
    spread.y_here()
    copies.append(one(ny, 2))
    spread.far_here()
    copies.append(one(far, 3))

    def make(mine, first, width):
        side = core if mine else 1 - core
        start = pl.multiple_of(side * (hidden // 2) + first, 128)
        return tn(df[...], act[:, pl.ds(start, width)])

    sends, stores = swap_sum(
        make, column_tiles(hidden // 2), ours, theirs, came, swap_send, swap_recv, dw_out, out_sems
    )
    spread.finish()
    for copy in sends:
        copy.wait_send()
    for copy in copies + stores:
        copy.wait()
    if extra_ref is not None:
        extra.wait()


def turn_kernel(
    h_ref, gain_ref, dy_ref, act_ref, w_ref, gu_ref, x_out, dgu_out, dw_out, dgain_out,
    act, w, parts, df, gu, ours, theirs, came, load, store, land, passing, fold_send, fold_recv, send, recv,
    swap_send, swap_recv, out_sems,
):
    count, model = h_ref.shape
    hidden = act.shape[1]
    me, nx, ny = neighbours()
    core = lax.axis_index("section")
    far = jnp.bitwise_xor(me, 3)
    met = greet({"narrow": nx}, {"narrow": ny}, {"section": 1 - core})
    first = w_ref.shape[1] - hidden
    weights = pltpu.make_async_copy(w_ref.at[:, pl.ds(first, hidden)], w, load.at[0, 0])
    weights.start()
    blocks = (far, nx, ny, me)
    for at, block in enumerate(blocks):
        here = rows_of(block, count)
        pltpu.make_async_copy(act_ref.at[here], act.at[here], load.at[1, at]).start()
    for at, block in enumerate(blocks):
        here = rows_of(block, count)
        pltpu.make_async_copy(gu_ref.at[here], gu.at[here], load.at[2, at]).start()

    def here_now(row, at):
        here = rows_of(blocks[at], count)
        src, dst = ((act_ref, act), (gu_ref, gu))[row - 1]
        pltpu.make_async_copy(src.at[here], dst.at[here], load.at[row, at]).wait()
        return here

    fold = Fold(halves_of(parts, count), land, passing, fold_send, fold_recv)
    weights.wait()
    met()

    def part(at):
        here = here_now(1, at)
        return here, nt(act[here, :], w[...])

    here, value = part(0)
    parts[here, :] = value.astype(BF16)
    fold.send_far()
    for at in (1, 2):
        here, value = part(at)
        parts[here, :] = value.astype(BF16)
    fold.send_near()
    _, value = part(3)
    fold.pass_on()
    f = fold.total(value)
    gain = gain_ref[...]
    by_value, by_gain = normed_gradient(f, gain, dy_ref[...])
    df[rows_of(me, count), :] = by_value.astype(BF16)
    spread = Spread(halves_of(df, count), send, recv)
    spread.start()
    dgain_out[...] = by_gain
    x_out[...] = (h_ref[...] + f * inverse_rms(f) * gain).astype(BF16)

    def one(at):
        here = here_now(2, at)
        gate_up_gradient(df, here, w, gu, hidden)
        copy = pltpu.make_async_copy(gu.at[here], dgu_out.at[here], store.at[at])
        copy.start()
        return copy

    copies = [one(3)]
    spread.pass_on()
    spread.x_here()
    copies.append(one(1))
    spread.y_here()
    copies.append(one(2))
    spread.far_here()
    copies.append(one(0))

    def make(mine, first, width):
        side = core if mine else 1 - core
        start = pl.multiple_of(side * (hidden // 2) + first, 128)
        return tn(df[...], act[:, pl.ds(start, width)])

    sends, stores = swap_sum(
        make, column_tiles(hidden // 2), ours, theirs, came, swap_send, swap_recv, dw_out, out_sems
    )
    spread.finish()
    fold.finish()
    for copy in sends:
        copy.wait_send()
    for copy in copies + stores:
        copy.wait()


def feed_turn(h, gain, dy, act, w_dt, gu, collective_id):
    count, model = h.shape
    total, hidden = act.shape
    tiles = pltpu.SemaphoreType.DMA((len(column_tiles(hidden // 2)),))
    dw = pltpu.VMEM((model, hidden // 2), BF16)
    return pl.pallas_call(
        turn_kernel,
        out_shape=[
            jax.ShapeDtypeStruct((count, model), BF16),
            jax.ShapeDtypeStruct(gu.shape, BF16),
            jax.ShapeDtypeStruct((model, hidden // 2), BF16),
            jax.ShapeDtypeStruct((1, model), F32),
        ],
        in_specs=[vmem_spec()] * 3 + [any_spec()] * 3,
        out_specs=[vmem_spec(), any_spec(), any_spec(), vmem_spec()],
        scratch_shapes=[
            pltpu.VMEM(act.shape, BF16),
            pltpu.VMEM((model, hidden), BF16),
            pltpu.VMEM((total, model), BF16),
            pltpu.VMEM((total, model), BF16),
            pltpu.VMEM(gu.shape, BF16),
            dw,
            dw,
            dw,
            pltpu.SemaphoreType.DMA((3, 4)),
            pltpu.SemaphoreType.DMA((4,)),
            *fold_spec(count, model),
            *spread_spec(),
            tiles,
            tiles,
            tiles,
        ],
        compiler_params=params(collective_id, 60),
    )(h, gain, dy, act, w_dt, gu)


def feed_back_up(dy, f, gain, gu, act, w_dt, extra, collective_id):
    count, model = dy.shape
    total, hidden = act.shape
    tiles = len(column_tiles(hidden // 2))
    extras = extra
    return pl.pallas_call(
        back_up_kernel,
        out_shape=[
            jax.ShapeDtypeStruct(gu.shape, BF16),
            jax.ShapeDtypeStruct((model, hidden // 2 + sum(e.shape[1] for e in extras[:-1])), BF16),
            jax.ShapeDtypeStruct((1, model), F32),
        ],
        in_specs=[vmem_spec()] * 3 + [any_spec()] * (3 + len(extras)),
        out_specs=[any_spec(), any_spec(), vmem_spec()],
        scratch_shapes=[
            pltpu.VMEM((total, model), BF16),
            pltpu.VMEM(gu.shape, BF16),
            pltpu.VMEM(act.shape, BF16),
            pltpu.VMEM((model, hidden), BF16),
            pltpu.VMEM((model, hidden // 2), BF16),
            pltpu.VMEM((model, hidden // 2), BF16),
            pltpu.VMEM((model, hidden // 2), BF16),
            pltpu.SemaphoreType.DMA((3, 4)),
            pltpu.SemaphoreType.DMA((4,)),
            *spread_spec(),
            pltpu.SemaphoreType.DMA((tiles,)),
            pltpu.SemaphoreType.DMA((tiles,)),
            pltpu.SemaphoreType.DMA((tiles,)),
        ],
        compiler_params=params(collective_id, 60),
    )(dy, f, gain, gu, act, w_dt, *extras)


def back_down_kernel(
    dy_ref, h_ref, gain_ref, dgu_ref, rows_ref, w_ref, dh_out, dw_out, dgain_out,
    dgu, rows, w, parts, ours, theirs, came, load, land, passing, send, recv, swap_send, swap_recv, out_sems,
):
    count, model = dy_ref.shape
    hidden = dgu.shape[1] // 2
    me, nx, ny = neighbours()
    core = lax.axis_index("section")
    far = jnp.bitwise_xor(me, 3)
    met = greet({"narrow": nx}, {"narrow": ny}, {"section": 1 - core})
    weights = pltpu.make_async_copy(w_ref.at[:, pl.ds(0, 2 * hidden)], w, load.at[0])
    weights.start()
    arrivals = []
    for at, block in enumerate((far, nx, ny, me)):
        here = rows_of(block, count)
        arrivals.append(pltpu.make_async_copy(dgu_ref.at[here], dgu.at[here], load.at[1 + at]))
        arrivals[-1].start()
    kept = pltpu.make_async_copy(rows_ref, rows, load.at[5])
    kept.start()
    fold = Fold(halves_of(parts, count), land, passing, send, recv)
    weights.wait()
    met()

    def one(block, at, out, here):
        arrivals[at].wait()
        out[here, :] = nt(dgu[rows_of(block, count), :], w[...]).astype(out.dtype)

    one(far, 0, parts, rows_of(far, count))
    fold.send_far()
    one(nx, 1, parts, rows_of(nx, count))
    one(ny, 2, parts, rows_of(ny, count))
    fold.send_near()
    one(me, 3, dh_out, pl.ds(0, count))
    fold.pass_on()
    kept.wait()

    def make(mine, first, width):
        side = core if mine else 1 - core
        start = pl.multiple_of(side * hidden + first, 128)
        return tn(rows[...], dgu[:, pl.ds(start, width)])

    sends, stores = swap_sum(
        make, column_tiles(hidden), ours, theirs, came, swap_send, swap_recv, dw_out, out_sems
    )
    total = fold.total(dh_out[...])
    by_value, by_gain = normed_gradient(h_ref[...], gain_ref[...], total)
    dh_out[...] = dy_ref[...].astype(BF16).astype(F32) + by_value
    dgain_out[...] = by_gain
    fold.finish()
    for copy in sends:
        copy.wait_send()
    for copy in stores:
        copy.wait()


def feed_back_down(dy, h, gain, dgu, rows, w_gu, collective_id):
    count, model = dy.shape
    total, hidden = dgu.shape[0], dgu.shape[1] // 2
    tiles = len(column_tiles(hidden))
    return pl.pallas_call(
        back_down_kernel,
        out_shape=[
            jax.ShapeDtypeStruct((count, model), F32),
            jax.ShapeDtypeStruct((model, hidden), BF16),
            jax.ShapeDtypeStruct((1, model), F32),
        ],
        in_specs=[vmem_spec()] * 3 + [any_spec()] * 3,
        out_specs=[vmem_spec(), any_spec(), vmem_spec()],
        scratch_shapes=[
            pltpu.VMEM(dgu.shape, BF16),
            pltpu.VMEM(rows.shape, BF16),
            pltpu.VMEM((model, 2 * hidden), BF16),
            pltpu.VMEM((total, model), BF16),
            pltpu.VMEM((model, hidden), BF16),
            pltpu.VMEM((model, hidden), BF16),
            pltpu.VMEM((model, hidden), BF16),
            pltpu.SemaphoreType.DMA((6,)),
            *fold_spec(count, model),
            pltpu.SemaphoreType.DMA((tiles,)),
            pltpu.SemaphoreType.DMA((tiles,)),
            pltpu.SemaphoreType.DMA((tiles,)),
        ],
        compiler_params=params(collective_id, 60),
    )(dy, h, gain, dgu, rows, w_gu)


def pack_kernel(p_ref, o_ref, g_ref, local, send, recv, peer_send, peer_recv):
    model, width = o_ref.shape[2:]
    half = model // 2
    wides, extra = g_ref.shape[1:3]
    rows = model // wides
    core = lax.axis_index("section")
    me, nx, ny = neighbours()
    met = greet({"narrow": nx}, {"narrow": ny}, {"section": 1 - core})
    whole = p_ref.shape[0] == model
    owns = []
    if whole:
        owns.append(pltpu.make_async_copy(p_ref, o_ref.at[core, me], local.at[0, 0]))
    else:
        for w in range(wides):
            first = w * (rows + extra)
            place = o_ref.at[core, me, pl.ds(w * rows, rows)]
            owns.append(pltpu.make_async_copy(p_ref.at[pl.ds(first, rows)], place, local.at[0, w]))
            part = p_ref.at[pl.ds(first + rows, extra)]
            owns.append(pltpu.make_async_copy(part, g_ref.at[core, w], local.at[1, w]))
    start_all(owns)
    spread = Spread(lambda block, which: o_ref.at[core, block, pl.ds(which * half, half)], send, recv)
    wait_all(owns)
    met()
    spread.start()
    copies = []

    def across(ref):
        copy = pltpu.make_async_remote_copy(
            src_ref=ref,
            dst_ref=ref,
            send_sem=peer_send.at[len(copies)],
            recv_sem=peer_recv.at[len(copies)],
            device_id={"section": 1 - core},
            device_id_type=MESH,
        )
        copy.start()
        copies.append(copy)

    if not whole:
        across(g_ref.at[core])
    across(o_ref.at[core, me])
    spread.pass_on()
    spread.x_here()
    across(o_ref.at[core, nx])
    spread.y_here()
    across(o_ref.at[core, ny])
    spread.far_here()
    across(o_ref.at[core, spread.far])
    for copy in copies:
        copy.wait_recv()
    spread.finish()
    for copy in copies:
        copy.wait_send()


def gather_pack(pack, model, wides, collective_id):
    width = pack.shape[1]
    return pl.pallas_call(
        pack_kernel,
        out_shape=[
            jax.ShapeDtypeStruct((2, 4, model, width), pack.dtype),
            jax.ShapeDtypeStruct((2, wides, GAIN_ROWS, width), pack.dtype),
        ],
        in_specs=[any_spec()],
        out_specs=[vmem_spec()] * 2,
        scratch_shapes=[
            pltpu.SemaphoreType.DMA((2, wides)),
            *spread_spec(),
            pltpu.SemaphoreType.DMA((5,)),
            pltpu.SemaphoreType.DMA((5,)),
        ],
        compiler_params=params(collective_id, 32),
    )(pack)


def finish_kernel(
    zero_ref, one_ref, early_ref, dep_ref, q_out, kv_out, o_out, came, kv, send, recv, kv_send, kv_recv
):
    core = lax.axis_index("section")
    me, nx, ny = neighbours()
    others = (nx, ny, jnp.bitwise_xor(me, 3))
    met = greet({"section": 1 - core}, *[{"narrow": other} for other in others])
    head = q_out.shape[1]
    first = core == 0
    by_qkv = jnp.where(first, zero_ref[...], early_ref[...])
    kv[me] = by_qkv[:, head:]
    met()
    across = pltpu.make_async_remote_copy(
        src_ref=zero_ref,
        dst_ref=came,
        send_sem=send,
        recv_sem=recv,
        device_id={"section": 1 - core},
        device_id_type=MESH,
    )
    across.start()
    copies = []
    for at, other in enumerate(others):
        copies.append(remote(kv.at[me], kv.at[me], kv_send.at[at], kv_recv.at[at], other))
        copies[-1].start()
    q_out[...] = by_qkv[:, :head].astype(F32)
    across.wait_recv()
    o_out[...] = jnp.where(first, came[:, :head], one_ref[:, :head]).astype(F32)
    for copy in copies:
        copy.wait_recv()
    width = kv.shape[2]
    for n in range(4):
        kv_out[:, n * width : (n + 1) * width] = kv[n].astype(F32)
    across.wait_send()
    for copy in copies:
        copy.wait_send()


def finish_attention(zero, one, early, dep, head, collective_id):
    block, width = zero.shape
    return pl.pallas_call(
        finish_kernel,
        out_shape=[
            jax.ShapeDtypeStruct((block, head), F32),
            jax.ShapeDtypeStruct((block, 4 * (width - head)), F32),
            jax.ShapeDtypeStruct((block, head), F32),
        ],
        in_specs=[vmem_spec()] * 3 + [any_spec()],
        out_specs=[vmem_spec()] * 3,
        scratch_shapes=[
            pltpu.VMEM((block, width), BF16),
            pltpu.VMEM((4, block, width - head), BF16),
            pltpu.SemaphoreType.DMA,
            pltpu.SemaphoreType.DMA,
            pltpu.SemaphoreType.DMA((3,)),
            pltpu.SemaphoreType.DMA((3,)),
        ],
        compiler_params=params(collective_id, 16),
    )(zero, one, early, dep)


def pair_kernel(zero_ref, one_ref, came_zero_ref, came_one_ref, down_zero_ref, down_one_ref, down_came_ref, out_ref, down_ref):
    hidden = out_ref.shape[2]
    first = lax.axis_index("section") == 0
    keep = jnp.where(first, zero_ref[:, :hidden], one_ref[:, :hidden])
    came = jnp.where(first, came_zero_ref[:, :hidden], came_one_ref[:, :hidden])
    out_ref[:, 0, :] = jnp.where(first, keep, came).astype(F32)
    out_ref[:, 1, :] = jnp.where(first, came, keep).astype(F32)
    width = down_came_ref.shape[1]
    keep = jnp.where(first, down_zero_ref[...], down_one_ref[...])
    came = down_came_ref[...]
    down_ref[:, :width] = jnp.where(first, keep, came).astype(F32)
    rest = hidden - width
    down_ref[:, width:] = jnp.where(first, came[:, :rest], keep[:, :rest]).astype(F32)


def pair_up(zero, one, came_zero, came_one, down_zero, down_one, down_came, hidden):
    return pl.pallas_call(
        pair_kernel,
        out_shape=[
            jax.ShapeDtypeStruct((zero.shape[0], 2, hidden), F32),
            jax.ShapeDtypeStruct((zero.shape[0], hidden), F32),
        ],
        in_specs=[vmem_spec()] * 7,
        out_specs=[vmem_spec()] * 2,
        compiler_params=pltpu.CompilerParams(vmem_limit_bytes=40 * MIB),
    )(zero, one, came_zero, came_one, down_zero, down_one, down_came)


class Share:
    def __init__(self, xn_ref, o_ref, xn, o, loads, spread_send, spread_recv, deal_send, deal_recv):
        count, head = xn_ref.shape[0], o.shape[1]
        me = lax.axis_index("narrow")
        self.loads = [
            pltpu.make_async_copy(xn_ref, xn.at[rows_of(me, count)], loads.at[0]),
            pltpu.make_async_copy(o_ref.at[:, columns_of(me, head)], o.at[rows_of(me, count)], loads.at[1]),
        ]
        self.spread = Spread(halves_of(xn, count), spread_send, spread_recv)
        self.deal = Deal(
            lambda other: o_ref.at[:, columns_of(other, head)],
            lambda mine: o.at[rows_of(mine, count)],
            deal_send,
            deal_recv,
        )

    def start_rows(self):
        self.loads[0].start()
        self.loads[0].wait()
        self.spread.start()

    def start_deal(self):
        self.loads[1].start()
        self.deal.start()

    def all_here(self):
        self.spread.all_here()
        self.deal.here()

    def finish(self):
        self.spread.finish()
        self.deal.finish()
        self.loads[1].wait()


def share_spec(count, model, head):
    return [
        pltpu.VMEM((4 * count, model), BF16),
        pltpu.VMEM((4 * count, head), BF16),
        pltpu.SemaphoreType.DMA((4,)),
        *spread_spec(),
        pltpu.SemaphoreType.DMA((3,)),
        pltpu.SemaphoreType.DMA((3,)),
    ]


def share_shapes(xn, o):
    total = 4 * xn.shape[0]
    return [
        jax.ShapeDtypeStruct((total, xn.shape[1]), BF16),
        jax.ShapeDtypeStruct((total, o.shape[1] // 4), BF16),
    ]


def gain_stages():
    wides = lax.axis_size("wide")
    core, wide = lax.axis_index("section"), lax.axis_index("wide")
    me, nx, ny = neighbours()
    return [
        [{"narrow": nx}, {"narrow": ny}, {"narrow": jnp.bitwise_xor(me, 3)}],
        [{"section": 1 - core}],
        [{"wide": lax.rem(wide + step, wides)} for step in range(1, wides)],
    ]


class GainSum:
    def __init__(self, land, total, send, recv):
        self.land, self.total, self.send, self.recv = land, total, send, recv
        self.copies = []
        self.waiting = []

    def start(self, stage):
        for other in gain_stages()[stage]:
            at = len(self.copies)
            copy = pltpu.make_async_remote_copy(
                src_ref=self.total.at[stage],
                dst_ref=self.land.at[at],
                send_sem=self.send.at[at],
                recv_sem=self.recv.at[at],
                device_id=other,
                device_id_type=MESH,
            )
            copy.start()
            self.copies.append(copy)
            self.waiting.append(at)

    def add(self, stage):
        value = self.total[stage]
        for at in self.waiting:
            self.copies[at].wait_recv()
            value = value + self.land[at]
        self.waiting = []
        self.total[stage + 1] = value

    def close(self):
        for copy in self.copies:
            copy.wait_send()


def gain_spec(wides, shape):
    return [
        pltpu.VMEM((wides + 3, *shape), F32),
        pltpu.VMEM((4, *shape), F32),
        pltpu.SemaphoreType.DMA((wides + 3,)),
        pltpu.SemaphoreType.DMA((wides + 3,)),
    ]


def trade_kernel(keep_ref, give_ref, zero_ref, one_ref, came, send, recv):
    core = lax.axis_index("section")
    met = greet({"section": 1 - core})
    met()
    copy = pltpu.make_async_remote_copy(
        src_ref=give_ref,
        dst_ref=came,
        send_sem=send,
        recv_sem=recv,
        device_id={"section": 1 - core},
        device_id_type=MESH,
    )
    copy.start()

    @pl.when(core == 0)
    def _():
        zero_ref[...] = keep_ref[...]

    @pl.when(core == 1)
    def _():
        one_ref[...] = keep_ref[...]

    copy.wait_recv()

    @pl.when(core == 0)
    def _():
        one_ref[...] = came[...]

    @pl.when(core == 1)
    def _():
        zero_ref[...] = came[...]

    copy.wait_send()


def trade(keep, give, collective_id):
    shape = jax.ShapeDtypeStruct(keep.shape, keep.dtype)
    return pl.pallas_call(
        trade_kernel,
        out_shape=[shape, shape],
        in_specs=[vmem_spec()] * 2,
        out_specs=[vmem_spec()] * 2,
        scratch_shapes=[
            pltpu.VMEM(keep.shape, keep.dtype),
            pltpu.SemaphoreType.DMA,
            pltpu.SemaphoreType.DMA,
        ],
        compiler_params=params(collective_id, 16),
    )(keep, give)


def turn_back(grad, cosine, sine_table):
    half = grad.shape[1] // 2
    front, back = grad[:, :half], grad[:, half:]
    return jnp.concatenate(
        [front * cosine + back * sine_table, back * cosine - front * sine_table], axis=1
    )


def pack_loads(pack_ref, layer, head, wq, wot, wkv, sems):
    kv_part = wkv.shape[1] // 4
    loads = []
    for at, (w, first, width) in enumerate(
        ((wq, 0, head), (wot, head, head), (wkv, 2 * head, kv_part))
    ):
        loads.append(
            [
                pltpu.make_async_copy(
                    pack_ref.at[layer, n, :, pl.ds(first, width)], w.at[:, pl.ds(n * width, width)], sems.at[at, n]
                )
                for n in range(4)
            ]
        )
    return loads


def start_all(copies):
    for copy in copies:
        copy.start()


def wait_all(copies):
    for copy in copies:
        copy.wait()


def window_mask(me, count, window, length):
    rows_at = me * count + lax.broadcasted_iota(jnp.int32, (count, 1), 0)
    cols_at = me * count - WINDOW + lax.broadcasted_iota(jnp.int32, (1, window), 1)
    return (
        (cols_at <= rows_at)
        & (rows_at - cols_at < WINDOW)
        & (cols_at >= 0)
        & ((cols_at < length) | (cols_at == rows_at))
    )


def attend_kernel(layer, length_ref, x_ref, gains_ref, head_ref, trig_ref, pack_ref, *refs):
    (
        h_out, xn_out, q_out, k_out, win_out, lse_out, o_out, a_out, *refs
    ) = refs
    sharing = len(refs) > 9
    if sharing:
        xn_all_out, o_all_out, *refs = refs
    kv, wq, wot, wkv, load, send, recv, *share_refs = refs
    count, model = x_ref.shape
    head = k_out.shape[1]
    heads = q_out.shape[1] // head
    me, nx, ny = neighbours()
    met = greet({"narrow": nx}, {"narrow": ny}, {"narrow": jnp.bitwise_xor(me, 3)})
    q_loads, out_loads, kv_loads = pack_loads(pack_ref, layer, head, wq, wot, wkv, load)
    start_all(kv_loads + q_loads + out_loads)
    scaling = head ** (-0.5)
    cosine, sine_table = trig_ref[:, : head // 2], trig_ref[:, head // 2 :]
    x = x_ref[...].astype(F32)
    xn_out[...] = (x * inverse_rms(x) * gains_ref[0:1, :]).astype(BF16)
    kv[pl.ds(0, WINDOW), :] = jnp.zeros((WINDOW, 2 * head), BF16)
    wait_all(kv_loads)
    raw = nn(xn_out[...], wkv[...])
    k_raw = raw[:, :head]
    k_out[...] = k_raw
    k_rot = rotate(k_raw * inverse_rms(k_raw) * head_ref[1:2, :], cosine, sine_table)
    here = pl.ds(pl.multiple_of(WINDOW + me * count, count), count)
    kv[here, :head] = k_rot.astype(BF16)
    kv[here, head:] = raw[:, head:].astype(BF16)
    spread = Spread(halves_of(kv, count, WINDOW), send, recv)
    met()
    spread.start()
    if sharing:
        share = Share(xn_out, o_out, *share_refs)
    wait_all(q_loads)
    q_out[...] = nn(xn_out[...], wq[...])
    spread.pass_on()
    if sharing:
        share.start_rows()
    spread.all_here()
    window = win_out.shape[0]
    win_out[...] = kv[pl.ds(pl.multiple_of(me * count, count), window), :]
    visible = window_mask(me, count, window, length_ref[0])
    k_win, v_win = win_out[:, :head], win_out[:, head:]
    q_gain = head_ref[0:1, :]

    def one_head(i):
        columns = columns_of(i, head)
        q_raw = q_out[:, columns]
        qr = rotate(q_raw * inverse_rms(q_raw) * q_gain, cosine, sine_table).astype(BF16)
        scores = jnp.where(visible, nt(qr, k_win) * scaling, NEGATIVE)
        most = jnp.max(scores, axis=-1, keepdims=True)
        exponent = jnp.exp(scores - most)
        total = jnp.sum(exponent, axis=-1, keepdims=True)
        lse_out[i] = most + jnp.log(total)
        o_out[:, columns] = nn((exponent / total).astype(BF16), v_win).astype(BF16)

    for i in range(heads):
        one_head(i)
    if sharing:
        share.start_deal()
        share.spread.pass_on()
    wait_all(out_loads)
    a = nt(o_out[...], wot[...])
    a_out[...] = a
    h_out[...] = x_ref[...].astype(F32) + a * inverse_rms(a) * gains_ref[1:2, :]
    spread.finish()
    if sharing:
        share.all_here()
        share.finish()
        xn, o, loads = share_refs[:3]
        stores = [
            pltpu.make_async_copy(xn, xn_all_out, loads.at[2]),
            pltpu.make_async_copy(o, o_all_out, loads.at[3]),
        ]
        start_all(stores)
        wait_all(stores)


def attend(length, x, gains, head_gains, trig, pack, head, layer, collective_id):
    count, model = x.shape
    kv_width = 2 * head
    width = 4 * head
    window = count + WINDOW
    sharing = True
    xn_shape = jax.ShapeDtypeStruct((count, model), BF16)
    o_shape = jax.ShapeDtypeStruct((count, width), BF16)
    shapes = [
        jax.ShapeDtypeStruct((count, model), F32),
        xn_shape,
        jax.ShapeDtypeStruct((count, width), F32),
        jax.ShapeDtypeStruct((count, head), F32),
        jax.ShapeDtypeStruct((window, kv_width), BF16),
        jax.ShapeDtypeStruct((4, count, 1), F32),
        o_shape,
        jax.ShapeDtypeStruct((count, model), F32),
    ]
    outs = [vmem_spec()] * 8
    if sharing:
        shapes += share_shapes(xn_shape, o_shape)
        outs += [any_spec()] * 2
    return pl.pallas_call(
        functools.partial(attend_kernel, layer),
        out_shape=shapes,
        in_specs=[pl.BlockSpec(memory_space=pltpu.SMEM)] + [vmem_spec()] * 4 + [any_spec()],
        out_specs=outs,
        scratch_shapes=[
            pltpu.VMEM((4 * count + WINDOW, kv_width), BF16),
            pltpu.VMEM((model, width), BF16),
            pltpu.VMEM((model, width), BF16),
            pltpu.VMEM((model, kv_width), BF16),
            pltpu.SemaphoreType.DMA((3, 4)),
            *spread_spec(),
            *(share_spec(count, model, head) if sharing else []),
        ],
        compiler_params=params(collective_id, 40),
    )(length, x, gains, head_gains, trig, pack)


def attend_back_kernel(
    layer, length_ref, dh_ref, a_ref, x_ref, gains_ref, head_ref, trig_ref, q_ref, k_ref, win_ref, lse_ref,
    pack_ref, xn_ref, o_ref, *refs
):
    if layer == 0:
        block_ref, dx_one_ref, lined_ref, early_ref, *refs = refs
        block_out, both_out, lined_out, came_out, q_out, kv_out, o_out = refs[4:11]
        refs = refs[:4] + refs[11:]
        gain_refs, (dx_give, dx_send, dx_recv), line_refs = refs[36:40], refs[40:43], refs[43:]
        refs = refs[:36]
    (
    dx_out, dw_out, dgain_out, dhead_out,
    da, do, dq, dk, dv, parts, dq_all, dkv, dkv_all, wq, wot, wkv, xn, o, ours, theirs, came,
    pack_load, load, send, recv, land, passing, fold_send, fold_recv, q_send, q_recv, kv_send, kv_recv, swap_send, swap_recv, out_sem,
    ) = refs
    count = dh_ref.shape[0]
    head = k_ref.shape[1]
    heads = q_ref.shape[1] // head
    kv_part = dkv_all.shape[1]
    me, nx, ny = neighbours()
    core = lax.axis_index("section")
    far = jnp.bitwise_xor(me, 3)
    lined = layer == 0 and len(line_refs) > 0
    if layer == 0:
        met = greet(*sum(gain_stages(), []))
        sums = GainSum(*gain_refs)
    else:
        met = greet({"narrow": nx}, {"narrow": ny}, {"narrow": far}, {"section": 1 - core})
    if lined:
        line = LineSum(lined_ref, lined_out, *line_refs[:7])
        early = LineSum(early_ref, None, *line_refs[7:14])
        late = LineSum(ours, None, *line_refs[14:21])
        came_line, came_store, came_early, came_late, kv_all, cross_send, cross_recv, narrow_send, narrow_recv = (
            line_refs[21:]
        )

        def across(at, src, dst):
            return pltpu.make_async_remote_copy(
                src_ref=src,
                dst_ref=dst,
                send_sem=cross_send.at[at],
                recv_sem=cross_recv.at[at],
                device_id={"section": 1 - core},
                device_id_type=MESH,
            )

        early.load()
        line.load()
    q_loads, out_loads, kv_loads = pack_loads(pack_ref, layer, head, wq, wot, wkv, pack_load)
    loads = [
        pltpu.make_async_copy(src, dst, load.at[at])
        for at, (src, dst) in enumerate(((xn_ref, xn), (o_ref, o)))
    ]
    start_all(out_loads + q_loads + kv_loads + loads)
    here = rows_of(me, count)
    scaling = head ** (-0.5)
    cosine, sine_table = trig_ref[:, : head // 2], trig_ref[:, head // 2 :]

    dh = dh_ref[...]
    by_value, dg1 = normed_gradient(a_ref[...], gains_ref[1:2, :], dh)
    da[here, :] = by_value.astype(BF16)
    dgain_out[1:2, :] = dg1
    spread = Spread(halves_of(da, count), send, recv)
    met()
    spread.start()
    if lined:
        early.begin()
        line.begin()
    wait_all(out_loads)
    do[...] = nn(da[here, :], wot[...]).astype(BF16)

    visible = window_mask(me, count, win_ref.shape[0], length_ref[0])
    k_win, v_win = win_ref[:, :head], win_ref[:, head:]
    dk[...] = jnp.zeros_like(dk)
    dv[...] = jnp.zeros_like(dv)
    dhead_out[...] = jnp.zeros_like(dhead_out)
    q_gain, k_gain = head_ref[0:1, :], head_ref[1:2, :]

    def one_head(i):
        columns = columns_of(i, head)
        raw = q_ref[:, columns]
        inverse = inverse_rms(raw)
        unit = raw * inverse
        qr = rotate(unit * q_gain, cosine, sine_table).astype(BF16)
        scores = jnp.where(visible, nt(qr, k_win) * scaling, NEGATIVE)
        probs = jnp.exp(scores - lse_ref[i])
        do_head = do[:, columns]
        dp = nt(do_head, v_win)
        ds = (probs * (dp - jnp.sum(probs * dp, axis=-1, keepdims=True))).astype(BF16)
        dk[...] += tn(ds, qr)
        dv[...] += tn(probs.astype(BF16), do_head)
        grad = turn_back(nn(ds, k_win) * scaling, cosine, sine_table)
        scaled = grad * q_gain
        dq_raw = inverse * (scaled - unit * jnp.mean(scaled * unit, axis=-1, keepdims=True))
        dq[:, columns] = dq_raw.astype(BF16)
        dhead_out[0:1, :] += jnp.sum(grad * unit, axis=0, keepdims=True)

    for i in range(heads):
        one_head(i)
    parts[...] = jnp.zeros_like(parts)
    window = pl.ds(pl.multiple_of(me * count, count), win_ref.shape[0])
    parts[window, :head] = (dk[...] * scaling).astype(BF16)
    parts[window, head:] = dv[...].astype(BF16)
    fold = Fold(halves_of(parts, count, WINDOW), land, passing, fold_send, fold_recv)
    fold.send_far()
    fold.send_near()
    deal_q = Deal(
        lambda other: dq.at[:, columns_of(other, head)],
        lambda mine: dq_all.at[rows_of(mine, count)],
        q_send,
        q_recv,
    )
    deal_q.start()
    dq_all[here, :] = dq[:, columns_of(me, head)]
    spread.pass_on()
    if lined:
        early.step(1, 0)
        line.step(1, 0)
    wait_all(q_loads)
    dx_out[...] = nt(dq[...], wq[...])
    fold.pass_on()
    spread.all_here()
    wait_all(loads)
    first = core == 0
    swaps = []

    def exchange(at, columns, a, b):
        ours[:, columns] = jnp.where(first, a, b).astype(BF16)
        theirs[:, columns] = jnp.where(first, b, a).astype(BF16)
        copy = pltpu.make_async_remote_copy(
            src_ref=theirs.at[:, columns],
            dst_ref=came.at[:, columns],
            send_sem=swap_send.at[at],
            recv_sem=swap_recv.at[at],
            device_id={"section": 1 - core},
            device_id_type=MESH,
        )
        copy.start()
        swaps.append(copy)

    if lined:
        line.step(1, 1)
    by_out = tn(da[...], o[...])
    deal_q.here()
    exchange(0, pl.ds(0, head), tn(xn[...], dq_all[...]), by_out)
    own = jnp.concatenate([dk[WINDOW:, :] * scaling, dv[WINDOW:, :]], axis=1)
    total = fold.total(own)
    grad = turn_back(total[:, :head], cosine, sine_table)
    dk_raw, dk_gain = normed_gradient(k_ref[...], k_gain, grad)
    dhead_out[1:2, :] = dk_gain
    dkv[:, :head] = dk_raw.astype(BF16)
    dkv[:, head:] = total[:, head:].astype(BF16)
    deal_kv = Deal(
        lambda other: dkv.at[:, columns_of(other, kv_part)],
        lambda mine: dkv_all.at[rows_of(mine, count)],
        kv_send,
        kv_recv,
    )
    deal_kv.start()
    dkv_all[here, :] = dkv[:, columns_of(me, kv_part)]
    wait_all(kv_loads)
    dxn = dx_out[...] + nt(dkv[...], wkv[...])
    by_value, dg0 = normed_gradient(x_ref[...].astype(F32), gains_ref[0:1, :], dxn)
    dx_out[...] = dh_ref[...] + by_value
    dgain_out[0:1, :] = dg0
    if layer == 0:
        zero = core == 0
        both_out[core] = jnp.where(zero, dx_out[...], dx_one_ref[...])
        dx_give[...] = jnp.where(zero, dx_one_ref[...], dx_out[...])
        dx_copy = pltpu.make_async_remote_copy(
            src_ref=dx_give,
            dst_ref=both_out.at[core],
            send_sem=dx_send,
            recv_sem=dx_recv,
            device_id={"section": 1 - core},
            device_id_type=MESH,
        )
        dx_copy.start()
    if lined:
        line.step(2, 0)
        for step in range(2, early.steps):
            early.step(step, 0)
    if layer == 0:
        own_total = sums.total.at[0]
        own_total[...] = block_ref[...]
        own_total[0:2, :] = dgain_out[...]
        own_total[4:5, :head] = dhead_out[0:1, :]
        own_total[4:5, head : 2 * head] = dhead_out[1:2, :]
        sums.start(0)

    deal_kv.here()
    by_kv = tn(xn[...], dkv_all[...])
    if layer == 0:
        sums.add(0)
        sums.start(1)
    exchange(1, pl.ds(head, kv_part), by_kv, jnp.zeros_like(by_kv))
    for copy in swaps:
        copy.wait_recv()
    ours[...] = (ours[...].astype(F32) + came[...].astype(F32)).astype(BF16)
    out = pltpu.make_async_copy(ours, dw_out, out_sem)
    out.start()
    if layer == 0:
        sums.add(1)
        sums.start(2)
    if lined:
        late.load()
        late.begin()
        for step in range(2, line.steps):
            if step > 2:
                line.step(step, 0)
            late.step(step - 1, 0)
            line.step(step, 1)
        early.end()
        crosses = [across(0, early.result, came_early)]
        crosses[0].start()
        late.step(late.steps - 1, 0)
        line.folds[0].finish(line.result)
        half = line.folds[0].columns
        crosses.append(across(1, line.result.at[:, half], came_line.at[:, half]))
        crosses[1].start()
        rest = line.folds[1].columns
        line.folds[1].finish(line.result)
        last = across(3, line.result.at[:, rest], came_line.at[:, rest])
        last.start()
        late.end()
        crosses.append(across(2, late.result, came_late))
        crosses[2].start()
        crosses[0].wait_recv()
        by_qkv = jnp.where(zero, late.result[...], came_early[...])
        kv_all[me] = by_qkv[:, head:]
        narrows = [
            remote(kv_all.at[me], kv_all.at[me], narrow_send.at[at], narrow_recv.at[at], other)
            for at, other in enumerate((nx, ny, far))
        ]
        start_all(narrows)
        q_out[...] = by_qkv[:, :head].astype(F32)
        crosses[2].wait_recv()
        o_out[...] = jnp.where(zero, came_late[:, :head], early.result[:, :head]).astype(F32)
        for copy in narrows:
            copy.wait_recv()
        for n in range(4):
            kv_out[:, n * kv_part : (n + 1) * kv_part] = kv_all[n].astype(F32)
        crosses.append(last)
        crosses[1].wait_recv()
        crosses[3].wait_recv()
        keep = pltpu.make_async_copy(came_line, came_out, came_store)
        keep.start()
        line.end(2)
        for copy in crosses + narrows:
            copy.wait_send()
        keep.wait()
    if layer == 0:
        dx_copy.wait_recv()
        dx_copy.wait_send()
    if layer == 0:
        sums.add(2)
        block_out[...] = sums.total[3]
        sums.close()
    spread.finish()
    fold.finish()
    deal_q.finish()
    deal_kv.finish()
    for copy in swaps:
        copy.wait_send()
    out.wait()


def attend_back(length, dh, a, x, gains, head_gains, trig, q_raw, k_raw, window, lse, pack, xn, o, deps, layer, collective_id):
    count, model = dh.shape
    head = k_raw.shape[1]
    width = q_raw.shape[1]
    kv_part = pack.shape[3] - 2 * head
    if layer == 0:
        wides = lax.axis_size("wide")
        block, dx_one, lined, early = deps
        rows = model // wides
    deal = pltpu.SemaphoreType.DMA((3,))
    dw = pltpu.VMEM((model, head + kv_part), BF16)
    return pl.pallas_call(
        functools.partial(attend_back_kernel, layer),
        out_shape=[
            jax.ShapeDtypeStruct((count, model), F32),
            jax.ShapeDtypeStruct((model, head + kv_part), BF16),
            jax.ShapeDtypeStruct((2, model), F32),
            jax.ShapeDtypeStruct((2, head), F32),
            *(
                [
                    jax.ShapeDtypeStruct(block.shape, F32),
                    jax.ShapeDtypeStruct((2, count, model), F32),
                    jax.ShapeDtypeStruct((rows, lined.shape[1]), BF16),
                    jax.ShapeDtypeStruct((rows, lined.shape[1]), BF16),
                    jax.ShapeDtypeStruct((rows, head), F32),
                    jax.ShapeDtypeStruct((rows, 4 * kv_part), F32),
                    jax.ShapeDtypeStruct((rows, head), F32),
                ]
                if layer == 0
                else []
            ),
        ],
        in_specs=[pl.BlockSpec(memory_space=pltpu.SMEM)] + [vmem_spec()] * 10 + [any_spec()] * 3 + ([vmem_spec()] * 2 + [any_spec()] * 2 if layer == 0 else []),
        out_specs=[vmem_spec(), any_spec(), vmem_spec(), vmem_spec()]
        + ([vmem_spec()] * 2 + [any_spec()] * 2 + [vmem_spec()] * 3 if layer == 0 else []),
        scratch_shapes=[
            pltpu.VMEM((4 * count, model), BF16),
            pltpu.VMEM((count, width), BF16),
            pltpu.VMEM((count, width), BF16),
            pltpu.VMEM((window.shape[0], head), F32),
            pltpu.VMEM((window.shape[0], head), F32),
            pltpu.VMEM((4 * count + WINDOW, 2 * head), BF16),
            pltpu.VMEM((4 * count, head), BF16),
            pltpu.VMEM((count, 2 * head), BF16),
            pltpu.VMEM((4 * count, kv_part), BF16),
            pltpu.VMEM((model, width), BF16),
            pltpu.VMEM((model, width), BF16),
            pltpu.VMEM((model, 2 * head), BF16),
            pltpu.VMEM(xn.shape, BF16),
            pltpu.VMEM(o.shape, BF16),
            dw,
            dw,
            dw,
            pltpu.SemaphoreType.DMA((3, 4)),
            pltpu.SemaphoreType.DMA((2,)),
            *spread_spec(),
            *fold_spec(count, 2 * head),
            deal,
            deal,
            deal,
            deal,
            pltpu.SemaphoreType.DMA((2,)),
            pltpu.SemaphoreType.DMA((2,)),
            pltpu.SemaphoreType.DMA,
            *(
                [
                    *gain_spec(wides, block.shape),
                    pltpu.VMEM((count, model), F32),
                    pltpu.SemaphoreType.DMA,
                    pltpu.SemaphoreType.DMA,
                ]
                if layer == 0
                else []
            ),
            *(
                [
                    *line_spec(wides, rows, lined.shape[1], 2),
                    *line_spec(wides, rows, head + kv_part, 1),
                    *line_spec(wides, rows, head + kv_part, 1),
                    pltpu.VMEM((rows, lined.shape[1]), BF16),
                    pltpu.SemaphoreType.DMA,
                    pltpu.VMEM((rows, head + kv_part), BF16),
                    pltpu.VMEM((rows, head + kv_part), BF16),
                    pltpu.VMEM((4, rows, kv_part), BF16),
                    pltpu.SemaphoreType.DMA((4,)),
                    pltpu.SemaphoreType.DMA((4,)),
                    pltpu.SemaphoreType.DMA((3,)),
                    pltpu.SemaphoreType.DMA((3,)),
                ]
                if layer == 0 and rows % 16 == 0
                else []
            ),
        ],
        compiler_params=params(collective_id, 60 if layer == 0 else 48),
    )(length, dh, a, x, gains, head_gains, trig, q_raw, k_raw, window, lse, pack, xn, o, *deps)


def after(value, *others):
    return pl.pallas_call(
        lambda *refs: None,
        out_shape=jax.ShapeDtypeStruct(value.shape, value.dtype),
        in_specs=[any_spec()] * (1 + len(others)),
        out_specs=any_spec(),
        input_output_aliases={0: 0},
    )(value, *others)


def scatter(member):
    return lax.psum_scatter(member, "wide", scatter_dimension=0, tiled=True)


def on_device(
    inputs, cotangent, lengths, norm_gains, head_gains, w_q, w_kv, w_o, w_gate_up, w_down
):
    core = lax.axis_index("section")
    narrow = lax.axis_index("narrow")
    n_narrow = lax.axis_size("narrow")
    is_zero = core == 0
    rows, model = inputs.shape[1], inputs.shape[2]
    block = w_q.shape[1]
    head_width = w_q.shape[2]
    n_wide = lax.axis_size("wide")
    hidden = w_down.shape[1]
    kv_part = w_kv.shape[2] // n_narrow

    def swap(value):
        return lax.ppermute(value, "section", [(0, 1), (1, 0)])

    def by_core(first, second):
        return jnp.where(is_zero, first, second)

    half = block // 2

    pad = -hidden % TILE
    kv_own = lax.dynamic_slice_in_dim(w_kv[0], narrow * kv_part, kv_part, 1)
    pack_width = 2 * head_width + kv_part
    pack = [w_q[0], w_o[0].T, kv_own]
    pack = jnp.concatenate(pack, axis=1)
    if block % 16 == 0:
        norm_rows = jnp.pad(norm_gains[0], ((0, 0), (0, pack_width - block)))
        head_rows = jnp.pad(head_gains[0], ((0, GAIN_ROWS - 6), (0, pack_width - head_width // n_wide)))
        pack = jnp.concatenate([pack, norm_rows, head_rows], axis=0)
    late = after(core.reshape(1), pack)[0]
    pack = lax.all_gather(pack, "wide", axis=0, tiled=True)

    def half_of(side):
        gate_up = lax.dynamic_slice_in_dim(w_gate_up[0], side * half, half, 0)
        gate_up = jnp.pad(gate_up, ((0, 0), (0, 0), (0, pad))).reshape(half, -1)
        down = lax.dynamic_slice_in_dim(w_down[0].T, side * half, half, 0)
        return jnp.concatenate([gate_up, jnp.pad(down, ((0, 0), (0, pad)))], axis=1)

    feed = trade(half_of(late), half_of(1 - late), 7)
    padded = hidden + pad

    def gather(member):
        return lax.all_gather(member, ("wide", "section"), axis=0, tiled=True)

    both = gather(feed[0])
    feeds = [
        (both, both, padded),
        (gather(feed[1][:, : 2 * padded]), gather(feed[1][:, 2 * padded :]), padded),
    ]
    packs, gain_packs = gather_pack(pack, model, n_wide, 6)
    if block % 16:
        norm_own = lax.all_gather(norm_gains[0], "wide", axis=1, tiled=True)
        head_own = lax.all_gather(head_gains[0], "wide", axis=1, tiled=True)
        norm_came, head_came = swap(norm_own), swap(head_own)

    def gains_of(section):
        if block % 16:
            mine = core == section
            norm_part = jnp.where(mine, norm_own, norm_came)
            head_part = jnp.where(mine, head_own, head_came)
        else:
            tail = gain_packs[section]
            norm_part = tail[:, :4, :block].transpose(1, 0, 2).reshape(4, model)
            head_part = tail[:, 4:6, : head_width // n_wide].transpose(1, 0, 2).reshape(2, head_width)
        return norm_part.astype(F32), head_part.astype(F32)

    start = narrow * rows
    positions = start + jnp.arange(rows, dtype=jnp.int32)
    trig = tables(positions, head_width)
    length = lax.dynamic_index_in_dim(lengths[:, 0], core, 0, keepdims=False)

    x = lax.dynamic_index_in_dim(inputs, core, 0, keepdims=False)
    length_one = length.reshape(1)
    outs, kept, gains = [], [], []
    for section in range(2):
        layer_gains, head_gain = gains_of(section)
        gains.append((layer_gains, head_gain))
        h, xn, q_raw, k_raw, window, lse, o, a, *shared = attend(
            length_one, x, layer_gains, head_gain, trig, packs, head_width, section, 8 + section
        )
        w_up, w_down, _ = feeds[section]
        mid_rows, gu, act = feed_up(h, layer_gains[2:3], w_up, padded, (), 10 + section)
        kept.append(((a, x, q_raw, k_raw, window, lse), (h, mid_rows, gu, act), shared))
        if section == 0:
            x, f = feed_down(h, layer_gains[3:4], act, w_down, 12)
            outs.append(x)

    def by_section(first, second):
        stays, came = by_core(first, second), swap(by_core(second, first))
        return jnp.stack([by_core(stays, came), by_core(came, stays)])

    real = (positions < length).astype(F32)[:, None]
    dy = lax.dynamic_index_in_dim(cotangent, core, 0, keepdims=False).astype(F32) * real
    dxs, gain_grads = [None, None], [None, None]
    up_sums, down_sums, attention_sums = [None, None], [None, None], [None, None]
    extra = None
    for section in (1, 0):
        kept_a, (h, mid_rows, gu, act), (xn, o) = kept[section]
        layer_gains, head_gain = gains[section]
        w_up, w_down, _ = feeds[section]
        if section:
            out, dgu, d_down, dg3 = feed_turn(h, layer_gains[3:4], dy, act, w_down, gu, 13)
            outs.append(out)
        else:
            dgu, d_down, dg3 = feed_back_up(
                dy, f, layer_gains[3:4], gu, act, w_down,
                (extra, down_sums[1]) if block % 16 else (down_sums[1],), 14,
            )
        down_sums[section] = scatter(d_down)
        dh, d_up, dg2 = feed_back_down(dy, h, layer_gains[2:3], dgu, mid_rows, w_up, 16 + section)
        if section or block % 16:
            up_sums[section] = scatter(d_up)
        a, x, q_raw, k_raw, window, lse = kept_a
        if section == 0:
            zeros = jnp.zeros((2, model), F32)
            gain_grads[0] = jnp.concatenate([zeros, dg2, dg3, zeros, zeros])
            section_out = by_section(*outs)
            lined = after(d_up, up_sums[1], section_out)
            deps = (jnp.concatenate(gain_grads), dxs[1], lined, extra)
        dx, extra, dg01, dhead, *more = attend_back(
            length_one, dh, a, x, layer_gains, head_gain, trig, q_raw, k_raw, window, lse, packs, xn, o,
            () if section else deps, section, 18 + section,
        )
        dxs[section] = dx
        if section:
            head_row = jnp.pad(dhead.reshape(1, -1), ((0, 0), (0, model - dhead.size)))
            gain_grads[1] = jnp.concatenate([dg01, dg2, dg3, head_row, jnp.zeros((3, model), F32)])
        else:
            gain_sums, input_grad, up_lined, came_up, grad_q, grad_kv, grad_o = more
            if block % 16 == 0:
                up_sums[0] = up_lined
            else:
                came_up = swap(up_sums[0])
        dy = dx
    if block % 16:
        split = down_sums[1].shape[1]
        attention_sums = (scatter(extra), down_sums[0][:, split:])
        down_sums[0] = down_sums[0][:, :split]
        grad_q, grad_kv, grad_o = finish_attention(
            *attention_sums, swap(attention_sums[1]), up_sums[0], head_width, 2
        )
    grad_o = grad_o.T
    down_sums[0] = after(down_sums[0], gain_sums)
    grad_gate_up, grad_down = pair_up(
        *up_sums, came_up, swap(up_sums[1]), *down_sums, swap(by_core(down_sums[1], down_sums[0])), hidden
    )
    grad_down = grad_down.T
    gain_sums = lax.dynamic_slice_in_dim(gain_sums, core * 8, 8, 0)
    wide = lax.axis_index("wide")
    grad_norm = lax.dynamic_slice_in_dim(gain_sums[:4], wide * block, block, 1)
    grad_head = gain_sums[4, : 2 * head_width].reshape(2, head_width)
    head_block = head_width // n_wide
    grad_head = lax.dynamic_slice_in_dim(grad_head, wide * head_block, head_block, 1)

    return (
        section_out[None],
        input_grad[None],
        grad_norm[None],
        grad_head[None],
        grad_q[None],
        grad_kv[None],
        grad_o[None],
        grad_gate_up[None],
        grad_down[None],
    )


def solution(mesh):
    return jax.shard_map(
        on_device,
        mesh=mesh,
        in_specs=(
            P(None, ("wide", "narrow"), None),
            P(None, ("wide", "narrow"), None),
            P(None, "wide"),
            P("section", None, "wide"),
            P("section", None, "wide"),
            P("section", "wide", "narrow"),
            P("section", "wide", None),
            P("section", "narrow", "wide"),
            P("section", "wide", None, "narrow"),
            P("section", "narrow", "wide"),
        ),
        out_specs=(
            P("section", None, ("wide", "narrow"), None),
            P("section", None, ("wide", "narrow"), None),
            P("section", None, "wide"),
            P("section", None, "wide"),
            P("section", "wide", "narrow"),
            P("section", "wide", None),
            P("section", "narrow", "wide"),
            P("section", "wide", None, "narrow"),
            P("section", "narrow", "wide"),
        ),
        check_vma=False,
    )
```
